32 devices in a mesh: rows: 16 (over z, x, core), tp: 2 (over y).
Axes of the slice: x: 2, y: 2, z: 4, core: 2. Of those that a mesh axis runs over, the one named last changes fastest.
Arguments:
- section_rows: bfloat16 [51200, 1024], P(('rows', 'tp')), may hold values from -100 to 100
- window_mask: int32 [51200], P('rows'), may hold values from 0 to 1, as said below
- cotangent: bfloat16 [51200, 512], P(('rows', 'tp')), may hold values from -6 to 6
- merge_weight: bfloat16 [1024, 512], P('tp'), may hold values from -0.1875 to 0.1875
- merge_gain: bfloat16 [1024], P('tp'), may hold values from 0.099609375 to 1.8984375
- merge_bias: bfloat16 [1024], P('tp'), may hold values from -3 to 3
- norm1_gain: float32 [512], replicated, may hold values from 0.1 to 1.9
- norm1_bias: float32 [512], replicated, may hold values from -3 to 3
- qkv_weight: bfloat16 [3, 512, 512], P(None, None, 'tp'), may hold values from -0.25 to 0.25
- qv_bias: float32 [2, 512], P(None, 'tp'), may hold values from -3 to 3
- bias_table: float32 [361, 16], P(None, 'tp'), may hold values from -4 to 4
- proj_weight: bfloat16 [512, 512], P('tp'), may hold values from -1 to 1
- proj_bias: float32 [512], replicated, may hold values from -3 to 3
- norm2_gain: float32 [512], replicated, may hold values from 0.1 to 1.9
- norm2_bias: float32 [512], replicated, may hold values from -3 to 3
- up_weight: bfloat16 [512, 2048], P(None, 'tp'), may hold values from -0.25 to 0.25
- up_bias: float32 [2048], P('tp'), may hold values from -3 to 3
- down_weight: bfloat16 [2048, 512], P('tp'), may hold values from -0.125 to 0.125
- down_bias: float32 [512], replicated, may hold values from -3 to 3
Outputs:
- block_out: bfloat16 [51200, 512], P(('rows', 'tp'))
- section_rows_grad: bfloat16 [51200, 1024], P(('rows', 'tp'))
- merge_weight_grad: float32 [1024, 512], P('tp')
- merge_gain_grad: float32 [1024], P('tp')
- merge_bias_grad: float32 [1024], P('tp')
- norm1_gain_grad: float32 [512], replicated
- norm1_bias_grad: float32 [512], replicated
- qkv_weight_grad: float32 [3, 512, 512], P(None, None, 'tp')
- qv_bias_grad: float32 [2, 512], P(None, 'tp')
- bias_table_grad: float32 [361, 16], P(None, 'tp')
- proj_weight_grad: float32 [512, 512], P('tp')
- proj_bias_grad: float32 [512], replicated
- norm2_gain_grad: float32 [512], replicated
- norm2_bias_grad: float32 [512], replicated
- up_weight_grad: float32 [512, 2048], P(None, 'tp')
- up_bias_grad: float32 [2048], P('tp')
- down_weight_grad: float32 [2048, 512], P('tp')
- down_bias_grad: float32 [512], replicated
The draws below stay inside these ranges and needn't reach their ends.
Inputs may be any that keep to these rules, and one draw needn't show every extreme that they name: `window_mask`: 1 marks a real patch; in every window of 10 x 10 patches the padded patches fill whole trailing columns, and a window may be padded throughout.
All inputs are finite; a program needn't handle non-finite values.
Results may differ from the reference program's by a relative error of at most 0.019.
Values may be sent and summed in bfloat16 or wider, within the bound.
No kernel may reach another device: no remote copies, remote signals or barrier semaphores. Data moves between devices by JAX's collectives and lax.ppermute only.
A program may use at most 256 MiB of HBM per device.

```python
import math
import jax
import jax.numpy as jnp
from jax import lax

C2 = 256
MERGE_IN = 1024
D = 512
HEADS = 16
HEAD_DIM = 32
FFN = 2048
WINDOW = 10
TABLE = 361
WINDOWS = 512
TOKENS = 51200


def draw_section_rows(key, part):
    key = jax.random.fold_in(key, 11)
    subkeys = jax.random.split(key, 3)
    ramp = jnp.exp(jnp.linspace(-0.55, 0.55, 4 * C2))
    col_scale = ramp * jnp.exp(jax.random.uniform(subkeys[0], (4 * C2,), minval=-1.15, maxval=1.15))
    row_scale = jnp.exp(jax.random.uniform(subkeys[1], (TOKENS, 1), minval=-1.15, maxval=1.15))
    jitter = jnp.clip(jax.random.normal(subkeys[2], (TOKENS, 4 * C2)), -4.0, 4.0)
    values = row_scale * jitter * col_scale
    return values.astype(jnp.bfloat16)


def draw_window_mask(key, part):
    key = jax.random.fold_in(key, 7)
    padded = jnp.minimum(jax.random.randint(key, (WINDOWS, 1, 1), 0, 14), WINDOW)
    column = jnp.arange(WINDOW, dtype=jnp.int32)[None, None, :]
    filled = (column < WINDOW - padded).astype(jnp.int32)
    return jnp.broadcast_to(filled, (WINDOWS, WINDOW, WINDOW)).reshape(WINDOWS * WINDOW * WINDOW)


def shard_levels(rng, dims, cuts, least, largest):
    factor_of, own = 1.0, jax.random.fold_in(rng, 6)
    for dim, blocks in cuts:
        draws = jnp.exp(jax.random.uniform(jax.random.fold_in(own, dim), (blocks,), jnp.float32, least / len(cuts), largest / len(cuts)))
        factor_of = factor_of * jnp.repeat(draws, dims[dim] // blocks).reshape([-1 if axis == dim else 1 for axis in range(len(dims))])
    return factor_of


def gaussian(stream_key, dims, scale, most, cuts=(), kind=jnp.bfloat16):
    values = scale * jax.random.normal(stream_key, dims, jnp.float32)
    if cuts:
        values = values * shard_levels(stream_key, dims, cuts, -0.22, 0.18)
    return jnp.clip(values, -most, most).astype(kind)


def setup_inputs(seed: int = 0) -> dict:
    seeds = jax.random.split(jax.random.key(seed), 20)
    section_rows = draw_section_rows(jax.random.fold_in(seeds[19], 71), 0)
    window_mask = draw_window_mask(jax.random.fold_in(seeds[19], 71), 0)
    cotangent = gaussian(seeds[2], (TOKENS, D), 1.0, 6.0, ((0, 32),))
    merge_weight = gaussian(seeds[3], (MERGE_IN, D), MERGE_IN ** -0.5, 0.1875, ((0, 2),))
    merge_gain = jnp.clip(1.0 + 0.18 * jax.random.normal(seeds[4], (MERGE_IN,), jnp.float32), 0.099609375, 1.8984375).astype(jnp.bfloat16)
    merge_bias = gaussian(seeds[5], (MERGE_IN,), 0.3, 3.0, ((0, 2),))
    norm1_gain = jnp.clip(1.0 + 0.18 * jax.random.normal(seeds[6], (D,), jnp.float32), 0.1, 1.9)
    norm1_bias = gaussian(seeds[7], (D,), 0.3, 3.0, (), jnp.float32)
    qkv_weight = gaussian(seeds[8], (3, D, D), D ** -0.5, 0.25, ((2, 2),))
    qv_bias = gaussian(seeds[9], (2, D), 0.5, 3.0, ((1, 2),), jnp.float32)
    bias_table = gaussian(seeds[10], (TABLE, HEADS), 1.0, 4.0, ((1, 2),), jnp.float32)
    proj_weight = gaussian(seeds[11], (D, D), (D // 16) ** -0.5, 1.0, ((0, 2),))
    proj_bias = gaussian(seeds[12], (D,), 0.3, 3.0, (), jnp.float32)
    norm2_gain = jnp.clip(1.0 + 0.18 * jax.random.normal(seeds[13], (D,), jnp.float32), 0.1, 1.9)
    norm2_bias = gaussian(seeds[14], (D,), 0.3, 3.0, (), jnp.float32)
    up_weight = gaussian(seeds[15], (D, FFN), D ** -0.5, 0.25, ((1, 2),))
    up_bias = gaussian(seeds[16], (FFN,), 0.3, 3.0, ((0, 2),), jnp.float32)
    down_weight = gaussian(seeds[17], (FFN, D), FFN ** -0.5, 0.125, ((0, 2),))
    down_bias = gaussian(seeds[18], (D,), 0.3, 3.0, (), jnp.float32)
    return dict(section_rows=section_rows, window_mask=window_mask, cotangent=cotangent, merge_weight=merge_weight, merge_gain=merge_gain, merge_bias=merge_bias, norm1_gain=norm1_gain, norm1_bias=norm1_bias, qkv_weight=qkv_weight, qv_bias=qv_bias, bias_table=bias_table, proj_weight=proj_weight, proj_bias=proj_bias, norm2_gain=norm2_gain, norm2_bias=norm2_bias, up_weight=up_weight, up_bias=up_bias, down_weight=down_weight, down_bias=down_bias)


@jax.custom_vjp
def low(v):
    return lax.optimization_barrier(v.astype(jnp.bfloat16)).astype(jnp.float32)

@jax.custom_vjp
def low_back(v):
    return v

def low_keep(v):
    return (low(v), None)

def low_pass(kept, grad):
    return (grad,)

def back_keep(v):
    return (v, None)

def back_low(kept, grad):
    return (low(grad),)
low.defvjp(low_keep, low_pass)
low_back.defvjp(back_keep, back_low)
EPSILON = 1e-05
MASKED_SCORE = -1e+30
EXACT = lax.Precision.HIGHEST

def normalize(values):
    center = lax.optimization_barrier(jnp.mean(values, axis=-1, keepdims=True))
    spread = lax.optimization_barrier(jnp.mean(values * values, axis=-1, keepdims=True)) - center * center
    return (values - center) * lax.rsqrt(spread + EPSILON)

def matmul(operand, partner):
    return jnp.dot(operand, partner, precision=EXACT)

def table_lookup(bias_table):
    positions = jnp.arange(WINDOW * WINDOW, dtype=jnp.int32)
    row_place = positions // WINDOW
    col_place = positions % WINDOW
    offsets = (row_place[:, None] - row_place[None, :] + WINDOW - 1) * (2 * WINDOW - 1) + (col_place[:, None] - col_place[None, :] + WINDOW - 1)
    return jnp.transpose(bias_table[offsets.astype(jnp.int32)], (2, 0, 1))

def forward(section_rows, key_keep, params):
    merge_weight, merge_gain, merge_bias, norm1_gain, norm1_bias, qkv_weight, qv_bias, bias_table, proj_weight, proj_bias, norm2_gain, norm2_bias, up_weight, up_bias, down_weight, down_bias = params
    window_area = WINDOW * WINDOW
    row_total = section_rows.shape[0]
    window_count = row_total // window_area
    head_shape = (window_count, window_area, HEADS, HEAD_DIM)
    scaling = 1.0 / math.sqrt(HEAD_DIM)
    merged_in = low(normalize(section_rows) * merge_gain + merge_bias)
    merged = low_back(matmul(merged_in, merge_weight))
    normed_one = low(normalize(merged) * norm1_gain + norm1_bias)
    projected = jnp.einsum('td,cde->cte', normed_one, qkv_weight, precision=EXACT)
    queries = low(scaling * low_back(projected[0] + qv_bias[0]))
    attn_keys = low(low_back(projected[1]))
    attn_values = low(low_back(projected[2] + qv_bias[1]))
    scores = jnp.einsum('wihe,wjhe->whij', queries.reshape(head_shape), attn_keys.reshape(head_shape), precision=EXACT)
    scores = low_back(scores + table_lookup(bias_table)[None])
    scores = jnp.where(key_keep[:, None, None, :], scores, MASKED_SCORE)
    weights = low(jax.nn.softmax(scores, axis=-1))
    attended = jnp.einsum('whij,wjhe->wihe', weights, attn_values.reshape(head_shape), precision=EXACT)
    attended = low(low_back(attended.reshape(row_total, HEADS * HEAD_DIM)))
    residual = merged + low_back(matmul(attended, proj_weight)) + proj_bias
    second = low(normalize(residual) * norm2_gain + norm2_bias)
    raised = low_back(matmul(second, up_weight) + up_bias)
    active = low(jax.nn.gelu(raised, approximate=False))
    return residual + low_back(matmul(active, down_weight)) + down_bias

def reference(section_rows, window_mask, cotangent, merge_weight, merge_gain, merge_bias, norm1_gain, norm1_bias, qkv_weight, qv_bias, bias_table, proj_weight, proj_bias, norm2_gain, norm2_bias, up_weight, up_bias, down_weight, down_bias):
    window_area = WINDOW * WINDOW
    per_step = math.gcd(WINDOWS, 32)
    step_count = WINDOWS // per_step
    step_rows = per_step * window_area
    params = tuple((weight.astype(jnp.float32) for weight in (merge_weight, merge_gain, merge_bias, norm1_gain, norm1_bias, qkv_weight, qv_bias, bias_table, proj_weight, proj_bias, norm2_gain, norm2_bias, up_weight, up_bias, down_weight, down_bias)))
    patch_mask = window_mask.reshape(WINDOWS, window_area) > 0
    blank_win = jnp.logical_not(jnp.any(patch_mask, axis=1))
    key_keep = jnp.logical_or(patch_mask, blank_win[:, None])
    live_rows = jnp.broadcast_to(1.0 - blank_win.astype(jnp.float32)[:, None], (WINDOWS, window_area)).reshape(TOKENS)
    stacked = (section_rows.astype(jnp.float32).reshape(step_count, step_rows, 4 * C2), key_keep.reshape(step_count, per_step, window_area), (cotangent.astype(jnp.float32) * live_rows[:, None]).reshape(step_count, step_rows, D))

    def one_step(totals, pieces):
        rows_in, keep_in, grad_in = pieces

        def local_layer(values, weights):
            return forward(values, keep_in, weights)
        result, pullback = jax.vjp(local_layer, rows_in, params)
        grad_rows, grad_params = pullback(grad_in)
        totals = jax.tree.map(lambda total, extra: total + extra, totals, grad_params)
        return (totals, (result.astype(jnp.bfloat16), grad_rows.astype(jnp.bfloat16)))
    zeros = jax.tree.map(jnp.zeros_like, params)
    totals, (outputs, row_grads) = lax.scan(one_step, zeros, stacked)
    return (outputs.reshape(TOKENS, D), row_grads.reshape(TOKENS, 4 * C2), totals[0], totals[1], totals[2], totals[3], totals[4], totals[5], totals[6], totals[7], totals[8], totals[9], totals[10], totals[11], totals[12], totals[13], totals[14], totals[15])
```

```python
from functools import partial
import math

import jax
import jax.numpy as jnp
from jax import lax
from jax.experimental import pallas as pl
from jax.experimental.pallas import tpu as pltpu
from jax.sharding import PartitionSpec as P

MERGE_IN = 1024
D = 512
HEADS = 16
HEAD_DIM = 32
FFN = 2048
WINDOW = 10
AREA = WINDOW * WINDOW
SIDE = 2 * WINDOW - 1
EPSILON = 1e-05
MASKED_SCORE = -1e30
EXACT = lax.Precision.HIGHEST
SCALING = 1.0 / math.sqrt(HEAD_DIM)
GROUP = 4
ROWS = GROUP * AREA
KEYS = 112
QUERIES = 128
QUADS = 4
QUAD = 4 * HEAD_DIM
LANES = 4 * QUERIES
VMEM_LIMIT = 60 * 1024 * 1024

bf16 = jnp.bfloat16
f32 = jnp.float32


def mm(a, b):
    return jnp.dot(a, b, preferred_element_type=f32)


def mm_t(a, b):
    return lax.dot_general(a, b, (((1,), (1,)), ((), ())), preferred_element_type=f32)


def t_mm(a, b):
    return lax.dot_general(a, b, (((0,), (0,)), ((), ())), preferred_element_type=f32)


def normalize(values):
    center = jnp.mean(values, axis=-1, keepdims=True)
    spread = jnp.mean(values * values, axis=-1, keepdims=True) - center * center
    inverse = lax.rsqrt(spread + EPSILON)
    return (values - center) * inverse, inverse


def norm_back(grad_hat, normed, inverse):
    first_mean = jnp.mean(grad_hat, axis=-1, keepdims=True)
    second_mean = jnp.mean(grad_hat * normed, axis=-1, keepdims=True)
    return inverse * (grad_hat - first_mean - normed * second_mean)


def column_sum(values):
    return jnp.sum(values, axis=0, keepdims=True)


def head_masks():
    lane = lax.broadcasted_iota(jnp.int32, (1, QUAD), 1) // HEAD_DIM
    return [(lane == head).astype(f32).astype(bf16) for head in range(4)]


def spread_heads(rows, masks):
    return jnp.concatenate([rows * mask for mask in masks], axis=0)


def kernel_call(body, grid, in_specs, out_specs, out_shape, scratch=(), flops=0, moved=0):
    return pl.pallas_call(
        body,
        grid=grid,
        in_specs=in_specs,
        out_specs=out_specs,
        out_shape=out_shape,
        scratch_shapes=list(scratch),
        compiler_params=pltpu.CompilerParams(
            dimension_semantics=("arbitrary",) * len(grid), vmem_limit_bytes=VMEM_LIMIT
        ),
        cost_estimate=pl.CostEstimate(flops=flops, bytes_accessed=moved, transcendentals=0),
    )


def whole(shape):
    return pl.BlockSpec(shape, lambda *_: (0,) * len(shape), pipeline_mode=pl.Buffered(1))


def by_rows(rows, columns):
    return pl.BlockSpec((rows, columns), lambda i: (i, 0))


def by_windows(shape):
    return pl.BlockSpec((GROUP,) + shape, lambda i: (i,) + (0,) * len(shape))


SCALARS = pl.BlockSpec(memory_space=pltpu.SMEM)
FEED_PACK = 1152
LAST_PACK = 768
PIECES = 8


def shape_of(shape, dtype):
    return jax.ShapeDtypeStruct(shape, dtype)


def section_norm_body(rows_ref, hat_ref, inverse_ref):
    hat, inverse = normalize(rows_ref[...].astype(f32))
    hat_ref[...] = hat.astype(bf16)
    inverse_ref[...] = inverse


def section_norm(rows):
    count = rows.shape[0]
    return kernel_call(
        section_norm_body,
        (count // ROWS,),
        [by_rows(ROWS, MERGE_IN)],
        [by_rows(ROWS, MERGE_IN), by_rows(ROWS, 1)],
        [shape_of((count, MERGE_IN), bf16), shape_of((count, 1), f32)],
        flops=10 * count * MERGE_IN,
        moved=4 * count * MERGE_IN,
    )(rows)


def attend_body(
    hat_ref, merge_ref, shift_ref, gain_ref, bias_ref, qkv_ref, qv_ref, place_ref, mask_ref,
    merged_ref, first_ref, qkv_out_ref, weights_ref, attended_ref,
    stage, mixed,
):
    merged = mm(hat_ref[...], merge_ref[...]) + shift_ref[...]
    merged_ref[...] = merged
    hat, _ = normalize(merged)
    first = hat * gain_ref[...] + bias_ref[...]
    first_ref[...] = first.astype(bf16)
    stage[pl.ds(0, ROWS), :] = first
    stage[pl.ds(ROWS, 32), :] = jnp.zeros((32, D), f32)
    padded = jnp.concatenate(
        [stage[pl.ds(AREA * w, QUERIES), :].astype(bf16) for w in range(GROUP)], axis=0
    )
    queries = (SCALING * (mm(padded, qkv_ref[0]) + qv_ref[0:1, :])).astype(bf16)
    keys = mm(padded, qkv_ref[1]).astype(bf16)
    values = (mm(padded, qkv_ref[2]) + qv_ref[1:2, :]).astype(bf16)
    for w in range(GROUP):
        block = slice(QUERIES * w, QUERIES * (w + 1))
        qkv_out_ref[w, :, 0:D] = queries[block]
        qkv_out_ref[w, :, D : 2 * D] = keys[block]
        qkv_out_ref[w, :, 2 * D :] = values[block]
    masks = head_masks()
    for w in range(GROUP):
        mask = mask_ref[w]
        for quad in range(QUADS):
            columns = slice(QUAD * quad, QUAD * (quad + 1))
            rows = QUERIES * w
            spread = spread_heads(queries[rows : rows + QUERIES, columns], masks)
            scores = mm_t(keys[rows : rows + KEYS, columns], spread) + place_ref[quad] + mask
            raised = jnp.exp(scores - jnp.max(scores, axis=0, keepdims=True))
            weights = (raised * (1.0 / jnp.sum(raised, axis=0, keepdims=True))).astype(bf16)
            weights_ref[w, quad] = weights
            turned = values[rows : rows + QUERIES, columns].T[:, :KEYS]
            parts = []
            for pair in range(2):
                both = mm(turned[64 * pair : 64 * pair + 64], weights[:, 256 * pair : 256 * pair + 256])
                parts += [both[0:32, 0:128], both[32:64, 128:256]]
            mixed[pl.ds(AREA * w, AREA), columns] = jnp.concatenate(parts, axis=0).T[0:AREA]
    attended_ref[...] = mixed[...].astype(bf16)


def attend(hat, merge, shift, gain, bias, qkv, qv, place, mask):
    count = hat.shape[0]
    windows = count // AREA
    return kernel_call(
        attend_body,
        (count // ROWS,),
        [
            by_rows(ROWS, MERGE_IN), whole((MERGE_IN, D)), whole((1, D)), whole((1, D)), whole((1, D)),
            whole((3, D, D)), whole((2, D)), whole((QUADS, KEYS, LANES)), by_windows((KEYS, 1)),
        ],
        [
            by_rows(ROWS, D), by_rows(ROWS, D), by_windows((QUERIES, 3 * D)),
            by_windows((QUADS, KEYS, LANES)), by_rows(ROWS, D),
        ],
        [
            shape_of((count, D), f32), shape_of((count, D), bf16),
            shape_of((windows, QUERIES, 3 * D), bf16),
            shape_of((windows, QUADS, KEYS, LANES), bf16), shape_of((count, D), bf16),
        ],
        [pltpu.VMEM((ROWS + 32, D), f32), pltpu.VMEM((ROWS, D), f32)],
        flops=2 * count * D * (MERGE_IN + 3 * D + 4 * AREA),
        moved=count * 20 * D + windows * QUADS * KEYS * LANES * 2,
    )(hat, merge, shift, gain, bias, qkv, qv, place, mask)


def gelu_parts(t):
    chance = 0.5 * lax.erf(t * math.sqrt(0.5)) + 0.5
    density = jnp.exp(t * t * -0.5) * (1.0 / math.sqrt(2.0 * math.pi))
    return t * chance, chance + t * density


TILE = 512


def feed_body(
    place, attended_ref, merged_ref, cotangent_ref, live_ref, proj_ref, rows_ref, up_ref, up_bias_ref, down_ref,
    out_ref, grad_residual_ref, grad_attn_ref, send_ref, keep_ref, vectors_ref, up_vector_ref,
    active_s, raise_s, second_s, branch_s, attended_s, attn_s,
):
    step = pl.program_id(0)
    here = pl.ds(pl.multiple_of(step * ROWS, 16), ROWS)

    @pl.when(step == 0)
    def _():
        vectors_ref[...] = jnp.zeros_like(vectors_ref)
        up_vector_ref[...] = jnp.zeros_like(up_vector_ref)

    attended = attended_ref[...]
    residual = merged_ref[...] + mm(attended, proj_ref[...]) + rows_ref[0:1, :]
    hat, inverse = normalize(residual)
    second = (hat * rows_ref[1:2, :] + rows_ref[2:3, :]).astype(bf16)
    grad_out = cotangent_ref[...].astype(f32) * live_ref[...]
    branch = grad_out.astype(bf16)
    total = residual + rows_ref[3:4, :]
    grad_second = jnp.zeros((ROWS, D), f32)
    for tile in range(FFN // TILE):
        columns = slice(TILE * tile, TILE * (tile + 1))
        up = up_ref[:, columns]
        down = down_ref[columns, :]
        raised = mm(second, up) + up_bias_ref[:, columns]
        value, slope = gelu_parts(raised)
        active = value.astype(bf16)
        grad_raised = (mm_t(branch, down) * slope).astype(bf16)
        total += mm(active, down)
        grad_second += mm_t(grad_raised, up)
        active_s[here, columns] = active
        raise_s[here, columns] = grad_raised
        up_vector_ref[:, columns] += column_sum(grad_raised.astype(f32))
    out_ref[...] = total.astype(bf16)
    grad_residual = grad_out + norm_back(grad_second * rows_ref[1:2, :], hat, inverse)
    grad_residual_ref[...] = grad_residual
    attn = grad_residual.astype(bf16)
    grad_attn_ref[...] = attn
    vectors_ref[0:1, :] += column_sum(grad_residual)
    vectors_ref[1:2, :] += column_sum(grad_second * hat)
    vectors_ref[2:3, :] += column_sum(grad_second)
    vectors_ref[3:4, :] += column_sum(grad_out)
    second_s[here, :] = second
    branch_s[here, :] = branch
    attended_s[here, :] = attended
    attn_s[here, :] = attn

    @pl.when(step == pl.num_programs(0) - 1)
    def _():
        core, tp = place[0], place[3]
        for target, half in ((send_ref, 1 - core), (keep_ref, core)):
            for other in range(2):
                shard = 2 * jnp.where(other == 0, tp, 1 - tp) + half
                wide = pl.ds(pl.multiple_of(512 * shard, 512), 512)
                narrow = pl.ds(pl.multiple_of(128 * shard, 128), 128)
                base = FEED_PACK * other
                target[base : base + 512, :] = t_mm(active_s[:, wide], branch_s[...]).astype(bf16)
                target[base + 512 : base + 1024, :] = t_mm(second_s[...], raise_s[:, wide]).astype(bf16)
                target[base + 1024 : base + 1152, :] = t_mm(attended_s[:, narrow], attn_s[...]).astype(bf16)


def feed(place, attended, merged, cotangent, live, proj, rows, up, up_bias, down):
    count = attended.shape[0]
    return kernel_call(
        feed_body,
        (count // ROWS,),
        [
            SCALARS, by_rows(ROWS, D), by_rows(ROWS, D), by_rows(ROWS, D), by_rows(ROWS, 1), whole((D, D)), whole((4, D)),
            whole((D, FFN)), whole((1, FFN)), whole((FFN, D)),
        ],
        [
            by_rows(ROWS, D), by_rows(ROWS, D), by_rows(ROWS, D),
            whole((2 * FEED_PACK, D)), whole((2 * FEED_PACK, D)), whole((4, D)), whole((1, FFN)),
        ],
        [
            shape_of((count, D), bf16), shape_of((count, D), f32), shape_of((count, D), bf16),
            shape_of((2 * FEED_PACK, D), bf16), shape_of((2 * FEED_PACK, D), bf16),
            shape_of((4, D), f32), shape_of((1, FFN), f32),
        ],
        [
            pltpu.VMEM((count, FFN), bf16), pltpu.VMEM((count, FFN), bf16), pltpu.VMEM((count, D), bf16),
            pltpu.VMEM((count, D), bf16), pltpu.VMEM((count, D), bf16), pltpu.VMEM((count, D), bf16),
        ],
        flops=2 * count * D * (6 * FFN + 2 * D),
        moved=count * 18 * D + 20 * D * FFN,
    )(place, attended, merged, cotangent, live, proj, rows, up, up_bias, down)


def attend_back_body(
    place, attn_ref, grad_residual_ref, merged_ref, first_ref, hat_ref, qkv_in_ref, weights_ref,
    proj_ref, qkv_ref, rows_ref, merge_ref, gain_ref, bias_ref, feed_vectors_ref, up_vector_ref,
    low_ref, send_ref, keep_ref,
    stage, grads, stack_s, first_s, low_s, hat_s, vectors_ref, qv_ref, place_ref, fold_s, all_s, pack_s,
):
    step = pl.program_id(0)
    here = pl.ds(pl.multiple_of(step * ROWS, 16), ROWS)

    @pl.when(step == 0)
    def _():
        vectors_ref[...] = jnp.zeros_like(vectors_ref)
        qv_ref[...] = jnp.zeros_like(qv_ref)
        place_ref[...] = jnp.zeros_like(place_ref)

    stage[pl.ds(0, ROWS), :] = attn_ref[...].astype(f32)
    stage[pl.ds(ROWS, 32), :] = jnp.zeros((32, D), f32)
    real = lax.broadcasted_iota(jnp.int32, (QUERIES, 1), 0) < AREA
    padded = jnp.concatenate(
        [jnp.where(real, stage[pl.ds(AREA * w, QUERIES), :], 0.0).astype(bf16) for w in range(GROUP)], axis=0
    )
    grad_attended = mm_t(padded, proj_ref[...]).astype(bf16)
    masks = head_masks()
    for quad in range(QUADS):
        columns = slice(QUAD * quad, QUAD * (quad + 1))
        total_place = place_ref[quad]
        for w in range(GROUP):
            rows = QUERIES * w
            queries = qkv_in_ref[w, :, QUAD * quad : QUAD * (quad + 1)]
            keys = qkv_in_ref[w, :, D + QUAD * quad : D + QUAD * (quad + 1)]
            values = qkv_in_ref[w, 0:KEYS, 2 * D + QUAD * quad : 2 * D + QUAD * (quad + 1)]
            spread_grad = spread_heads(grad_attended[rows : rows + QUERIES, columns], masks)
            spread = spread_heads(queries, masks)
            weights = weights_ref[w, quad]
            grad_probs = mm_t(values, spread_grad)
            probs = weights.astype(f32)
            product = probs * grad_probs
            grad_scores = (product - probs * jnp.sum(product, axis=0, keepdims=True)).astype(bf16)
            total_place += grad_scores.astype(f32)
            grad_values = mm(weights, spread_grad)
            grad_keys = mm(grad_scores, spread)
            turned = keys.T[:, :KEYS]
            parts = []
            for pair in range(2):
                both = mm(
                    turned[64 * pair : 64 * pair + 64], grad_scores[:, 256 * pair : 256 * pair + 256]
                )
                parts += [both[0:32, 0:128], both[32:64, 128:256]]
            grad_queries = jnp.concatenate(parts, axis=0).T * SCALING
            to = pl.ds(AREA * w, AREA)
            grads[to, QUAD * quad : QUAD * (quad + 1)] = grad_queries[0:AREA]
            grads[to, D + QUAD * quad : D + QUAD * (quad + 1)] = grad_keys[0:AREA]
            grads[to, 2 * D + QUAD * quad : 2 * D + QUAD * (quad + 1)] = grad_values[0:AREA]
        place_ref[quad] = total_place
    stack = grads[...].astype(bf16)
    qv_ref[...] += column_sum(stack.astype(f32))
    grad_first = (
        mm_t(stack[:, 0:D], qkv_ref[0]) + mm_t(stack[:, D : 2 * D], qkv_ref[1]) + mm_t(stack[:, 2 * D :], qkv_ref[2])
    )
    normed, inverse = normalize(merged_ref[...])
    grad_merged = grad_residual_ref[...] + norm_back(grad_first * rows_ref[0:1, :], normed, inverse)
    low = grad_merged.astype(bf16)
    low_ref[...] = low
    vectors_ref[0:1, :] += column_sum(grad_first * normed)
    vectors_ref[1:2, :] += column_sum(grad_first)
    vectors_ref[2:3, :] += column_sum(low.astype(f32))
    stack_s[here, :] = stack
    first_s[here, :] = first_ref[...]
    low_s[here, :] = low
    hat_s[here, :] = hat_ref[...]

    @pl.when(step == pl.num_programs(0) - 1)
    def _():
        core, tp = place[0], place[3]
        total = vectors_ref[2:3, :]
        high = total.astype(bf16)
        rest = (total - high.astype(f32)).astype(bf16)
        sums = jnp.concatenate([high, rest, jnp.zeros((14, D), bf16)], axis=0)
        ones = jnp.ones((16, D), bf16)
        all_s[...] = jnp.zeros_like(all_s)
        all_s[0:2, :] = vectors_ref[0:2, :]
        all_s[2:6, :] = feed_vectors_ref[...]
        all_s[6:7, :] = qv_ref[:, 0:D]
        all_s[7:8, :] = qv_ref[:, 2 * D :]
        for part in range(4):
            all_s[8 + part : 9 + part, :] = up_vector_ref[:, D * part : D * (part + 1)]
        all_s[16:32, 0:384] = fold_place(place_ref, fold_s)
        for target, half in ((send_ref, 1 - core), (keep_ref, core)):
            for other in range(2):
                shard = jnp.where(other == 0, tp, 1 - tp)
                rows = pl.ds(pl.multiple_of(256 * half, 256), 256)
                for part in range(3):
                    columns = pl.ds(pl.multiple_of(D * part + 256 * shard, 256), 256)
                    block = t_mm(first_s[:, rows], stack_s[:, columns]).astype(bf16)
                    if part < 2:
                        pack_s[0:256, 256 * part : 256 * part + 256] = block
                    else:
                        pack_s[256:384, 0:256] = block[0:128]
                        pack_s[256:384, 256:512] = block[128:256]
                begin = pl.multiple_of(512 * shard + 256 * half, 256)
                rows = pl.ds(begin, 256)
                raw = t_mm(hat_s[:, rows], low_s[...])
                pack_s[384:640, :] = (raw * gain_ref[rows, :] + bias_ref[rows, :] * total).astype(bf16)
                merge = merge_ref[rows, :]
                scaled = raw * merge.astype(f32)
                scaled_high = scaled.astype(bf16)
                scaled_rest = (scaled - scaled_high.astype(f32)).astype(bf16)
                line = pl.ds(shard, 1)
                to = pl.ds(pl.multiple_of(256 * half, 256), 256)
                all_s[pl.ds(12 + shard, 1), to] = (mm_t(ones, scaled_high) + mm_t(ones, scaled_rest))[0:1]
                all_s[pl.ds(14 + shard, 1), to] = column_sum(mm_t(sums, merge))
                for piece in range(PIECES):
                    begin = LAST_PACK * other + 96 * piece
                    target[begin : begin + 80, :] = pack_s[80 * piece : 80 * piece + 80, :]
        for target, half in ((send_ref, 1 - core), (keep_ref, core)):
            for piece in range(PIECES):
                if piece < 2:
                    rows = all_s[pl.ds(pl.multiple_of(16 * half + 8 * piece, 8), 8), :]
                    high = rows.astype(bf16)
                    rest = rows - high.astype(f32)
                    block = jnp.concatenate([high.astype(f32), rest], axis=0).astype(bf16)
                else:
                    block = jnp.zeros((16, D), bf16)
                for other in range(2):
                    begin = LAST_PACK * other + 96 * piece + 80
                    target[begin : begin + 16, :] = block


def attend_back(place, attn, grad_residual, merged, first, hat, qkv_in, weights, proj, qkv, rows, merge, gain, bias, vectors, up_vector):
    count = attn.shape[0]
    return kernel_call(
        attend_back_body,
        (count // ROWS,),
        [
            SCALARS, by_rows(ROWS, D), by_rows(ROWS, D), by_rows(ROWS, D), by_rows(ROWS, D), by_rows(ROWS, MERGE_IN),
            by_windows((QUERIES, 3 * D)), by_windows((QUADS, KEYS, LANES)),
            whole((D, D)), whole((3, D, D)), whole((1, D)), whole((MERGE_IN, D)), whole((MERGE_IN, 1)), whole((MERGE_IN, 1)),
            whole((4, D)), whole((1, FFN)),
        ],
        [by_rows(ROWS, D), whole((2 * LAST_PACK, D)), whole((2 * LAST_PACK, D))],
        [shape_of((count, D), bf16), shape_of((2 * LAST_PACK, D), bf16), shape_of((2 * LAST_PACK, D), bf16)],
        [
            pltpu.VMEM((ROWS + 32, D), f32), pltpu.VMEM((ROWS, 3 * D), f32), pltpu.VMEM((count, 3 * D), bf16),
            pltpu.VMEM((count, D), bf16), pltpu.VMEM((count, D), bf16), pltpu.VMEM((count, MERGE_IN), bf16),
            pltpu.VMEM((3, D), f32), pltpu.VMEM((1, 3 * D), f32), pltpu.VMEM((QUADS, KEYS, LANES), f32),
            pltpu.VMEM((KEYS, 256), f32), pltpu.VMEM((32, D), f32), pltpu.VMEM((640, D), bf16),
        ],
        flops=2 * count * D * (7 * D + MERGE_IN + 10 * AREA),
        moved=count * 26 * D + count // AREA * QUADS * KEYS * LANES * 2,
    )(place, attn, grad_residual, merged, first, hat, qkv_in, weights, proj, qkv, rows, merge, gain, bias, vectors, up_vector)


def section_back_body(low_ref, hat_ref, inverse_ref, merge_ref, out_ref):
    scaled = mm_t(low_ref[...], merge_ref[...])
    out_ref[...] = norm_back(scaled, hat_ref[...].astype(f32), inverse_ref[...]).astype(bf16)


def section_back(low, hat, inverse, merge):
    count = low.shape[0]
    return kernel_call(
        section_back_body,
        (count // ROWS,),
        [by_rows(ROWS, D), by_rows(ROWS, MERGE_IN), by_rows(ROWS, 1), whole((MERGE_IN, D))],
        by_rows(ROWS, MERGE_IN),
        shape_of((count, MERGE_IN), bf16),
        flops=2 * count * D * MERGE_IN,
        moved=count * 5 * MERGE_IN,
    )(low, hat, inverse, merge)


def spread_matrix():
    place = lax.broadcasted_iota(jnp.int32, (QUERIES, 256), 0)
    lane = lax.broadcasted_iota(jnp.int32, (QUERIES, 256), 1)
    target = place + (SIDE - WINDOW) * (place // WINDOW)
    return jnp.logical_and(lane == target, place < AREA).astype(f32)


def expand_body(table_ref, place_ref, stage):
    spread = spread_matrix().astype(bf16)
    stage[...] = jnp.zeros_like(stage)
    for head in range(HEADS):
        line = table_ref[head : head + 1, :]
        lines = jnp.concatenate(
            [pltpu.roll(line, (384 - (WINDOW - 1) * (SIDE + 1) + x) % 384, 1) for x in range(WINDOW)]
            + [jnp.zeros((6, 384), f32)],
            axis=0,
        )
        for y in range(WINDOW):
            moved = pltpu.roll(lines, SIDE * y, 1) if y else lines
            stage[pl.ds(WINDOW * y, WINDOW), :] = moved[0:WINDOW, 0:256]
        rows = stage[...]
        high = rows.astype(bf16)
        rest = rows - high.astype(f32)
        middle = rest.astype(bf16)
        low = (rest - middle.astype(f32)).astype(bf16)
        block = mm_t(high, spread) + mm_t(middle, spread) + mm_t(low, spread)
        place_ref[head // 4, :, QUERIES * (head % 4) : QUERIES * (head % 4 + 1)] = block


def expand(table):
    return kernel_call(
        expand_body,
        (1,),
        [whole((HEADS, 384))],
        whole((QUADS, KEYS, LANES)),
        shape_of((QUADS, KEYS, LANES), f32),
        [pltpu.VMEM((KEYS, 256), f32)],
    )(table)


def fold_place(place_ref, stage):
    spread = spread_matrix().astype(bf16)
    lines = []
    for head in range(HEADS):
        rows = place_ref[head // 4, :, QUERIES * (head % 4) : QUERIES * (head % 4 + 1)]
        high = rows.astype(bf16)
        rest = (rows - high.astype(f32)).astype(bf16)
        stage[...] = mm(high, spread) + mm(rest, spread)
        total = jnp.zeros((WINDOW, 384), f32)
        for y in range(WINDOW):
            part = jnp.concatenate(
                [stage[pl.ds(WINDOW * y, WINDOW), :], jnp.zeros((WINDOW, 128), f32)], axis=1
            )
            total += pltpu.roll(part, SIDE * (WINDOW - 1 - y), 1) if y < WINDOW - 1 else part
        line = total[WINDOW - 1 : WINDOW, :]
        for x in range(WINDOW - 1):
            line += pltpu.roll(total[x : x + 1, :], WINDOW - 1 - x, 1)
        lines.append(line)
    return jnp.concatenate(lines, axis=0)


def add_pieces(blocks, vectors):
    total = blocks[0].astype(f32)
    for block in blocks[1:]:
        total = total + block.astype(f32)
    if not vectors:
        return total.astype(bf16)
    rows = total.shape[0] - 16
    sums = total[rows : rows + 8] + total[rows + 8 :]
    high = sums.astype(bf16).astype(f32)
    return jnp.concatenate([total[:rows], high, sums - high], axis=0).astype(bf16)


def stage_call(body, outs, *operands):
    return pl.pallas_call(
        body,
        in_specs=[SCALARS] + [pl.BlockSpec(memory_space=pltpu.VMEM)] * (len(operands) - 1),
        out_specs=[pl.BlockSpec(memory_space=pltpu.VMEM)] * len(outs),
        out_shape=[shape_of((rows, D), bf16) for rows in outs],
        compiler_params=pltpu.CompilerParams(vmem_limit_bytes=VMEM_LIMIT),
    )(*operands)


def piece_at(ref, begin, rows):
    return ref[pl.ds(pl.multiple_of(begin, 16), rows), :]


def other_shard_body(vectors, rows, place, keep, received, out):
    for piece in range(PIECES):
        here = slice(PIECES * rows + rows * piece, PIECES * rows + rows * (piece + 1))
        out[rows * piece : rows * (piece + 1), :] = add_pieces([keep[here, :], received[here, :]], vectors)


def split_x_body(vectors, rows, half, place, keep, received, shard, send, kept):
    for target, side in ((send, 1 - place[1]), (kept, place[1])):
        for piece in range(half):
            begin = side * (half * rows) + piece * rows
            target[rows * piece : rows * (piece + 1), :] = add_pieces(
                [piece_at(ref, begin, rows) for ref in (keep, received, shard)], vectors
            )


def split_z_body(vectors, rows, along, place, kept, received, *outs):
    span = kept.shape[0] // along
    for step in range(along):
        for piece in range(span // rows):
            begin = (place[2] ^ step) * span + piece * rows
            outs[step][rows * piece : rows * (piece + 1), :] = add_pieces(
                [piece_at(ref, begin, rows) for ref in (kept, received)], vectors
            )


def join_z_body(vectors, rows, place, *refs):
    out = refs[-1]
    for piece in range(out.shape[0] // rows):
        here = slice(rows * piece, rows * (piece + 1))
        out[here, :] = add_pieces([ref[here, :] for ref in refs[:-1]], vectors)


def place_z_body(place, *refs):
    out = refs[-1]
    span = refs[0].shape[0]
    for step, ref in enumerate(refs[:-1]):
        out[pl.ds(pl.multiple_of((place[2] ^ step) * span, 16), span), :] = ref[...]


class Ring:
    def __init__(self, place, rows_size, tp_size):
        self.place = place
        self.rows_size = rows_size
        self.tp_size = tp_size
        self.along = rows_size // 4

    def to(self, array, bits):
        return lax.ppermute(array, "rows", [(i, i ^ bits) for i in range(self.rows_size)])

    def core(self, array):
        return self.to(array, 1)

    def x(self, array):
        return self.to(array, 2)

    def z(self, array, step):
        return self.to(array, 4 * step)

    def y(self, array):
        return lax.ppermute(array, "tp", [(0, 1), (1, 0)])


def reduce_all(ring, send, keep, vectors):
    place = ring.place
    count = send.shape[0] // 2
    rows = count // PIECES
    along = ring.along
    received = ring.core(send)
    (out,) = stage_call(partial(other_shard_body, vectors, rows), [count], place, keep, received)
    shard = ring.y(out)
    x_send, x_keep = stage_call(
        partial(split_x_body, vectors, rows, PIECES // 2), [count // 2] * 2, place, keep, received, shard
    )
    x_received = ring.x(x_send)
    parts = stage_call(
        partial(split_z_body, vectors, rows, along), [count // 2 // along] * along, place, x_keep, x_received
    )
    z_received = [ring.z(parts[step], step) for step in range(1, along)]
    (total,) = stage_call(partial(join_z_body, vectors, rows), [count // 2 // along], place, parts[0], *z_received)
    gathered = [total] + [ring.z(total, step) for step in range(1, along)]
    (mine,) = stage_call(place_z_body, [count // 2], place, *gathered)
    beside = ring.x(mine)
    return mine, beside, ring.core(mine), ring.core(beside)


def both_sides(place, mine, beside, half):
    return [jnp.where(place[1] == side, mine, beside) for side in range(2)]


def feed_unpack_body(place, mine, beside, core_mine, core_beside, down_ref, up_ref, proj_ref, stage):
    half = mine.shape[0]
    for target, near, far in ((place[0], mine, beside), (1 - place[0], core_mine, core_beside)):
        stage[pl.ds(pl.multiple_of(place[1] * half, 16), half), :] = near[...]
        stage[pl.ds(pl.multiple_of((1 - place[1]) * half, 16), half), :] = far[...]
        wide = pl.ds(pl.multiple_of(512 * target, 512), 512)
        down_ref[wide, :] = stage[0:512, :].astype(f32)
        up_ref[:, wide] = stage[512:1024, :].astype(f32)
        proj_ref[pl.ds(pl.multiple_of(128 * target, 128), 128), :] = stage[1024:1152, :].astype(f32)


def last_unpack_body(place, mine, beside, core_mine, core_beside, qkv_ref, merge_ref, vectors_ref, stage, main):
    half = mine.shape[0]
    for target, near, far in ((place[0], mine, beside), (1 - place[0], core_mine, core_beside)):
        stage[pl.ds(pl.multiple_of(place[1] * half, 16), half), :] = near[...]
        stage[pl.ds(pl.multiple_of((1 - place[1]) * half, 16), half), :] = far[...]
        for piece in range(PIECES):
            main[80 * piece : 80 * piece + 80, :] = stage[96 * piece : 96 * piece + 80, :]
            if piece < 2:
                pair = stage[96 * piece + 80 : 96 * piece + 96, :].astype(f32)
                to = pl.ds(pl.multiple_of(16 * target + 8 * piece, 8), 8)
                vectors_ref[to, :] = pair[0:8] + pair[8:16]
        rows = pl.multiple_of(256 * target, 256)
        for part in range(2):
            qkv_ref[part, pl.ds(rows, 256), :] = main[0:256, 256 * part : 256 * part + 256].astype(f32)
        qkv_ref[2, pl.ds(rows, 128), :] = main[256:384, 0:256].astype(f32)
        qkv_ref[2, pl.ds(rows + 128, 128), :] = main[256:384, 256:512].astype(f32)
        merge_ref[pl.ds(rows, 256), :] = main[384:640, :].astype(f32)


def unpack_call(body, shapes, scratch, *operands):
    return pl.pallas_call(
        body,
        in_specs=[SCALARS] + [pl.BlockSpec(memory_space=pltpu.VMEM)] * (len(operands) - 1),
        out_specs=[pl.BlockSpec(memory_space=pltpu.VMEM)] * len(shapes),
        out_shape=[shape_of(shape, f32) for shape in shapes],
        scratch_shapes=[pltpu.VMEM(shape, bf16) for shape in scratch],
        compiler_params=pltpu.CompilerParams(vmem_limit_bytes=VMEM_LIMIT),
    )(*operands)


def feed_unpack(place, parts):
    return unpack_call(
        feed_unpack_body, [(FFN // 2, D), (D, FFN // 2), (D // 2, D)], [(FEED_PACK, D)], place, *parts
    )


def last_unpack(place, parts):
    return unpack_call(
        last_unpack_body,
        [(3, D, D // 2), (MERGE_IN // 2, D), (32, D)],
        [(LAST_PACK, D), (640, D)],
        place,
        *parts,
    )


def sum_plainly(feed_packs, last_packs, tp_size):
    feed_packs, last_packs = lax.psum((feed_packs, last_packs), ("rows", "tp"))
    send, keep = feed_packs
    blocks = {(1, 0): send[:FEED_PACK], (1, 1): send[FEED_PACK:], (0, 0): keep[:FEED_PACK], (0, 1): keep[FEED_PACK:]}
    order = [(0, 0), (1, 0), (0, 1), (1, 1)]
    down = jnp.concatenate([blocks[key][0:512] for key in order], axis=0)
    up = jnp.concatenate([blocks[key][512:1024] for key in order], axis=1)
    proj = jnp.concatenate([blocks[key][1024:1152] for key in order], axis=0)
    send, keep = last_packs
    blocks = {(1, 0): send[:LAST_PACK], (1, 1): send[LAST_PACK:], (0, 0): keep[:LAST_PACK], (0, 1): keep[LAST_PACK:]}
    split = {key: block.reshape(PIECES, 96, D) for key, block in blocks.items()}
    main = {key: block[:, :80].reshape(640, D) for key, block in split.items()}
    vectors = jnp.concatenate(
        [
            (block[:2, 80:88].astype(f32) + block[:2, 88:].astype(f32)).reshape(16, D)
            for block in (split[0, 0], split[1, 0])
        ],
        axis=0,
    )

    def qkv_rows(half, shard):
        block = main[half, shard]
        return jnp.stack(
            [
                block[0:256, 0:256],
                block[0:256, 256:512],
                jnp.concatenate([block[256:384, 0:256], block[256:384, 256:512]], axis=0),
            ]
        )

    qkv = jnp.concatenate(
        [jnp.concatenate([qkv_rows(half, shard) for half in range(2)], axis=1) for shard in range(2)], axis=2
    )
    merge = jnp.concatenate([main[key][384:640] for key in order], axis=0)
    index = lax.axis_index("tp")

    def own(array, axis):
        size = array.shape[axis] // tp_size
        return lax.dynamic_slice_in_dim(array, index * size, size, axis).astype(f32)

    return own(down, 0), own(up, 1), own(proj, 0), own(qkv, 2), own(merge, 0), vectors


def masks_of(window_mask, windows):
    patch = window_mask.reshape(windows, AREA) > 0
    blank = jnp.logical_not(jnp.any(patch, axis=1))
    keep = jnp.logical_or(patch, blank[:, None])
    mask = jnp.where(jnp.pad(keep, ((0, 0), (0, KEYS - AREA))), 0.0, MASKED_SCORE).astype(f32)[:, :, None]
    live = jnp.broadcast_to(1.0 - blank.astype(f32)[:, None], (windows, AREA)).reshape(windows * AREA, 1)
    return mask, live


def gather_plainly(arrays_axes):
    return [lax.all_gather(array, "tp", axis=axis, tiled=True) for array, axis in arrays_axes]


def per_device(
    rows_size, tp_size,
    section_rows, window_mask, cotangent, merge_weight, merge_gain, merge_bias, norm1_gain, norm1_bias,
    qkv_weight, qv_bias, bias_table, proj_weight, proj_bias, norm2_gain, norm2_bias,
    up_weight, up_bias, down_weight, down_bias,
):
    fast = tp_size == 2 and rows_size >= 8 and rows_size & (rows_size - 1) == 0 and rows_size <= 16
    count = cotangent.shape[0]
    index = lax.axis_index("rows")
    tp = lax.axis_index("tp")
    place = jnp.stack([index & 1, (index >> 1) & 1, index >> 2, tp]).astype(jnp.int32)
    ring = Ring(place, rows_size, tp_size)
    core = place[0]
    mask, live = masks_of(lax.dynamic_slice_in_dim(window_mask, tp * count, count, 0), count // AREA)

    small = [merge_gain.astype(f32), merge_bias.astype(f32), qv_bias.reshape(-1), up_bias, bias_table.T.reshape(-1)]

    def join(own, other, axis):
        return jnp.where(
            tp == 0, jnp.concatenate([own, other], axis=axis), jnp.concatenate([other, own], axis=axis)
        )

    if fast:

        def fetch(array):
            half = array.shape[0] // 2
            near = ring.y(lax.dynamic_slice_in_dim(array, core * half, half, 0))
            far = ring.core(near)
            return jnp.where(core == 0, jnp.concatenate([near, far]), jnp.concatenate([far, near]))

        flat = jnp.concatenate(small)
        flat = ring.y(flat)
        offset = 0
        others = []
        for array in small:
            others.append(flat[offset : offset + array.size])
            offset += array.size
        merge_full = join(merge_weight, fetch(merge_weight), 0)
        qkv_full = join(qkv_weight, fetch(qkv_weight.reshape(3 * D, -1)).reshape(qkv_weight.shape), 2)
        proj_full = join(proj_weight, fetch(proj_weight), 0)
        up_full = join(up_weight, fetch(up_weight), 1)
        down_full = join(down_weight, fetch(down_weight), 0)
        gain_full = join(small[0], others[0], 0)
        bias_full = join(small[1], others[1], 0)
        qv_full = join(qv_bias, others[2].reshape(qv_bias.shape), 1)
        up_bias_full = join(up_bias, others[3], 0)
        table_full = join(bias_table.T, others[4].reshape(bias_table.shape[::-1]), 0)
    else:
        merge_full, qkv_full, proj_full, up_full, down_full, gain_full, bias_full, qv_full, up_bias_full, table_full = (
            gather_plainly(
                [
                    (merge_weight, 0), (qkv_weight, 2), (proj_weight, 0), (up_weight, 1), (down_weight, 0),
                    (small[0], 0), (small[1], 0), (qv_bias, 1), (up_bias, 0), (bias_table.T, 0),
                ]
            )
        )

    hat, inverse = section_norm(section_rows)
    gain = gain_full[:, None]
    bias = bias_full[:, None]
    scaled = (merge_full.astype(f32) * gain).astype(bf16)
    shift = jnp.dot(bias_full[None].astype(bf16), merge_full, preferred_element_type=f32)
    position = expand(jnp.pad(table_full, ((0, 0), (0, 384 - SIDE * SIDE))))
    merged, first, qkv_rows, weights, attended = attend(
        hat, scaled, shift, norm1_gain[None], norm1_bias[None], qkv_full, qv_full, position, mask
    )
    vectors = jnp.stack([proj_bias, norm2_gain, norm2_bias, down_bias])
    order = place if fast else jnp.zeros_like(place)
    block_out, grad_residual, grad_attn, feed_send, feed_keep, feed_vectors, up_vector = feed(
        order, attended, merged, cotangent, live, proj_full, vectors, up_full, up_bias_full[None], down_full
    )
    if fast:
        feed_parts = reduce_all(ring, feed_send, feed_keep, False)
    low, last_send, last_keep = attend_back(
        order, grad_attn, grad_residual, merged, first, hat, qkv_rows, weights,
        proj_full, qkv_full, norm1_gain[None], merge_full, gain, bias, feed_vectors, up_vector,
    )
    section_grad = section_back(low, hat, inverse, scaled)
    if fast:
        last_parts = reduce_all(ring, last_send, last_keep, True)
        down_grad, up_grad, proj_grad = feed_unpack(place, feed_parts)
        qkv_grad, merge_grad, sums = last_unpack(place, last_parts)
    else:
        down_grad, up_grad, proj_grad, qkv_grad, merge_grad, sums = sum_plainly(
            (feed_send, feed_keep), (last_send, last_keep), tp_size
        )

    def own(rows, axis):
        size = rows.shape[axis] // tp_size
        return lax.dynamic_slice_in_dim(rows, tp * size, size, axis)

    return (
        block_out,
        section_grad,
        merge_grad,
        own(sums[12:14].reshape(-1), 0),
        own(sums[14:16].reshape(-1), 0),
        sums[0],
        sums[1],
        qkv_grad,
        own(sums[6:8], 1),
        own(sums[16:32, : SIDE * SIDE], 0).T,
        proj_grad,
        sums[2],
        sums[3],
        sums[4],
        up_grad,
        own(sums[8:12].reshape(-1), 0),
        down_grad,
        sums[5],
    )


def solution(mesh):
    rows_size, tp_size = mesh.shape["rows"], mesh.shape["tp"]
    both = ("rows", "tp")
    return jax.shard_map(
        partial(per_device, rows_size, tp_size),
        mesh=mesh,
        in_specs=(
            P(both, None), P("rows"), P(both, None), P("tp", None), P("tp"), P("tp"), P(), P(),
            P(None, None, "tp"), P(None, "tp"), P(None, "tp"), P("tp", None), P(), P(), P(),
            P(None, "tp"), P("tp"), P("tp", None), P(),
        ),
        out_specs=(
            P(both, None), P(both, None), P("tp", None), P("tp"), P("tp"), P(), P(),
            P(None, None, "tp"), P(None, "tp"), P(None, "tp"), P("tp", None), P(), P(), P(),
            P(None, "tp"), P("tp"), P("tp", None), P(),
        ),
        check_vma=False,
    )
```

```python
from functools import partial
import math

import jax
import jax.numpy as jnp
from jax import lax
from jax.experimental import pallas as pl
from jax.experimental.pallas import tpu as pltpu
from jax.sharding import PartitionSpec as P

MERGE_IN = 1024
D = 512
HEADS = 16
HEAD_DIM = 32
FFN = 2048
WINDOW = 10
AREA = WINDOW * WINDOW
SIDE = 2 * WINDOW - 1
EPSILON = 1e-05
MASKED_SCORE = -1e30
EXACT = lax.Precision.HIGHEST
SCALING = 1.0 / math.sqrt(HEAD_DIM)
GROUP = 4
ROWS = GROUP * AREA
KEYS = 112
QUERIES = 128
QUADS = 4
QUAD = 4 * HEAD_DIM
LANES = 4 * QUERIES

bf16 = jnp.bfloat16
f32 = jnp.float32


def mm(a, b):
    return jnp.dot(a, b, preferred_element_type=f32)


def mm_t(a, b):
    return lax.dot_general(a, b, (((1,), (1,)), ((), ())), preferred_element_type=f32)


def t_mm(a, b):
    return lax.dot_general(a, b, (((0,), (0,)), ((), ())), preferred_element_type=f32)


def normalize(values):
    center = jnp.mean(values, axis=-1, keepdims=True)
    spread = jnp.mean(values * values, axis=-1, keepdims=True) - center * center
    inverse = lax.rsqrt(spread + EPSILON)
    return (values - center) * inverse, inverse


def norm_back(grad_hat, normed, inverse):
    first_mean = jnp.mean(grad_hat, axis=-1, keepdims=True)
    second_mean = jnp.mean(grad_hat * normed, axis=-1, keepdims=True)
    return inverse * (grad_hat - first_mean - normed * second_mean)


def column_sum(values):
    return jnp.sum(values, axis=0, keepdims=True)


def head_masks():
    lane = lax.broadcasted_iota(jnp.int32, (1, QUAD), 1) // HEAD_DIM
    return [(lane == head).astype(f32).astype(bf16) for head in range(4)]


def spread_heads(rows, masks):
    return jnp.concatenate([rows * mask for mask in masks], axis=0)


def kernel_call(body, grid, in_specs, out_specs, out_shape, scratch=(), flops=0, moved=0, room=32):
    return pl.pallas_call(
        body,
        grid=grid,
        in_specs=in_specs,
        out_specs=out_specs,
        out_shape=out_shape,
        scratch_shapes=list(scratch),
        compiler_params=pltpu.CompilerParams(
            dimension_semantics=("arbitrary",) * len(grid), vmem_limit_bytes=room * 1024 * 1024
        ),
        cost_estimate=COST,
    )


def whole(shape):
    return pl.BlockSpec(shape, lambda *_: (0,) * len(shape), pipeline_mode=pl.Buffered(1))


def by_rows(rows, columns):
    return pl.BlockSpec((rows, columns), lambda i: (i, 0))


def by_windows(shape):
    return pl.BlockSpec((GROUP,) + shape, lambda i: (i,) + (0,) * len(shape))


SCALARS = pl.BlockSpec(memory_space=pltpu.SMEM)


def in_hbm(array):
    return pltpu.with_memory_space_constraint(array, pltpu.HBM)


FEED_PACK = 1024
QKV_PACK = 512
MERGE_PACK = 256
STAGE_ROOM = 16
COST = pl.CostEstimate(flops=1, bytes_accessed=1, transcendentals=0)
LONG = pl.CostEstimate(flops=10**12, bytes_accessed=1, transcendentals=0)
SUMS = 16
PARAMS = 16


def shape_of(shape, dtype):
    return jax.ShapeDtypeStruct(shape, dtype)


def split(rows):
    high = rows.astype(bf16).astype(f32)
    return jnp.concatenate([high, rows - high], axis=0).astype(bf16)


def joined(pair):
    half = pair.shape[0] // 2
    return pair[:half].astype(f32) + pair[half:].astype(f32)


def both_shards(tp, mine, other, axis):
    return jnp.where(
        tp == 0, jnp.concatenate([mine, other], axis=axis), jnp.concatenate([other, mine], axis=axis)
    )


def pack_merge_body(place, merge_ref, out_ref):
    out_ref[...] = merge_ref[pl.ds(pl.multiple_of(256 * place[0], 256), 256), :]


def pack_params_body(place, gain_ref, bias_ref, qv_ref, up_bias_ref, table_ref, params_ref, out_ref):
    params_ref[...] = jnp.zeros_like(params_ref)
    params_ref[0:1, :] = gain_ref[...].astype(f32)
    params_ref[1:2, :] = bias_ref[...].astype(f32)
    params_ref[2:3, 0:256] = qv_ref[0:1, :]
    params_ref[2:3, 256:512] = qv_ref[1:2, :]
    params_ref[3:4, :] = up_bias_ref[:, 0:512]
    params_ref[4:5, :] = up_bias_ref[:, 512:1024]
    params_ref[8:16, 0 : SIDE * SIDE] = table_ref[...]
    out_ref[...] = split(params_ref[...])


def plain_call(body, outs, operands, room=16, scratch=(), flops=0):
    return pl.pallas_call(
        body,
        in_specs=[SCALARS] + [pl.BlockSpec(memory_space=pltpu.VMEM)] * (len(operands) - 1),
        out_specs=[pl.BlockSpec(memory_space=pltpu.VMEM)] * len(outs),
        out_shape=outs,
        scratch_shapes=list(scratch),
        compiler_params=pltpu.CompilerParams(vmem_limit_bytes=room * 1024 * 1024),
        cost_estimate=COST,
    )(*operands)


def pack_qkv_body(place, qkv_ref, proj_ref, out):
    core = place[0]
    for side in range(2):
        rows = pl.ds(pl.multiple_of(768 * core + 384 * side, 128), 384)
        out[0:384, 256 * side : 256 * side + 256] = qkv_ref[rows, :]
    out[384:512, :] = proj_ref[pl.ds(pl.multiple_of(128 * core, 128), 128), :]


def pack_feed_body(place, up_ref, down_ref, out):
    half = pl.ds(pl.multiple_of(512 * place[0], 512), 512)
    out[0:512, :] = down_ref[half, :]
    out[512:1024, :] = up_ref[:, half]


def plain_call_after(body, outs, place, after, operands, room=16, scratch=(), flops=0, cost=COST):
    after = after if isinstance(after, tuple) else (after,)

    def without_after(place, *refs):
        return body(place, *refs[len(after) :])

    return pl.pallas_call(
        without_after,
        in_specs=[SCALARS] + [pl.BlockSpec(memory_space=pl.ANY)] * len(after) + [pl.BlockSpec(memory_space=pltpu.VMEM)] * len(operands),
        out_specs=[pl.BlockSpec(memory_space=pltpu.VMEM)] * len(outs),
        out_shape=outs,
        scratch_shapes=list(scratch),
        compiler_params=pltpu.CompilerParams(vmem_limit_bytes=room * 1024 * 1024),
        cost_estimate=cost,
    )(place, *after, *operands)


def hold_body(array_ref, *refs):
    pass


def hold(array, *after):
    anywhere = pl.BlockSpec(memory_space=pl.ANY)
    return pl.pallas_call(
        hold_body,
        in_specs=[anywhere] * (1 + len(after)),
        out_specs=anywhere,
        out_shape=shape_of(array.shape, array.dtype),
        input_output_aliases={0: 0},
        cost_estimate=COST,
    )(array, *after)


def masks_body(place, window_ref, mask_ref, live_ref):
    windows = mask_ref.shape[0]
    patch = jnp.minimum(window_ref[pl.ds(pl.multiple_of(windows * place[3], 8), windows), :], 1).astype(f32)
    live = jnp.max(patch, axis=1, keepdims=True)
    added = jnp.where(jnp.maximum(patch, 1.0 - live) > 0.5, 0.0, MASKED_SCORE)
    added = jnp.concatenate([added, jnp.full((windows, QUERIES - AREA), MASKED_SCORE, f32)], axis=1)
    for window in range(windows):
        mask_ref[window] = added[window : window + 1, :]
        live_ref[AREA * window : AREA * (window + 1), :] = jnp.broadcast_to(live[window : window + 1, :], (AREA, 1))


def masks_of(place, after, window_mask, count):
    windows = count // AREA
    return plain_call_after(
        masks_body,
        [shape_of((windows, 1, QUERIES), f32), shape_of((count, 1), f32)],
        place,
        after,
        (window_mask.reshape(-1, AREA),),
    )


def section_norm_body(after, rows_ref, hat_ref, inverse_ref, turned_ref):
    step = pl.program_id(0)
    hat, inverse = normalize(rows_ref[...].astype(f32))
    hat = hat.astype(bf16)
    hat_ref[pl.ds(pl.multiple_of(step * ROWS, 16), ROWS), :] = hat
    inverse_ref[...] = inverse

    @pl.when(step == pl.num_programs(0) - 1)
    def _():
        turned_ref[...] = hat_ref[...].T


def section_norm(after, rows):
    count = rows.shape[0]
    return kernel_call(
        section_norm_body,
        (count // ROWS,),
        [pl.BlockSpec(memory_space=pl.ANY), by_rows(ROWS, MERGE_IN)],
        [whole((count, MERGE_IN)), by_rows(ROWS, 1), whole((MERGE_IN, count))],
        [shape_of((count, MERGE_IN), bf16), shape_of((count, 1), f32), pltpu.HBM((MERGE_IN, count), bf16)],
        flops=10 * count * MERGE_IN,
        moved=4 * count * MERGE_IN,
    )(after, rows)


def gain_rows(tp, params, others):
    return both_shards(tp, params[0:1], others[0:1], 1), both_shards(tp, params[1:2], others[1:2], 1)


def merge_body(
    place, hat_ref, own_ref, near_ref, far_ref, params_ref, others_ref, rows_ref,
    merged_ref, first_ref, merge_ref, params_out_ref, turned_ref, column_ref,
    merge_s, shift_s, gain_s, first_s,
):
    step = pl.program_id(0)

    @pl.when(pl.program_id(0) == 0)
    def _():
        core, tp = place[0], place[3]
        merge_s[pl.ds(pl.multiple_of(512 * tp, 512), 512), :] = own_ref[...]
        other = 512 * (1 - tp)
        merge_s[pl.ds(pl.multiple_of(other + 256 * core, 256), 256), :] = near_ref[...]
        merge_s[pl.ds(pl.multiple_of(other + 256 * (1 - core), 256), 256), :] = far_ref[...]
        merge_ref[...] = merge_s[...]
        params = params_ref[...]
        others = joined(others_ref[...])
        gain, bias = gain_rows(tp, params, others)
        gain_s[...] = gain.astype(bf16)
        shift_s[...] = mm(jnp.broadcast_to(bias, (16, MERGE_IN)).astype(bf16), merge_s[...])[0:1]
        params_out_ref[0:1, 0:1024] = gain
        params_out_ref[0:1, 1024:2048] = bias
        params_out_ref[1:2, 0:512] = both_shards(tp, params[2:3, 0:256], others[2:3, 0:256], 1)
        params_out_ref[1:2, 512:1024] = both_shards(tp, params[2:3, 256:512], others[2:3, 256:512], 1)
        params_out_ref[1:2, 1024:2048] = jnp.zeros((1, 1024), f32)
        params_out_ref[2:3, :] = both_shards(
            tp,
            jnp.concatenate([params[3:4], params[4:5]], axis=1),
            jnp.concatenate([others[3:4], others[4:5]], axis=1),
            1,
        )
        params_out_ref[3:8, :] = jnp.zeros((5, 2048), f32)
        params_out_ref[8:24, 0:512] = both_shards(tp, params[8:16], others[8:16], 0)
        params_out_ref[8:24, 512:2048] = jnp.zeros((16, 1536), f32)
        column_ref[...] = jnp.broadcast_to(gain, (128, MERGE_IN)).T

    merged = mm(hat_ref[...] * gain_s[...], merge_s[...]) + shift_s[...]
    merged_ref[...] = merged
    hat, _ = normalize(merged)
    first = (hat * rows_ref[0:1, :] + rows_ref[1:2, :]).astype(bf16)
    first_ref[...] = first
    first_s[pl.ds(pl.multiple_of(step * ROWS, 16), ROWS), :] = first

    @pl.when(step == pl.num_programs(0) - 1)
    def _():
        turned_ref[...] = first_s[...].T


def merge_rows(place, hat, own, near, far, params, others, rows):
    count = hat.shape[0]
    return kernel_call(
        merge_body,
        (count // ROWS,),
        [
            SCALARS, by_rows(ROWS, MERGE_IN), whole((512, D)), whole((256, D)), whole((256, D)),
            whole((PARAMS, D)), whole((2 * PARAMS, D)), whole((2, D)),
        ],
        [by_rows(ROWS, D), by_rows(ROWS, D), whole((MERGE_IN, D)), whole((24, 2048)), whole((D, count)), whole((MERGE_IN, 128))],
        [
            pltpu.HBM((count, D), f32), shape_of((count, D), bf16), pltpu.HBM((MERGE_IN, D), bf16),
            shape_of((24, 2048), f32), pltpu.HBM((D, count), bf16), pltpu.HBM((MERGE_IN, 128), f32),
        ],
        [
            pltpu.VMEM((MERGE_IN, D), bf16), pltpu.VMEM((1, D), f32), pltpu.VMEM((1, MERGE_IN), bf16),
            pltpu.VMEM((count, D), bf16),
        ],
        flops=2 * count * D * MERGE_IN,
        moved=count * 10 * D + 4 * D * MERGE_IN,
        room=24,
    )(place, hat, own, near, far, params, others, rows)


def value_blocks(values, masks):
    return [jnp.concatenate([values * mask, jnp.broadcast_to(mask, (QUERIES, QUAD))], axis=1) for mask in masks]


def turned_products(turned, scores):
    parts = []
    for pair in range(2):
        both = mm(turned[64 * pair : 64 * pair + 64], scores[:, 256 * pair : 256 * pair + 256])
        parts += [both[0:32, 0:128], both[32:64, 128:256]]
    return jnp.concatenate(parts, axis=0).T


def attend_body(
    place, first_ref, own_ref, near_ref, far_ref, params_ref, position_ref, mask_ref,
    qkv_out_ref, weights_ref, attended_ref, padded_ref, inverse_ref, qkv_ref,
    stage, mixed,
):
    @pl.when(pl.program_id(0) == 0)
    def _():
        core, tp = place[0], place[3]
        other = pl.ds(pl.multiple_of(256 * (1 - tp), 256), 256)
        qkv_ref[:, pl.ds(pl.multiple_of(256 * tp, 256), 256)] = own_ref[...]
        for ref, half in ((near_ref, core), (far_ref, 1 - core)):
            for side in range(2):
                rows = pl.ds(pl.multiple_of(768 * half + 384 * side, 128), 384)
                qkv_ref[rows, other] = ref[0:384, 256 * side : 256 * side + 256]

    stage[pl.ds(0, ROWS), :] = first_ref[...].astype(f32)
    stage[pl.ds(ROWS, 32), :] = jnp.zeros((32, D), f32)
    padded = jnp.concatenate(
        [stage[pl.ds(AREA * w, QUERIES), :].astype(bf16) for w in range(GROUP)], axis=0
    )
    queries = (SCALING * (mm(padded, qkv_ref[0:512, :]) + params_ref[1:2, 0:512])).astype(bf16)
    keys = mm(padded, qkv_ref[512:1024, :]).astype(bf16)
    values = (mm(padded, qkv_ref[1024:1536, :]) + params_ref[1:2, 512:1024]).astype(bf16)
    for w in range(GROUP):
        block = slice(QUERIES * w, QUERIES * (w + 1))
        qkv_out_ref[w, :, 0:D] = queries[block]
        qkv_out_ref[w, :, D : 2 * D] = keys[block]
        qkv_out_ref[w, :, 2 * D :] = values[block]
    masks = head_masks()
    for w in range(GROUP):
        mask = mask_ref[w]
        for quad in range(QUADS):
            columns = slice(QUAD * quad, QUAD * (quad + 1))
            rows = QUERIES * w
            spread = spread_heads(keys[rows : rows + QUERIES, columns], masks)
            scores = mm_t(queries[rows : rows + KEYS, columns], spread)
            raised = []
            for head in range(4):
                lanes = slice(QUERIES * head, QUERIES * (head + 1))
                part = scores[:, lanes] + position_ref[quad, :, lanes] + mask
                raised.append(jnp.exp(part - jnp.max(part, axis=1, keepdims=True)).astype(bf16))
            weights = jnp.concatenate(raised, axis=1)
            weights_ref[w, quad] = weights
            blocks = value_blocks(values[rows : rows + QUERIES, columns], masks)
            out = mm(weights, jnp.concatenate(blocks, axis=0))
            inverse = 1.0 / out[:, QUAD:]
            both = out[:, :QUAD] * inverse
            inverse_ref[w, :, columns] = inverse
            padded_ref[w, :, columns] = both.astype(bf16)
            mixed[pl.ds(AREA * w, AREA), columns] = both[0:AREA]
    attended_ref[...] = mixed[...].astype(bf16)


def attend(place, first, own, near, far, params, position, mask):
    count = first.shape[0]
    windows = count // AREA
    return kernel_call(
        attend_body,
        (count // ROWS,),
        [
            SCALARS, by_rows(ROWS, D), whole((3 * D, 256)), whole((512, D)), whole((512, D)),
            whole((24, 2048)), whole((QUADS, KEYS, LANES)), by_windows((1, QUERIES)),
        ],
        [
            by_windows((QUERIES, 3 * D)), by_windows((QUADS, KEYS, LANES)), by_rows(ROWS, D),
            by_windows((KEYS, D)), by_windows((KEYS, D)), whole((3 * D, D)),
        ],
        [
            pltpu.HBM((windows, QUERIES, 3 * D), bf16), pltpu.HBM((windows, QUADS, KEYS, LANES), bf16),
            shape_of((count, D), bf16), pltpu.HBM((windows, KEYS, D), bf16), pltpu.HBM((windows, KEYS, D), f32),
            pltpu.HBM((3 * D, D), bf16),
        ],
        [pltpu.VMEM((ROWS + 32, D), f32), pltpu.VMEM((ROWS, D), f32)],
        flops=2 * count * D * (3 * D + 4 * AREA),
        moved=count * 10 * D + windows * QUADS * KEYS * LANES * 2,
        room=32,
    )(place, first, own, near, far, params, position, mask)


def gelu_parts(t):
    chance = 0.5 * lax.erf(t * math.sqrt(0.5)) + 0.5
    density = jnp.exp(t * t * -0.5) * (1.0 / math.sqrt(2.0 * math.pi))
    return t * chance, chance + t * density


TILE = 512
FEED_ROWS = 400
OWN_ROOM = 18
OTHER_ROOM = 22


def feed_tile(up, down, bias, second_ref, turned_ref, branch_ref, total_s, back_s, active_s, raise_s, target, first):
    sums = jnp.zeros((1, TILE), f32)
    for begin in range(0, second_ref.shape[0], FEED_ROWS):
        here = slice(begin, begin + FEED_ROWS)
        value, slope = gelu_parts(mm(second_ref[here, :], up) + bias)
        active = value.astype(bf16)
        grad_raised = (mm_t(branch_ref[here, :], down) * slope).astype(bf16)
        active_s[here, :] = active
        raise_s[here, :] = grad_raised
        sums += column_sum(grad_raised.astype(f32))
        out = mm(active, down)
        back = mm_t(grad_raised, up)
        if first:
            total_s[here, :] = out
            back_s[here, :] = back
        else:
            total_s[here, :] += out
            back_s[here, :] += back
    target[0:512, :] = t_mm(active_s[...], branch_ref[...]).astype(bf16)
    target[512:1024, :] = mm(turned_ref[...], raise_s[...]).astype(bf16)
    return sums


def feed_own_body(
    place, attended_ref, merged_ref, cotangent_ref, live_ref, rows_ref, params_ref, proj_own, near_ref, far_ref,
    up_own, down_own,
    residual_ref, total_ref, back_ref, second_ref, turned_ref, branch_ref, send_ref, keep_ref, sums_ref, proj_ref,
    active_s, raise_s,
):
    step = pl.program_id(0)
    blocks = pl.num_programs(0) - 2
    core, tp = place[0], place[3]

    @pl.when(step == 0)
    def _():
        proj_ref[pl.ds(pl.multiple_of(256 * tp, 256), 256), :] = proj_own[...]
        for ref, which in ((near_ref, core), (far_ref, 1 - core)):
            proj_ref[pl.ds(pl.multiple_of(256 * (1 - tp) + 128 * which, 128), 128), :] = ref[384:512, :]
        sums_ref[...] = jnp.zeros_like(sums_ref)

    @pl.when(step < blocks)
    def _():
        here = pl.ds(pl.multiple_of(step * ROWS, 16), ROWS)
        residual = merged_ref[...] + mm(attended_ref[...], proj_ref[...]) + rows_ref[0:1, :]
        residual_ref[here, :] = residual
        hat, _ = normalize(residual)
        second_ref[here, :] = (hat * rows_ref[1:2, :] + rows_ref[2:3, :]).astype(bf16)
        branch = cotangent_ref[...].astype(f32) * live_ref[...]
        branch_ref[here, :] = branch.astype(bf16)
        sums_ref[7:8, :] += column_sum(branch)

    for index, (target, half) in enumerate(((send_ref, 1 - core), (keep_ref, core))):

        @pl.when(step == blocks + index)
        def _():
            if index == 0:
                turned_ref[...] = second_ref[...].T
            units = pl.ds(pl.multiple_of(TILE * half, TILE), TILE)
            shard = 2 * tp + half
            bias = params_ref[2:3, pl.ds(pl.multiple_of(TILE * shard, TILE), TILE)]
            sums_ref[pl.ds(shard, 1), :] = feed_tile(
                up_own[:, units], down_own[units, :], bias, second_ref, turned_ref, branch_ref, total_ref, back_ref,
                active_s, raise_s, target, index == 0,
            )


RESIDENT = pl.BlockSpec(memory_space=pltpu.VMEM)


def feed_own(place, attended, merged, cotangent, live, rows, params, proj, near, far, up, down):
    count = attended.shape[0]
    blocks = count // ROWS

    def taken(columns):
        return pl.BlockSpec((ROWS, columns), lambda i: (jnp.minimum(i, blocks - 1), 0))

    return kernel_call(
        feed_own_body,
        (blocks + 2,),
        [
            SCALARS, taken(D), taken(D), taken(D), taken(1), whole((4, D)), whole((24, 2048)), whole((256, D)),
            whole((512, D)), whole((512, D)), RESIDENT, RESIDENT,
        ],
        [RESIDENT] * 8 + [whole((8, D)), whole((D, D))],
        [pltpu.VMEM((count, D), f32)] * 3
        + [pltpu.VMEM((count, D), bf16), pltpu.VMEM((D, count), bf16), pltpu.VMEM((count, D), bf16)]
        + [pltpu.VMEM((FEED_PACK, D), bf16)] * 2
        + [shape_of((8, D), f32), pltpu.HBM((D, D), bf16)],
        [pltpu.VMEM((count, TILE), bf16)] * 2,
        room=OWN_ROOM,
    )(place, attended, merged, cotangent, live, rows, params, proj, near, far, up, down)


def feed_other_body(
    place, residual_ref, total_ref, back_ref, second_ref, turned_ref, branch_ref, rows_ref, params_ref, sums_in,
    near_ref, far_ref,
    out_ref, grad_residual_ref, attn_ref, send_ref, keep_ref, sums_ref,
    total_s, back_s, active_s, raise_s,
):
    step = pl.program_id(0)
    core, tp = place[0], place[3]

    @pl.when(step == 0)
    def _():
        sums_ref[...] = sums_in[...]

    for index, (target, ref, half) in enumerate(((send_ref, far_ref, 1 - core), (keep_ref, near_ref, core))):

        @pl.when(step == index)
        def _():
            shard = 2 * (1 - tp) + half
            bias = params_ref[2:3, pl.ds(pl.multiple_of(TILE * shard, TILE), TILE)]
            sums_ref[pl.ds(shard, 1), :] = feed_tile(
                ref[512:1024, :], ref[0:512, :], bias, second_ref, turned_ref, branch_ref, total_s, back_s,
                active_s, raise_s, target, index == 0,
            )

    @pl.when(step >= 2)
    def _():
        here = pl.ds(pl.multiple_of((step - 2) * ROWS, 16), ROWS)
        residual = residual_ref[here, :]
        out_ref[...] = (residual + rows_ref[3:4, :] + total_ref[here, :] + total_s[here, :]).astype(bf16)
        hat, inverse = normalize(residual)
        grad_second = back_ref[here, :] + back_s[here, :]
        grad_residual = branch_ref[here, :].astype(f32) + norm_back(grad_second * rows_ref[1:2, :], hat, inverse)
        grad_residual_ref[...] = grad_residual
        attn_ref[...] = grad_residual.astype(bf16)
        sums_ref[4:5, :] += column_sum(grad_residual)
        sums_ref[5:6, :] += column_sum(grad_second * hat)
        sums_ref[6:7, :] += column_sum(grad_second)


def feed_other(place, state, rows, params, sums, near, far):
    count = state[0].shape[0]
    blocks = count // ROWS

    def given(columns):
        return pl.BlockSpec((ROWS, columns), lambda i: (jnp.maximum(i - 2, 0), 0))

    return kernel_call(
        feed_other_body,
        (blocks + 2,),
        [SCALARS] + [RESIDENT] * 6 + [whole((4, D)), whole((24, 2048)), whole((8, D)), RESIDENT, RESIDENT],
        [given(D), given(D), given(D), RESIDENT, RESIDENT, whole((8, D))],
        [shape_of((count, D), bf16), pltpu.HBM((count, D), f32), shape_of((count, D), bf16)]
        + [pltpu.VMEM((FEED_PACK, D), bf16)] * 2
        + [shape_of((8, D), f32)],
        [pltpu.VMEM((count, D), f32)] * 2 + [pltpu.VMEM((count, TILE), bf16)] * 2,
        room=OTHER_ROOM,
    )(place, *state, rows, params, sums, near, far)


def attend_back_body(
    after, attn_ref, qkv_in_ref, weights_ref, padded_ref, inverse_ref, proj_ref, sums_in, position_in,
    stack_ref, sums_ref, position_ref,
    stage, grads,
):
    @pl.when(pl.program_id(0) == 0)
    def _():
        sums_ref[...] = sums_in[...]
        position_ref[...] = position_in[...]

    stage[pl.ds(0, ROWS), :] = attn_ref[...].astype(f32)
    stage[pl.ds(ROWS, 32), :] = jnp.zeros((32, D), f32)
    real = lax.broadcasted_iota(jnp.int32, (KEYS, 1), 0) < AREA
    padded = jnp.concatenate(
        [jnp.where(real, stage[pl.ds(AREA * w, KEYS), :], 0.0).astype(bf16) for w in range(GROUP)], axis=0
    )
    grad_attended = mm_t(padded, proj_ref[...])
    masks = head_masks()
    empty = jnp.zeros((QUERIES - KEYS, QUAD), bf16)
    kept = {}
    for w in range(GROUP):
        for quad in range(QUADS):
            columns = slice(QUAD * quad, QUAD * (quad + 1))
            values = qkv_in_ref[w, :, 2 * D + QUAD * quad : 2 * D + QUAD * (quad + 1)]
            grad = grad_attended[KEYS * w : KEYS * (w + 1), columns] * inverse_ref[w, :, columns]
            low = grad.astype(bf16)
            taken = (grad * padded_ref[w, :, columns].astype(f32)).astype(bf16)
            both = jnp.concatenate([low, -taken], axis=1)
            change = jnp.concatenate([mm_t(both, block) for block in value_blocks(values, masks)], axis=1)
            grad_scores = (weights_ref[w, quad].astype(f32) * change).astype(bf16)
            position_ref[quad] += grad_scores.astype(f32)
            kept[w, quad] = (low, grad_scores)
    for w in range(GROUP):
        to = pl.ds(AREA * w, AREA)
        for quad in range(QUADS):
            low, grad_scores = kept[w, quad]
            queries = qkv_in_ref[w, :, QUAD * quad : QUAD * (quad + 1)]
            keys = qkv_in_ref[w, :, D + QUAD * quad : D + QUAD * (quad + 1)]
            grad_queries = mm(grad_scores, spread_heads(keys, masks)) * SCALING
            grad_keys = turned_products(queries.T[:, :KEYS], grad_scores)
            grad_values = turned_products(jnp.concatenate([low, empty], axis=0).T[:, :KEYS], weights_ref[w, quad])
            for part, grad in enumerate((grad_queries, grad_keys, grad_values)):
                grads[to, D * part + QUAD * quad : D * part + QUAD * (quad + 1)] = grad[0:AREA]
    stack = grads[...].astype(bf16)
    stack_ref[...] = stack
    sums_ref[...] += column_sum(stack.astype(f32))


def attend_back(after, stack, attn, qkv_in, weights, padded, inverse, proj, sums, position, begin, steps):
    count = steps * ROWS
    anywhere = pl.BlockSpec(memory_space=pl.ANY)

    def rows_at(columns):
        return pl.BlockSpec((ROWS, columns), lambda i: (i + begin, 0))

    def windows_at(shape):
        return pl.BlockSpec((GROUP,) + shape, lambda i: (i + begin,) + (0,) * len(shape))

    outs = [pltpu.HBM((attn.shape[0], 3 * D), bf16), shape_of((1, 3 * D), f32), shape_of((QUADS, KEYS, LANES), f32)]
    qkv_in, weights, padded, inverse = [in_hbm(array) for array in (qkv_in, weights, padded, inverse)]
    first = stack is None

    def body(*refs):
        attend_back_body(*(refs if first else refs[1:]))

    return pl.pallas_call(
        body,
        grid=(steps,),
        in_specs=([] if first else [anywhere])
        + [
            anywhere, rows_at(D), windows_at((QUERIES, 3 * D)), windows_at((QUADS, KEYS, LANES)),
            windows_at((KEYS, D)), windows_at((KEYS, D)), whole((D, D)), whole((1, 3 * D)), whole((QUADS, KEYS, LANES)),
        ],
        out_specs=[rows_at(3 * D), whole((1, 3 * D)), whole((QUADS, KEYS, LANES))],
        out_shape=outs,
        scratch_shapes=[pltpu.VMEM((ROWS + 32, D), f32), pltpu.VMEM((ROWS, 3 * D), f32)],
        input_output_aliases={} if first else {0: 0},
        compiler_params=pltpu.CompilerParams(
            dimension_semantics=("arbitrary",), vmem_limit_bytes=32 * 1024 * 1024
        ),
        cost_estimate=COST,
    )(*([] if first else [stack]), after, attn, qkv_in, weights, padded, inverse, proj, sums, position)


def qkv_back_body(
    place, after, turned_ref, stack_ref, attended_ref, attn_ref, send_ref, keep_ref, qkv_s, proj_s
):
    part = pl.program_id(0)
    core, tp = place[0], place[3]
    qkv_s[...] = mm(turned_ref[...], stack_ref[...]).astype(bf16)

    @pl.when(part == 0)
    def _():
        proj_s[...] = t_mm(attended_ref[...], attn_ref[...]).astype(bf16)

    for target, half in ((send_ref, 1 - core), (keep_ref, core)):
        for other in range(2):
            shard = jnp.where(other == 0, tp, 1 - tp)
            base = QKV_PACK * other
            rows = pl.ds(pl.multiple_of(256 * half, 256), 256)
            columns = pl.ds(pl.multiple_of(256 * shard, 256), 256)

            @pl.when(part < 2)
            def _():
                target[base : base + 256, pl.ds(pl.multiple_of(256 * part, 256), 256)] = qkv_s[rows, columns]

            @pl.when(part == 2)
            def _():
                block = qkv_s[rows, columns]
                target[base + 256 : base + 384, 0:256] = block[0:128]
                target[base + 256 : base + 384, 256:512] = block[128:256]
                rows_proj = pl.ds(pl.multiple_of(256 * shard + 128 * half, 128), 128)
                target[base + 384 : base + 512, :] = proj_s[rows_proj, :]


def qkv_back(place, after, turned, stack, attended, attn):
    count = attended.shape[0]
    return kernel_call(
        qkv_back_body,
        (3,),
        [
            SCALARS, pl.BlockSpec(memory_space=pl.ANY), whole((D, count)),
            pl.BlockSpec((count, D), lambda i: (0, i)), whole((count, D)), whole((count, D)),
        ],
        [RESIDENT, RESIDENT],
        [pltpu.VMEM((2 * QKV_PACK, D), bf16), pltpu.VMEM((2 * QKV_PACK, D), bf16)],
        [pltpu.VMEM((D, D), bf16), pltpu.VMEM((D, D), bf16)],
        room=24,
    )(place, after, in_hbm(turned), in_hbm(stack), in_hbm(attended), in_hbm(attn))


def merge_back_body(
    place, after, stack_ref, grad_residual_ref, merged_ref, turned_ref,
    qkv_ref, rows_ref, merge_ref, params_ref, column_ref, feed_sums_ref, qkv_sums_ref, position_ref,
    low_ref, send_ref, keep_ref,
    low_s, turned_s, vectors_ref, fold_s, all_s, raw_s, sem,
):
    step = pl.program_id(0)
    here = pl.ds(pl.multiple_of(step * ROWS, 16), ROWS)

    fetch = pltpu.make_async_copy(turned_ref, turned_s, sem)

    @pl.when(step == 0)
    def _():
        fetch.start()
        vectors_ref[...] = jnp.zeros_like(vectors_ref)

    stack = stack_ref[...]
    grad_first = (
        mm_t(stack[:, 0:D], qkv_ref[0:D, :])
        + mm_t(stack[:, D : 2 * D], qkv_ref[D : 2 * D, :])
        + mm_t(stack[:, 2 * D :], qkv_ref[2 * D :, :])
    )
    normed, inverse = normalize(merged_ref[...])
    grad_merged = grad_residual_ref[...] + norm_back(grad_first * rows_ref[0:1, :], normed, inverse)
    low = grad_merged.astype(bf16)
    low_ref[...] = low
    vectors_ref[0:1, :] += column_sum(grad_first * normed)
    vectors_ref[1:2, :] += column_sum(grad_first)
    vectors_ref[2:3, :] += column_sum(low.astype(f32))
    low_s[here, :] = low

    @pl.when(step == pl.num_programs(0) - 1)
    def _():
        core, tp = place[0], place[3]
        total = vectors_ref[2:3, :]
        pair = jnp.concatenate([split(total), jnp.zeros((14, D), bf16)], axis=0)
        ones = jnp.ones((16, D), bf16)
        fetch.wait()
        raw_s[...] = mm(turned_s[...], low_s[...])
        all_s[...] = jnp.zeros_like(all_s)
        all_s[0:2, :] = vectors_ref[0:2, :]
        all_s[2:6, :] = feed_sums_ref[4:8, :]
        all_s[6:7, :] = qkv_sums_ref[:, 0:D]
        all_s[7:8, :] = qkv_sums_ref[:, 2 * D :]
        all_s[8:12, :] = feed_sums_ref[0:4, :]
        all_s[16:32, 0:384] = fold_place(position_ref, fold_s)
        for tile in range(2):
            rows = slice(512 * tile, 512 * (tile + 1))
            merge = merge_ref[rows, :]
            scaled = raw_s[rows, :] * merge.astype(f32)
            scaled_high = scaled.astype(bf16)
            scaled_rest = (scaled - scaled_high.astype(f32)).astype(bf16)
            all_s[12 + tile : 13 + tile, :] = (mm_t(ones, scaled_high) + mm_t(ones, scaled_rest))[0:1]
            all_s[14 + tile : 15 + tile, :] = column_sum(mm_t(pair, merge))
        for target, half in ((send_ref, 1 - core), (keep_ref, core)):
            for other in range(2):
                begin = pl.multiple_of(512 * jnp.where(other == 0, tp, 1 - tp) + 256 * half, 256)
                bias = jnp.broadcast_to(params_ref[0:1, pl.ds(1024 + begin, 256)], (16, 256)).astype(bf16)
                gain = column_ref[pl.ds(begin, 256), 0:1]
                block = raw_s[pl.ds(begin, 256), :] * gain + t_mm(bias, pair)
                target[MERGE_PACK * other : MERGE_PACK * (other + 1), :] = block.astype(bf16)
            target[2 * MERGE_PACK :, :] = split(all_s[pl.ds(pl.multiple_of(SUMS * half, SUMS), SUMS), :])


def merge_back(
    place, after, stack, grad_residual, merged, turned, qkv, rows, merge, params, column, feed_sums, sums, position
):
    count = merged.shape[0]
    pack = 2 * MERGE_PACK + 2 * SUMS
    return kernel_call(
        merge_back_body,
        (count // ROWS,),
        [
            SCALARS, pl.BlockSpec(memory_space=pl.ANY), by_rows(ROWS, 3 * D), by_rows(ROWS, D), by_rows(ROWS, D),
            pl.BlockSpec(memory_space=pl.ANY), whole((3 * D, D)), whole((1, D)), whole((MERGE_IN, D)),
            whole((24, 2048)), whole((MERGE_IN, 128)), whole((8, D)), whole((1, 3 * D)), whole((QUADS, KEYS, LANES)),
        ],
        [by_rows(ROWS, D)] + [pl.BlockSpec(memory_space=pltpu.VMEM)] * 2,
        [shape_of((count, D), bf16), pltpu.VMEM((pack, D), bf16), pltpu.VMEM((pack, D), bf16)],
        [
            pltpu.VMEM((count, D), bf16), pltpu.VMEM((MERGE_IN, count), bf16), pltpu.VMEM((3, D), f32),
            pltpu.VMEM((HEADS, KEYS, 256), f32), pltpu.VMEM((32, D), f32), pltpu.VMEM((MERGE_IN, D), f32),
            pltpu.SemaphoreType.DMA,
        ],
        flops=2 * count * D * (3 * D + MERGE_IN),
        moved=count * 20 * D,
        room=32,
    )(
        place, after, in_hbm(stack), in_hbm(grad_residual), in_hbm(merged), in_hbm(turned), qkv, rows, merge, params,
        column, feed_sums, sums, position,
    )


def section_back_body(after, low_ref, hat_ref, inverse_ref, merge_ref, params_ref, out_ref, token_ref):
    token_ref[...] = jnp.zeros_like(token_ref)
    scaled = mm_t(low_ref[...], merge_ref[...]) * params_ref[0:1, 0:MERGE_IN]
    out_ref[...] = norm_back(scaled, hat_ref[...].astype(f32), inverse_ref[...]).astype(bf16)


def section_back(after, low, hat, inverse, merge, params):
    count = low.shape[0]
    return kernel_call(
        section_back_body,
        (count // ROWS,),
        [
            pl.BlockSpec(memory_space=pl.ANY), by_rows(ROWS, D), by_rows(ROWS, MERGE_IN), by_rows(ROWS, 1),
            whole((MERGE_IN, D)), whole((24, 2048)),
        ],
        [by_rows(ROWS, MERGE_IN), whole((8, 128))],
        [pltpu.HBM((count, MERGE_IN), bf16), shape_of((8, 128), f32)],
        flops=2 * count * D * MERGE_IN,
        moved=count * 5 * MERGE_IN,
        room=24,
    )(after, in_hbm(low), in_hbm(hat), inverse, merge, params)


def spread_matrix():
    place = lax.broadcasted_iota(jnp.int32, (QUERIES, 256), 0)
    lane = lax.broadcasted_iota(jnp.int32, (QUERIES, 256), 1)
    target = place + (SIDE - WINDOW) * (place // WINDOW)
    return jnp.logical_and(lane == target, place < AREA).astype(f32)


def expand_body(params_ref, place_ref, stage_s):
    spread = spread_matrix().astype(bf16)
    for head in range(HEADS):
        stage = stage_s.at[head]
        stage[96:KEYS, :] = jnp.zeros((KEYS - 96, 256), f32)
        line = params_ref[8 + head : 9 + head, 0:384]
        lines = jnp.concatenate(
            [pltpu.roll(line, (384 - (WINDOW - 1) * (SIDE + 1) + x) % 384, 1) for x in range(WINDOW)]
            + [jnp.zeros((6, 384), f32)],
            axis=0,
        )
        for y in range(WINDOW):
            moved = pltpu.roll(lines, SIDE * y, 1) if y else lines
            stage[pl.ds(WINDOW * y, WINDOW), :] = moved[0:WINDOW, 0:256]
        rows = stage[...]
        high = rows.astype(bf16)
        rest = rows - high.astype(f32)
        middle = rest.astype(bf16)
        low = (rest - middle.astype(f32)).astype(bf16)
        block = mm_t(high, spread) + mm_t(middle, spread) + mm_t(low, spread)
        block = jnp.concatenate([block, jnp.zeros((QUERIES - KEYS, QUERIES), f32)], axis=0).T[:KEYS]
        place_ref[head // 4, :, QUERIES * (head % 4) : QUERIES * (head % 4 + 1)] = block


def expand(params):
    return kernel_call(
        expand_body,
        (1,),
        [whole((24, 2048))],
        whole((QUADS, KEYS, LANES)),
        shape_of((QUADS, KEYS, LANES), f32),
        [pltpu.VMEM((HEADS, KEYS, 256), f32)],
        room=24,
    )(params)


def fold_place(place_ref, stage_s):
    spread = spread_matrix().astype(bf16)
    lines = []
    for head in range(HEADS):
        stage = stage_s.at[head]
        rows = place_ref[head // 4, :, QUERIES * (head % 4) : QUERIES * (head % 4 + 1)]
        rows = jnp.concatenate([rows, jnp.zeros((QUERIES - KEYS, QUERIES), f32)], axis=0).T[:KEYS]
        high = rows.astype(bf16)
        rest = (rows - high.astype(f32)).astype(bf16)
        stage[...] = mm(high, spread) + mm(rest, spread)
        total = jnp.zeros((WINDOW, 384), f32)
        for y in range(WINDOW):
            part = jnp.concatenate(
                [stage[pl.ds(WINDOW * y, WINDOW), :], jnp.zeros((WINDOW, 128), f32)], axis=1
            )
            total += pltpu.roll(part, SIDE * (WINDOW - 1 - y), 1) if y < WINDOW - 1 else part
        line = total[WINDOW - 1 : WINDOW, :]
        for x in range(WINDOW - 1):
            line += pltpu.roll(total[x : x + 1, :], WINDOW - 1 - x, 1)
        lines.append(line)
    return jnp.concatenate(lines, axis=0)


class Ring:
    def __init__(self, place, rows_size):
        self.place = place
        self.rows_size = rows_size
        self.along = rows_size // 4

    def to(self, array, bits):
        return lax.ppermute(array, "rows", [(i, i ^ bits) for i in range(self.rows_size)])

    def core(self, array):
        return self.to(array, 1)

    def x(self, array):
        return self.to(array, 2)

    def z(self, array, step):
        return self.to(array, 4 * step)

    def y(self, array):
        return lax.ppermute(array, "tp", [(0, 1), (1, 0)])


def rows_of(array, begin, rows):
    return lax.dynamic_slice_in_dim(array, begin, rows, 0).astype(f32)


def stage(body, place, after, rows, *operands, cost=COST):
    return plain_call_after(
        body, [pltpu.VMEM((count, D), bf16) for count in rows], place, after, operands, room=STAGE_ROOM, cost=cost
    )


def added(refs, begin, rows):
    here = pl.ds(pl.multiple_of(begin, 16), rows)
    total = refs[0][here, :].astype(f32)
    for ref in refs[1:]:
        total = total + ref[here, :].astype(f32)
    return total


def part(ref, begin, rows):
    return ref.at[begin : begin + rows, :]


def feed_first_body(place, own_keep, own_got, other_keep, other_got, down_y, up_x):
    down_y[...] = added((other_keep, other_got), 0, 512).astype(bf16)
    begin = 512 + 256 * (1 - place[1])
    up_x[0:256, :] = added((own_keep, own_got), begin, 256).astype(bf16)
    up_x[256:512, :] = added((other_keep, other_got), begin, 256).astype(bf16)


def feed_second_body(
    place, own_keep, own_got, other_keep, other_got, down_shard, up_got, down_x, up_y, kept
):
    x = place[1]
    down = (own_keep, own_got, down_shard)
    down_x[...] = added(down, 256 * (1 - x), 256).astype(bf16)
    kept[0:256, :] = added(down, 256 * x, 256).astype(bf16)
    begin = 512 + 256 * x
    up_y[...] = (added((other_keep, other_got), begin, 256) + up_got[256:512, :].astype(f32)).astype(bf16)
    kept[256:512, :] = (added((own_keep, own_got), begin, 256) + up_got[0:256, :].astype(f32)).astype(bf16)


def feed_third_body(place, kept, down_got, up_shard, *outs):
    span = 256 // len(outs)
    for step, out in enumerate(outs):
        begin = (place[2] ^ step) * span
        out[0:span, :] = added((part(kept, 0, 256), down_got), begin, span).astype(bf16)
        out[span : 2 * span, :] = added((part(kept, 256, 256), up_shard), begin, span).astype(bf16)


def total_body(place, *refs):
    refs[-1][...] = added(refs[:-1], 0, refs[-1].shape[0]).astype(bf16)


def beside_body(place, *refs):
    rows = refs[0].shape[0]
    for index, ref in enumerate(refs[:-1]):
        refs[-1][rows * index : rows * (index + 1), :] = ref[...]


def qkv_first_body(place, keep, got, out):
    out[...] = added((keep, got), 512, 512).astype(bf16)


def qkv_second_body(place, keep, got, shard, send, kept):
    x = place[1]
    blocks = (keep, got, shard)
    send[...] = added(blocks, 256 * (1 - x), 256).astype(bf16)
    kept[...] = added(blocks, 256 * x, 256).astype(bf16)


def merge_first_body(place, keep, got, out):
    out[0:256, :] = added((keep, got), 256, 256).astype(bf16)
    out[256:288, :] = split(joined(keep[512:544, :]) + joined(got[512:544, :]))


def merge_second_body(place, keep, got, shard, qkv_kept, qkv_got, send, kept, qkv_sum):
    qkv_sum[...] = added((qkv_kept, qkv_got), 0, 256).astype(bf16)
    x = place[1]
    blocks = (keep, got, shard)
    vectors = split(joined(keep[512:544, :]) + joined(got[512:544, :]) + joined(shard[256:288, :]))
    send[0:128, :] = added(blocks, 128 * (1 - x), 128).astype(bf16)
    send[128:160, :] = vectors
    kept[0:128, :] = added(blocks, 128 * x, 128).astype(bf16)
    kept[128:160, :] = vectors


def merge_third_body(place, qkv_sum, merge_kept, merge_got, *outs):
    vectors = split(joined(merge_kept[128:160, :]) + joined(merge_got[128:160, :]))
    wide, narrow = 256 // len(outs), 128 // len(outs)
    for step, out in enumerate(outs):
        to = place[2] ^ step
        out[0:wide, :] = added((qkv_sum,), to * wide, wide).astype(bf16)
        out[wide : wide + narrow, :] = added((merge_kept, merge_got), to * narrow, narrow).astype(bf16)
        out[wide + narrow :, :] = vectors


def merge_total_body(place, *refs):
    blocks, (out, vectors) = refs[:-2], refs[-2:]
    rows = out.shape[0]
    out[...] = added(blocks, 0, rows).astype(bf16)
    vectors[...] = split(sum(joined(ref[rows : rows + 32, :]) for ref in blocks))


def in_order(place, near, far, stage, rows, along):
    piece = near.shape[0] // along
    for side, ref in ((place[1], near), (1 - place[1], far)):
        for step in range(along):
            begin, offset = 0, piece * step
            for size in rows:
                span = size // 2 // along
                to = begin + side * (size // 2) + (place[2] ^ step) * span
                stage[pl.ds(pl.multiple_of(to, 16), span), :] = ref[offset : offset + span, :]
                begin += size
                offset += span


def feed_unpack_body(along, place, near, far, core_near, core_far, down_ref, up_ref, stage):
    for target, mine, beside in ((place[0], near, far), (1 - place[0], core_near, core_far)):
        in_order(place, mine, beside, stage, (512, 512), along)
        wide = pl.ds(pl.multiple_of(512 * target, 512), 512)
        down_ref[wide, :] = stage[0:512, :].astype(f32)
        up_ref[:, wide] = stage[512:1024, :].astype(f32)


def feed_unpack(along, place, after, parts):
    return plain_call_after(
        partial(feed_unpack_body, along),
        [shape_of((FFN // 2, D), f32), shape_of((D, FFN // 2), f32)],
        place,
        after,
        parts,
        scratch=[pltpu.VMEM((FEED_PACK, D), bf16)],
        room=24,
    )


def last_unpack_body(
    along, place, near, far, core_near, core_far, sums, core_sums, qkv_ref, proj_ref, merge_ref, *refs
):
    vectors, stage, all_s = refs[:-2], refs[-2], refs[-1]
    for target, mine, beside, pair in (
        (place[0], near, far, sums), (1 - place[0], core_near, core_far, core_sums)
    ):
        in_order(place, mine, beside, stage, (QKV_PACK, MERGE_PACK), along)
        all_s[pl.ds(pl.multiple_of(SUMS * target, SUMS), SUMS), :] = joined(pair[...])
        rows = pl.multiple_of(256 * target, 256)
        for part in range(2):
            qkv_ref[part, pl.ds(rows, 256), :] = stage[0:256, 256 * part : 256 * part + 256].astype(f32)
        qkv_ref[2, pl.ds(rows, 128), :] = stage[256:384, 0:256].astype(f32)
        qkv_ref[2, pl.ds(rows + 128, 128), :] = stage[256:384, 256:512].astype(f32)
        proj_ref[pl.ds(pl.multiple_of(128 * target, 128), 128), :] = stage[384:512, :].astype(f32)
        merge_ref[pl.ds(rows, 256), :] = stage[512:768, :].astype(f32)
    write_vectors(place[3], all_s, vectors)


VECTORS = [(1, D)] * 6 + [(2, D // 2), (1, FFN // 2), (1, MERGE_IN // 2), (1, MERGE_IN // 2), (HEADS // 2, SIDE * SIDE)]


def write_vectors(tp, sums, refs):
    for row in range(6):
        refs[row][...] = sums[row : row + 1, :]
    columns = pl.ds(pl.multiple_of(256 * tp, 256), 256)
    refs[6][...] = sums[6:8, columns]
    refs[7][:, 0:512] = sums[pl.ds(8 + 2 * tp, 1), :]
    refs[7][:, 512:1024] = sums[pl.ds(9 + 2 * tp, 1), :]
    refs[8][...] = sums[pl.ds(12 + tp, 1), :]
    refs[9][...] = sums[pl.ds(14 + tp, 1), :]
    refs[10][...] = sums[pl.ds(pl.multiple_of(16 + 8 * tp, 8), 8), 0 : SIDE * SIDE]


def last_unpack(along, place, parts):
    outs = plain_call(
        partial(last_unpack_body, along),
        [shape_of(shape, f32) for shape in [(3, D, D // 2), (D // 2, D), (MERGE_IN // 2, D)] + VECTORS],
        (place, *parts),
        scratch=[pltpu.VMEM((QKV_PACK + MERGE_PACK, D), bf16), pltpu.VMEM((2 * SUMS, D), f32)],
    )
    return outs[0], outs[1], outs[2], outs[3:]


def fetch_by_tp(ring, piece_of):
    near = ring.y(piece_of)
    return near, ring.core(near)


def plain_pieces(tp_size, weights, params):
    merge, qkv, proj, up, down = [
        lax.all_gather(array, "tp", axis=axis, tiled=True) for array, axis in zip(weights, (0, 2, 0, 1, 0))
    ]
    gain, bias, qv, up_bias, table = [
        lax.all_gather(array, "tp", axis=axis, tiled=True) for array, axis in zip(params, (0, 0, 1, 0, 1))
    ]

    def shard(array, axis, which):
        size = array.shape[axis] // 2
        return lax.slice_in_dim(array, which * size, (which + 1) * size, axis=axis)

    def rows_of(which):
        rows = jnp.zeros((PARAMS, D), f32)
        rows = rows.at[0].set(shard(gain.astype(f32), 0, which)).at[1].set(shard(bias.astype(f32), 0, which))
        rows = rows.at[2].set(shard(qv, 1, which).reshape(-1)).at[3:5].set(shard(up_bias, 0, which).reshape(2, D))
        return rows.at[8:16, : SIDE * SIDE].set(shard(table, 1, which).T)

    merge_other = shard(merge, 0, 1)
    qkv_other = shard(qkv, 2, 1).reshape(3 * D, 256)
    proj_other, up_other, down_other = shard(proj, 0, 1), shard(up, 1, 1), shard(down, 0, 1)

    def qkv_piece(half):
        rows = qkv_other[768 * half : 768 * half + 768]
        return jnp.concatenate(
            [jnp.concatenate([rows[:384], rows[384:]], axis=1), proj_other[128 * half : 128 * half + 128]], axis=0
        )

    def feed_piece(half):
        tile = slice(512 * half, 512 * half + 512)
        return jnp.concatenate([down_other[tile], up_other[:, tile]], axis=0)

    own = (
        shard(merge, 0, 0), shard(qkv, 2, 0).reshape(3 * D, 256), shard(proj, 0, 0), shard(up, 1, 0), shard(down, 0, 0)
    )
    return own, (rows_of(0), split(rows_of(1))), (merge_other[:256], merge_other[256:]), (qkv_piece(0), qkv_piece(1)), (feed_piece(0), feed_piece(1))


def sum_plainly(tp_size, feed_packs, qkv_packs, merge_packs):
    feed_packs, qkv_packs, merge_packs = lax.psum((feed_packs, qkv_packs, merge_packs), ("rows", "tp"))
    own_send, own_keep, other_send, other_keep = feed_packs
    order = [own_keep, own_send, other_keep, other_send]
    down = jnp.concatenate([block[0:512] for block in order], axis=0)
    up = jnp.concatenate([block[512:1024] for block in order], axis=1)

    def blocks(packs, size):
        send, keep = packs
        return [keep[:size], send[:size], keep[size : 2 * size], send[size : 2 * size]]

    def qkv_rows(block):
        return jnp.stack(
            [block[0:256, 0:256], block[0:256, 256:512], jnp.concatenate([block[256:384, 0:256], block[256:384, 256:512]])]
        )

    order = blocks(qkv_packs, QKV_PACK)
    qkv = jnp.concatenate(
        [jnp.concatenate([qkv_rows(order[2 * shard + half]) for half in range(2)], axis=1) for shard in range(2)], axis=2
    )
    proj = jnp.concatenate([block[384:512] for block in order], axis=0)
    merge = jnp.concatenate(blocks(merge_packs, MERGE_PACK), axis=0)
    sums = jnp.concatenate([joined(merge_packs[1][2 * MERGE_PACK :]), joined(merge_packs[0][2 * MERGE_PACK :])], axis=0)
    index = lax.axis_index("tp")

    def own(array, axis):
        size = array.shape[axis] // tp_size
        return lax.dynamic_slice_in_dim(array, index * size, size, axis).astype(f32)

    vectors = [sums[row] for row in range(6)] + [
        own(sums[6:8], 1), own(sums[8:12].reshape(-1), 0), own(sums[12:14].reshape(-1), 0),
        own(sums[14:16].reshape(-1), 0), own(sums[16:32, : SIDE * SIDE], 0),
    ]
    return own(down, 0), own(up, 1), own(qkv, 2), own(proj, 0), own(merge, 0), vectors


def per_device(
    rows_size, tp_size,
    section_rows, window_mask, cotangent, merge_weight, merge_gain, merge_bias, norm1_gain, norm1_bias,
    qkv_weight, qv_bias, bias_table, proj_weight, proj_bias, norm2_gain, norm2_bias,
    up_weight, up_bias, down_weight, down_bias,
):
    fast = tp_size == 2 and rows_size in (8, 16)
    count = cotangent.shape[0]
    index, tp = lax.axis_index("rows"), lax.axis_index("tp")
    place = jnp.stack([index & 1, (index >> 1) & 1, index >> 2, tp]).astype(jnp.int32)
    ring = Ring(place, rows_size)
    if fast:
        flat_qkv = qkv_weight.reshape(3 * D, D // 2)
        (merge_piece,) = plain_call(pack_merge_body, [shape_of((256, D), bf16)], (place, merge_weight))
        merge_near = ring.y(merge_piece)
        params, piece = plain_call_after(
            pack_params_body, [shape_of((PARAMS, D), f32), shape_of((2 * PARAMS, D), bf16)], place, merge_piece,
            (merge_gain[None], merge_bias[None], qv_bias, up_bias[None], bias_table.T),
        )
        others = ring.y(piece)
        hat, inverse, turned_hat = section_norm(piece, section_rows)
        (qkv_piece,) = plain_call_after(
            pack_qkv_body, [shape_of((QKV_PACK, D), bf16)], place, (others, merge_near, inverse), (flat_qkv, proj_weight)
        )
        qkv_near = ring.y(qkv_piece)
        mask, live = masks_of(place, qkv_piece, window_mask, count)
        merge_far = ring.core(merge_near)
        kernel_place = place
    else:
        (merge_weight, flat_qkv, proj_weight, up_weight, down_weight), (params, others), merge_pair, qkv_pair, feed_pair = plain_pieces(
            tp_size,
            (merge_weight, qkv_weight, proj_weight, up_weight, down_weight),
            (merge_gain, merge_bias, qv_bias, up_bias, bias_table),
        )
        (merge_near, merge_far), (qkv_near, qkv_far), (feed_near, feed_far) = merge_pair, qkv_pair, feed_pair
        kernel_place = jnp.zeros_like(place)
        hat, inverse, turned_hat = section_norm(params, section_rows)
        own_mask = lax.dynamic_slice_in_dim(window_mask, tp * count, count, 0)
        mask, live = masks_of(kernel_place, params, own_mask, count)

    merged, first, merge_full, params, turned_first, column = merge_rows(
        kernel_place, hat, merge_weight, merge_near, merge_far, params, others, jnp.stack([norm1_gain, norm1_bias])
    )
    if fast:
        (feed_piece,) = plain_call_after(
            pack_feed_body, [shape_of((FEED_PACK, D), bf16)], place, (merged, qkv_near), (up_weight, down_weight)
        )
        qkv_far = ring.core(qkv_near)
        feed_near = ring.y(feed_piece)
    position = expand(params)
    qkv_rows, weights, attended, padded, inverse_sums, qkv_full = attend(
        kernel_place, first, flat_qkv, qkv_near, qkv_far, params, position, mask
    )
    if fast:
        feed_near = hold(feed_near, attended)
        feed_far = ring.core(feed_near)
    rows = jnp.stack([proj_bias, norm2_gain, norm2_bias, down_bias])
    *state, own_send, own_keep, feed_sums, proj_full = feed_own(
        kernel_place, attended, merged, cotangent, live, rows, params, proj_weight, qkv_near, qkv_far,
        up_weight, down_weight,
    )
    block_out, grad_residual, attn, other_send, other_keep, feed_sums = feed_other(
        kernel_place, state, rows, params, feed_sums, feed_near, feed_far
    )
    stack = None
    sums = jnp.zeros((1, 3 * D), f32)
    position_grad = jnp.zeros((QUADS, KEYS, LANES), f32)
    steps = count // ROWS

    def back(after, stack, sums, position_grad, begin, steps):
        return attend_back(
            after, stack, attn, qkv_rows, weights, padded, inverse_sums, proj_full, sums, position_grad, begin, steps
        )

    stack, sums, position_grad = back(attn, stack, sums, position_grad, 0, 1)
    after = attn
    if fast:
        other_got, own_got = ring.core(other_send), ring.core(own_send)
        feed_keeps = (own_keep, own_got, other_keep, other_got)
        down_y, up_x = stage(feed_first_body, place, sums, (512, 512), *feed_keeps)
        down_shard, up_got = ring.y(down_y), ring.x(up_x)
        after = up_x
    stack, sums, position_grad = back(after, stack, sums, position_grad, 1, steps - 1)
    after = attn
    if fast:
        down_x, up_y, feed_kept = stage(
            feed_second_body, place, sums, (256, 256, 512), *feed_keeps, down_shard, up_got
        )
        down_got, up_shard = ring.x(down_x), ring.y(up_y)
        after = up_y
    qkv_send, qkv_keep = qkv_back(kernel_place, after, turned_first, stack, attended, attn)
    after = qkv_send
    if fast:
        along = ring.along
        qkv_got = ring.core(qkv_send)
        span = 512 // along
        feed_parts = stage(
            feed_third_body, place, qkv_send, (span,) * along, feed_kept, down_got, up_shard, cost=LONG
        )
        feed_got = [ring.z(feed_parts[step], step) for step in range(1, along)]
        (qkv_y,) = stage(qkv_first_body, place, feed_parts[0], (512,), qkv_keep, qkv_got)
        qkv_shard = ring.y(qkv_y)
        after = qkv_y
    low, merge_send, merge_keep = merge_back(
        kernel_place, after, stack, grad_residual, merged, turned_hat, qkv_full, norm1_gain[None], merge_full, params,
        column, feed_sums, sums, position_grad,
    )
    if fast:
        merge_got = ring.core(merge_send)
        (feed_total,) = stage(total_body, place, merge_send, (span,), feed_parts[0], *feed_got)
        feed_all = [feed_total] + [ring.z(feed_total, step) for step in range(1, along)]
        qkv_x, qkv_kept = stage(
            qkv_second_body, place, feed_total, (256, 256), qkv_keep, qkv_got, qkv_shard, cost=LONG
        )
        qkv_x_got = ring.x(qkv_x)
        (merge_y,) = stage(merge_first_body, place, qkv_x, (288,), merge_keep, merge_got)
        merge_shard = ring.y(merge_y)
        section_grad, token = section_back(merge_y, low, hat, inverse, merge_full, params)
        merge_x, merge_kept, qkv_sum = stage(
            merge_second_body, place, token, (160, 160, 256), merge_keep, merge_got, merge_shard, qkv_kept, qkv_x_got
        )
        merge_x_got = ring.x(merge_x)
        (feed_near,) = stage(beside_body, place, merge_x, (span * along,), *feed_all)
        feed_far = ring.x(feed_near)
        span = 384 // along
        last_parts = stage(
            merge_third_body, place, feed_near, (span + 32,) * along, qkv_sum, merge_kept, merge_x_got
        )
        last_got = [ring.z(last_parts[step], step) for step in range(1, along)]
        last_total, vectors = stage(merge_total_body, place, last_parts[0], (span, 32), *([last_parts[0]] + last_got))
        last_all = [last_total] + [ring.z(last_total, step) for step in range(1, along)]
        feed_far = hold(feed_far, last_parts[0])
        feed_cores = ring.core(feed_near), ring.core(feed_far)
        down_grad, up_grad = feed_unpack(along, place, last_total, (feed_near, feed_far, *feed_cores))
        (last_near,) = stage(beside_body, place, down_grad, (384,), *last_all)
        last_far = ring.x(last_near)
        qkv_grad, proj_grad, merge_grad, vectors = last_unpack(
            along,
            place,
            (last_near, last_far, ring.core(last_near), ring.core(last_far), vectors, ring.core(vectors)),
        )
    else:
        section_grad, _ = section_back(low, low, hat, inverse, merge_full, params)
        down_grad, up_grad, qkv_grad, proj_grad, merge_grad, vectors = sum_plainly(
            tp_size, (own_send, own_keep, other_send, other_keep), (qkv_send, qkv_keep), (merge_send, merge_keep)
        )
    norm1_gain_grad, norm1_bias_grad, proj_bias_grad, norm2_gain_grad, norm2_bias_grad, down_bias_grad = [
        row.reshape(D) for row in vectors[0:6]
    ]
    qv_grad, up_bias_grad, gain_grad, bias_grad, table_grad = vectors[6:]
    return (
        block_out, section_grad, merge_grad, gain_grad.reshape(-1), bias_grad.reshape(-1),
        norm1_gain_grad, norm1_bias_grad, qkv_grad, qv_grad, table_grad.T, proj_grad, proj_bias_grad,
        norm2_gain_grad, norm2_bias_grad, up_grad, up_bias_grad.reshape(-1), down_grad, down_bias_grad,
    )


def solution(mesh):
    rows_size, tp_size = mesh.shape["rows"], mesh.shape["tp"]
    both = ("rows", "tp")
    return jax.shard_map(
        partial(per_device, rows_size, tp_size),
        mesh=mesh,
        in_specs=(
            P(both, None), P("rows"), P(both, None), P("tp", None), P("tp"), P("tp"), P(), P(),
            P(None, None, "tp"), P(None, "tp"), P(None, "tp"), P("tp", None), P(), P(), P(),
            P(None, "tp"), P("tp"), P("tp", None), P(),
        ),
        out_specs=(
            P(both, None), P(both, None), P("tp", None), P("tp"), P("tp"), P(), P(),
            P(None, None, "tp"), P(None, "tp"), P(None, "tp"), P("tp", None), P(), P(), P(),
            P(None, "tp"), P("tp"), P("tp", None), P(),
        ),
        check_vma=False,
    )
```

```python
from functools import partial
import math

import jax
import jax.numpy as jnp
from jax import lax
from jax.experimental import pallas as pl
from jax.experimental.pallas import tpu as pltpu
from jax.sharding import PartitionSpec as P

MERGE_IN = 1024
D = 512
HEADS = 16
HEAD_DIM = 32
FFN = 2048
WINDOW = 10
AREA = WINDOW * WINDOW
SIDE = 2 * WINDOW - 1
EPSILON = 1e-05
MASKED_SCORE = -1e30
EXACT = lax.Precision.HIGHEST
SCALING = 1.0 / math.sqrt(HEAD_DIM)
GROUP = 4
ROWS = GROUP * AREA
KEYS = 112
QUERIES = 128
QUADS = 4
QUAD = 4 * HEAD_DIM
LANES = 4 * QUERIES

bf16 = jnp.bfloat16
f32 = jnp.float32


def mm(a, b):
    return jnp.dot(a, b, preferred_element_type=f32)


def mm_t(a, b):
    return lax.dot_general(a, b, (((1,), (1,)), ((), ())), preferred_element_type=f32)


def t_mm(a, b):
    return lax.dot_general(a, b, (((0,), (0,)), ((), ())), preferred_element_type=f32)


def normalize(values):
    center = jnp.mean(values, axis=-1, keepdims=True)
    spread = jnp.mean(values * values, axis=-1, keepdims=True) - center * center
    inverse = lax.rsqrt(spread + EPSILON)
    return (values - center) * inverse, inverse


def norm_back(grad_hat, normed, inverse):
    first_mean = jnp.mean(grad_hat, axis=-1, keepdims=True)
    second_mean = jnp.mean(grad_hat * normed, axis=-1, keepdims=True)
    return inverse * (grad_hat - first_mean - normed * second_mean)


def column_sum(values):
    return jnp.sum(values, axis=0, keepdims=True)


def head_masks():
    lane = lax.broadcasted_iota(jnp.int32, (1, QUAD), 1) // HEAD_DIM
    return [(lane == head).astype(f32).astype(bf16) for head in range(4)]


def spread_heads(rows, masks):
    return jnp.concatenate([rows * mask for mask in masks], axis=0)


def kernel_call(body, grid, in_specs, out_specs, out_shape, scratch=(), flops=0, moved=0, room=32, cost=None):
    return pl.pallas_call(
        body,
        grid=grid,
        in_specs=in_specs,
        out_specs=out_specs,
        out_shape=out_shape,
        scratch_shapes=list(scratch),
        compiler_params=pltpu.CompilerParams(
            dimension_semantics=("arbitrary",) * len(grid), vmem_limit_bytes=room * 1024 * 1024
        ),
        cost_estimate=cost or COST,
    )


def whole(shape):
    return pl.BlockSpec(shape, lambda *_: (0,) * len(shape), pipeline_mode=pl.Buffered(1))


def by_rows(rows, columns):
    return pl.BlockSpec((rows, columns), lambda i: (i, 0))


def by_windows(shape):
    return pl.BlockSpec((GROUP,) + shape, lambda i: (i,) + (0,) * len(shape))


SCALARS = pl.BlockSpec(memory_space=pltpu.SMEM)
RESIDENT = pl.BlockSpec(memory_space=pltpu.VMEM)
ANYWHERE = pl.BlockSpec(memory_space=pl.ANY)


def in_hbm(array):
    return pltpu.with_memory_space_constraint(array, pltpu.HBM)


FEED_PACK = 1024
QKV_PACK = 384
PROJ_PACK = 128
MERGE_PACK = 256
STAGE_ROOM = 16
COST = pl.CostEstimate(flops=1, bytes_accessed=1, transcendentals=0)
LONG = pl.CostEstimate(flops=10**12, bytes_accessed=1, transcendentals=0)
SUMS = 16
PARAMS = 16


def shape_of(shape, dtype):
    return jax.ShapeDtypeStruct(shape, dtype)


def split(rows):
    high = rows.astype(bf16).astype(f32)
    return jnp.concatenate([high, rows - high], axis=0).astype(bf16)


def joined(pair):
    half = pair.shape[0] // 2
    return pair[:half].astype(f32) + pair[half:].astype(f32)


def both_shards(tp, mine, other, axis):
    return jnp.where(
        tp == 0, jnp.concatenate([mine, other], axis=axis), jnp.concatenate([other, mine], axis=axis)
    )


def pack_merge_body(place, merge_ref, out_ref):
    out_ref[...] = merge_ref[pl.ds(pl.multiple_of(256 * place[0], 256), 256), :]


def pack_params_body(
    place, after, merge_ref, qv_ref, up_bias_ref, table_ref, params_ref, out_ref, merge_s, qv_s, up_bias_s, table_s, sems
):
    pairs = ((merge_ref, merge_s), (qv_ref, qv_s), (up_bias_ref, up_bias_s), (table_ref, table_s))
    copies = [pltpu.make_async_copy(source, target, sems.at[index]) for index, (source, target) in enumerate(pairs)]
    for copy in copies:
        copy.start()
    params_ref[...] = jnp.zeros_like(params_ref)
    for copy in copies:
        copy.wait()
    params_ref[0:1, :] = merge_s[:, 0:512]
    params_ref[1:2, :] = merge_s[:, 512:1024]
    params_ref[2:3, 0:256] = qv_s[0:1, :]
    params_ref[2:3, 256:512] = qv_s[1:2, :]
    params_ref[3:4, :] = up_bias_s[:, 0:512]
    params_ref[4:5, :] = up_bias_s[:, 512:1024]
    params_ref[8:16, 0 : SIDE * SIDE] = table_s[...]
    out_ref[...] = split(params_ref[...])


def pack_params(place, after, merge, qv, up_bias, table):
    operands = [in_hbm(array) for array in (merge, qv, up_bias, table)]
    return pl.pallas_call(
        pack_params_body,
        in_specs=[SCALARS] + [ANYWHERE] * 5,
        out_specs=[RESIDENT] * 2,
        out_shape=[shape_of((PARAMS, D), f32), shape_of((2 * PARAMS, D), bf16)],
        scratch_shapes=[pltpu.VMEM(array.shape, f32) for array in operands] + [pltpu.SemaphoreType.DMA((4,))],
        cost_estimate=COST,
    )(place, after, *operands)


def plain_call(body, outs, operands, room=16, scratch=(), flops=0):
    return pl.pallas_call(
        body,
        in_specs=[SCALARS] + [pl.BlockSpec(memory_space=pltpu.VMEM)] * (len(operands) - 1),
        out_specs=[pl.BlockSpec(memory_space=pltpu.VMEM)] * len(outs),
        out_shape=outs,
        scratch_shapes=list(scratch),
        compiler_params=pltpu.CompilerParams(vmem_limit_bytes=room * 1024 * 1024),
        cost_estimate=COST,
    )(*operands)


def pack_qkv_body(place, qkv_ref, proj_ref, out):
    core = place[0]
    for side in range(2):
        rows = pl.ds(pl.multiple_of(768 * core + 384 * side, 128), 384)
        out[0:384, 256 * side : 256 * side + 256] = qkv_ref[rows, :]
    out[384:512, :] = proj_ref[pl.ds(pl.multiple_of(128 * core, 128), 128), :]


def pack_feed_body(place, up_ref, down_ref, out):
    half = pl.ds(pl.multiple_of(512 * place[0], 512), 512)
    out[0:512, :] = down_ref[half, :]
    out[512:1024, :] = up_ref[:, half]


def plain_call_after(body, outs, place, after, operands, room=16, scratch=(), flops=0, cost=COST):
    after = after if isinstance(after, tuple) else (after,)

    def without_after(place, *refs):
        return body(place, *refs[len(after) :])

    return pl.pallas_call(
        without_after,
        in_specs=[SCALARS] + [pl.BlockSpec(memory_space=pl.ANY)] * len(after) + [pl.BlockSpec(memory_space=pltpu.VMEM)] * len(operands),
        out_specs=[pl.BlockSpec(memory_space=pltpu.VMEM)] * len(outs),
        out_shape=outs,
        scratch_shapes=list(scratch),
        compiler_params=pltpu.CompilerParams(vmem_limit_bytes=room * 1024 * 1024),
        cost_estimate=cost,
    )(place, *after, *operands)


def masks_body(place, window_ref, mask_ref, live_ref, stage):
    windows = mask_ref.shape[0]
    shards = window_ref.shape[1] // (windows * AREA)
    stage[...] = jnp.zeros_like(stage)
    for window in range(windows):
        patch = window_ref[:, AREA * window : AREA * (window + 1)]
        for shard in range(1, shards):
            begin = AREA * (windows * shard + window)
            patch = jnp.where(place[3] == shard, window_ref[:, begin : begin + AREA], patch)
        stage[window : window + 1, 0:AREA] = patch
    patches = jnp.minimum(stage[...], 1).astype(f32)
    live = jnp.max(patches, axis=1, keepdims=True)
    inside = lax.broadcasted_iota(jnp.int32, (windows, QUERIES), 1) < AREA
    keep = jnp.logical_and(jnp.maximum(patches, 1.0 - live) > 0.5, inside)
    added = jnp.where(keep, 0.0, MASKED_SCORE)
    for window in range(windows):
        mask_ref[window] = added[window : window + 1, :]
        live_ref[AREA * window : AREA * (window + 1), :] = jnp.broadcast_to(live[window : window + 1, :], (AREA, 1))


def masks_of(place, after, window_mask, count):
    windows = count // AREA
    return plain_call_after(
        masks_body,
        [shape_of((windows, 1, QUERIES), f32), shape_of((count, 1), f32)],
        place,
        after,
        (window_mask[None],),
        scratch=[pltpu.VMEM((windows, QUERIES), jnp.int32)],
    )


def section_norm_body(after, rows_ref, hat_ref, inverse_ref, rows_s, sems):
    steps = rows_s.shape[0] // ROWS
    copies = []
    for step in range(steps):
        here = slice(ROWS * step, ROWS * (step + 1))
        copies.append(pltpu.make_async_copy(rows_ref.at[here, :], rows_s.at[here, :], sems.at[step]))
        copies[step].start()
    for step in range(steps):
        here = slice(ROWS * step, ROWS * (step + 1))
        copies[step].wait()
        hat, inverse = normalize(rows_s[here, :].astype(f32))
        hat_ref[here, :] = hat.astype(bf16)
        inverse_ref[here, :] = inverse


def section_norm(after, rows):
    count = rows.shape[0]
    return kernel_call(
        section_norm_body,
        (1,),
        [ANYWHERE, ANYWHERE],
        [RESIDENT, RESIDENT],
        [pltpu.VMEM((count, MERGE_IN), bf16), shape_of((count, 1), f32)],
        [pltpu.VMEM((count, MERGE_IN), bf16), pltpu.SemaphoreType.DMA((count // ROWS,))],
        room=16,
    )(after, in_hbm(rows))


def turn_body(after, first_ref, hat_ref, first_out, hat_out, hat_copy):
    columns = first_out.shape[0]
    first_out[...] = first_ref[:, pl.ds(pl.multiple_of(columns * pl.program_id(0), 128), columns)].T
    columns = hat_out.shape[0]
    hat = hat_ref[:, pl.ds(pl.multiple_of(columns * pl.program_id(0), 128), columns)]
    hat_out[...] = hat.T
    hat_copy[...] = hat


def turn(after, first, hat):
    count = hat.shape[0]
    steps = 4
    return kernel_call(
        turn_body,
        (steps,),
        [ANYWHERE, RESIDENT, RESIDENT],
        [
            pl.BlockSpec((D // steps, count), lambda i: (i, 0)),
            pl.BlockSpec((MERGE_IN // steps, count), lambda i: (i, 0)),
            pl.BlockSpec((count, MERGE_IN // steps), lambda i: (0, i)),
        ],
        [pltpu.HBM((D, count), bf16), pltpu.HBM((MERGE_IN, count), bf16), pltpu.HBM((count, MERGE_IN), bf16)],
        room=16,
    )(after, first, hat)


def gain_rows(tp, params, others):
    return both_shards(tp, params[0:1], others[0:1], 1), both_shards(tp, params[1:2], others[1:2], 1)


def merge_body(
    place, hat_ref, own_ref, near_ref, far_ref, params_ref, others_ref, rows_ref,
    merged_ref, first_ref, merge_ref, params_out_ref, column_ref,
    merge_s, shift_s, gain_s,
):

    @pl.when(pl.program_id(0) == 0)
    def _():
        core, tp = place[0], place[3]
        merge_s[pl.ds(pl.multiple_of(512 * tp, 512), 512), :] = own_ref[...]
        other = 512 * (1 - tp)
        merge_s[pl.ds(pl.multiple_of(other + 256 * core, 256), 256), :] = near_ref[...]
        merge_s[pl.ds(pl.multiple_of(other + 256 * (1 - core), 256), 256), :] = far_ref[...]
        merge_ref[...] = merge_s[...]
        params = params_ref[...]
        others = joined(others_ref[...])
        gain, bias = gain_rows(tp, params, others)
        gain_s[...] = gain.astype(bf16)
        shift_s[...] = mm(jnp.broadcast_to(bias, (16, MERGE_IN)).astype(bf16), merge_s[...])[0:1]
        params_out_ref[0:1, 0:1024] = gain
        params_out_ref[0:1, 1024:2048] = bias
        params_out_ref[1:2, 0:512] = both_shards(tp, params[2:3, 0:256], others[2:3, 0:256], 1)
        params_out_ref[1:2, 512:1024] = both_shards(tp, params[2:3, 256:512], others[2:3, 256:512], 1)
        params_out_ref[1:2, 1024:2048] = jnp.zeros((1, 1024), f32)
        params_out_ref[2:3, :] = both_shards(
            tp,
            jnp.concatenate([params[3:4], params[4:5]], axis=1),
            jnp.concatenate([others[3:4], others[4:5]], axis=1),
            1,
        )
        params_out_ref[3:8, :] = jnp.zeros((5, 2048), f32)
        params_out_ref[8:24, 0:512] = both_shards(tp, params[8:16], others[8:16], 0)
        params_out_ref[8:24, 512:2048] = jnp.zeros((16, 1536), f32)
        column_ref[...] = jnp.broadcast_to(gain, (128, MERGE_IN)).T

    here = pl.ds(pl.multiple_of(pl.program_id(0) * ROWS, 16), ROWS)
    merged = mm(hat_ref[here, :] * gain_s[...], merge_s[...]) + shift_s[...]
    merged_ref[...] = merged
    hat, _ = normalize(merged)
    first_ref[here, :] = (hat * rows_ref[0:1, :] + rows_ref[1:2, :]).astype(bf16)


def merge_rows(place, hat, own, near, far, params, others, rows):
    count = hat.shape[0]
    return kernel_call(
        merge_body,
        (count // ROWS,),
        [
            SCALARS, RESIDENT, RESIDENT, RESIDENT, RESIDENT, RESIDENT, RESIDENT, whole((2, D)),
        ],
        [by_rows(ROWS, D), RESIDENT, whole((MERGE_IN, D)), RESIDENT, whole((MERGE_IN, 128))],
        [
            pltpu.HBM((count, D), f32), pltpu.VMEM((count, D), bf16), pltpu.HBM((MERGE_IN, D), bf16),
            shape_of((24, 2048), f32), pltpu.HBM((MERGE_IN, 128), f32),
        ],
        [pltpu.VMEM((MERGE_IN, D), bf16), pltpu.VMEM((1, D), f32), pltpu.VMEM((1, MERGE_IN), bf16)],
        flops=2 * count * D * MERGE_IN,
        moved=count * 10 * D + 4 * D * MERGE_IN,
        room=24,
    )(place, hat, own, near, far, params, others, rows)


def value_blocks(values, masks):
    return [jnp.concatenate([values * mask, jnp.broadcast_to(mask, (QUERIES, QUAD))], axis=1) for mask in masks]


def turned_products(turned, scores):
    parts = []
    for pair in range(2):
        both = mm(turned[64 * pair : 64 * pair + 64], scores[:, 256 * pair : 256 * pair + 256])
        parts += [both[0:32, 0:128], both[32:64, 128:256]]
    return jnp.concatenate(parts, axis=0).T


def attend_body(
    place, first_ref, own_ref, near_ref, far_ref, params_ref, position_ref, mask_ref,
    qkv_out_ref, weights_ref, attended_ref, padded_ref, inverse_ref, qkv_ref,
    stage, mixed,
):
    @pl.when(pl.program_id(0) == 0)
    def _():
        core, tp = place[0], place[3]
        other = pl.ds(pl.multiple_of(256 * (1 - tp), 256), 256)
        qkv_ref[:, pl.ds(pl.multiple_of(256 * tp, 256), 256)] = own_ref[...]
        for ref, half in ((near_ref, core), (far_ref, 1 - core)):
            for side in range(2):
                rows = pl.ds(pl.multiple_of(768 * half + 384 * side, 128), 384)
                qkv_ref[rows, other] = ref[0:384, 256 * side : 256 * side + 256]

    here = pl.ds(pl.multiple_of(pl.program_id(0) * ROWS, 16), ROWS)
    stage[pl.ds(0, ROWS), :] = first_ref[here, :].astype(f32)
    stage[pl.ds(ROWS, 32), :] = jnp.zeros((32, D), f32)
    padded = jnp.concatenate(
        [stage[pl.ds(AREA * w, QUERIES), :].astype(bf16) for w in range(GROUP)], axis=0
    )
    queries = (SCALING * (mm(padded, qkv_ref[0:512, :]) + params_ref[1:2, 0:512])).astype(bf16)
    keys = mm(padded, qkv_ref[512:1024, :]).astype(bf16)
    values = (mm(padded, qkv_ref[1024:1536, :]) + params_ref[1:2, 512:1024]).astype(bf16)
    for w in range(GROUP):
        block = slice(QUERIES * w, QUERIES * (w + 1))
        qkv_out_ref[w, :, 0:D] = queries[block]
        qkv_out_ref[w, :, D : 2 * D] = keys[block]
        qkv_out_ref[w, :, 2 * D :] = values[block]
    masks = head_masks()
    for w in range(GROUP):
        mask = mask_ref[w]
        for quad in range(QUADS):
            columns = slice(QUAD * quad, QUAD * (quad + 1))
            rows = QUERIES * w
            spread = spread_heads(keys[rows : rows + QUERIES, columns], masks)
            scores = mm_t(queries[rows : rows + KEYS, columns], spread)
            raised = []
            for head in range(4):
                lanes = slice(QUERIES * head, QUERIES * (head + 1))
                part = scores[:, lanes] + position_ref[quad, :, lanes] + mask
                raised.append(jnp.exp(part - jnp.max(part, axis=1, keepdims=True)).astype(bf16))
            weights = jnp.concatenate(raised, axis=1)
            weights_ref[w, quad] = weights
            blocks = value_blocks(values[rows : rows + QUERIES, columns], masks)
            out = mm(weights, jnp.concatenate(blocks, axis=0))
            inverse = 1.0 / out[:, QUAD:]
            both = out[:, :QUAD] * inverse
            inverse_ref[w, :, columns] = inverse
            padded_ref[w, :, columns] = both.astype(bf16)
            mixed[pl.ds(AREA * w, AREA), columns] = both[0:AREA]
    attended_ref[...] = mixed[...].astype(bf16)


def attend(place, first, own, near, far, params, position, mask):
    count = first.shape[0]
    windows = count // AREA
    return kernel_call(
        attend_body,
        (count // ROWS,),
        [
            SCALARS, RESIDENT, RESIDENT, RESIDENT, RESIDENT, RESIDENT, RESIDENT, by_windows((1, QUERIES)),
        ],
        [
            by_windows((QUERIES, 3 * D)), by_windows((QUADS, KEYS, LANES)), by_rows(ROWS, D),
            by_windows((KEYS, D)), by_windows((KEYS, D)), RESIDENT,
        ],
        [
            pltpu.HBM((windows, QUERIES, 3 * D), bf16), pltpu.HBM((windows, QUADS, KEYS, LANES), bf16),
            pltpu.HBM((count, D), bf16), pltpu.HBM((windows, KEYS, D), bf16), pltpu.HBM((windows, KEYS, D), f32),
            shape_of((3 * D, D), bf16),
        ],
        [pltpu.VMEM((ROWS + 32, D), f32), pltpu.VMEM((ROWS, D), f32)],
        flops=2 * count * D * (3 * D + 4 * AREA),
        moved=count * 10 * D + windows * QUADS * KEYS * LANES * 2,
        room=20,
    )(place, first, own, near, far, params, position, mask)


def gelu_parts(t):
    chance = 0.5 * lax.erf(t * math.sqrt(0.5)) + 0.5
    density = jnp.exp(t * t * -0.5) * (1.0 / math.sqrt(2.0 * math.pi))
    return t * chance, chance + t * density


TILE = 512
FEED_ROWS = 400
OWN_ROOM = 18
OTHER_ROOM = 12
AB_ROOM = 20
NEAR_ROOM = 20


def feed_tile(up, down, bias, second_ref, turned_ref, branch_ref, total_s, back_s, active_s, raise_s, target, first):
    sums = jnp.zeros((1, TILE), f32)
    for begin in range(0, second_ref.shape[0], FEED_ROWS):
        here = slice(begin, begin + FEED_ROWS)
        value, slope = gelu_parts(mm(second_ref[here, :], up) + bias)
        active = value.astype(bf16)
        grad_raised = (mm_t(branch_ref[here, :], down) * slope).astype(bf16)
        active_s[here, :] = active
        raise_s[here, :] = grad_raised
        sums += column_sum(grad_raised.astype(f32))
        out = mm(active, down)
        back = mm_t(grad_raised, up)
        if first:
            total_s[here, :] = out
            back_s[here, :] = back
        else:
            total_s[here, :] += out
            back_s[here, :] += back
    target[0:512, :] = t_mm(active_s[...], branch_ref[...]).astype(bf16)
    target[512:1024, :] = mm(turned_ref[...], raise_s[...]).astype(bf16)
    return sums


def feed_own_body(
    place, attended_ref, merged_ref, cotangent_ref, live_ref, proj_bias, norm_gain, norm_bias, params_ref,
    proj_own, near_ref, far_ref, up_own, down_own,
    residual_ref, total_ref, back_ref, second_ref, turned_ref, branch_ref, send_ref, sums_ref, proj_ref,
    active_s, raise_s,
):
    step = pl.program_id(0)
    blocks = pl.num_programs(0) - 1
    core, tp = place[0], place[3]

    @pl.when(step == 0)
    def _():
        proj_ref[pl.ds(pl.multiple_of(256 * tp, 256), 256), :] = proj_own[...]
        for ref, which in ((near_ref, core), (far_ref, 1 - core)):
            proj_ref[pl.ds(pl.multiple_of(256 * (1 - tp) + 128 * which, 128), 128), :] = ref[384:512, :]
        sums_ref[...] = jnp.zeros_like(sums_ref)

    @pl.when(step < blocks)
    def _():
        here = pl.ds(pl.multiple_of(step * ROWS, 16), ROWS)
        residual = merged_ref[...] + mm(attended_ref[...], proj_ref[...]) + proj_bias[...]
        residual_ref[here, :] = residual
        hat, _ = normalize(residual)
        second_ref[here, :] = (hat * norm_gain[...] + norm_bias[...]).astype(bf16)
        branch = cotangent_ref[...].astype(f32) * live_ref[...]
        branch_ref[here, :] = branch.astype(bf16)
        sums_ref[7:8, :] += column_sum(branch)

    @pl.when(step == blocks)
    def _():
        turned_ref[...] = second_ref[...].T
        shard = 2 * tp + 1 - core
        units = pl.ds(pl.multiple_of(TILE * (1 - core), TILE), TILE)
        bias = params_ref[2:3, pl.ds(pl.multiple_of(TILE * shard, TILE), TILE)]
        sums_ref[pl.ds(shard, 1), :] = feed_tile(
            up_own[:, units], down_own[units, :], bias, second_ref, turned_ref, branch_ref, total_ref, back_ref,
            active_s, raise_s, send_ref, True,
        )


def feed_own(
    place, attended, merged, cotangent, live, proj_bias, gain, bias, down_bias, params, proj, near, far, up, down
):
    count = attended.shape[0]
    blocks = count // ROWS

    def taken(columns):
        return pl.BlockSpec((ROWS, columns), lambda i: (jnp.minimum(i, blocks - 1), 0))

    return kernel_call(
        feed_own_body,
        (blocks + 1,),
        [
            SCALARS, taken(D), taken(D), taken(D), taken(1), RESIDENT, RESIDENT, RESIDENT, RESIDENT, RESIDENT, RESIDENT, RESIDENT,
            RESIDENT, RESIDENT,
        ],
        [RESIDENT] * 9,
        [pltpu.VMEM((count, D), f32)] * 3
        + [pltpu.VMEM((count, D), bf16), pltpu.VMEM((D, count), bf16), pltpu.VMEM((count, D), bf16)]
        + [pltpu.VMEM((FEED_PACK, D), bf16), shape_of((8, D), f32), shape_of((D, D), bf16)],
        [pltpu.VMEM((count, TILE), bf16)] * 2,
        room=OWN_ROOM,
    )(
        place, in_hbm(attended), in_hbm(merged), in_hbm(cotangent), in_hbm(live), proj_bias, gain, bias, params, proj,
        near, far, up, down,
    )


def feed_middle_body(
    own, place, second_ref, turned_ref, branch_ref, total_in, back_in, params_ref, sums_in, *refs
):
    weights, (total_ref, back_ref, target_ref, sums_ref, active_s, raise_s) = refs[:-6], refs[-6:]
    core, tp = place[0], place[3]
    sums_ref[...] = sums_in[...]
    if own:
        shard = 2 * tp + core
        units = pl.ds(pl.multiple_of(TILE * core, TILE), TILE)
        up, down = weights[0][:, units], weights[1][units, :]
    else:
        shard = 2 * (1 - tp) + 1 - core
        up, down = weights[0][512:1024, :], weights[0][0:512, :]
    bias = params_ref[2:3, pl.ds(pl.multiple_of(TILE * shard, TILE), TILE)]
    sums_ref[pl.ds(shard, 1), :] = feed_tile(
        up, down, bias, second_ref, turned_ref, branch_ref, total_ref, back_ref, active_s, raise_s, target_ref, False
    )


def feed_middle(own, place, second, turned, branch, total, back, params, sums, weights, cost=COST):
    count = second.shape[0]
    return pl.pallas_call(
        partial(feed_middle_body, own),
        in_specs=[SCALARS] + [RESIDENT] * (7 + len(weights)),
        out_specs=[RESIDENT] * 4,
        out_shape=[pltpu.VMEM((count, D), f32)] * 2 + [pltpu.VMEM((FEED_PACK, D), bf16), shape_of((8, D), f32)],
        scratch_shapes=[pltpu.VMEM((count, TILE), bf16)] * 2,
        input_output_aliases={4: 0, 5: 1},
        compiler_params=pltpu.CompilerParams(vmem_limit_bytes=OTHER_ROOM * 1024 * 1024),
        cost_estimate=cost,
    )(place, second, turned, branch, total, back, params, sums, *weights)


def feed_near_body(
    place, residual_ref, second_ref, turned_ref, branch_ref, total_in, back_in, down_bias, norm_gain, params_ref,
    sums_in, near_ref, attended_ref,
    out_ref, grad_residual_ref, attn_ref, keep_ref, proj_send, proj_keep, sums_ref,
    total_s, back_s, active_s, raise_s, attended_s, proj_s, sem,
):
    step = pl.program_id(0)
    core, tp = place[0], place[3]
    fetch = pltpu.make_async_copy(attended_ref, attended_s, sem)

    @pl.when(step == 0)
    def _():
        fetch.start()
        sums_ref[...] = sums_in[...]
        shard = 2 * (1 - tp) + core
        bias = params_ref[2:3, pl.ds(pl.multiple_of(TILE * shard, TILE), TILE)]
        sums_ref[pl.ds(shard, 1), :] = feed_tile(
            near_ref[512:1024, :], near_ref[0:512, :], bias, second_ref, turned_ref, branch_ref, total_s, back_s,
            active_s, raise_s, keep_ref, True,
        )

    @pl.when(step >= 1)
    def _():
        here = pl.ds(pl.multiple_of((step - 1) * ROWS, 16), ROWS)
        residual = residual_ref[here, :]
        out_ref[...] = (residual + down_bias[...] + total_in[here, :] + total_s[here, :]).astype(bf16)
        hat, inverse = normalize(residual)
        grad_second = back_in[here, :] + back_s[here, :]
        grad_residual = branch_ref[here, :].astype(f32) + norm_back(grad_second * norm_gain[...], hat, inverse)
        grad_residual_ref[here, :] = grad_residual
        attn_ref[here, :] = grad_residual.astype(bf16)
        sums_ref[4:5, :] += column_sum(grad_residual)
        sums_ref[5:6, :] += column_sum(grad_second * hat)
        sums_ref[6:7, :] += column_sum(grad_second)

    @pl.when(step == pl.num_programs(0) - 1)
    def _():
        fetch.wait()
        proj_s[...] = t_mm(attended_s[...], attn_ref[...]).astype(bf16)
        for target, half in ((proj_send, 1 - core), (proj_keep, core)):
            for other in range(2):
                shard = jnp.where(other == 0, tp, 1 - tp)
                rows = pl.ds(pl.multiple_of(256 * shard + 128 * half, 128), 128)
                target[PROJ_PACK * other : PROJ_PACK * (other + 1), :] = proj_s[rows, :]


def feed_near(place, residual, second, turned, branch, total, back, down_bias, gain, params, sums, near, attended):
    count = residual.shape[0]
    blocks = count // ROWS

    def given(columns):
        return pl.BlockSpec((ROWS, columns), lambda i: (jnp.maximum(i - 1, 0), 0))

    return kernel_call(
        feed_near_body,
        (blocks + 1,),
        [SCALARS] + [RESIDENT] * 9 + [whole((8, D)), RESIDENT]
        + [pl.BlockSpec(memory_space=pl.ANY)],
        [given(D)] + [RESIDENT] * 5 + [whole((8, D))],
        [pltpu.HBM((count, D), bf16), pltpu.VMEM((count, D), f32), pltpu.VMEM((count, D), bf16)]
        + [pltpu.VMEM((FEED_PACK, D), bf16)] + [pltpu.VMEM((2 * PROJ_PACK, D), bf16)] * 2
        + [shape_of((8, D), f32)],
        [pltpu.VMEM((count, D), f32)] * 2 + [pltpu.VMEM((count, TILE), bf16)] * 2
        + [pltpu.VMEM((count, D), bf16), pltpu.VMEM((D, D), bf16), pltpu.SemaphoreType.DMA],
        room=NEAR_ROOM,
    )(
        place, residual, second, turned, branch, total, back, down_bias, gain, params, sums, near, in_hbm(attended)
    )


def attend_back_body(
    after, attn_ref, qkv_in_ref, weights_ref, padded_ref, inverse_ref, proj_ref,
    merged_ref, grad_residual_ref, qkv_ref, rows_ref,
    stack_ref, low_ref, sums_ref, vectors_ref, position_ref,
    stage, grads,
):
    @pl.when(pl.program_id(0) == 0)
    def _():
        vectors_ref[...] = jnp.zeros_like(vectors_ref)
        sums_ref[...] = jnp.zeros_like(sums_ref)
        position_ref[...] = jnp.zeros_like(position_ref)

    here = pl.ds(pl.multiple_of(pl.program_id(0) * ROWS, 16), ROWS)
    stage[pl.ds(0, ROWS), :] = attn_ref[here, :].astype(f32)
    stage[pl.ds(ROWS, 32), :] = jnp.zeros((32, D), f32)
    real = lax.broadcasted_iota(jnp.int32, (KEYS, 1), 0) < AREA
    padded = jnp.concatenate(
        [jnp.where(real, stage[pl.ds(AREA * w, KEYS), :], 0.0).astype(bf16) for w in range(GROUP)], axis=0
    )
    grad_attended = mm_t(padded, proj_ref[...])
    masks = head_masks()
    empty = jnp.zeros((QUERIES - KEYS, QUAD), bf16)
    kept = {}
    for w in range(GROUP):
        for quad in range(QUADS):
            columns = slice(QUAD * quad, QUAD * (quad + 1))
            values = qkv_in_ref[w, :, 2 * D + QUAD * quad : 2 * D + QUAD * (quad + 1)]
            grad = grad_attended[KEYS * w : KEYS * (w + 1), columns] * inverse_ref[w, :, columns]
            low = grad.astype(bf16)
            taken = (grad * padded_ref[w, :, columns].astype(f32)).astype(bf16)
            both = jnp.concatenate([low, -taken], axis=1)
            change = jnp.concatenate([mm_t(both, block) for block in value_blocks(values, masks)], axis=1)
            grad_scores = (weights_ref[w, quad].astype(f32) * change).astype(bf16)
            position_ref[quad] += grad_scores.astype(f32)
            kept[w, quad] = (low, grad_scores)
    for w in range(GROUP):
        to = pl.ds(AREA * w, AREA)
        for quad in range(QUADS):
            low, grad_scores = kept[w, quad]
            queries = qkv_in_ref[w, :, QUAD * quad : QUAD * (quad + 1)]
            keys = qkv_in_ref[w, :, D + QUAD * quad : D + QUAD * (quad + 1)]
            grad_queries = mm(grad_scores, spread_heads(keys, masks)) * SCALING
            grad_keys = turned_products(queries.T[:, :KEYS], grad_scores)
            grad_values = turned_products(jnp.concatenate([low, empty], axis=0).T[:, :KEYS], weights_ref[w, quad])
            for part, grad in enumerate((grad_queries, grad_keys, grad_values)):
                grads[to, D * part + QUAD * quad : D * part + QUAD * (quad + 1)] = grad[0:AREA]
    stack = grads[...].astype(bf16)
    stack_ref[here, :] = stack
    sums_ref[...] += column_sum(stack.astype(f32))
    grad_first = (
        mm_t(stack[:, 0:D], qkv_ref[0:D, :])
        + mm_t(stack[:, D : 2 * D], qkv_ref[D : 2 * D, :])
        + mm_t(stack[:, 2 * D :], qkv_ref[2 * D :, :])
    )
    normed, inverse = normalize(merged_ref[...])
    grad_merged = grad_residual_ref[here, :] + norm_back(grad_first * rows_ref[0:1, :], normed, inverse)
    low = grad_merged.astype(bf16)
    low_ref[here, :] = low
    vectors_ref[0:1, :] += column_sum(grad_first * normed)
    vectors_ref[1:2, :] += column_sum(grad_first)
    vectors_ref[2:3, :] += column_sum(low.astype(f32))


def attend_back(after, attn, qkv_in, weights, padded, inverse, proj, merged, grad_residual, qkv, rows):
    count = attn.shape[0]
    return kernel_call(
        attend_back_body,
        (count // ROWS,),
        [
            ANYWHERE, RESIDENT, by_windows((QUERIES, 3 * D)), by_windows((QUADS, KEYS, LANES)),
            by_windows((KEYS, D)), by_windows((KEYS, D)), RESIDENT, by_rows(ROWS, D), RESIDENT, RESIDENT, RESIDENT,
        ],
        [RESIDENT] * 5,
        [
            pltpu.VMEM((count, 3 * D), bf16), pltpu.VMEM((count, D), bf16), shape_of((1, 3 * D), f32),
            shape_of((8, D), f32), shape_of((QUADS, KEYS, LANES), f32),
        ],
        [pltpu.VMEM((ROWS + 32, D), f32), pltpu.VMEM((ROWS, 3 * D), f32)],
        room=AB_ROOM,
    )(
        after, attn, *[in_hbm(array) for array in (qkv_in, weights, padded, inverse)], proj, in_hbm(merged),
        grad_residual, qkv, rows,
    )


def qkv_back_body(place, after, turned_ref, stack_ref, send_ref, keep_ref, qkv_s):
    part = pl.program_id(0)
    core, tp = place[0], place[3]
    qkv_s[...] = mm(turned_ref[...], stack_ref[:, pl.ds(pl.multiple_of(D * part, D), D)]).astype(bf16)
    for target, half in ((send_ref, 1 - core), (keep_ref, core)):
        for other in range(2):
            shard = jnp.where(other == 0, tp, 1 - tp)
            base = QKV_PACK * other
            rows = pl.ds(pl.multiple_of(256 * half, 256), 256)
            columns = pl.ds(pl.multiple_of(256 * shard, 256), 256)

            @pl.when(part < 2)
            def _():
                target[base : base + 256, pl.ds(pl.multiple_of(256 * part, 256), 256)] = qkv_s[rows, columns]

            @pl.when(part == 2)
            def _():
                block = qkv_s[rows, columns]
                target[base + 256 : base + 384, 0:256] = block[0:128]
                target[base + 256 : base + 384, 256:512] = block[128:256]


def qkv_back(place, after, turned, stack):
    count = stack.shape[0]
    return kernel_call(
        qkv_back_body,
        (3,),
        [
            SCALARS, ANYWHERE, RESIDENT, RESIDENT,
        ],
        [RESIDENT, RESIDENT],
        [pltpu.VMEM((2 * QKV_PACK, D), bf16), pltpu.VMEM((2 * QKV_PACK, D), bf16)],
        [pltpu.VMEM((D, D), bf16)],
        room=12,
    )(place, after, turned, stack)


def merge_back_body(
    place, after, low_ref, turned_ref, merge_ref, params_ref, column_ref, feed_sums_ref, qkv_sums_ref, vectors_ref,
    position_ref,
    send_ref, keep_ref,
    fold_s, all_s, raw_s,
):
    core, tp = place[0], place[3]
    total = vectors_ref[2:3, :]
    pair = jnp.concatenate([split(total), jnp.zeros((14, D), bf16)], axis=0)
    ones = jnp.ones((16, D), bf16)
    raw_s[...] = mm(turned_ref[...], low_ref[...])
    all_s[...] = jnp.zeros_like(all_s)
    all_s[0:2, :] = vectors_ref[0:2, :]
    all_s[2:6, :] = feed_sums_ref[4:8, :]
    all_s[6:7, :] = qkv_sums_ref[:, 0:D]
    all_s[7:8, :] = qkv_sums_ref[:, 2 * D :]
    all_s[8:12, :] = feed_sums_ref[0:4, :]
    all_s[16:32, 0:384] = fold_place(position_ref, fold_s)
    for tile in range(2):
        rows = slice(512 * tile, 512 * (tile + 1))
        merge = merge_ref[rows, :]
        scaled = raw_s[rows, :] * merge.astype(f32)
        scaled_high = scaled.astype(bf16)
        scaled_rest = (scaled - scaled_high.astype(f32)).astype(bf16)
        all_s[12 + tile : 13 + tile, :] = (mm_t(ones, scaled_high) + mm_t(ones, scaled_rest))[0:1]
        all_s[14 + tile : 15 + tile, :] = column_sum(mm_t(pair, merge))
    for target, half in ((send_ref, 1 - core), (keep_ref, core)):
        for other in range(2):
            begin = pl.multiple_of(512 * jnp.where(other == 0, tp, 1 - tp) + 256 * half, 256)
            bias = jnp.broadcast_to(params_ref[0:1, pl.ds(1024 + begin, 256)], (16, 256)).astype(bf16)
            gain = column_ref[pl.ds(begin, 256), 0:1]
            block = raw_s[pl.ds(begin, 256), :] * gain + t_mm(bias, pair)
            target[MERGE_PACK * other : MERGE_PACK * (other + 1), :] = block.astype(bf16)
        target[2 * MERGE_PACK :, :] = split(all_s[pl.ds(pl.multiple_of(SUMS * half, SUMS), SUMS), :])


def merge_back(place, after, low, turned, merge, params, column, feed_sums, sums, vectors, position):
    pack = 2 * MERGE_PACK + 2 * SUMS
    return pl.pallas_call(
        merge_back_body,
        in_specs=[SCALARS, ANYWHERE] + [RESIDENT] * 9,
        out_specs=[RESIDENT] * 2,
        out_shape=[pltpu.VMEM((pack, D), bf16), pltpu.VMEM((pack, D), bf16)],
        scratch_shapes=[
            pltpu.VMEM((HEADS, KEYS, 256), f32), pltpu.VMEM((32, D), f32), pltpu.VMEM((MERGE_IN, D), f32),
        ],
        compiler_params=pltpu.CompilerParams(vmem_limit_bytes=20 * 1024 * 1024),
        cost_estimate=COST,
    )(place, after, low, turned, merge, params, column, feed_sums, sums, vectors, position)


def section_back_body(after, low_ref, hat_ref, inverse_ref, merge_ref, params_ref, out_ref, token_ref):
    token_ref[...] = jnp.zeros_like(token_ref)
    scaled = mm_t(low_ref[...], merge_ref[...]) * params_ref[0:1, 0:MERGE_IN]
    out_ref[...] = norm_back(scaled, hat_ref[...].astype(f32), inverse_ref[...]).astype(bf16)


def section_back(after, low, hat, inverse, merge, params):
    count = low.shape[0]
    return kernel_call(
        section_back_body,
        (count // ROWS,),
        [
            pl.BlockSpec(memory_space=pl.ANY), by_rows(ROWS, D), by_rows(ROWS, MERGE_IN), by_rows(ROWS, 1),
            whole((MERGE_IN, D)), whole((24, 2048)),
        ],
        [by_rows(ROWS, MERGE_IN), whole((8, 128))],
        [pltpu.HBM((count, MERGE_IN), bf16), shape_of((8, 128), f32)],
        flops=2 * count * D * MERGE_IN,
        moved=count * 5 * MERGE_IN,
        room=24,
    )(after, in_hbm(low), in_hbm(hat), inverse, merge, params)


def spread_matrix():
    place = lax.broadcasted_iota(jnp.int32, (QUERIES, 256), 0)
    lane = lax.broadcasted_iota(jnp.int32, (QUERIES, 256), 1)
    target = place + (SIDE - WINDOW) * (place // WINDOW)
    return jnp.logical_and(lane == target, place < AREA).astype(f32)


def expand_body(params_ref, place_ref, stage_s):
    spread = spread_matrix().astype(bf16)
    for head in range(HEADS):
        stage = stage_s.at[head]
        stage[96:KEYS, :] = jnp.zeros((KEYS - 96, 256), f32)
        line = params_ref[8 + head : 9 + head, 0:384]
        lines = jnp.concatenate(
            [pltpu.roll(line, (384 - (WINDOW - 1) * (SIDE + 1) + x) % 384, 1) for x in range(WINDOW)]
            + [jnp.zeros((6, 384), f32)],
            axis=0,
        )
        for y in range(WINDOW):
            moved = pltpu.roll(lines, SIDE * y, 1) if y else lines
            stage[pl.ds(WINDOW * y, WINDOW), :] = moved[0:WINDOW, 0:256]
        rows = stage[...]
        high = rows.astype(bf16)
        rest = rows - high.astype(f32)
        middle = rest.astype(bf16)
        low = (rest - middle.astype(f32)).astype(bf16)
        block = mm_t(high, spread) + mm_t(middle, spread) + mm_t(low, spread)
        block = jnp.concatenate([block, jnp.zeros((QUERIES - KEYS, QUERIES), f32)], axis=0).T[:KEYS]
        place_ref[head // 4, :, QUERIES * (head % 4) : QUERIES * (head % 4 + 1)] = block


def expand(params):
    return kernel_call(
        expand_body,
        (1,),
        [whole((24, 2048))],
        whole((QUADS, KEYS, LANES)),
        shape_of((QUADS, KEYS, LANES), f32),
        [pltpu.VMEM((HEADS, KEYS, 256), f32)],
        room=24,
    )(params)


def fold_place(place_ref, stage_s):
    spread = spread_matrix().astype(bf16)
    lines = []
    for head in range(HEADS):
        stage = stage_s.at[head]
        rows = place_ref[head // 4, :, QUERIES * (head % 4) : QUERIES * (head % 4 + 1)]
        rows = jnp.concatenate([rows, jnp.zeros((QUERIES - KEYS, QUERIES), f32)], axis=0).T[:KEYS]
        high = rows.astype(bf16)
        rest = (rows - high.astype(f32)).astype(bf16)
        stage[...] = mm(high, spread) + mm(rest, spread)
        total = jnp.zeros((WINDOW, 384), f32)
        for y in range(WINDOW):
            part = jnp.concatenate(
                [stage[pl.ds(WINDOW * y, WINDOW), :], jnp.zeros((WINDOW, 128), f32)], axis=1
            )
            total += pltpu.roll(part, SIDE * (WINDOW - 1 - y), 1) if y < WINDOW - 1 else part
        line = total[WINDOW - 1 : WINDOW, :]
        for x in range(WINDOW - 1):
            line += pltpu.roll(total[x : x + 1, :], WINDOW - 1 - x, 1)
        lines.append(line)
    return jnp.concatenate(lines, axis=0)


class Ring:
    def __init__(self, place, rows_size):
        self.place = place
        self.rows_size = rows_size
        self.along = rows_size // 4

    def to(self, array, bits):
        return lax.ppermute(array, "rows", [(i, i ^ bits) for i in range(self.rows_size)])

    def core(self, array):
        return self.to(array, 1)

    def x(self, array):
        return self.to(array, 2)

    def z(self, array, step):
        return self.to(array, 4 * step)

    def y(self, array):
        return lax.ppermute(array, "tp", [(0, 1), (1, 0)])

    def xy(self, array):
        pairs = [(2 * i + t, 2 * (i ^ 2) + 1 - t) for i in range(self.rows_size) for t in range(2)]
        return lax.ppermute(array, ("rows", "tp"), pairs)


def rows_of(array, begin, rows):
    return lax.dynamic_slice_in_dim(array, begin, rows, 0).astype(f32)


def stage(body, place, after, rows, *operands, cost=COST, scratch=()):
    return plain_call_after(
        body, [pltpu.VMEM((count, D), bf16) for count in rows], place, after, operands, room=STAGE_ROOM, cost=cost,
        scratch=scratch,
    )


def added(refs, begin, rows):
    here = pl.ds(pl.multiple_of(begin, 16), rows)
    total = refs[0][here, :].astype(f32)
    for ref in refs[1:]:
        total = total + ref[here, :].astype(f32)
    return total


def part(ref, begin, rows):
    return ref.at[begin : begin + rows, :]


def feed_first_body(
    place, own_keep, own_got, other_keep, other_got, proj_keep, proj_got, down_y, up_x
):
    down_y[0:512, :] = added((other_keep, other_got), 0, 512).astype(bf16)
    down_y[512:640, :] = added((proj_keep, proj_got), 128, 128).astype(bf16)
    begin = 512 + 256 * (1 - place[1])
    up_x[0:256, :] = added((own_keep, own_got), begin, 256).astype(bf16)
    up_x[256:512, :] = added((other_keep, other_got), begin, 256).astype(bf16)


def feed_second_body(
    place, own_keep, own_got, other_keep, other_got, proj_keep, proj_got, down_shard, up_got, down_x, up_y, kept
):
    x = place[1]
    for target, side in ((down_x, 1 - x), (kept, x)):
        target[0:256, :] = added((own_keep, own_got, down_shard), 256 * side, 256).astype(bf16)
        proj = (proj_keep, proj_got, part(down_shard, 512, 128))
        target[256:320, :] = added(proj, 64 * side, 64).astype(bf16)
    begin = 512 + 256 * x
    up_y[...] = (added((other_keep, other_got), begin, 256) + up_got[256:512, :].astype(f32)).astype(bf16)
    kept[320:576, :] = (added((own_keep, own_got), begin, 256) + up_got[0:256, :].astype(f32)).astype(bf16)


def feed_third_body(place, kept, down_got, up_shard, *outs):
    for step, out in enumerate(outs):
        to = place[2] ^ step
        offset = 0
        for ref, got, begin, size in ((kept, down_got, 0, 256), (kept, down_got, 256, 64), (kept, up_shard, 320, 256)):
            span = size // len(outs)
            mine = part(ref, begin, size)
            theirs = part(got, begin if got is down_got else 0, size)
            out[offset : offset + span, :] = added((mine, theirs), to * span, span).astype(bf16)
            offset += span


def total_body(place, *refs):
    refs[-1][...] = added(refs[:-1], 0, refs[-1].shape[0]).astype(bf16)


def beside_body(place, *refs):
    rows = refs[0].shape[0]
    for index, ref in enumerate(refs[:-1]):
        refs[-1][rows * index : rows * (index + 1), :] = ref[...]


def last_first_body(place, keep, got, qkv_keep, qkv_got, to_y, to_x, to_both, kept, sums_s):
    x = place[1]
    sums_s[...] = joined(keep[512:544, :]) + joined(got[512:544, :])
    for target, other, side in ((to_y, 1, x), (to_x, 0, 1 - x), (to_both, 1, 1 - x), (kept, 0, x)):
        target[0:192, :] = added((qkv_keep, qkv_got), QKV_PACK * other + 192 * side, 192).astype(bf16)
        target[192:320, :] = added((keep, got), MERGE_PACK * other + 128 * side, 128).astype(bf16)
        target[320:336, :] = split(sums_s[pl.ds(pl.multiple_of(8 * side, 8), 8), :])


def last_second_body(place, *refs):
    blocks, outs = refs[:4], refs[4:]
    vectors = split(sum(joined(ref[320:336, :]) for ref in blocks))
    wide, narrow = 192 // len(outs), 128 // len(outs)
    for step, out in enumerate(outs):
        to = place[2] ^ step
        out[0:wide, :] = added(blocks, to * wide, wide).astype(bf16)
        out[wide : wide + narrow, :] = added(blocks, 192 + to * narrow, narrow).astype(bf16)
        out[wide + narrow :, :] = vectors


def merge_total_body(place, *refs):
    blocks, (out, vectors) = refs[:-2], refs[-2:]
    rows = out.shape[0]
    out[...] = added(blocks, 0, rows).astype(bf16)
    vectors[...] = split(sum(joined(ref[rows : rows + 16, :]) for ref in blocks))


def last_beside_body(place, vectors, *refs):
    rows = refs[0].shape[0]
    for index, ref in enumerate(refs[:-1]):
        refs[-1][rows * index : rows * (index + 1), :] = ref[...]
    refs[-1][rows * (len(refs) - 1) :, :] = vectors[...]


def in_order(place, near, far, stage, rows, along):
    piece = sum(rows) // 2 // along
    for side, ref in ((place[1], near), (1 - place[1], far)):
        for step in range(along):
            begin, offset = 0, piece * step
            for size in rows:
                span = size // 2 // along
                to = begin + side * (size // 2) + (place[2] ^ step) * span
                stage[pl.ds(pl.multiple_of(to, 16), span), :] = ref[offset : offset + span, :]
                begin += size
                offset += span


def feed_unpack_body(along, place, near, far, core_near, core_far, down_ref, up_ref, proj_ref, token_ref, stage):
    token_ref[...] = jnp.zeros_like(token_ref)
    for target, mine, beside in ((place[0], near, far), (1 - place[0], core_near, core_far)):
        in_order(place, mine, beside, stage, (512, PROJ_PACK, 512), along)
        wide = pl.ds(pl.multiple_of(512 * target, 512), 512)
        down_ref[wide, :] = stage[0:512, :].astype(f32)
        proj_ref[pl.ds(pl.multiple_of(128 * target, 128), 128), :] = stage[512:640, :].astype(f32)
        up_ref[:, wide] = stage[640:1152, :].astype(f32)


def feed_unpack(along, place, after, parts):
    return plain_call_after(
        partial(feed_unpack_body, along),
        [pltpu.HBM((FFN // 2, D), f32), pltpu.HBM((D, FFN // 2), f32), pltpu.HBM((D // 2, D), f32), shape_of((8, 128), f32)],
        place,
        after,
        parts,
        scratch=[pltpu.VMEM((FEED_PACK + PROJ_PACK, D), bf16)],
        room=24,
    )


def last_unpack_body(along, place, mine, other, qkv_ref, merge_ref, *refs):
    vectors, stage, all_s = refs[:-2], refs[-2], refs[-1]
    half = mine.shape[0] // 2
    rows = half - 16
    for target, ref in ((place[0], mine), (1 - place[0], other)):
        near, far = ref.at[0:half, :], ref.at[half:, :]
        in_order(place, near, far, stage, (QKV_PACK, MERGE_PACK), along)
        for side, ref in ((place[1], near), (1 - place[1], far)):
            all_s[pl.ds(pl.multiple_of(SUMS * target + 8 * side, 8), 8), :] = joined(ref[rows:, :])
        begin = pl.multiple_of(256 * target, 256)
        for part in range(2):
            qkv_ref[part, pl.ds(begin, 256), :] = stage[0:256, 256 * part : 256 * part + 256].astype(f32)
        qkv_ref[2, pl.ds(begin, 128), :] = stage[256:384, 0:256].astype(f32)
        qkv_ref[2, pl.ds(begin + 128, 128), :] = stage[256:384, 256:512].astype(f32)
        merge_ref[pl.ds(begin, 256), :] = stage[384:640, :].astype(f32)
    write_vectors(place[3], all_s, vectors)


VECTORS = [(1, D)] * 6 + [(2, D // 2), (1, FFN // 2), (1, MERGE_IN // 2), (1, MERGE_IN // 2), (HEADS // 2, SIDE * SIDE)]


def write_vectors(tp, sums, refs):
    for row in range(6):
        refs[row][...] = sums[row : row + 1, :]
    columns = pl.ds(pl.multiple_of(256 * tp, 256), 256)
    refs[6][...] = sums[6:8, columns]
    refs[7][:, 0:512] = sums[pl.ds(8 + 2 * tp, 1), :]
    refs[7][:, 512:1024] = sums[pl.ds(9 + 2 * tp, 1), :]
    refs[8][...] = sums[pl.ds(12 + tp, 1), :]
    refs[9][...] = sums[pl.ds(14 + tp, 1), :]
    refs[10][...] = sums[pl.ds(pl.multiple_of(16 + 8 * tp, 8), 8), 0 : SIDE * SIDE]


def last_unpack(along, place, mine, other):
    outs = plain_call(
        partial(last_unpack_body, along),
        [pltpu.HBM(shape, f32) if shape[-2] >= 128 else shape_of(shape, f32) for shape in [(3, D, D // 2), (MERGE_IN // 2, D)] + VECTORS],
        (place, mine, other),
        scratch=[pltpu.VMEM((QKV_PACK + MERGE_PACK, D), bf16), pltpu.VMEM((2 * SUMS, D), f32)],
    )
    return outs[0], outs[1], outs[2:]


def fetch_by_tp(ring, piece_of):
    near = ring.y(piece_of)
    return near, ring.core(near)


def plain_pieces(tp_size, weights, params):
    merge, qkv, proj, up, down = [
        lax.all_gather(array, "tp", axis=axis, tiled=True) for array, axis in zip(weights, (0, 2, 0, 1, 0))
    ]
    gain, bias, qv, up_bias, table = [
        lax.all_gather(array, "tp", axis=axis, tiled=True) for array, axis in zip(params, (0, 0, 1, 0, 1))
    ]

    def shard(array, axis, which):
        size = array.shape[axis] // 2
        return lax.slice_in_dim(array, which * size, (which + 1) * size, axis=axis)

    def rows_of(which):
        rows = jnp.zeros((PARAMS, D), f32)
        rows = rows.at[0].set(shard(gain.astype(f32), 0, which)).at[1].set(shard(bias.astype(f32), 0, which))
        rows = rows.at[2].set(shard(qv, 1, which).reshape(-1)).at[3:5].set(shard(up_bias, 0, which).reshape(2, D))
        return rows.at[8:16, : SIDE * SIDE].set(shard(table, 1, which).T)

    merge_other = shard(merge, 0, 1)
    qkv_other = shard(qkv, 2, 1).reshape(3 * D, 256)
    proj_other, up_other, down_other = shard(proj, 0, 1), shard(up, 1, 1), shard(down, 0, 1)

    def qkv_piece(half):
        rows = qkv_other[768 * half : 768 * half + 768]
        return jnp.concatenate(
            [jnp.concatenate([rows[:384], rows[384:]], axis=1), proj_other[128 * half : 128 * half + 128]], axis=0
        )

    def feed_piece(half):
        tile = slice(512 * half, 512 * half + 512)
        return jnp.concatenate([down_other[tile], up_other[:, tile]], axis=0)

    own = (
        shard(merge, 0, 0), shard(qkv, 2, 0).reshape(3 * D, 256), shard(proj, 0, 0), shard(up, 1, 0), shard(down, 0, 0)
    )
    return own, (rows_of(0), split(rows_of(1))), (merge_other[:256], merge_other[256:]), (qkv_piece(0), qkv_piece(1)), (feed_piece(0), feed_piece(1))


def sum_plainly(tp_size, feed_packs, proj_packs, qkv_packs, merge_packs):
    feed_packs, proj_packs, qkv_packs, merge_packs = lax.psum(
        (feed_packs, proj_packs, qkv_packs, merge_packs), ("rows", "tp")
    )
    own_send, own_keep, other_send, other_keep = feed_packs
    order = [own_keep, own_send, other_keep, other_send]
    down = jnp.concatenate([block[0:512] for block in order], axis=0)
    up = jnp.concatenate([block[512:1024] for block in order], axis=1)

    def blocks(packs, size):
        send, keep = packs
        return [keep[:size], send[:size], keep[size : 2 * size], send[size : 2 * size]]

    def qkv_rows(block):
        return jnp.stack(
            [block[0:256, 0:256], block[0:256, 256:512], jnp.concatenate([block[256:384, 0:256], block[256:384, 256:512]])]
        )

    order = blocks(qkv_packs, QKV_PACK)
    qkv = jnp.concatenate(
        [jnp.concatenate([qkv_rows(order[2 * shard + half]) for half in range(2)], axis=1) for shard in range(2)], axis=2
    )
    proj = jnp.concatenate(blocks(proj_packs, PROJ_PACK), axis=0)
    merge = jnp.concatenate(blocks(merge_packs, MERGE_PACK), axis=0)
    sums = jnp.concatenate([joined(merge_packs[1][2 * MERGE_PACK :]), joined(merge_packs[0][2 * MERGE_PACK :])], axis=0)
    index = lax.axis_index("tp")

    def own(array, axis):
        size = array.shape[axis] // tp_size
        return lax.dynamic_slice_in_dim(array, index * size, size, axis).astype(f32)

    vectors = [sums[row] for row in range(6)] + [
        own(sums[6:8], 1), own(sums[8:12].reshape(-1), 0), own(sums[12:14].reshape(-1), 0),
        own(sums[14:16].reshape(-1), 0), own(sums[16:32, : SIDE * SIDE], 0),
    ]
    return own(down, 0), own(up, 1), own(qkv, 2), own(proj, 0), own(merge, 0), vectors


def per_device(
    rows_size, tp_size,
    section_rows, window_mask, cotangent, merge_weight, merge_gain, merge_bias, norm1_gain, norm1_bias,
    qkv_weight, qv_bias, bias_table, proj_weight, proj_bias, norm2_gain, norm2_bias,
    up_weight, up_bias, down_weight, down_bias,
):
    fast = tp_size == 2 and rows_size in (8, 16)
    count = cotangent.shape[0]
    index, tp = lax.axis_index("rows"), lax.axis_index("tp")
    place = jnp.stack([index & 1, (index >> 1) & 1, index >> 2, tp]).astype(jnp.int32)
    ring = Ring(place, rows_size)
    if fast:
        flat_qkv = qkv_weight.reshape(3 * D, D // 2)
        (merge_piece,) = plain_call(pack_merge_body, [shape_of((256, D), bf16)], (place, merge_weight))
        merge_near = ring.y(merge_piece)
        params, piece = pack_params(
            place, merge_piece, jnp.concatenate([merge_gain, merge_bias]).astype(f32)[None], qv_bias, up_bias[None], bias_table.T
        )
        others = ring.y(piece)
        mask, live = masks_of(place, piece, window_mask, count)
        hat, inverse = section_norm(mask, section_rows)
        (qkv_piece,) = plain_call_after(
            pack_qkv_body, [shape_of((QKV_PACK + PROJ_PACK, D), bf16)], place, (others, merge_near, hat), (flat_qkv, proj_weight)
        )
        qkv_near = ring.y(qkv_piece)
        merge_far = ring.core(merge_near)
        kernel_place = place
    else:
        (merge_weight, flat_qkv, proj_weight, up_weight, down_weight), (params, others), merge_pair, qkv_pair, feed_pair = plain_pieces(
            tp_size,
            (merge_weight, qkv_weight, proj_weight, up_weight, down_weight),
            (merge_gain, merge_bias, qv_bias, up_bias, bias_table),
        )
        (merge_near, merge_far), (qkv_near, qkv_far), (feed_near_piece, feed_far_piece) = merge_pair, qkv_pair, feed_pair
        kernel_place = jnp.zeros_like(place)
        hat, inverse = section_norm(params, section_rows)
        own_mask = lax.dynamic_slice_in_dim(window_mask, tp * count, count, 0)
        mask, live = masks_of(kernel_place, params, own_mask, count)

    merged, first, merge_full, params, column = merge_rows(
        kernel_place, hat, merge_weight, merge_near, merge_far, params, others, jnp.stack([norm1_gain, norm1_bias])
    )
    position = expand(params)
    turned_first, turned_hat, hat = turn(position, first, hat)
    if fast:
        (feed_piece,) = plain_call_after(
            pack_feed_body, [shape_of((FEED_PACK, D), bf16)], place, (position, qkv_near), (up_weight, down_weight)
        )
        qkv_far = ring.core(qkv_near)
        feed_near_piece = ring.y(feed_piece)
        feed_far_piece = ring.core(feed_near_piece)
    qkv_rows, weights, attended, padded, inverse_sums, qkv_full = attend(
        kernel_place, first, flat_qkv, qkv_near, qkv_far, params, position, mask
    )
    rows = [row[None] for row in (proj_bias, norm2_gain, norm2_bias, down_bias)]
    residual, total, back, second, turned, branch, own_send, feed_sums, proj_full = feed_own(
        kernel_place, attended, merged, cotangent, live, *rows, params, proj_weight, qkv_near, qkv_far,
        up_weight, down_weight,
    )
    total, back, own_keep, feed_sums = feed_middle(
        True, kernel_place, second, turned, branch, total, back, params, feed_sums, (up_weight, down_weight), LONG
    )
    total, back, other_send, feed_sums = feed_middle(
        False, kernel_place, second, turned, branch, total, back, params, feed_sums, (feed_far_piece,)
    )
    block_out, grad_residual, attn, other_keep, proj_send, proj_keep, feed_sums = feed_near(
        kernel_place, residual, second, turned, branch, total, back, rows[3], rows[1], params, feed_sums, feed_near_piece,
        attended,
    )
    after = feed_sums
    if fast:
        own_got, other_got, proj_got = ring.core(own_send), ring.core(other_send), ring.core(proj_send)
        feed_keeps = (own_keep, own_got, other_keep, other_got, proj_keep, proj_got)
        down_y, up_x = stage(feed_first_body, place, feed_sums, (640, 512), *feed_keeps)
        down_shard, up_got = ring.y(down_y), ring.x(up_x)
        after = up_x
    stack, low, sums, vectors, position_grad = attend_back(
        after, attn, qkv_rows, weights, padded, inverse_sums, proj_full, merged, grad_residual, qkv_full,
        norm1_gain[None],
    )
    after = sums
    if fast:
        down_x, up_y, feed_kept = stage(
            feed_second_body, place, sums, (320, 256, 576), *feed_keeps, down_shard, up_got
        )
        down_got, up_shard = ring.x(down_x), ring.y(up_y)
        after = up_y
    qkv_send, qkv_keep = qkv_back(kernel_place, after, turned_first, stack)
    after = sums
    if fast:
        along = ring.along
        qkv_got = ring.core(qkv_send)
        span = 576 // along
        feed_parts = stage(
            feed_third_body, place, qkv_send, (span,) * along, feed_kept, down_got, up_shard, cost=LONG
        )
        feed_got = [ring.z(feed_parts[step], step) for step in range(1, along)]
        after = feed_parts[0]
    merge_send, merge_keep = merge_back(
        kernel_place, after, low, turned_hat, merge_full, params, column, feed_sums, sums, vectors, position_grad
    )
    if fast:
        merge_got = ring.core(merge_send)
        (feed_total,) = stage(total_body, place, merge_send, (span,), feed_parts[0], *feed_got, cost=LONG)
        feed_all = [feed_total] + [ring.z(feed_total, step) for step in range(1, along)]
        to_y, to_x, to_both, last_kept = stage(
            last_first_body, place, feed_total, (336,) * 4, merge_keep, merge_got, qkv_keep, qkv_got,
            scratch=[pltpu.VMEM((SUMS, D), f32)],
        )
        last_span = 320 // along
        last_parts = stage(
            last_second_body, place, to_y, (last_span + 16,) * along,
            last_kept, ring.y(to_y), ring.x(to_x), ring.xy(to_both),
        )
        last_got = [ring.z(last_parts[step], step) for step in range(1, along)]
        (feed_mine,) = stage(beside_body, place, last_parts[0], (span * along,), *feed_all)
        feed_beside = ring.x(feed_mine)
        last_total, vectors = stage(
            merge_total_body, place, feed_mine, (last_span, 16), *([last_parts[0]] + last_got), cost=LONG
        )
        last_all = [last_total] + [ring.z(last_total, step) for step in range(1, along)]
        section_grad, token = section_back(last_total, low, hat, inverse, merge_full, params)
        (last_near,) = stage(
            last_beside_body, place, (token, feed_beside), (336,), vectors, *last_all, cost=LONG
        )
        last_far = ring.x(last_near)
        feed_cores = ring.core(feed_mine), ring.core(feed_beside)
        down_grad, up_grad, proj_grad, token = feed_unpack(
            along, place, last_near, (feed_mine, feed_beside, *feed_cores)
        )
        (last_half,) = stage(beside_body, place, token, (672,), last_near, last_far)
        qkv_grad, merge_grad, vectors = last_unpack(along, place, last_half, ring.core(last_half))
    else:
        section_grad, _ = section_back(low, low, hat, inverse, merge_full, params)
        down_grad, up_grad, qkv_grad, proj_grad, merge_grad, vectors = sum_plainly(
            tp_size, (own_send, own_keep, other_send, other_keep), (proj_send, proj_keep), (qkv_send, qkv_keep),
            (merge_send, merge_keep),
        )
    norm1_gain_grad, norm1_bias_grad, proj_bias_grad, norm2_gain_grad, norm2_bias_grad, down_bias_grad = [
        row.reshape(D) for row in vectors[0:6]
    ]
    qv_grad, up_bias_grad, gain_grad, bias_grad, table_grad = vectors[6:]
    return (
        block_out, section_grad, merge_grad, gain_grad.reshape(-1), bias_grad.reshape(-1),
        norm1_gain_grad, norm1_bias_grad, qkv_grad, qv_grad, table_grad.T, proj_grad, proj_bias_grad,
        norm2_gain_grad, norm2_bias_grad, up_grad, up_bias_grad.reshape(-1), down_grad, down_bias_grad,
    )


def solution(mesh):
    rows_size, tp_size = mesh.shape["rows"], mesh.shape["tp"]
    both = ("rows", "tp")
    return jax.shard_map(
        partial(per_device, rows_size, tp_size),
        mesh=mesh,
        in_specs=(
            P(both, None), P("rows"), P(both, None), P("tp", None), P("tp"), P("tp"), P(), P(),
            P(None, None, "tp"), P(None, "tp"), P(None, "tp"), P("tp", None), P(), P(), P(),
            P(None, "tp"), P("tp"), P("tp", None), P(),
        ),
        out_specs=(
            P(both, None), P(both, None), P("tp", None), P("tp"), P("tp"), P(), P(),
            P(None, None, "tp"), P(None, "tp"), P(None, "tp"), P("tp", None), P(), P(), P(),
            P(None, "tp"), P("tp"), P("tp", None), P(),
        ),
        check_vma=False,
    )
```

```python
from functools import partial
import math

import jax
import jax.numpy as jnp
from jax import lax
from jax.experimental import pallas as pl
from jax.experimental.pallas import tpu as pltpu
from jax.sharding import PartitionSpec as P

MERGE_IN = 1024
D = 512
HEADS = 16
HEAD_DIM = 32
FFN = 2048
WINDOW = 10
AREA = WINDOW * WINDOW
SIDE = 2 * WINDOW - 1
EPSILON = 1e-05
MASKED_SCORE = -1e30
EXACT = lax.Precision.HIGHEST
SCALING = 1.0 / math.sqrt(HEAD_DIM)
GROUP = 4
ROWS = GROUP * AREA
KEYS = 112
QUERIES = 128
QUADS = 4
QUAD = 4 * HEAD_DIM
LANES = 4 * QUERIES

bf16 = jnp.bfloat16
f32 = jnp.float32


def mm(a, b):
    return jnp.dot(a, b, preferred_element_type=f32)


def mm_t(a, b):
    return lax.dot_general(a, b, (((1,), (1,)), ((), ())), preferred_element_type=f32)


def t_mm(a, b):
    return lax.dot_general(a, b, (((0,), (0,)), ((), ())), preferred_element_type=f32)


def normalize(values):
    center = jnp.mean(values, axis=-1, keepdims=True)
    spread = jnp.mean(values * values, axis=-1, keepdims=True) - center * center
    inverse = lax.rsqrt(spread + EPSILON)
    return (values - center) * inverse, inverse


def norm_back(grad_hat, normed, inverse):
    first_mean = jnp.mean(grad_hat, axis=-1, keepdims=True)
    second_mean = jnp.mean(grad_hat * normed, axis=-1, keepdims=True)
    return inverse * (grad_hat - first_mean - normed * second_mean)


def column_sum(values):
    return jnp.sum(values, axis=0, keepdims=True)


def head_masks():
    lane = lax.broadcasted_iota(jnp.int32, (1, QUAD), 1) // HEAD_DIM
    return [(lane == head).astype(f32).astype(bf16) for head in range(4)]


def spread_heads(rows, masks):
    return jnp.concatenate([rows * mask for mask in masks], axis=0)


def kernel_call(body, grid, in_specs, out_specs, out_shape, scratch=(), flops=0, moved=0, room=32, cost=None):
    return pl.pallas_call(
        body,
        grid=grid,
        in_specs=in_specs,
        out_specs=out_specs,
        out_shape=out_shape,
        scratch_shapes=list(scratch),
        compiler_params=pltpu.CompilerParams(
            dimension_semantics=("arbitrary",) * len(grid), vmem_limit_bytes=room * 1024 * 1024
        ),
        cost_estimate=cost or COST,
    )


def whole(shape):
    return pl.BlockSpec(shape, lambda *_: (0,) * len(shape), pipeline_mode=pl.Buffered(1))


def by_rows(rows, columns):
    return pl.BlockSpec((rows, columns), lambda i: (i, 0))


def by_windows(shape):
    return pl.BlockSpec((GROUP,) + shape, lambda i: (i,) + (0,) * len(shape))


SCALARS = pl.BlockSpec(memory_space=pltpu.SMEM)
RESIDENT = pl.BlockSpec(memory_space=pltpu.VMEM)
ANYWHERE = pl.BlockSpec(memory_space=pl.ANY)


def in_hbm(array):
    return pltpu.with_memory_space_constraint(array, pltpu.HBM)


FEED_PACK = 1024
QKV_PACK = 384
PROJ_PACK = 128
MERGE_PACK = 256
STAGE_ROOM = 16
COST = pl.CostEstimate(flops=1, bytes_accessed=1, transcendentals=0)
LONG = pl.CostEstimate(flops=10**12, bytes_accessed=1, transcendentals=0)
SUMS = 16
PARAMS = 16


def shape_of(shape, dtype):
    return jax.ShapeDtypeStruct(shape, dtype)


def split(rows):
    high = rows.astype(bf16).astype(f32)
    return jnp.concatenate([high, rows - high], axis=0).astype(bf16)


def joined(pair):
    half = pair.shape[0] // 2
    return pair[:half].astype(f32) + pair[half:].astype(f32)


def both_shards(tp, mine, other, axis):
    return jnp.where(
        tp == 0, jnp.concatenate([mine, other], axis=axis), jnp.concatenate([other, mine], axis=axis)
    )


def pack_merge_body(place, merge_ref, out_ref, sem):
    half = pl.ds(pl.multiple_of(256 * place[0], 256), 256)
    copy = pltpu.make_async_copy(merge_ref.at[half, :], out_ref, sem)
    copy.start()
    copy.wait()


def pack_merge(place, merge):
    return pl.pallas_call(
        pack_merge_body,
        in_specs=[SCALARS, ANYWHERE],
        out_specs=RESIDENT,
        out_shape=pltpu.VMEM((256, D), bf16),
        scratch_shapes=[pltpu.SemaphoreType.DMA],
        cost_estimate=COST,
    )(place, in_hbm(merge))


def pack_params_body(
    place, after, gain_ref, bias_ref, qv_ref, up_bias_ref, table_ref,
    params_ref, out_ref, gain_s, bias_s, qv_s, up_bias_s, table_s, sems,
):
    pairs = (
        (gain_ref, gain_s), (bias_ref, bias_s), (qv_ref, qv_s), (up_bias_ref, up_bias_s), (table_ref, table_s)
    )
    copies = [pltpu.make_async_copy(source, target, sems.at[index]) for index, (source, target) in enumerate(pairs)]
    for copy in copies:
        copy.start()
    params_ref[...] = jnp.zeros_like(params_ref)
    for copy in copies:
        copy.wait()
    params_ref[0:1, :] = gain_s[...].astype(f32).reshape(1, D)
    params_ref[1:2, :] = bias_s[...].astype(f32).reshape(1, D)
    params_ref[2:3, 0:256] = qv_s[0:1, :]
    params_ref[2:3, 256:512] = qv_s[1:2, :]
    params_ref[3:4, :] = up_bias_s[:, 0:512]
    params_ref[4:5, :] = up_bias_s[:, 512:1024]
    params_ref[8:16, 0 : SIDE * SIDE] = table_s[...]
    out_ref[...] = split(params_ref[...])


def pack_params(place, after, *operands):
    operands = [in_hbm(array) for array in operands]
    return pl.pallas_call(
        pack_params_body,
        in_specs=[SCALARS] + [ANYWHERE] * 6,
        out_specs=[RESIDENT] * 2,
        out_shape=[pltpu.VMEM((PARAMS, D), f32), pltpu.VMEM((2 * PARAMS, D), bf16)],
        scratch_shapes=[pltpu.VMEM(array.shape, array.dtype) for array in operands] + [pltpu.SemaphoreType.DMA((5,))],
        cost_estimate=COST,
    )(place, after, *operands)


def plain_call(body, outs, operands, room=16, scratch=(), flops=0):
    return pl.pallas_call(
        body,
        in_specs=[SCALARS] + [pl.BlockSpec(memory_space=pltpu.VMEM)] * (len(operands) - 1),
        out_specs=[pl.BlockSpec(memory_space=pltpu.VMEM)] * len(outs),
        out_shape=outs,
        scratch_shapes=list(scratch),
        compiler_params=pltpu.CompilerParams(vmem_limit_bytes=room * 1024 * 1024),
        cost_estimate=COST,
    )(*operands)


def pack_qkv_body(place, qkv_ref, proj_ref, *refs):
    out, qkv_s, proj_s, sems = refs[-4:]
    core = place[0]
    copies = [
        pltpu.make_async_copy(qkv_ref.at[pl.ds(pl.multiple_of(768 * core, 256), 768), :], qkv_s, sems.at[0]),
        pltpu.make_async_copy(proj_ref.at[pl.ds(pl.multiple_of(128 * core, 128), 128), :], proj_s, sems.at[1]),
    ]
    for copy in copies:
        copy.start()
    for copy in copies:
        copy.wait()
    for side in range(2):
        out[0:384, 256 * side : 256 * side + 256] = qkv_s[384 * side : 384 * side + 384, :]
    out[384:512, :] = proj_s[...]


def pack_qkv(place, after, qkv, proj):
    return pl.pallas_call(
        pack_qkv_body,
        in_specs=[SCALARS] + [ANYWHERE] * (2 + len(after)),
        out_specs=RESIDENT,
        out_shape=pltpu.VMEM((QKV_PACK + PROJ_PACK, D), bf16),
        scratch_shapes=[
            pltpu.VMEM((768, 256), bf16), pltpu.VMEM((128, D), bf16), pltpu.SemaphoreType.DMA((2,)),
        ],
        cost_estimate=COST,
    )(place, in_hbm(qkv), in_hbm(proj), *after)


def pack_feed_body(place, up_ref, down_ref, out):
    half = pl.ds(pl.multiple_of(512 * place[0], 512), 512)
    out[0:512, :] = down_ref[half, :]
    out[512:1024, :] = up_ref[:, half]


def plain_call_after(body, outs, place, after, operands, room=16, scratch=(), flops=0, cost=COST):
    after = after if isinstance(after, tuple) else (after,)

    def without_after(place, *refs):
        return body(place, *refs[len(after) :])

    return pl.pallas_call(
        without_after,
        in_specs=[SCALARS] + [pl.BlockSpec(memory_space=pl.ANY)] * len(after) + [pl.BlockSpec(memory_space=pltpu.VMEM)] * len(operands),
        out_specs=[pl.BlockSpec(memory_space=pltpu.VMEM)] * len(outs),
        out_shape=outs,
        scratch_shapes=list(scratch),
        compiler_params=pltpu.CompilerParams(vmem_limit_bytes=room * 1024 * 1024),
        cost_estimate=cost,
    )(place, *after, *operands)


def nothing(array_ref, *refs):
    pass


def gate(array, *after):
    return pl.pallas_call(
        nothing,
        in_specs=[RESIDENT] + [ANYWHERE] * len(after),
        out_specs=RESIDENT,
        out_shape=pltpu.VMEM(array.shape, array.dtype),
        input_output_aliases={0: 0},
        cost_estimate=COST,
    )(array, *after)


def masks_body(place, window_in, mask_ref, live_ref, stage, window_s, sem):
    copy = pltpu.make_async_copy(window_in, window_s, sem)
    copy.start()
    copy.wait()
    window_ref = window_s[...].reshape(1, window_s.shape[0])
    windows = mask_ref.shape[0]
    shards = window_ref.shape[1] // (windows * AREA)
    stage[...] = jnp.zeros_like(stage)
    for window in range(windows):
        patch = window_ref[:, AREA * window : AREA * (window + 1)]
        for shard in range(1, shards):
            begin = AREA * (windows * shard + window)
            patch = jnp.where(place[3] == shard, window_ref[:, begin : begin + AREA], patch)
        stage[window : window + 1, 0:AREA] = patch
    patches = jnp.minimum(stage[...], 1).astype(f32)
    live = jnp.max(patches, axis=1, keepdims=True)
    inside = lax.broadcasted_iota(jnp.int32, (windows, QUERIES), 1) < AREA
    keep = jnp.logical_and(jnp.maximum(patches, 1.0 - live) > 0.5, inside)
    added = jnp.where(keep, 0.0, MASKED_SCORE)
    for window in range(windows):
        mask_ref[window] = added[window : window + 1, :]
        live_ref[window] = jnp.broadcast_to(live[window : window + 1, :], (1, QUERIES))


def masks_of(place, after, window_mask, count):
    windows = count // AREA
    return pl.pallas_call(
        lambda place, after, *refs: masks_body(place, *refs),
        in_specs=[SCALARS, ANYWHERE, ANYWHERE],
        out_specs=[RESIDENT] * 2,
        out_shape=[pltpu.VMEM((windows, 1, QUERIES), f32)] * 2,
        scratch_shapes=[
            pltpu.VMEM((windows, QUERIES), jnp.int32), pltpu.VMEM(window_mask.shape, jnp.int32), pltpu.SemaphoreType.DMA,
        ],
        cost_estimate=COST,
    )(place, after, in_hbm(window_mask))


def section_norm_body(after, rows_ref, hat_ref, inverse_ref, rows_s, sems):
    steps = rows_s.shape[0] // ROWS
    copies = []
    for step in range(steps):
        here = slice(ROWS * step, ROWS * (step + 1))
        copies.append(pltpu.make_async_copy(rows_ref.at[here, :], rows_s.at[here, :], sems.at[step]))
        copies[step].start()
    for step in range(steps):
        here = slice(ROWS * step, ROWS * (step + 1))
        copies[step].wait()
        hat, inverse = normalize(rows_s[here, :].astype(f32))
        hat_ref[here, :] = hat.astype(bf16)
        inverse_ref[here, :] = inverse


def section_norm(after, rows):
    count = rows.shape[0]
    return kernel_call(
        section_norm_body,
        (1,),
        [ANYWHERE, ANYWHERE],
        [RESIDENT, RESIDENT],
        [pltpu.VMEM((count, MERGE_IN), bf16), shape_of((count, 1), f32)],
        [pltpu.VMEM((count, MERGE_IN), bf16), pltpu.SemaphoreType.DMA((count // ROWS,))],
        room=16,
    )(after, in_hbm(rows))


def gain_rows(tp, params, others):
    return both_shards(tp, params[0:1], others[0:1], 1), both_shards(tp, params[1:2], others[1:2], 1)


def merge_body(
    place, hat_ref, own_ref, near_ref, far_ref, params_ref, others_ref, norm_gain, norm_bias,
    merged_ref, first_ref, first_copy, merge_ref, params_out_ref, column_ref,
    merge_s, shift_s, gain_s,
):

    @pl.when(pl.program_id(0) == 0)
    def _():
        core, tp = place[0], place[3]
        merge_s[pl.ds(pl.multiple_of(512 * tp, 512), 512), :] = own_ref[...]
        other = 512 * (1 - tp)
        merge_s[pl.ds(pl.multiple_of(other + 256 * core, 256), 256), :] = near_ref[...]
        merge_s[pl.ds(pl.multiple_of(other + 256 * (1 - core), 256), 256), :] = far_ref[...]
        merge_ref[...] = merge_s[...]
        params = params_ref[...]
        others = joined(others_ref[...])
        gain, bias = gain_rows(tp, params, others)
        gain_s[...] = gain.astype(bf16)
        shift_s[...] = mm(jnp.broadcast_to(bias, (16, MERGE_IN)).astype(bf16), merge_s[...])[0:1]
        params_out_ref[0:1, 0:1024] = gain
        params_out_ref[0:1, 1024:2048] = bias
        params_out_ref[1:2, 0:512] = both_shards(tp, params[2:3, 0:256], others[2:3, 0:256], 1)
        params_out_ref[1:2, 512:1024] = both_shards(tp, params[2:3, 256:512], others[2:3, 256:512], 1)
        params_out_ref[1:2, 1024:2048] = jnp.zeros((1, 1024), f32)
        params_out_ref[2:3, :] = both_shards(
            tp,
            jnp.concatenate([params[3:4], params[4:5]], axis=1),
            jnp.concatenate([others[3:4], others[4:5]], axis=1),
            1,
        )
        params_out_ref[3:8, :] = jnp.zeros((5, 2048), f32)
        params_out_ref[8:24, 0:512] = both_shards(tp, params[8:16], others[8:16], 0)
        params_out_ref[8:24, 512:2048] = jnp.zeros((16, 1536), f32)
        column_ref[...] = jnp.broadcast_to(gain, (128, MERGE_IN)).T

    here = pl.ds(pl.multiple_of(pl.program_id(0) * ROWS, 16), ROWS)
    merged = mm(hat_ref[here, :] * gain_s[...], merge_s[...]) + shift_s[...]
    merged_ref[...] = merged
    hat, _ = normalize(merged)
    first = (hat * norm_gain[...] + norm_bias[...]).astype(bf16)
    first_ref[here, :] = first
    first_copy[...] = first


def merge_rows(place, hat, own, near, far, params, others, gain, bias):
    count = hat.shape[0]
    return kernel_call(
        merge_body,
        (count // ROWS,),
        [
            SCALARS, RESIDENT, RESIDENT, RESIDENT, RESIDENT, RESIDENT, RESIDENT, RESIDENT, RESIDENT,
        ],
        [
            by_rows(ROWS, D), RESIDENT, by_rows(ROWS, D), whole((MERGE_IN, D)), RESIDENT,
            whole((MERGE_IN, 128)),
        ],
        [
            pltpu.HBM((count, D), f32), pltpu.VMEM((count, D), bf16), pltpu.HBM((count, D), bf16),
            pltpu.HBM((MERGE_IN, D), bf16),
            shape_of((24, 2048), f32), pltpu.HBM((MERGE_IN, 128), f32),
        ],
        [
            pltpu.VMEM((MERGE_IN, D), bf16), pltpu.VMEM((1, D), f32), pltpu.VMEM((1, MERGE_IN), bf16),
        ],
        flops=2 * count * D * MERGE_IN,
        moved=count * 10 * D + 4 * D * MERGE_IN,
        room=24,
    )(place, hat, own, near, far, params, others, gain, bias)


def value_blocks(values, masks):
    return [jnp.concatenate([values * mask, jnp.broadcast_to(mask, (QUERIES, QUAD))], axis=1) for mask in masks]


def turned_products(turned, scores):
    parts = []
    for pair in range(2):
        both = mm(turned[64 * pair : 64 * pair + 64], scores[:, 256 * pair : 256 * pair + 256])
        parts += [both[0:32, 0:128], both[32:64, 128:256]]
    return jnp.concatenate(parts, axis=0).T


def attend_body(
    place, first_ref, own_ref, near_ref, far_ref, params_ref, position_ref, mask_ref,
    qkv_out_ref, weights_ref, attended_ref, padded_ref, inverse_ref, qkv_ref,
    stage, mixed,
):
    @pl.when(pl.program_id(0) == 0)
    def _():
        core, tp = place[0], place[3]
        other = pl.ds(pl.multiple_of(256 * (1 - tp), 256), 256)
        qkv_ref[:, pl.ds(pl.multiple_of(256 * tp, 256), 256)] = own_ref[...]
        for ref, half in ((near_ref, core), (far_ref, 1 - core)):
            for side in range(2):
                rows = pl.ds(pl.multiple_of(768 * half + 384 * side, 128), 384)
                qkv_ref[rows, other] = ref[0:384, 256 * side : 256 * side + 256]

    here = pl.ds(pl.multiple_of(pl.program_id(0) * ROWS, 16), ROWS)
    stage[pl.ds(0, ROWS), :] = first_ref[here, :].astype(f32)
    stage[pl.ds(ROWS, 32), :] = jnp.zeros((32, D), f32)
    padded = jnp.concatenate(
        [stage[pl.ds(AREA * w, QUERIES), :].astype(bf16) for w in range(GROUP)], axis=0
    )
    queries = (SCALING * (mm(padded, qkv_ref[0:512, :]) + params_ref[1:2, 0:512])).astype(bf16)
    keys = mm(padded, qkv_ref[512:1024, :]).astype(bf16)
    values = (mm(padded, qkv_ref[1024:1536, :]) + params_ref[1:2, 512:1024]).astype(bf16)
    for w in range(GROUP):
        block = slice(QUERIES * w, QUERIES * (w + 1))
        qkv_out_ref[w, :, 0:D] = queries[block]
        qkv_out_ref[w, :, D : 2 * D] = keys[block]
        qkv_out_ref[w, :, 2 * D :] = values[block]
    masks = head_masks()
    for w in range(GROUP):
        mask = mask_ref[w]
        for quad in range(QUADS):
            columns = slice(QUAD * quad, QUAD * (quad + 1))
            rows = QUERIES * w
            spread = spread_heads(keys[rows : rows + QUERIES, columns], masks)
            scores = mm_t(queries[rows : rows + KEYS, columns], spread)
            raised = []
            for head in range(4):
                lanes = slice(QUERIES * head, QUERIES * (head + 1))
                part = scores[:, lanes] + position_ref[quad, :, lanes] + mask
                raised.append(jnp.exp(part - jnp.max(part, axis=1, keepdims=True)).astype(bf16))
            weights = jnp.concatenate(raised, axis=1)
            weights_ref[w, quad] = weights
            blocks = value_blocks(values[rows : rows + QUERIES, columns], masks)
            out = mm(weights, jnp.concatenate(blocks, axis=0))
            inverse = 1.0 / out[:, QUAD:]
            both = out[:, :QUAD] * inverse
            inverse_ref[w, :, columns] = inverse.astype(bf16)
            padded_ref[w, :, columns] = both.astype(bf16)
            mixed[pl.ds(AREA * w, AREA), columns] = both[0:AREA]
    attended_ref[...] = mixed[...].astype(bf16)


def attend(place, first, own, near, far, params, position, mask):
    count = first.shape[0]
    windows = count // AREA
    return kernel_call(
        attend_body,
        (count // ROWS,),
        [
            SCALARS, RESIDENT, RESIDENT, RESIDENT, RESIDENT, RESIDENT, RESIDENT, by_windows((1, QUERIES)),
        ],
        [
            by_windows((QUERIES, 3 * D)), by_windows((QUADS, KEYS, LANES)), by_rows(ROWS, D),
            by_windows((KEYS, D)), by_windows((KEYS, D)), RESIDENT,
        ],
        [
            pltpu.HBM((windows, QUERIES, 3 * D), bf16), pltpu.HBM((windows, QUADS, KEYS, LANES), bf16),
            pltpu.HBM((count, D), bf16), pltpu.HBM((windows, KEYS, D), bf16), pltpu.HBM((windows, KEYS, D), bf16),
            shape_of((3 * D, D), bf16),
        ],
        [pltpu.VMEM((ROWS + 32, D), f32), pltpu.VMEM((ROWS, D), f32)],
        flops=2 * count * D * (3 * D + 4 * AREA),
        moved=count * 10 * D + windows * QUADS * KEYS * LANES * 2,
        room=20,
    )(place, first, own, near, far, params, position, mask)


def gelu_parts(t):
    chance = 0.5 * lax.erf(t * math.sqrt(0.5)) + 0.5
    density = jnp.exp(t * t * -0.5) * (1.0 / math.sqrt(2.0 * math.pi))
    return t * chance, chance + t * density


TILE = 512
FEED_ROWS = 400
OWN_ROOM = 18
OTHER_ROOM = 12
AB_ROOM = 20
NEAR_ROOM = 20


def feed_tile(up, down, bias, second_ref, turned_ref, branch_ref, total_s, back_s, active_s, raise_s, target, first):
    sums = jnp.zeros((1, TILE), f32)
    for begin in range(0, second_ref.shape[0], FEED_ROWS):
        here = slice(begin, begin + FEED_ROWS)
        value, slope = gelu_parts(mm(second_ref[here, :], up) + bias)
        active = value.astype(bf16)
        grad_raised = (mm_t(branch_ref[here, :], down) * slope).astype(bf16)
        active_s[here, :] = active
        raise_s[here, :] = grad_raised
        sums += column_sum(grad_raised.astype(f32))
        out = mm(active, down)
        back = mm_t(grad_raised, up)
        if first:
            total_s[here, :] = out
            back_s[here, :] = back
        else:
            total_s[here, :] += out
            back_s[here, :] += back
    target[0:512, :] = t_mm(active_s[...], branch_ref[...]).astype(bf16)
    target[512:1024, :] = mm(turned_ref[...], raise_s[...]).astype(bf16)
    return sums


def feed_own_body(
    place, attended_ref, merged_ref, cotangent_ref, live_ref, proj_bias, norm_gain, norm_bias, params_ref,
    proj_own, near_ref, far_ref, up_own, down_own,
    residual_ref, total_ref, back_ref, second_ref, turned_ref, branch_ref, send_ref, sums_ref, proj_ref,
    active_s, raise_s,
):
    step = pl.program_id(0)
    blocks = pl.num_programs(0) - 1
    core, tp = place[0], place[3]

    @pl.when(step == 0)
    def _():
        proj_ref[pl.ds(pl.multiple_of(256 * tp, 256), 256), :] = proj_own[...]
        for ref, which in ((near_ref, core), (far_ref, 1 - core)):
            proj_ref[pl.ds(pl.multiple_of(256 * (1 - tp) + 128 * which, 128), 128), :] = ref[384:512, :]
        sums_ref[...] = jnp.zeros_like(sums_ref)

    @pl.when(step < blocks)
    def _():
        here = pl.ds(pl.multiple_of(step * ROWS, 16), ROWS)
        residual = merged_ref[...] + mm(attended_ref[...], proj_ref[...]) + proj_bias[...]
        residual_ref[here, :] = residual
        hat, _ = normalize(residual)
        second_ref[here, :] = (hat * norm_gain[...] + norm_bias[...]).astype(bf16)
        row = lax.broadcasted_iota(jnp.int32, (ROWS, 1), 0)
        live = live_ref[GROUP - 1, :, 0:1]
        for window in range(GROUP - 2, -1, -1):
            live = jnp.where(row < AREA * (window + 1), live_ref[window, :, 0:1], live)
        branch = cotangent_ref[...].astype(f32) * live
        branch_ref[here, :] = branch.astype(bf16)
        sums_ref[7:8, :] += column_sum(branch)

    @pl.when(step == blocks)
    def _():
        turned_ref[...] = second_ref[...].T
        shard = 2 * tp + 1 - core
        units = pl.ds(pl.multiple_of(TILE * (1 - core), TILE), TILE)
        bias = params_ref[2:3, pl.ds(pl.multiple_of(TILE * shard, TILE), TILE)]
        sums_ref[pl.ds(shard, 1), :] = feed_tile(
            up_own[:, units], down_own[units, :], bias, second_ref, turned_ref, branch_ref, total_ref, back_ref,
            active_s, raise_s, send_ref, True,
        )


def feed_own(
    place, attended, merged, cotangent, live, proj_bias, gain, bias, down_bias, params, proj, near, far, up, down
):
    count = attended.shape[0]
    blocks = count // ROWS

    def taken(columns):
        return pl.BlockSpec((ROWS, columns), lambda i: (jnp.minimum(i, blocks - 1), 0))

    return kernel_call(
        feed_own_body,
        (blocks + 1,),
        [
            SCALARS, taken(D), taken(D), taken(D),
            pl.BlockSpec((GROUP, 1, QUERIES), lambda i: (jnp.minimum(i, blocks - 1), 0, 0)), RESIDENT, RESIDENT, RESIDENT, RESIDENT, RESIDENT, RESIDENT, RESIDENT,
            RESIDENT, RESIDENT,
        ],
        [RESIDENT] * 9,
        [pltpu.VMEM((count, D), f32)] * 3
        + [pltpu.VMEM((count, D), bf16), pltpu.VMEM((D, count), bf16), pltpu.VMEM((count, D), bf16)]
        + [pltpu.VMEM((FEED_PACK, D), bf16), shape_of((8, D), f32), shape_of((D, D), bf16)],
        [pltpu.VMEM((count, TILE), bf16)] * 2,
        room=OWN_ROOM,
    )(
        place, in_hbm(attended), in_hbm(merged), in_hbm(cotangent), live, proj_bias, gain, bias, params, proj,
        near, far, up, down,
    )


def feed_middle_body(
    own, place, second_ref, turned_ref, branch_ref, total_in, back_in, params_ref, sums_in, *refs
):
    weights, (total_ref, back_ref, target_ref, sums_ref, active_s, raise_s) = refs[:-6], refs[-6:]
    core, tp = place[0], place[3]
    sums_ref[...] = sums_in[...]
    if own:
        shard = 2 * tp + core
        units = pl.ds(pl.multiple_of(TILE * core, TILE), TILE)
        up, down = weights[0][:, units], weights[1][units, :]
    else:
        shard = 2 * (1 - tp) + 1 - core
        up, down = weights[0][512:1024, :], weights[0][0:512, :]
    bias = params_ref[2:3, pl.ds(pl.multiple_of(TILE * shard, TILE), TILE)]
    sums_ref[pl.ds(shard, 1), :] = feed_tile(
        up, down, bias, second_ref, turned_ref, branch_ref, total_ref, back_ref, active_s, raise_s, target_ref, False
    )


def feed_middle(own, place, second, turned, branch, total, back, params, sums, weights, cost=COST):
    count = second.shape[0]
    return pl.pallas_call(
        partial(feed_middle_body, own),
        in_specs=[SCALARS] + [RESIDENT] * (7 + len(weights)),
        out_specs=[RESIDENT] * 4,
        out_shape=[pltpu.VMEM((count, D), f32)] * 2 + [pltpu.VMEM((FEED_PACK, D), bf16), shape_of((8, D), f32)],
        scratch_shapes=[pltpu.VMEM((count, TILE), bf16)] * 2,
        input_output_aliases={4: 0, 5: 1},
        compiler_params=pltpu.CompilerParams(vmem_limit_bytes=OTHER_ROOM * 1024 * 1024),
        cost_estimate=cost,
    )(place, second, turned, branch, total, back, params, sums, *weights)


def feed_near_body(
    place, residual_ref, second_ref, turned_ref, branch_ref, total_in, back_in, down_bias, norm_gain, params_ref,
    sums_in, near_ref, attended_ref,
    out_ref, grad_residual_ref, attn_ref, keep_ref, proj_send, proj_keep, sums_ref,
    total_s, back_s, active_s, raise_s, attended_s, proj_s, sem,
):
    step = pl.program_id(0)
    core, tp = place[0], place[3]
    fetch = pltpu.make_async_copy(attended_ref, attended_s, sem)

    @pl.when(step == 0)
    def _():
        fetch.start()
        sums_ref[...] = sums_in[...]
        shard = 2 * (1 - tp) + core
        bias = params_ref[2:3, pl.ds(pl.multiple_of(TILE * shard, TILE), TILE)]
        sums_ref[pl.ds(shard, 1), :] = feed_tile(
            near_ref[512:1024, :], near_ref[0:512, :], bias, second_ref, turned_ref, branch_ref, total_s, back_s,
            active_s, raise_s, keep_ref, True,
        )

    @pl.when(step >= 1)
    def _():
        here = pl.ds(pl.multiple_of((step - 1) * ROWS, 16), ROWS)
        residual = residual_ref[here, :]
        out_ref[...] = (residual + down_bias[...] + total_in[here, :] + total_s[here, :]).astype(bf16)
        hat, inverse = normalize(residual)
        grad_second = back_in[here, :] + back_s[here, :]
        grad_residual = branch_ref[here, :].astype(f32) + norm_back(grad_second * norm_gain[...], hat, inverse)
        grad_residual_ref[here, :] = grad_residual
        attn_ref[here, :] = grad_residual.astype(bf16)
        sums_ref[4:5, :] += column_sum(grad_residual)
        sums_ref[5:6, :] += column_sum(grad_second * hat)
        sums_ref[6:7, :] += column_sum(grad_second)

    @pl.when(step == pl.num_programs(0) - 1)
    def _():
        fetch.wait()
        proj_s[...] = t_mm(attended_s[...], attn_ref[...]).astype(bf16)
        for target, half in ((proj_send, 1 - core), (proj_keep, core)):
            for other in range(2):
                shard = jnp.where(other == 0, tp, 1 - tp)
                rows = pl.ds(pl.multiple_of(256 * shard + 128 * half, 128), 128)
                target[PROJ_PACK * other : PROJ_PACK * (other + 1), :] = proj_s[rows, :]


def feed_near(place, residual, second, turned, branch, total, back, down_bias, gain, params, sums, near, attended):
    count = residual.shape[0]
    blocks = count // ROWS

    def given(columns):
        return pl.BlockSpec((ROWS, columns), lambda i: (jnp.maximum(i - 1, 0), 0))

    return kernel_call(
        feed_near_body,
        (blocks + 1,),
        [SCALARS] + [RESIDENT] * 9 + [whole((8, D)), RESIDENT]
        + [pl.BlockSpec(memory_space=pl.ANY)],
        [given(D)] + [RESIDENT] * 5 + [whole((8, D))],
        [pltpu.HBM((count, D), bf16), pltpu.VMEM((count, D), f32), pltpu.VMEM((count, D), bf16)]
        + [pltpu.VMEM((FEED_PACK, D), bf16)] + [pltpu.VMEM((2 * PROJ_PACK, D), bf16)] * 2
        + [shape_of((8, D), f32)],
        [pltpu.VMEM((count, D), f32)] * 2 + [pltpu.VMEM((count, TILE), bf16)] * 2
        + [pltpu.VMEM((count, D), bf16), pltpu.VMEM((D, D), bf16), pltpu.SemaphoreType.DMA],
        room=NEAR_ROOM,
    )(
        place, residual, second, turned, branch, total, back, down_bias, gain, params, sums, near, in_hbm(attended)
    )


def attend_back_body(
    after, attn_ref, qkv_in_ref, weights_ref, padded_ref, inverse_ref, proj_ref,
    merged_ref, grad_residual_ref, qkv_ref, rows_ref, first_in,
    stack_ref, low_ref, sums_ref, vectors_ref, position_ref, first_ref,
    stage, grads, sem,
):
    fetch = pltpu.make_async_copy(first_in, first_ref, sem)

    @pl.when(pl.program_id(0) == pl.num_programs(0) - 1)
    def _():
        fetch.wait()

    @pl.when(pl.program_id(0) == 0)
    def _():
        fetch.start()
        vectors_ref[...] = jnp.zeros_like(vectors_ref)
        sums_ref[...] = jnp.zeros_like(sums_ref)
        position_ref[...] = jnp.zeros_like(position_ref)

    here = pl.ds(pl.multiple_of(pl.program_id(0) * ROWS, 16), ROWS)
    stage[pl.ds(0, ROWS), :] = attn_ref[here, :].astype(f32)
    stage[pl.ds(ROWS, 32), :] = jnp.zeros((32, D), f32)
    real = lax.broadcasted_iota(jnp.int32, (KEYS, 1), 0) < AREA
    padded = jnp.concatenate(
        [jnp.where(real, stage[pl.ds(AREA * w, KEYS), :], 0.0).astype(bf16) for w in range(GROUP)], axis=0
    )
    grad_attended = mm_t(padded, proj_ref[...])
    masks = head_masks()
    empty = jnp.zeros((QUERIES - KEYS, QUAD), bf16)
    kept = {}
    for w in range(GROUP):
        for quad in range(QUADS):
            columns = slice(QUAD * quad, QUAD * (quad + 1))
            values = qkv_in_ref[w, :, 2 * D + QUAD * quad : 2 * D + QUAD * (quad + 1)]
            grad = grad_attended[KEYS * w : KEYS * (w + 1), columns] * inverse_ref[w, :, columns].astype(f32)
            low = grad.astype(bf16)
            taken = (grad * padded_ref[w, :, columns].astype(f32)).astype(bf16)
            both = jnp.concatenate([low, -taken], axis=1)
            change = jnp.concatenate([mm_t(both, block) for block in value_blocks(values, masks)], axis=1)
            grad_scores = (weights_ref[w, quad].astype(f32) * change).astype(bf16)
            position_ref[quad] += grad_scores.astype(f32)
            kept[w, quad] = (low, grad_scores)
    for w in range(GROUP):
        to = pl.ds(AREA * w, AREA)
        for quad in range(QUADS):
            low, grad_scores = kept[w, quad]
            queries = qkv_in_ref[w, :, QUAD * quad : QUAD * (quad + 1)]
            keys = qkv_in_ref[w, :, D + QUAD * quad : D + QUAD * (quad + 1)]
            grad_queries = mm(grad_scores, spread_heads(keys, masks)) * SCALING
            grad_keys = turned_products(queries.T[:, :KEYS], grad_scores)
            grad_values = turned_products(jnp.concatenate([low, empty], axis=0).T[:, :KEYS], weights_ref[w, quad])
            for part, grad in enumerate((grad_queries, grad_keys, grad_values)):
                grads[to, D * part + QUAD * quad : D * part + QUAD * (quad + 1)] = grad[0:AREA]
    stack = grads[...].astype(bf16)
    stack_ref[here, :] = stack
    sums_ref[...] += column_sum(stack.astype(f32))
    grad_first = (
        mm_t(stack[:, 0:D], qkv_ref[0:D, :])
        + mm_t(stack[:, D : 2 * D], qkv_ref[D : 2 * D, :])
        + mm_t(stack[:, 2 * D :], qkv_ref[2 * D :, :])
    )
    normed, inverse = normalize(merged_ref[...])
    grad_merged = grad_residual_ref[here, :] + norm_back(grad_first * rows_ref[0:1, :], normed, inverse)
    low = grad_merged.astype(bf16)
    low_ref[here, :] = low
    vectors_ref[0:1, :] += column_sum(grad_first * normed)
    vectors_ref[1:2, :] += column_sum(grad_first)
    vectors_ref[2:3, :] += column_sum(low.astype(f32))


def attend_back(after, attn, qkv_in, weights, padded, inverse, proj, merged, grad_residual, qkv, rows, first):
    count = attn.shape[0]
    return kernel_call(
        attend_back_body,
        (count // ROWS,),
        [
            ANYWHERE, RESIDENT, by_windows((QUERIES, 3 * D)), by_windows((QUADS, KEYS, LANES)),
            by_windows((KEYS, D)), by_windows((KEYS, D)), RESIDENT, by_rows(ROWS, D), RESIDENT, RESIDENT, RESIDENT,
            ANYWHERE,
        ],
        [RESIDENT] * 6,
        [
            pltpu.VMEM((count, 3 * D), bf16), pltpu.VMEM((count, D), bf16), shape_of((1, 3 * D), f32),
            shape_of((8, D), f32), shape_of((QUADS, KEYS, LANES), f32), pltpu.VMEM((count, D), bf16),
        ],
        [pltpu.VMEM((ROWS + 32, D), f32), pltpu.VMEM((ROWS, 3 * D), f32), pltpu.SemaphoreType.DMA],
        room=AB_ROOM,
    )(
        after, attn, *[in_hbm(array) for array in (qkv_in, weights, padded, inverse)], proj, in_hbm(merged),
        grad_residual, qkv, rows, in_hbm(first),
    )


def qkv_back_body(place, after, first_ref, stack_ref, hat_in, send_ref, keep_ref, hat_ref, qkv_s, turned_s, sem):
    part = pl.program_id(0)
    fetch = pltpu.make_async_copy(hat_in, hat_ref, sem)

    @pl.when(part == 0)
    def _():
        fetch.start()
        turned_s[...] = first_ref[...].T

    @pl.when(part == pl.num_programs(0) - 1)
    def _():
        fetch.wait()

    core, tp = place[0], place[3]
    qkv_s[...] = mm(turned_s[...], stack_ref[:, pl.ds(pl.multiple_of(D * part, D), D)]).astype(bf16)
    for target, half in ((send_ref, 1 - core), (keep_ref, core)):
        for other in range(2):
            shard = jnp.where(other == 0, tp, 1 - tp)
            base = QKV_PACK * other
            rows = pl.ds(pl.multiple_of(256 * half, 256), 256)
            columns = pl.ds(pl.multiple_of(256 * shard, 256), 256)

            @pl.when(part < 2)
            def _():
                target[base : base + 256, pl.ds(pl.multiple_of(256 * part, 256), 256)] = qkv_s[rows, columns]

            @pl.when(part == 2)
            def _():
                block = qkv_s[rows, columns]
                target[base + 256 : base + 384, 0:256] = block[0:128]
                target[base + 256 : base + 384, 256:512] = block[128:256]


def qkv_back(place, after, first, stack, hat):
    count = stack.shape[0]
    return kernel_call(
        qkv_back_body,
        (3,),
        [SCALARS, ANYWHERE, RESIDENT, RESIDENT, ANYWHERE],
        [RESIDENT] * 3,
        [pltpu.VMEM((2 * QKV_PACK, D), bf16)] * 2 + [pltpu.VMEM((count, MERGE_IN), bf16)],
        [pltpu.VMEM((D, D), bf16), pltpu.VMEM((D, count), bf16), pltpu.SemaphoreType.DMA],
        room=12,
    )(place, after, first, stack, in_hbm(hat))


def merge_back_body(
    place, after, low_ref, hat_ref, merge_ref, params_ref, column_ref, feed_sums_ref, qkv_sums_ref, vectors_ref,
    position_ref,
    send_ref, keep_ref,
    fold_s, all_s, raw_s,
):
    core, tp = place[0], place[3]
    total = vectors_ref[2:3, :]
    pair = jnp.concatenate([split(total), jnp.zeros((14, D), bf16)], axis=0)
    ones = jnp.ones((16, D), bf16)
    raw_s[...] = t_mm(hat_ref[...], low_ref[...])
    all_s[...] = jnp.zeros_like(all_s)
    all_s[0:2, :] = vectors_ref[0:2, :]
    all_s[2:6, :] = feed_sums_ref[4:8, :]
    all_s[6:7, :] = qkv_sums_ref[:, 0:D]
    all_s[7:8, :] = qkv_sums_ref[:, 2 * D :]
    all_s[8:12, :] = feed_sums_ref[0:4, :]
    all_s[16:32, 0:384] = fold_place(position_ref, fold_s)
    for tile in range(2):
        rows = slice(512 * tile, 512 * (tile + 1))
        merge = merge_ref[rows, :]
        scaled = raw_s[rows, :] * merge.astype(f32)
        scaled_high = scaled.astype(bf16)
        scaled_rest = (scaled - scaled_high.astype(f32)).astype(bf16)
        all_s[12 + tile : 13 + tile, :] = (mm_t(ones, scaled_high) + mm_t(ones, scaled_rest))[0:1]
        all_s[14 + tile : 15 + tile, :] = column_sum(mm_t(pair, merge))
    for target, half in ((send_ref, 1 - core), (keep_ref, core)):
        for other in range(2):
            begin = pl.multiple_of(512 * jnp.where(other == 0, tp, 1 - tp) + 256 * half, 256)
            bias = jnp.broadcast_to(params_ref[0:1, pl.ds(1024 + begin, 256)], (16, 256)).astype(bf16)
            gain = column_ref[pl.ds(begin, 256), 0:1]
            block = raw_s[pl.ds(begin, 256), :] * gain + t_mm(bias, pair)
            target[MERGE_PACK * other : MERGE_PACK * (other + 1), :] = block.astype(bf16)
        target[2 * MERGE_PACK :, :] = split(all_s[pl.ds(pl.multiple_of(SUMS * half, SUMS), SUMS), :])


def merge_back(place, after, low, hat, merge, params, column, feed_sums, sums, vectors, position):
    pack = 2 * MERGE_PACK + 2 * SUMS
    return pl.pallas_call(
        merge_back_body,
        in_specs=[SCALARS, ANYWHERE] + [RESIDENT] * 9,
        out_specs=[RESIDENT] * 2,
        out_shape=[pltpu.VMEM((pack, D), bf16), pltpu.VMEM((pack, D), bf16)],
        scratch_shapes=[
            pltpu.VMEM((HEADS, KEYS, 256), f32), pltpu.VMEM((32, D), f32), pltpu.VMEM((MERGE_IN, D), f32),
        ],
        compiler_params=pltpu.CompilerParams(vmem_limit_bytes=20 * 1024 * 1024),
        cost_estimate=COST,
    )(place, after, low, hat, merge, params, column, feed_sums, sums, vectors, position)


def section_back_body(after, low_ref, hat_ref, inverse_ref, merge_ref, params_ref, out_ref, token_ref):
    token_ref[...] = jnp.zeros_like(token_ref)
    scaled = mm_t(low_ref[...], merge_ref[...]) * params_ref[0:1, 0:MERGE_IN]
    out_ref[...] = norm_back(scaled, hat_ref[...].astype(f32), inverse_ref[...]).astype(bf16)


def section_back(after, low, hat, inverse, merge, params):
    count = low.shape[0]
    return kernel_call(
        section_back_body,
        (count // ROWS,),
        [
            pl.BlockSpec(memory_space=pl.ANY), by_rows(ROWS, D), by_rows(ROWS, MERGE_IN), by_rows(ROWS, 1),
            whole((MERGE_IN, D)), whole((24, 2048)),
        ],
        [by_rows(ROWS, MERGE_IN), whole((8, 128))],
        [pltpu.HBM((count, MERGE_IN), bf16), shape_of((8, 128), f32)],
        flops=2 * count * D * MERGE_IN,
        moved=count * 5 * MERGE_IN,
        room=24,
    )(after, in_hbm(low), in_hbm(hat), inverse, merge, params)


def spread_matrix():
    place = lax.broadcasted_iota(jnp.int32, (QUERIES, 256), 0)
    lane = lax.broadcasted_iota(jnp.int32, (QUERIES, 256), 1)
    target = place + (SIDE - WINDOW) * (place // WINDOW)
    return jnp.logical_and(lane == target, place < AREA).astype(f32)


def expand_body(params_ref, hat_ref, place_ref, hat_copy, lines_s, out_s, sem):
    save = pltpu.make_async_copy(hat_ref, hat_copy, sem)
    save.start()
    lane = lax.broadcasted_iota(jnp.int32, (384, QUERIES), 0)
    patch = lax.broadcasted_iota(jnp.int32, (384, QUERIES), 1)
    middle = (WINDOW - 1) * (SIDE + 1)
    picked = jnp.logical_and(lane == middle - patch - (SIDE - WINDOW) * (patch // WINDOW), patch < AREA)
    picked = picked.astype(f32).astype(bf16)
    tables = params_ref[8 : 8 + HEADS, 0:384]
    for place in range(AREA):
        offset = SIDE * (place // WINDOW) + place % WINDOW
        lines_s[HEADS * place : HEADS * (place + 1), :] = pltpu.roll(tables, (384 - offset) % 384, 1)
    for begin in range(0, HEADS * AREA, ROWS):
        here = slice(begin, begin + ROWS)
        rows = lines_s[here, :]
        high = rows.astype(bf16)
        rest = rows - high.astype(f32)
        middle_part = rest.astype(bf16)
        low = (rest - middle_part.astype(f32)).astype(bf16)
        out_s[here, :] = mm(high, picked) + mm(middle_part, picked) + mm(low, picked)
    for head in range(HEADS):
        lanes = slice(QUERIES * (head % 4), QUERIES * (head % 4 + 1))
        place_ref[head // 4, 0:AREA, lanes] = out_s[pl.ds(head, AREA, stride=HEADS), :]
        place_ref[head // 4, AREA:KEYS, lanes] = jnp.zeros((KEYS - AREA, QUERIES), f32)
    save.wait()


def expand(params, hat):
    return kernel_call(
        expand_body,
        (1,),
        [RESIDENT, RESIDENT],
        [RESIDENT, ANYWHERE],
        [shape_of((QUADS, KEYS, LANES), f32), pltpu.HBM(hat.shape, bf16)],
        [pltpu.VMEM((HEADS * AREA, 384), f32), pltpu.VMEM((HEADS * AREA, QUERIES), f32), pltpu.SemaphoreType.DMA],
        room=16,
    )(params, hat)


def fold_place(place_ref, stage_s):
    spread = spread_matrix().astype(bf16)
    lines = []
    for head in range(HEADS):
        stage = stage_s.at[head]
        rows = place_ref[head // 4, :, QUERIES * (head % 4) : QUERIES * (head % 4 + 1)]
        rows = jnp.concatenate([rows, jnp.zeros((QUERIES - KEYS, QUERIES), f32)], axis=0).T[:KEYS]
        high = rows.astype(bf16)
        rest = (rows - high.astype(f32)).astype(bf16)
        stage[...] = mm(high, spread) + mm(rest, spread)
        total = jnp.zeros((WINDOW, 384), f32)
        for y in range(WINDOW):
            part = jnp.concatenate(
                [stage[pl.ds(WINDOW * y, WINDOW), :], jnp.zeros((WINDOW, 128), f32)], axis=1
            )
            total += pltpu.roll(part, SIDE * (WINDOW - 1 - y), 1) if y < WINDOW - 1 else part
        line = total[WINDOW - 1 : WINDOW, :]
        for x in range(WINDOW - 1):
            line += pltpu.roll(total[x : x + 1, :], WINDOW - 1 - x, 1)
        lines.append(line)
    return jnp.concatenate(lines, axis=0)


class Ring:
    def __init__(self, place, rows_size):
        self.place = place
        self.rows_size = rows_size
        self.along = rows_size // 4

    def to(self, array, bits):
        return lax.ppermute(array, "rows", [(i, i ^ bits) for i in range(self.rows_size)])

    def core(self, array):
        return self.to(array, 1)

    def x(self, array):
        return self.to(array, 2)

    def z(self, array, step):
        return self.to(array, 4 * step)

    def y(self, array):
        return lax.ppermute(array, "tp", [(0, 1), (1, 0)])

    def xy(self, array):
        pairs = [(2 * i + t, 2 * (i ^ 2) + 1 - t) for i in range(self.rows_size) for t in range(2)]
        return lax.ppermute(array, ("rows", "tp"), pairs)


def rows_of(array, begin, rows):
    return lax.dynamic_slice_in_dim(array, begin, rows, 0).astype(f32)


def stage(body, place, after, rows, *operands, cost=COST, scratch=()):
    return plain_call_after(
        body, [pltpu.VMEM((count, D), bf16) for count in rows], place, after, operands, room=STAGE_ROOM, cost=cost,
        scratch=scratch,
    )


def added(refs, begin, rows):
    here = pl.ds(pl.multiple_of(begin, 16), rows)
    total = refs[0][here, :].astype(f32)
    for ref in refs[1:]:
        total = total + ref[here, :].astype(f32)
    return total


def part(ref, begin, rows):
    return ref.at[begin : begin + rows, :]


FEED_BLOCKS = ((0, 256), (256, 64), (320, 256))


def feed_first_body(
    place, own_keep, own_got, other_keep, other_got, proj_keep, proj_got, to_y, to_x, to_both, kept
):
    x = place[1]
    own, other = (own_keep, own_got), (other_keep, other_got)
    for target, blocks, shard, side in (
        (to_y, other, 1, x), (to_x, own, 0, 1 - x), (to_both, other, 1, 1 - x), (kept, own, 0, x)
    ):
        target[0:256, :] = added(blocks, 256 * side, 256).astype(bf16)
        target[256:320, :] = added((proj_keep, proj_got), PROJ_PACK * shard + 64 * side, 64).astype(bf16)
        target[320:576, :] = added(blocks, 512 + 256 * side, 256).astype(bf16)


def feed_second_body(place, *refs):
    blocks, outs = refs[:4], refs[4:]
    for step, out in enumerate(outs):
        offset = 0
        for begin, size in FEED_BLOCKS:
            span = size // len(outs)
            to = begin + (place[2] ^ step) * span
            out[offset : offset + span, :] = added(blocks, to, span).astype(bf16)
            offset += span


def total_body(place, *refs):
    refs[-1][...] = added(refs[:-1], 0, refs[-1].shape[0]).astype(bf16)


def beside_body(place, *refs):
    rows = refs[0].shape[0]
    for index, ref in enumerate(refs[:-1]):
        refs[-1][rows * index : rows * (index + 1), :] = ref[...]


def qkv_first_body(place, keep, got, to_y, to_x, to_both, kept):
    x = place[1]
    for target, other, side in ((to_y, 1, x), (to_x, 0, 1 - x), (to_both, 1, 1 - x), (kept, 0, x)):
        target[...] = added((keep, got), QKV_PACK * other + 192 * side, 192).astype(bf16)


def merge_first_body(place, keep, got, to_y, to_x, to_both, kept, sums_s):
    x = place[1]
    sums_s[...] = joined(keep[512:544, :]) + joined(got[512:544, :])
    for target, other, side in ((to_y, 1, x), (to_x, 0, 1 - x), (to_both, 1, 1 - x), (kept, 0, x)):
        target[0:128, :] = added((keep, got), MERGE_PACK * other + 128 * side, 128).astype(bf16)
        target[128:144, :] = split(sums_s[pl.ds(pl.multiple_of(8 * side, 8), 8), :])


def last_second_body(place, qkv_sum, *refs):
    blocks, outs = refs[:4], refs[4:]
    vectors = split(sum(joined(ref[128:144, :]) for ref in blocks))
    wide, narrow = 192 // len(outs), 128 // len(outs)
    for step, out in enumerate(outs):
        to = place[2] ^ step
        out[0:wide, :] = added((qkv_sum,), to * wide, wide).astype(bf16)
        out[wide : wide + narrow, :] = added(blocks, to * narrow, narrow).astype(bf16)
        out[wide + narrow :, :] = vectors


def merge_total_body(place, *refs):
    blocks, (out, vectors) = refs[:-2], refs[-2:]
    rows = out.shape[0]
    out[...] = added(blocks, 0, rows).astype(bf16)
    vectors[...] = split(sum(joined(ref[rows : rows + 16, :]) for ref in blocks))


def last_beside_body(place, vectors, *refs):
    rows = refs[0].shape[0]
    for index, ref in enumerate(refs[:-1]):
        refs[-1][rows * index : rows * (index + 1), :] = ref[...]
    refs[-1][rows * (len(refs) - 1) :, :] = vectors[...]


def in_order(place, near, far, stage, rows, along):
    piece = sum(rows) // 2 // along
    for side, ref in ((place[1], near), (1 - place[1], far)):
        for step in range(along):
            begin, offset = 0, piece * step
            for size in rows:
                span = size // 2 // along
                to = begin + side * (size // 2) + (place[2] ^ step) * span
                stage[pl.ds(pl.multiple_of(to, 16), span), :] = ref[offset : offset + span, :]
                begin += size
                offset += span


def feed_unpack_body(along, place, near, far, core_near, core_far, down_ref, up_ref, proj_ref, token_ref, stage):
    token_ref[...] = jnp.zeros_like(token_ref)
    for target, mine, beside in ((place[0], near, far), (1 - place[0], core_near, core_far)):
        in_order(place, mine, beside, stage, (512, PROJ_PACK, 512), along)
        wide = pl.ds(pl.multiple_of(512 * target, 512), 512)
        down_ref[wide, :] = stage[0:512, :].astype(f32)
        proj_ref[pl.ds(pl.multiple_of(128 * target, 128), 128), :] = stage[512:640, :].astype(f32)
        up_ref[:, wide] = stage[640:1152, :].astype(f32)


def feed_unpack(along, place, after, parts):
    return plain_call_after(
        partial(feed_unpack_body, along),
        [pltpu.HBM((FFN // 2, D), f32), pltpu.HBM((D, FFN // 2), f32), pltpu.HBM((D // 2, D), f32), shape_of((8, 128), f32)],
        place,
        after,
        parts,
        scratch=[pltpu.VMEM((FEED_PACK + PROJ_PACK, D), bf16)],
        room=24,
    )


def last_unpack_body(along, place, mine, beside, core_mine, core_beside, qkv_ref, merge_ref, *refs):
    vectors, stage, all_s = refs[:-2], refs[-2], refs[-1]
    rows = mine.shape[0] - 16
    for target, near, far in ((place[0], mine, beside), (1 - place[0], core_mine, core_beside)):
        in_order(place, near, far, stage, (QKV_PACK, MERGE_PACK), along)
        for side, ref in ((place[1], near), (1 - place[1], far)):
            all_s[pl.ds(pl.multiple_of(SUMS * target + 8 * side, 8), 8), :] = joined(ref[rows:, :])
        begin = pl.multiple_of(256 * target, 256)
        for part in range(2):
            qkv_ref[part, pl.ds(begin, 256), :] = stage[0:256, 256 * part : 256 * part + 256].astype(f32)
        qkv_ref[2, pl.ds(begin, 128), :] = stage[256:384, 0:256].astype(f32)
        qkv_ref[2, pl.ds(begin + 128, 128), :] = stage[256:384, 256:512].astype(f32)
        merge_ref[pl.ds(begin, 256), :] = stage[384:640, :].astype(f32)
    write_vectors(place[3], all_s, vectors)


VECTORS = [(1, D)] * 6 + [(2, D // 2), (1, FFN // 2), (1, MERGE_IN // 2), (1, MERGE_IN // 2), (HEADS // 2, SIDE * SIDE)]


def write_vectors(tp, sums, refs):
    for row in range(6):
        refs[row][...] = sums[row : row + 1, :]
    columns = pl.ds(pl.multiple_of(256 * tp, 256), 256)
    refs[6][...] = sums[6:8, columns]
    refs[7][:, 0:512] = sums[pl.ds(8 + 2 * tp, 1), :]
    refs[7][:, 512:1024] = sums[pl.ds(9 + 2 * tp, 1), :]
    refs[8][...] = sums[pl.ds(12 + tp, 1), :]
    refs[9][...] = sums[pl.ds(14 + tp, 1), :]
    refs[10][...] = sums[pl.ds(pl.multiple_of(16 + 8 * tp, 8), 8), 0 : SIDE * SIDE]


def last_unpack(along, place, *parts):
    outs = plain_call(
        partial(last_unpack_body, along),
        [pltpu.HBM(shape, f32) if shape[-2] >= 128 else shape_of(shape, f32) for shape in [(3, D, D // 2), (MERGE_IN // 2, D)] + VECTORS],
        (place, *parts),
        scratch=[pltpu.VMEM((QKV_PACK + MERGE_PACK, D), bf16), pltpu.VMEM((2 * SUMS, D), f32)],
    )
    return outs[0], outs[1], outs[2:]


def fetch_by_tp(ring, piece_of):
    near = ring.y(piece_of)
    return near, ring.core(near)


def plain_pieces(tp_size, weights, params):
    merge, qkv, proj, up, down = [
        lax.all_gather(array, "tp", axis=axis, tiled=True) for array, axis in zip(weights, (0, 2, 0, 1, 0))
    ]
    gain, bias, qv, up_bias, table = [
        lax.all_gather(array, "tp", axis=axis, tiled=True) for array, axis in zip(params, (0, 0, 1, 0, 1))
    ]

    def shard(array, axis, which):
        size = array.shape[axis] // 2
        return lax.slice_in_dim(array, which * size, (which + 1) * size, axis=axis)

    def rows_of(which):
        rows = jnp.zeros((PARAMS, D), f32)
        rows = rows.at[0].set(shard(gain.astype(f32), 0, which)).at[1].set(shard(bias.astype(f32), 0, which))
        rows = rows.at[2].set(shard(qv, 1, which).reshape(-1)).at[3:5].set(shard(up_bias, 0, which).reshape(2, D))
        return rows.at[8:16, : SIDE * SIDE].set(shard(table, 1, which).T)

    merge_other = shard(merge, 0, 1)
    qkv_other = shard(qkv, 2, 1).reshape(3 * D, 256)
    proj_other, up_other, down_other = shard(proj, 0, 1), shard(up, 1, 1), shard(down, 0, 1)

    def qkv_piece(half):
        rows = qkv_other[768 * half : 768 * half + 768]
        return jnp.concatenate(
            [jnp.concatenate([rows[:384], rows[384:]], axis=1), proj_other[128 * half : 128 * half + 128]], axis=0
        )

    def feed_piece(half):
        tile = slice(512 * half, 512 * half + 512)
        return jnp.concatenate([down_other[tile], up_other[:, tile]], axis=0)

    own = (
        shard(merge, 0, 0), shard(qkv, 2, 0).reshape(3 * D, 256), shard(proj, 0, 0), shard(up, 1, 0), shard(down, 0, 0)
    )
    return own, (rows_of(0), split(rows_of(1))), (merge_other[:256], merge_other[256:]), (qkv_piece(0), qkv_piece(1)), (feed_piece(0), feed_piece(1))


def sum_plainly(tp_size, feed_packs, proj_packs, qkv_packs, merge_packs):
    feed_packs, proj_packs, qkv_packs, merge_packs = lax.psum(
        (feed_packs, proj_packs, qkv_packs, merge_packs), ("rows", "tp")
    )
    own_send, own_keep, other_send, other_keep = feed_packs
    order = [own_keep, own_send, other_keep, other_send]
    down = jnp.concatenate([block[0:512] for block in order], axis=0)
    up = jnp.concatenate([block[512:1024] for block in order], axis=1)

    def blocks(packs, size):
        send, keep = packs
        return [keep[:size], send[:size], keep[size : 2 * size], send[size : 2 * size]]

    def qkv_rows(block):
        return jnp.stack(
            [block[0:256, 0:256], block[0:256, 256:512], jnp.concatenate([block[256:384, 0:256], block[256:384, 256:512]])]
        )

    order = blocks(qkv_packs, QKV_PACK)
    qkv = jnp.concatenate(
        [jnp.concatenate([qkv_rows(order[2 * shard + half]) for half in range(2)], axis=1) for shard in range(2)], axis=2
    )
    proj = jnp.concatenate(blocks(proj_packs, PROJ_PACK), axis=0)
    merge = jnp.concatenate(blocks(merge_packs, MERGE_PACK), axis=0)
    sums = jnp.concatenate([joined(merge_packs[1][2 * MERGE_PACK :]), joined(merge_packs[0][2 * MERGE_PACK :])], axis=0)
    index = lax.axis_index("tp")

    def own(array, axis):
        size = array.shape[axis] // tp_size
        return lax.dynamic_slice_in_dim(array, index * size, size, axis).astype(f32)

    vectors = [sums[row] for row in range(6)] + [
        own(sums[6:8], 1), own(sums[8:12].reshape(-1), 0), own(sums[12:14].reshape(-1), 0),
        own(sums[14:16].reshape(-1), 0), own(sums[16:32, : SIDE * SIDE], 0),
    ]
    return own(down, 0), own(up, 1), own(qkv, 2), own(proj, 0), own(merge, 0), vectors


def per_device(
    rows_size, tp_size,
    section_rows, window_mask, cotangent, merge_weight, merge_gain, merge_bias, norm1_gain, norm1_bias,
    qkv_weight, qv_bias, bias_table, proj_weight, proj_bias, norm2_gain, norm2_bias,
    up_weight, up_bias, down_weight, down_bias,
):
    fast = tp_size == 2 and rows_size in (8, 16)
    count = cotangent.shape[0]
    index, tp = lax.axis_index("rows"), lax.axis_index("tp")
    place = jnp.stack([index & 1, (index >> 1) & 1, index >> 2, tp]).astype(jnp.int32)
    ring = Ring(place, rows_size)
    if fast:
        flat_qkv = qkv_weight.reshape(3 * D, D // 2)
        merge_piece = pack_merge(place, merge_weight)
        merge_near = ring.y(merge_piece)
        params, piece = pack_params(
            place, merge_piece, merge_gain, merge_bias, qv_bias, up_bias[None], bias_table.T
        )
        others = ring.y(piece)
        mask, live = masks_of(place, params, window_mask, count)
        qkv_piece = gate(pack_qkv(place, (mask,), flat_qkv, proj_weight), others, merge_near)
        qkv_near = ring.y(qkv_piece)
        hat, inverse = section_norm(qkv_piece, section_rows)
        merge_far = ring.core(merge_near)
        kernel_place = place
    else:
        (merge_weight, flat_qkv, proj_weight, up_weight, down_weight), (params, others), merge_pair, qkv_pair, feed_pair = plain_pieces(
            tp_size,
            (merge_weight, qkv_weight, proj_weight, up_weight, down_weight),
            (merge_gain, merge_bias, qv_bias, up_bias, bias_table),
        )
        (merge_near, merge_far), (qkv_near, qkv_far), (feed_near_piece, feed_far_piece) = merge_pair, qkv_pair, feed_pair
        kernel_place = jnp.zeros_like(place)
        hat, inverse = section_norm(params, section_rows)
        own_mask = lax.dynamic_slice_in_dim(window_mask, tp * count, count, 0)
        mask, live = masks_of(kernel_place, params, own_mask, count)

    merged, first, first_copy, merge_full, params, column = merge_rows(
        kernel_place, hat, merge_weight, merge_near, merge_far, params, others, norm1_gain[None], norm1_bias[None]
    )
    position, hat = expand(params, hat)
    if fast:
        (feed_piece,) = plain_call_after(
            pack_feed_body, [shape_of((FEED_PACK, D), bf16)], place, (position, qkv_near), (up_weight, down_weight)
        )
        qkv_far = ring.core(qkv_near)
        feed_near_piece = ring.y(feed_piece)
        feed_far_piece = ring.core(feed_near_piece)
    qkv_rows, weights, attended, padded, inverse_sums, qkv_full = attend(
        kernel_place, first, flat_qkv, qkv_near, qkv_far, params, position, mask
    )
    rows = [row[None] for row in (proj_bias, norm2_gain, norm2_bias, down_bias)]
    residual, total, back, second, turned, branch, own_send, feed_sums, proj_full = feed_own(
        kernel_place, attended, merged, cotangent, live, *rows, params, proj_weight, qkv_near, qkv_far,
        up_weight, down_weight,
    )
    total, back, own_keep, feed_sums = feed_middle(
        True, kernel_place, second, turned, branch, total, back, params, feed_sums, (up_weight, down_weight), LONG
    )
    total, back, other_send, feed_sums = feed_middle(
        False, kernel_place, second, turned, branch, total, back, params, feed_sums, (feed_far_piece,)
    )
    block_out, grad_residual, attn, other_keep, proj_send, proj_keep, feed_sums = feed_near(
        kernel_place, residual, second, turned, branch, total, back, rows[3], rows[1], params, feed_sums, feed_near_piece,
        attended,
    )
    after = feed_sums
    if fast:
        own_got, other_got, proj_got = ring.core(own_send), ring.core(other_send), ring.core(proj_send)
        feed_keeps = (own_keep, own_got, other_keep, other_got, proj_keep, proj_got)
        to_y, to_x, to_both, feed_kept = stage(feed_first_body, place, feed_sums, (576,) * 4, *feed_keeps)
        feed_from = (ring.y(to_y), ring.x(to_x), ring.xy(to_both))
        after = to_y
    stack, low, sums, vectors, position_grad, first_near = attend_back(
        after, attn, qkv_rows, weights, padded, inverse_sums, proj_full, merged, grad_residual, qkv_full,
        norm1_gain[None], first_copy,
    )
    qkv_send, qkv_keep, hat_near = qkv_back(kernel_place, sums, first_near, stack, hat)
    after = sums
    if fast:
        along = ring.along
        qkv_got = ring.core(qkv_send)
        span = 576 // along
        feed_parts = stage(
            feed_second_body, place, qkv_send, (span,) * along, feed_kept, *feed_from, cost=LONG
        )
        feed_got = [ring.z(feed_parts[step], step) for step in range(1, along)]
        to_y, to_x, to_both, qkv_kept = stage(
            qkv_first_body, place, feed_parts[0], (192,) * 4, qkv_keep, qkv_got
        )
        qkv_from = (ring.y(to_y), ring.x(to_x), ring.xy(to_both))
        after = to_y
    merge_send, merge_keep = merge_back(
        kernel_place, after, low, hat_near, merge_full, params, column, feed_sums, sums, vectors, position_grad
    )
    if fast:
        merge_got = ring.core(merge_send)
        (feed_total,) = stage(total_body, place, merge_send, (span,), feed_parts[0], *feed_got, cost=LONG)
        feed_all = [feed_total] + [ring.z(feed_total, step) for step in range(1, along)]
        (qkv_sum,) = stage(total_body, place, feed_total, (192,), qkv_kept, *qkv_from)
        to_y, to_x, to_both, merge_kept = stage(
            merge_first_body, place, qkv_sum, (144,) * 4, merge_keep, merge_got, scratch=[pltpu.VMEM((SUMS, D), f32)]
        )
        last_span = 320 // along
        last_parts = stage(
            last_second_body, place, to_y, (last_span + 16,) * along, qkv_sum,
            merge_kept, ring.y(to_y), ring.x(to_x), ring.xy(to_both),
        )
        last_got = [ring.z(last_parts[step], step) for step in range(1, along)]
        section_grad, token = section_back(last_parts[0], low, hat, inverse, merge_full, params)
        (feed_mine,) = stage(beside_body, place, token, (span * along,), *feed_all)
        feed_beside = ring.x(feed_mine)
        last_total, vectors = stage(
            merge_total_body, place, feed_mine, (last_span, 16), *([last_parts[0]] + last_got), cost=LONG
        )
        last_all = [last_total] + [ring.z(last_total, step) for step in range(1, along)]
        (last_near,) = stage(
            last_beside_body, place, feed_beside, (336,), vectors, *last_all, cost=LONG
        )
        last_far = ring.x(last_near)
        feed_cores = ring.core(feed_mine), ring.core(feed_beside)
        down_grad, up_grad, proj_grad, token = feed_unpack(
            along, place, last_near, (feed_mine, feed_beside, *feed_cores)
        )
        (last_far,) = stage(beside_body, place, token, (336,), last_far)
        qkv_grad, merge_grad, vectors = last_unpack(
            along, place, last_near, last_far, ring.core(last_near), ring.core(last_far)
        )
    else:
        section_grad, _ = section_back(low, low, hat, inverse, merge_full, params)
        down_grad, up_grad, qkv_grad, proj_grad, merge_grad, vectors = sum_plainly(
            tp_size, (own_send, own_keep, other_send, other_keep), (proj_send, proj_keep), (qkv_send, qkv_keep),
            (merge_send, merge_keep),
        )
    norm1_gain_grad, norm1_bias_grad, proj_bias_grad, norm2_gain_grad, norm2_bias_grad, down_bias_grad = [
        row.reshape(D) for row in vectors[0:6]
    ]
    qv_grad, up_bias_grad, gain_grad, bias_grad, table_grad = vectors[6:]
    return (
        block_out, section_grad, merge_grad, gain_grad.reshape(-1), bias_grad.reshape(-1),
        norm1_gain_grad, norm1_bias_grad, qkv_grad, qv_grad, table_grad.T, proj_grad, proj_bias_grad,
        norm2_gain_grad, norm2_bias_grad, up_grad, up_bias_grad.reshape(-1), down_grad, down_bias_grad,
    )


def solution(mesh):
    rows_size, tp_size = mesh.shape["rows"], mesh.shape["tp"]
    both = ("rows", "tp")
    return jax.shard_map(
        partial(per_device, rows_size, tp_size),
        mesh=mesh,
        in_specs=(
            P(both, None), P("rows"), P(both, None), P("tp", None), P("tp"), P("tp"), P(), P(),
            P(None, None, "tp"), P(None, "tp"), P(None, "tp"), P("tp", None), P(), P(), P(),
            P(None, "tp"), P("tp"), P("tp", None), P(),
        ),
        out_specs=(
            P(both, None), P(both, None), P("tp", None), P("tp"), P("tp"), P(), P(),
            P(None, None, "tp"), P(None, "tp"), P(None, "tp"), P("tp", None), P(), P(), P(),
            P(None, "tp"), P("tp"), P("tp", None), P(),
        ),
        check_vma=False,
    )
```

```python
from functools import partial
import math

import jax
import jax.numpy as jnp
from jax import lax
from jax.experimental import pallas as pl
from jax.experimental.pallas import tpu as pltpu
from jax.sharding import PartitionSpec as P

MERGE_IN = 1024
D = 512
HEADS = 16
HEAD_DIM = 32
FFN = 2048
WINDOW = 10
AREA = WINDOW * WINDOW
SIDE = 2 * WINDOW - 1
EPSILON = 1e-05
MASKED_SCORE = -1e30
EXACT = lax.Precision.HIGHEST
SCALING = 1.0 / math.sqrt(HEAD_DIM)
GROUP = 4
ROWS = GROUP * AREA
KEYS = 112
QUERIES = 128
QUADS = 4
QUAD = 4 * HEAD_DIM
LANES = 4 * QUERIES

bf16 = jnp.bfloat16
f32 = jnp.float32


def mm(a, b):
    return jnp.dot(a, b, preferred_element_type=f32)


def mm_t(a, b):
    return lax.dot_general(a, b, (((1,), (1,)), ((), ())), preferred_element_type=f32)


def t_mm(a, b):
    return lax.dot_general(a, b, (((0,), (0,)), ((), ())), preferred_element_type=f32)


def normalize(values):
    center = jnp.mean(values, axis=-1, keepdims=True)
    spread = jnp.mean(values * values, axis=-1, keepdims=True) - center * center
    inverse = lax.rsqrt(spread + EPSILON)
    return (values - center) * inverse, inverse


def norm_back(grad_hat, normed, inverse):
    first_mean = jnp.mean(grad_hat, axis=-1, keepdims=True)
    second_mean = jnp.mean(grad_hat * normed, axis=-1, keepdims=True)
    return inverse * (grad_hat - first_mean - normed * second_mean)


def column_sum(values):
    return jnp.sum(values, axis=0, keepdims=True)


def head_masks():
    lane = lax.broadcasted_iota(jnp.int32, (1, QUAD), 1) // HEAD_DIM
    return [(lane == head).astype(f32).astype(bf16) for head in range(4)]


def spread_heads(rows, masks):
    return jnp.concatenate([rows * mask for mask in masks], axis=0)


def kernel_call(body, grid, in_specs, out_specs, out_shape, scratch=(), flops=0, moved=0, room=32, cost=None):
    return pl.pallas_call(
        body,
        grid=grid,
        in_specs=in_specs,
        out_specs=out_specs,
        out_shape=out_shape,
        scratch_shapes=list(scratch),
        compiler_params=pltpu.CompilerParams(
            dimension_semantics=("arbitrary",) * len(grid), vmem_limit_bytes=room * 1024 * 1024
        ),
        cost_estimate=cost or COST,
    )


def whole(shape):
    return pl.BlockSpec(shape, lambda *_: (0,) * len(shape), pipeline_mode=pl.Buffered(1))


def by_rows(rows, columns):
    return pl.BlockSpec((rows, columns), lambda i: (i, 0))


def by_windows(shape):
    return pl.BlockSpec((GROUP,) + shape, lambda i: (i,) + (0,) * len(shape))


SCALARS = pl.BlockSpec(memory_space=pltpu.SMEM)
RESIDENT = pl.BlockSpec(memory_space=pltpu.VMEM)
ANYWHERE = pl.BlockSpec(memory_space=pl.ANY)


def in_hbm(array):
    return pltpu.with_memory_space_constraint(array, pltpu.HBM)


FEED_PACK = 1024
QKV_PACK = 384
PROJ_PACK = 128
MERGE_PACK = 256
STAGE_ROOM = 9
COST = pl.CostEstimate(flops=1, bytes_accessed=1, transcendentals=0)
LONG = pl.CostEstimate(flops=10**12, bytes_accessed=1, transcendentals=0)
SUMS = 16
PARAMS = 16


def shape_of(shape, dtype):
    return jax.ShapeDtypeStruct(shape, dtype)


def split(rows):
    high = rows.astype(bf16).astype(f32)
    return jnp.concatenate([high, rows - high], axis=0).astype(bf16)


def joined(pair):
    half = pair.shape[0] // 2
    return pair[:half].astype(f32) + pair[half:].astype(f32)


def both_shards(tp, mine, other, axis):
    return jnp.where(
        tp == 0, jnp.concatenate([mine, other], axis=axis), jnp.concatenate([other, mine], axis=axis)
    )


def pack_merge_body(place, merge_ref, out_ref, sem):
    half = pl.ds(pl.multiple_of(256 * place[0], 256), 256)
    copy = pltpu.make_async_copy(merge_ref.at[half, :], out_ref, sem)
    copy.start()
    copy.wait()


def pack_merge(place, merge):
    return pl.pallas_call(
        pack_merge_body,
        in_specs=[SCALARS, ANYWHERE],
        out_specs=RESIDENT,
        out_shape=pltpu.VMEM((256, D), bf16),
        scratch_shapes=[pltpu.SemaphoreType.DMA],
        compiler_params=pltpu.CompilerParams(vmem_limit_bytes=4 * 1024 * 1024),
        cost_estimate=COST,
    )(place, in_hbm(merge))


def pack_params_body(
    place, after, gain_ref, bias_ref, qv_ref, up_bias_ref, table_ref,
    params_ref, out_ref, gain_s, bias_s, qv_s, up_bias_s, table_s, sems,
):
    pairs = (
        (gain_ref, gain_s), (bias_ref, bias_s), (qv_ref, qv_s), (up_bias_ref, up_bias_s), (table_ref, table_s)
    )
    copies = [pltpu.make_async_copy(source, target, sems.at[index]) for index, (source, target) in enumerate(pairs)]
    for copy in copies:
        copy.start()
    params_ref[...] = jnp.zeros_like(params_ref)
    for copy in copies:
        copy.wait()
    params_ref[0:1, :] = gain_s[...].astype(f32).reshape(1, D)
    params_ref[1:2, :] = bias_s[...].astype(f32).reshape(1, D)
    params_ref[2:3, 0:256] = qv_s[0:1, :]
    params_ref[2:3, 256:512] = qv_s[1:2, :]
    params_ref[3:4, :] = up_bias_s[:, 0:512]
    params_ref[4:5, :] = up_bias_s[:, 512:1024]
    params_ref[8:16, 0 : SIDE * SIDE] = table_s[...]
    out_ref[...] = split(params_ref[...])


def pack_params(place, after, *operands):
    operands = [in_hbm(array) for array in operands]
    return pl.pallas_call(
        pack_params_body,
        in_specs=[SCALARS] + [ANYWHERE] * 6,
        out_specs=[RESIDENT] * 2,
        out_shape=[pltpu.VMEM((PARAMS, D), f32), pltpu.VMEM((2 * PARAMS, D), bf16)],
        scratch_shapes=[pltpu.VMEM(array.shape, array.dtype) for array in operands] + [pltpu.SemaphoreType.DMA((5,))],
        compiler_params=pltpu.CompilerParams(vmem_limit_bytes=4 * 1024 * 1024),
        cost_estimate=COST,
    )(place, after, *operands)


def plain_call(body, outs, operands, room=16, scratch=(), flops=0):
    return pl.pallas_call(
        body,
        in_specs=[SCALARS] + [pl.BlockSpec(memory_space=pltpu.VMEM)] * (len(operands) - 1),
        out_specs=[pl.BlockSpec(memory_space=pltpu.VMEM)] * len(outs),
        out_shape=outs,
        scratch_shapes=list(scratch),
        compiler_params=pltpu.CompilerParams(vmem_limit_bytes=room * 1024 * 1024),
        cost_estimate=COST,
    )(*operands)


def pack_qkv_body(place, qkv_ref, proj_ref, *refs):
    out, qkv_s, proj_s, sems = refs[-4:]
    core = place[0]
    copies = [
        pltpu.make_async_copy(qkv_ref.at[pl.ds(pl.multiple_of(768 * core, 256), 768), :], qkv_s, sems.at[0]),
        pltpu.make_async_copy(proj_ref.at[pl.ds(pl.multiple_of(128 * core, 128), 128), :], proj_s, sems.at[1]),
    ]
    for copy in copies:
        copy.start()
    for copy in copies:
        copy.wait()
    for side in range(2):
        out[0:384, 256 * side : 256 * side + 256] = qkv_s[384 * side : 384 * side + 384, :]
    out[384:512, :] = proj_s[...]


def pack_qkv(place, after, qkv, proj):
    return pl.pallas_call(
        pack_qkv_body,
        in_specs=[SCALARS] + [ANYWHERE] * (2 + len(after)),
        out_specs=RESIDENT,
        out_shape=pltpu.VMEM((QKV_PACK + PROJ_PACK, D), bf16),
        scratch_shapes=[
            pltpu.VMEM((768, 256), bf16), pltpu.VMEM((128, D), bf16), pltpu.SemaphoreType.DMA((2,)),
        ],
        compiler_params=pltpu.CompilerParams(vmem_limit_bytes=4 * 1024 * 1024),
        cost_estimate=COST,
    )(place, in_hbm(qkv), in_hbm(proj), *after)


def pack_feed_body(place, up_ref, down_ref, out):
    half = pl.ds(pl.multiple_of(512 * place[0], 512), 512)
    out[0:512, :] = down_ref[half, :]
    out[512:1024, :] = up_ref[:, half]


def plain_call_after(body, outs, place, after, operands, room=16, scratch=(), flops=0, cost=COST):
    after = after if isinstance(after, tuple) else (after,)

    def without_after(place, *refs):
        return body(place, *refs[len(after) :])

    return pl.pallas_call(
        without_after,
        in_specs=[SCALARS] + [pl.BlockSpec(memory_space=pl.ANY)] * len(after) + [pl.BlockSpec(memory_space=pltpu.VMEM)] * len(operands),
        out_specs=[pl.BlockSpec(memory_space=pltpu.VMEM)] * len(outs),
        out_shape=outs,
        scratch_shapes=list(scratch),
        compiler_params=pltpu.CompilerParams(vmem_limit_bytes=room * 1024 * 1024),
        cost_estimate=cost,
    )(place, *after, *operands)


def nothing(array_ref, *refs):
    pass


def gate(array, *after):
    return pl.pallas_call(
        nothing,
        in_specs=[RESIDENT] + [ANYWHERE] * len(after),
        out_specs=RESIDENT,
        out_shape=pltpu.VMEM(array.shape, array.dtype),
        input_output_aliases={0: 0},
        compiler_params=pltpu.CompilerParams(vmem_limit_bytes=4 * 1024 * 1024),
        cost_estimate=COST,
    )(array, *after)


def masks_body(place, window_in, mask_ref, live_ref, stage, window_s, sem):
    copy = pltpu.make_async_copy(window_in, window_s, sem)
    copy.start()
    copy.wait()
    window_ref = window_s[...].reshape(1, window_s.shape[0])
    windows = mask_ref.shape[0]
    shards = window_ref.shape[1] // (windows * AREA)
    stage[...] = jnp.zeros_like(stage)
    for window in range(windows):
        patch = window_ref[:, AREA * window : AREA * (window + 1)]
        for shard in range(1, shards):
            begin = AREA * (windows * shard + window)
            patch = jnp.where(place[3] == shard, window_ref[:, begin : begin + AREA], patch)
        stage[window : window + 1, 0:AREA] = patch
    patches = jnp.minimum(stage[...], 1).astype(f32)
    live = jnp.max(patches, axis=1, keepdims=True)
    inside = lax.broadcasted_iota(jnp.int32, (windows, QUERIES), 1) < AREA
    keep = jnp.logical_and(jnp.maximum(patches, 1.0 - live) > 0.5, inside)
    added = jnp.where(keep, 0.0, MASKED_SCORE)
    for window in range(windows):
        mask_ref[window] = added[window : window + 1, :]
        live_ref[window] = jnp.broadcast_to(live[window : window + 1, :], (1, QUERIES))


def masks_of(place, after, window_mask, count):
    windows = count // AREA
    return pl.pallas_call(
        lambda place, after, *refs: masks_body(place, *refs),
        in_specs=[SCALARS, ANYWHERE, ANYWHERE],
        out_specs=[RESIDENT] * 2,
        out_shape=[pltpu.VMEM((windows, 1, QUERIES), f32)] * 2,
        scratch_shapes=[
            pltpu.VMEM((windows, QUERIES), jnp.int32), pltpu.VMEM(window_mask.shape, jnp.int32), pltpu.SemaphoreType.DMA,
        ],
        compiler_params=pltpu.CompilerParams(vmem_limit_bytes=4 * 1024 * 1024),
        cost_estimate=COST,
    )(place, after, in_hbm(window_mask))


def section_norm_body(after, rows_ref, hat_ref, inverse_ref, rows_s, sems):
    steps = rows_s.shape[0] // ROWS
    copies = []
    for step in range(steps):
        here = slice(ROWS * step, ROWS * (step + 1))
        copies.append(pltpu.make_async_copy(rows_ref.at[here, :], rows_s.at[here, :], sems.at[step]))
        copies[step].start()
    for step in range(steps):
        here = slice(ROWS * step, ROWS * (step + 1))
        copies[step].wait()
        hat, inverse = normalize(rows_s[here, :].astype(f32))
        hat_ref[here, :] = hat.astype(bf16)
        inverse_ref[here, :] = inverse


def section_norm(after, rows):
    count = rows.shape[0]
    return kernel_call(
        section_norm_body,
        (1,),
        [ANYWHERE, ANYWHERE],
        [RESIDENT, RESIDENT],
        [pltpu.VMEM((count, MERGE_IN), bf16), shape_of((count, 1), f32)],
        [pltpu.VMEM((count, MERGE_IN), bf16), pltpu.SemaphoreType.DMA((count // ROWS,))],
        room=16,
    )(after, in_hbm(rows))


def gain_rows(tp, params, others):
    return both_shards(tp, params[0:1], others[0:1], 1), both_shards(tp, params[1:2], others[1:2], 1)


def merge_body(
    place, hat_ref, own_ref, near_ref, far_ref, params_ref, others_ref, norm_gain, norm_bias,
    merged_ref, first_ref, first_copy, merge_ref, params_out_ref, column_ref,
    merge_s, shift_s, gain_s,
):

    @pl.when(pl.program_id(0) == 0)
    def _():
        core, tp = place[0], place[3]
        merge_s[pl.ds(pl.multiple_of(512 * tp, 512), 512), :] = own_ref[...]
        other = 512 * (1 - tp)
        merge_s[pl.ds(pl.multiple_of(other + 256 * core, 256), 256), :] = near_ref[...]
        merge_s[pl.ds(pl.multiple_of(other + 256 * (1 - core), 256), 256), :] = far_ref[...]
        merge_ref[...] = merge_s[...]
        params = params_ref[...]
        others = joined(others_ref[...])
        gain, bias = gain_rows(tp, params, others)
        gain_s[...] = gain.astype(bf16)
        shift_s[...] = mm(jnp.broadcast_to(bias, (16, MERGE_IN)).astype(bf16), merge_s[...])[0:1]
        params_out_ref[0:1, 0:1024] = gain
        params_out_ref[0:1, 1024:2048] = bias
        params_out_ref[1:2, 0:512] = both_shards(tp, params[2:3, 0:256], others[2:3, 0:256], 1)
        params_out_ref[1:2, 512:1024] = both_shards(tp, params[2:3, 256:512], others[2:3, 256:512], 1)
        params_out_ref[1:2, 1024:2048] = jnp.zeros((1, 1024), f32)
        params_out_ref[2:3, :] = both_shards(
            tp,
            jnp.concatenate([params[3:4], params[4:5]], axis=1),
            jnp.concatenate([others[3:4], others[4:5]], axis=1),
            1,
        )
        params_out_ref[3:8, :] = jnp.zeros((5, 2048), f32)
        params_out_ref[8:24, 0:512] = both_shards(tp, params[8:16], others[8:16], 0)
        params_out_ref[8:24, 512:2048] = jnp.zeros((16, 1536), f32)
        column_ref[...] = jnp.broadcast_to(gain, (128, MERGE_IN)).T

    here = pl.ds(pl.multiple_of(pl.program_id(0) * ROWS, 16), ROWS)
    merged = mm(hat_ref[here, :] * gain_s[...], merge_s[...]) + shift_s[...]
    merged_ref[...] = merged
    hat, _ = normalize(merged)
    first = (hat * norm_gain[...] + norm_bias[...]).astype(bf16)
    first_ref[here, :] = first
    first_copy[...] = first


def merge_rows(place, hat, own, near, far, params, others, gain, bias):
    count = hat.shape[0]
    return kernel_call(
        merge_body,
        (count // ROWS,),
        [
            SCALARS, RESIDENT, RESIDENT, RESIDENT, RESIDENT, RESIDENT, RESIDENT, RESIDENT, RESIDENT,
        ],
        [
            by_rows(ROWS, D), RESIDENT, by_rows(ROWS, D), whole((MERGE_IN, D)), RESIDENT,
            whole((MERGE_IN, 128)),
        ],
        [
            pltpu.HBM((count, D), f32), pltpu.VMEM((count, D), bf16), pltpu.HBM((count, D), bf16),
            pltpu.HBM((MERGE_IN, D), bf16),
            shape_of((24, 2048), f32), pltpu.HBM((MERGE_IN, 128), f32),
        ],
        [
            pltpu.VMEM((MERGE_IN, D), bf16), pltpu.VMEM((1, D), f32), pltpu.VMEM((1, MERGE_IN), bf16),
        ],
        flops=2 * count * D * MERGE_IN,
        moved=count * 10 * D + 4 * D * MERGE_IN,
        room=14,
    )(place, hat, own, near, far, params, others, gain, bias)


def value_blocks(values, masks):
    return [jnp.concatenate([values * mask, jnp.broadcast_to(mask, (QUERIES, QUAD))], axis=1) for mask in masks]


def turned_products(turned, scores):
    parts = []
    for pair in range(2):
        both = mm(turned[64 * pair : 64 * pair + 64], scores[:, 256 * pair : 256 * pair + 256])
        parts += [both[0:32, 0:128], both[32:64, 128:256]]
    return jnp.concatenate(parts, axis=0).T


def attend_body(
    place, first_ref, own_ref, near_ref, far_ref, params_ref, position_ref, mask_ref,
    qkv_out_ref, weights_ref, attended_ref, padded_ref, inverse_ref, qkv_ref,
    stage, mixed,
):
    @pl.when(pl.program_id(0) == 0)
    def _():
        core, tp = place[0], place[3]
        other = pl.ds(pl.multiple_of(256 * (1 - tp), 256), 256)
        qkv_ref[:, pl.ds(pl.multiple_of(256 * tp, 256), 256)] = own_ref[...]
        for ref, half in ((near_ref, core), (far_ref, 1 - core)):
            for side in range(2):
                rows = pl.ds(pl.multiple_of(768 * half + 384 * side, 128), 384)
                qkv_ref[rows, other] = ref[0:384, 256 * side : 256 * side + 256]

    here = pl.ds(pl.multiple_of(pl.program_id(0) * ROWS, 16), ROWS)
    stage[pl.ds(0, ROWS), :] = first_ref[here, :].astype(f32)
    stage[pl.ds(ROWS, 32), :] = jnp.zeros((32, D), f32)
    padded = jnp.concatenate(
        [stage[pl.ds(AREA * w, QUERIES), :].astype(bf16) for w in range(GROUP)], axis=0
    )
    queries = (SCALING * (mm(padded, qkv_ref[0:512, :]) + params_ref[1:2, 0:512])).astype(bf16)
    keys = mm(padded, qkv_ref[512:1024, :]).astype(bf16)
    values = (mm(padded, qkv_ref[1024:1536, :]) + params_ref[1:2, 512:1024]).astype(bf16)
    for w in range(GROUP):
        block = slice(QUERIES * w, QUERIES * (w + 1))
        qkv_out_ref[w, :, 0:D] = queries[block]
        qkv_out_ref[w, :, D : 2 * D] = keys[block]
        qkv_out_ref[w, :, 2 * D :] = values[block]
    masks = head_masks()
    for w in range(GROUP):
        mask = mask_ref[w]
        for quad in range(QUADS):
            columns = slice(QUAD * quad, QUAD * (quad + 1))
            rows = QUERIES * w
            spread = spread_heads(keys[rows : rows + QUERIES, columns], masks)
            scores = mm_t(queries[rows : rows + KEYS, columns], spread)
            raised = []
            for head in range(4):
                lanes = slice(QUERIES * head, QUERIES * (head + 1))
                part = scores[:, lanes] + position_ref[quad, :, lanes] + mask
                raised.append(jnp.exp(part - jnp.max(part, axis=1, keepdims=True)).astype(bf16))
            weights = jnp.concatenate(raised, axis=1)
            weights_ref[w, quad] = weights
            blocks = value_blocks(values[rows : rows + QUERIES, columns], masks)
            out = mm(weights, jnp.concatenate(blocks, axis=0))
            inverse = 1.0 / out[:, QUAD:]
            both = out[:, :QUAD] * inverse
            inverse_ref[w, :, columns] = inverse.astype(bf16)
            padded_ref[w, :, columns] = both.astype(bf16)
            mixed[pl.ds(AREA * w, AREA), columns] = both[0:AREA]
    attended_ref[...] = mixed[...].astype(bf16)


def attend(place, first, own, near, far, params, position, mask):
    count = first.shape[0]
    windows = count // AREA
    return kernel_call(
        attend_body,
        (count // ROWS,),
        [
            SCALARS, RESIDENT, RESIDENT, RESIDENT, RESIDENT, RESIDENT, RESIDENT, by_windows((1, QUERIES)),
        ],
        [
            by_windows((QUERIES, 3 * D)), by_windows((QUADS, KEYS, LANES)), by_rows(ROWS, D),
            by_windows((KEYS, D)), by_windows((KEYS, D)), RESIDENT,
        ],
        [
            pltpu.HBM((windows, QUERIES, 3 * D), bf16), pltpu.HBM((windows, QUADS, KEYS, LANES), bf16),
            pltpu.HBM((count, D), bf16), pltpu.HBM((windows, KEYS, D), bf16), pltpu.HBM((windows, KEYS, D), bf16),
            shape_of((3 * D, D), bf16),
        ],
        [pltpu.VMEM((ROWS + 32, D), f32), pltpu.VMEM((ROWS, D), f32)],
        flops=2 * count * D * (3 * D + 4 * AREA),
        moved=count * 10 * D + windows * QUADS * KEYS * LANES * 2,
        room=20,
    )(place, first, own, near, far, params, position, mask)


def gelu_parts(t):
    chance = 0.5 * lax.erf(t * math.sqrt(0.5)) + 0.5
    density = jnp.exp(t * t * -0.5) * (1.0 / math.sqrt(2.0 * math.pi))
    return t * chance, chance + t * density


TILE = 512
FEED_ROWS = 400
OWN_ROOM = 18
OTHER_ROOM = 12
AB_ROOM = 18
NEAR_ROOM = 20


def feed_tile(up, down, bias, second_ref, turned_ref, branch_ref, total_s, back_s, active_s, raise_s, target, first):
    sums = jnp.zeros((1, TILE), f32)

    def add_products(here, active, grad_raised):
        total_s[here, :] += mm(active, down)
        back = mm_t(grad_raised, up)
        if first:
            back_s[here, :] = back
        else:
            back_s[here, :] += back

    last = None
    for begin in range(0, second_ref.shape[0], FEED_ROWS):
        here = slice(begin, begin + FEED_ROWS)
        value, slope = gelu_parts(mm(second_ref[here, :], up) + bias)
        active = value.astype(bf16)
        grad_raised = (mm_t(branch_ref[here, :], down) * slope).astype(bf16)
        active_s[here, :] = active
        raise_s[here, :] = grad_raised
        sums += column_sum(grad_raised.astype(f32))
        if last is not None:
            add_products(*last)
        last = here, active, grad_raised
    add_products(*last)
    target[0:512, :] = t_mm(active_s[...], branch_ref[...]).astype(bf16)
    target[512:1024, :] = mm(turned_ref[...], raise_s[...]).astype(bf16)
    return sums


def feed_own_body(
    place, attended_ref, merged_ref, cotangent_ref, live_ref, proj_bias, norm_gain, norm_bias, down_bias, params_ref,
    proj_own, near_ref, far_ref, up_own, down_own,
    hat_ref, inverse_ref, total_ref, back_ref, second_ref, turned_ref, branch_ref, send_ref, sums_ref, proj_ref,
    active_s, raise_s,
):
    step = pl.program_id(0)
    blocks = pl.num_programs(0) - 1
    core, tp = place[0], place[3]

    @pl.when(step == 0)
    def _():
        proj_ref[pl.ds(pl.multiple_of(256 * tp, 256), 256), :] = proj_own[...]
        for ref, which in ((near_ref, core), (far_ref, 1 - core)):
            proj_ref[pl.ds(pl.multiple_of(256 * (1 - tp) + 128 * which, 128), 128), :] = ref[384:512, :]
        sums_ref[...] = jnp.zeros_like(sums_ref)

    @pl.when(step < blocks)
    def _():
        here = pl.ds(pl.multiple_of(step * ROWS, 16), ROWS)
        residual = merged_ref[...] + mm(attended_ref[...], proj_ref[...]) + proj_bias[...]
        total_ref[here, :] = residual + down_bias[...]
        hat, inverse = normalize(residual)
        hat_ref[here, :] = hat
        inverse_ref[here, :] = inverse
        second_ref[here, :] = (hat * norm_gain[...] + norm_bias[...]).astype(bf16)
        row = lax.broadcasted_iota(jnp.int32, (ROWS, 1), 0)
        live = live_ref[GROUP - 1, :, 0:1]
        for window in range(GROUP - 2, -1, -1):
            live = jnp.where(row < AREA * (window + 1), live_ref[window, :, 0:1], live)
        branch = cotangent_ref[...].astype(f32) * live
        branch_ref[here, :] = branch.astype(bf16)
        sums_ref[7:8, :] += column_sum(branch)

    @pl.when(step == blocks)
    def _():
        turned_ref[...] = second_ref[...].T
        shard = 2 * tp + 1 - core
        units = pl.ds(pl.multiple_of(TILE * (1 - core), TILE), TILE)
        bias = params_ref[2:3, pl.ds(pl.multiple_of(TILE * shard, TILE), TILE)]
        sums_ref[pl.ds(shard, 1), :] = feed_tile(
            up_own[:, units], down_own[units, :], bias, second_ref, turned_ref, branch_ref, total_ref, back_ref,
            active_s, raise_s, send_ref, True,
        )


def feed_own(
    place, attended, merged, cotangent, live, proj_bias, gain, bias, down_bias, params, proj, near, far, up, down
):
    count = attended.shape[0]
    blocks = count // ROWS

    def taken(columns):
        return pl.BlockSpec((ROWS, columns), lambda i: (jnp.minimum(i, blocks - 1), 0))

    return kernel_call(
        feed_own_body,
        (blocks + 1,),
        [
            SCALARS, taken(D), taken(D), taken(D),
            pl.BlockSpec((GROUP, 1, QUERIES), lambda i: (jnp.minimum(i, blocks - 1), 0, 0)), RESIDENT, RESIDENT, RESIDENT, RESIDENT, RESIDENT, RESIDENT, RESIDENT, RESIDENT,
            RESIDENT, RESIDENT,
        ],
        [RESIDENT] * 10,
        [pltpu.VMEM((count, D), f32), pltpu.VMEM((count, 1), f32)] + [pltpu.VMEM((count, D), f32)] * 2
        + [pltpu.VMEM((count, D), bf16), pltpu.VMEM((D, count), bf16), pltpu.VMEM((count, D), bf16)]
        + [pltpu.VMEM((FEED_PACK, D), bf16), shape_of((8, D), f32), shape_of((D, D), bf16)],
        [pltpu.VMEM((count, TILE), bf16)] * 2,
        room=OWN_ROOM,
    )(
        place, in_hbm(attended), in_hbm(merged), in_hbm(cotangent), live, proj_bias, gain, bias, down_bias, params, proj,
        near, far, up, down,
    )


def feed_middle_body(
    own, place, second_ref, turned_ref, branch_ref, total_in, back_in, params_ref, sums_in, *refs
):
    weights, (total_ref, back_ref, target_ref, sums_ref, active_s, raise_s) = refs[:-6], refs[-6:]
    core, tp = place[0], place[3]
    sums_ref[...] = sums_in[...]
    if own:
        shard = 2 * tp + core
        units = pl.ds(pl.multiple_of(TILE * core, TILE), TILE)
        up, down = weights[0][:, units], weights[1][units, :]
    else:
        shard = 2 * (1 - tp) + 1 - core
        up, down = weights[0][512:1024, :], weights[0][0:512, :]
    bias = params_ref[2:3, pl.ds(pl.multiple_of(TILE * shard, TILE), TILE)]
    sums_ref[pl.ds(shard, 1), :] = feed_tile(
        up, down, bias, second_ref, turned_ref, branch_ref, total_ref, back_ref, active_s, raise_s, target_ref, False
    )


def feed_middle(own, place, second, turned, branch, total, back, params, sums, weights, cost=COST):
    count = second.shape[0]
    return pl.pallas_call(
        partial(feed_middle_body, own),
        in_specs=[SCALARS] + [RESIDENT] * (7 + len(weights)),
        out_specs=[RESIDENT] * 4,
        out_shape=[pltpu.VMEM((count, D), f32)] * 2 + [pltpu.VMEM((FEED_PACK, D), bf16), shape_of((8, D), f32)],
        scratch_shapes=[pltpu.VMEM((count, TILE), bf16)] * 2,
        input_output_aliases={4: 0, 5: 1},
        compiler_params=pltpu.CompilerParams(vmem_limit_bytes=OTHER_ROOM * 1024 * 1024),
        cost_estimate=cost,
    )(place, second, turned, branch, total, back, params, sums, *weights)


def feed_near_body(
    place, hat_ref, inverse_ref, second_ref, turned_ref, branch_ref, total_in, back_in, norm_gain, params_ref,
    sums_in, near_ref, attended_ref,
    out_ref, grad_residual_ref, attn_ref, keep_ref, proj_send, proj_keep, sums_ref,
    total_s, back_s, active_s, raise_s, attended_s, proj_s, sem,
):
    step = pl.program_id(0)
    core, tp = place[0], place[3]
    fetch = pltpu.make_async_copy(attended_ref, attended_s, sem)

    @pl.when(step == 0)
    def _():
        fetch.start()
        sums_ref[...] = sums_in[...]
        total_s[...] = jnp.zeros_like(total_s)
        shard = 2 * (1 - tp) + core
        bias = params_ref[2:3, pl.ds(pl.multiple_of(TILE * shard, TILE), TILE)]
        sums_ref[pl.ds(shard, 1), :] = feed_tile(
            near_ref[512:1024, :], near_ref[0:512, :], bias, second_ref, turned_ref, branch_ref, total_s, back_s,
            active_s, raise_s, keep_ref, True,
        )

    @pl.when(step >= 1)
    def _():
        here = pl.ds(pl.multiple_of((step - 1) * ROWS, 16), ROWS)
        out_ref[...] = (total_in[here, :] + total_s[here, :]).astype(bf16)
        hat, inverse = hat_ref[here, :], inverse_ref[here, :]
        grad_second = back_in[here, :] + back_s[here, :]
        grad_residual = branch_ref[here, :].astype(f32) + norm_back(grad_second * norm_gain[...], hat, inverse)
        grad_residual_ref[here, :] = grad_residual
        attn_ref[here, :] = grad_residual.astype(bf16)
        sums_ref[4:5, :] += column_sum(grad_residual)
        sums_ref[5:6, :] += column_sum(grad_second * hat)
        sums_ref[6:7, :] += column_sum(grad_second)

    @pl.when(step == pl.num_programs(0) - 1)
    def _():
        fetch.wait()
        proj_s[...] = t_mm(attended_s[...], attn_ref[...]).astype(bf16)
        for target, half in ((proj_send, 1 - core), (proj_keep, core)):
            for other in range(2):
                shard = jnp.where(other == 0, tp, 1 - tp)
                rows = pl.ds(pl.multiple_of(256 * shard + 128 * half, 128), 128)
                target[PROJ_PACK * other : PROJ_PACK * (other + 1), :] = proj_s[rows, :]


def feed_near(place, hat, inverse, second, turned, branch, total, back, gain, params, sums, near, attended):
    count = hat.shape[0]
    blocks = count // ROWS

    def given(columns):
        return pl.BlockSpec((ROWS, columns), lambda i: (jnp.maximum(i - 1, 0), 0))

    return kernel_call(
        feed_near_body,
        (blocks + 1,),
        [SCALARS] + [RESIDENT] * 9 + [whole((8, D)), RESIDENT]
        + [pl.BlockSpec(memory_space=pl.ANY)],
        [given(D)] + [RESIDENT] * 5 + [whole((8, D))],
        [pltpu.HBM((count, D), bf16), pltpu.VMEM((count, D), f32), pltpu.VMEM((count, D), bf16)]
        + [pltpu.VMEM((FEED_PACK, D), bf16)] + [pltpu.VMEM((2 * PROJ_PACK, D), bf16)] * 2
        + [shape_of((8, D), f32)],
        [pltpu.VMEM((count, D), f32)] * 2 + [pltpu.VMEM((count, TILE), bf16)] * 2
        + [pltpu.VMEM((count, D), bf16), pltpu.VMEM((D, D), bf16), pltpu.SemaphoreType.DMA],
        room=NEAR_ROOM,
    )(
        place, hat, inverse, second, turned, branch, total, back, gain, params, sums, near, in_hbm(attended)
    )


def attend_back_body(
    after, attn_ref, qkv_in_ref, weights_ref, padded_ref, inverse_ref, proj_ref,
    merged_ref, grad_residual_ref, qkv_ref, rows_ref, first_in,
    stack_ref, low_ref, sums_ref, vectors_ref, position_ref, first_ref,
    stage, grads, sem,
):
    fetch = pltpu.make_async_copy(first_in, first_ref, sem)

    @pl.when(pl.program_id(0) == pl.num_programs(0) - 1)
    def _():
        fetch.wait()

    @pl.when(pl.program_id(0) == 0)
    def _():
        fetch.start()
        vectors_ref[...] = jnp.zeros_like(vectors_ref)
        sums_ref[...] = jnp.zeros_like(sums_ref)
        position_ref[...] = jnp.zeros_like(position_ref)

    here = pl.ds(pl.multiple_of(pl.program_id(0) * ROWS, 16), ROWS)
    stage[pl.ds(0, ROWS), :] = attn_ref[here, :].astype(f32)
    stage[pl.ds(ROWS, 32), :] = jnp.zeros((32, D), f32)
    real = lax.broadcasted_iota(jnp.int32, (KEYS, 1), 0) < AREA
    padded = jnp.concatenate(
        [jnp.where(real, stage[pl.ds(AREA * w, KEYS), :], 0.0).astype(bf16) for w in range(GROUP)], axis=0
    )
    grad_attended = mm_t(padded, proj_ref[...])
    masks = head_masks()
    empty = jnp.zeros((QUERIES - KEYS, QUAD), bf16)
    kept = {}
    for w in range(GROUP):
        for quad in range(QUADS):
            columns = slice(QUAD * quad, QUAD * (quad + 1))
            values = qkv_in_ref[w, :, 2 * D + QUAD * quad : 2 * D + QUAD * (quad + 1)]
            grad = grad_attended[KEYS * w : KEYS * (w + 1), columns] * inverse_ref[w, :, columns].astype(f32)
            low = grad.astype(bf16)
            taken = (grad * padded_ref[w, :, columns].astype(f32)).astype(bf16)
            both = jnp.concatenate([low, -taken], axis=1)
            change = jnp.concatenate([mm_t(both, block) for block in value_blocks(values, masks)], axis=1)
            grad_scores = (weights_ref[w, quad].astype(f32) * change).astype(bf16)
            position_ref[quad] += grad_scores.astype(f32)
            kept[w, quad] = (low, grad_scores)
    for w in range(GROUP):
        to = pl.ds(AREA * w, AREA)
        for quad in range(QUADS):
            low, grad_scores = kept[w, quad]
            queries = qkv_in_ref[w, :, QUAD * quad : QUAD * (quad + 1)]
            keys = qkv_in_ref[w, :, D + QUAD * quad : D + QUAD * (quad + 1)]
            grad_queries = mm(grad_scores, spread_heads(keys, masks)) * SCALING
            grad_keys = turned_products(queries.T[:, :KEYS], grad_scores)
            grad_values = turned_products(jnp.concatenate([low, empty], axis=0).T[:, :KEYS], weights_ref[w, quad])
            for part, grad in enumerate((grad_queries, grad_keys, grad_values)):
                grads[to, D * part + QUAD * quad : D * part + QUAD * (quad + 1)] = grad[0:AREA]
    stack = grads[...].astype(bf16)
    stack_ref[here, :] = stack
    sums_ref[...] += column_sum(stack.astype(f32))
    grad_first = (
        mm_t(stack[:, 0:D], qkv_ref[0:D, :])
        + mm_t(stack[:, D : 2 * D], qkv_ref[D : 2 * D, :])
        + mm_t(stack[:, 2 * D :], qkv_ref[2 * D :, :])
    )
    normed, inverse = normalize(merged_ref[...])
    grad_merged = grad_residual_ref[here, :] + norm_back(grad_first * rows_ref[0:1, :], normed, inverse)
    low = grad_merged.astype(bf16)
    low_ref[here, :] = low
    vectors_ref[0:1, :] += column_sum(grad_first * normed)
    vectors_ref[1:2, :] += column_sum(grad_first)
    vectors_ref[2:3, :] += column_sum(low.astype(f32))


def attend_back(after, attn, qkv_in, weights, padded, inverse, proj, merged, grad_residual, qkv, rows, first):
    count = attn.shape[0]
    return kernel_call(
        attend_back_body,
        (count // ROWS,),
        [
            ANYWHERE, RESIDENT, by_windows((QUERIES, 3 * D)), by_windows((QUADS, KEYS, LANES)),
            by_windows((KEYS, D)), by_windows((KEYS, D)), RESIDENT, by_rows(ROWS, D), RESIDENT, RESIDENT, RESIDENT,
            ANYWHERE,
        ],
        [RESIDENT] * 6,
        [
            pltpu.VMEM((count, 3 * D), bf16), pltpu.VMEM((count, D), bf16), shape_of((1, 3 * D), f32),
            shape_of((8, D), f32), shape_of((QUADS, KEYS, LANES), f32), pltpu.VMEM((count, D), bf16),
        ],
        [pltpu.VMEM((ROWS + 32, D), f32), pltpu.VMEM((ROWS, 3 * D), f32), pltpu.SemaphoreType.DMA],
        room=AB_ROOM,
    )(
        after, attn, *[in_hbm(array) for array in (qkv_in, weights, padded, inverse)], proj, in_hbm(merged),
        grad_residual, qkv, rows, in_hbm(first),
    )


def qkv_back_body(place, after, first_ref, stack_ref, hat_in, send_ref, keep_ref, hat_ref, qkv_s, turned_s, sem):
    part = pl.program_id(0)
    fetch = pltpu.make_async_copy(hat_in, hat_ref, sem)

    @pl.when(part == 0)
    def _():
        fetch.start()
        turned_s[...] = first_ref[...].T

    @pl.when(part == pl.num_programs(0) - 1)
    def _():
        fetch.wait()

    core, tp = place[0], place[3]
    qkv_s[...] = mm(turned_s[...], stack_ref[:, pl.ds(pl.multiple_of(D * part, D), D)]).astype(bf16)
    for target, half in ((send_ref, 1 - core), (keep_ref, core)):
        for other in range(2):
            shard = jnp.where(other == 0, tp, 1 - tp)
            base = QKV_PACK * other
            rows = pl.ds(pl.multiple_of(256 * half, 256), 256)
            columns = pl.ds(pl.multiple_of(256 * shard, 256), 256)

            @pl.when(part < 2)
            def _():
                target[base : base + 256, pl.ds(pl.multiple_of(256 * part, 256), 256)] = qkv_s[rows, columns]

            @pl.when(part == 2)
            def _():
                block = qkv_s[rows, columns]
                target[base + 256 : base + 384, 0:256] = block[0:128]
                target[base + 256 : base + 384, 256:512] = block[128:256]


def qkv_back(place, after, first, stack, hat):
    count = stack.shape[0]
    return kernel_call(
        qkv_back_body,
        (3,),
        [SCALARS, ANYWHERE, RESIDENT, RESIDENT, ANYWHERE],
        [RESIDENT] * 3,
        [pltpu.VMEM((2 * QKV_PACK, D), bf16)] * 2 + [pltpu.VMEM((count, MERGE_IN), bf16)],
        [pltpu.VMEM((D, D), bf16), pltpu.VMEM((D, count), bf16), pltpu.SemaphoreType.DMA],
        room=9,
    )(place, after, first, stack, in_hbm(hat))


def merge_back_body(
    place, after, low_ref, hat_ref, merge_ref, params_ref, column_ref, feed_sums_ref, qkv_sums_ref, vectors_ref,
    position_ref,
    send_ref, keep_ref,
    fold_s, all_s, raw_s,
):
    core, tp = place[0], place[3]
    total = vectors_ref[2:3, :]
    pair = jnp.concatenate([split(total), jnp.zeros((14, D), bf16)], axis=0)
    ones = jnp.ones((16, D), bf16)
    raw_s[...] = t_mm(hat_ref[...], low_ref[...])
    all_s[...] = jnp.zeros_like(all_s)
    all_s[0:2, :] = vectors_ref[0:2, :]
    all_s[2:6, :] = feed_sums_ref[4:8, :]
    all_s[6:7, :] = qkv_sums_ref[:, 0:D]
    all_s[7:8, :] = qkv_sums_ref[:, 2 * D :]
    all_s[8:12, :] = feed_sums_ref[0:4, :]
    all_s[16:32, 0:384] = fold_place(position_ref, fold_s)
    for tile in range(2):
        rows = slice(512 * tile, 512 * (tile + 1))
        merge = merge_ref[rows, :]
        scaled = raw_s[rows, :] * merge.astype(f32)
        scaled_high = scaled.astype(bf16)
        scaled_rest = (scaled - scaled_high.astype(f32)).astype(bf16)
        all_s[12 + tile : 13 + tile, :] = (mm_t(ones, scaled_high) + mm_t(ones, scaled_rest))[0:1]
        all_s[14 + tile : 15 + tile, :] = column_sum(mm_t(pair, merge))
    for target, half in ((send_ref, 1 - core), (keep_ref, core)):
        for other in range(2):
            begin = pl.multiple_of(512 * jnp.where(other == 0, tp, 1 - tp) + 256 * half, 256)
            bias = jnp.broadcast_to(params_ref[0:1, pl.ds(1024 + begin, 256)], (16, 256)).astype(bf16)
            gain = column_ref[pl.ds(begin, 256), 0:1]
            block = raw_s[pl.ds(begin, 256), :] * gain + t_mm(bias, pair)
            target[MERGE_PACK * other : MERGE_PACK * (other + 1), :] = block.astype(bf16)
        target[2 * MERGE_PACK :, :] = split(all_s[pl.ds(pl.multiple_of(SUMS * half, SUMS), SUMS), :])


def merge_back(place, after, low, hat, merge, params, column, feed_sums, sums, vectors, position):
    pack = 2 * MERGE_PACK + 2 * SUMS
    return pl.pallas_call(
        merge_back_body,
        in_specs=[SCALARS, ANYWHERE] + [RESIDENT] * 9,
        out_specs=[RESIDENT] * 2,
        out_shape=[pltpu.VMEM((pack, D), bf16), pltpu.VMEM((pack, D), bf16)],
        scratch_shapes=[
            pltpu.VMEM((HEADS, KEYS, 256), f32), pltpu.VMEM((32, D), f32), pltpu.VMEM((MERGE_IN, D), f32),
        ],
        compiler_params=pltpu.CompilerParams(vmem_limit_bytes=14 * 1024 * 1024),
        cost_estimate=COST,
    )(place, after, low, hat, merge, params, column, feed_sums, sums, vectors, position)


def section_back_body(after, low_ref, hat_ref, inverse_ref, merge_ref, params_ref, out_ref, token_ref):
    token_ref[...] = jnp.zeros_like(token_ref)
    scaled = mm_t(low_ref[...], merge_ref[...]) * params_ref[0:1, 0:MERGE_IN]
    out_ref[...] = norm_back(scaled, hat_ref[...].astype(f32), inverse_ref[...]).astype(bf16)


def section_back(after, low, hat, inverse, merge, params):
    count = low.shape[0]
    return kernel_call(
        section_back_body,
        (count // ROWS,),
        [
            pl.BlockSpec(memory_space=pl.ANY), by_rows(ROWS, D), by_rows(ROWS, MERGE_IN), by_rows(ROWS, 1),
            whole((MERGE_IN, D)), whole((24, 2048)),
        ],
        [by_rows(ROWS, MERGE_IN), whole((8, 128))],
        [pltpu.HBM((count, MERGE_IN), bf16), shape_of((8, 128), f32)],
        flops=2 * count * D * MERGE_IN,
        moved=count * 5 * MERGE_IN,
        room=16,
    )(after, in_hbm(low), in_hbm(hat), inverse, merge, params)


def spread_matrix():
    place = lax.broadcasted_iota(jnp.int32, (QUERIES, 256), 0)
    lane = lax.broadcasted_iota(jnp.int32, (QUERIES, 256), 1)
    target = place + (SIDE - WINDOW) * (place // WINDOW)
    return jnp.logical_and(lane == target, place < AREA).astype(f32)


def expand_body(params_ref, hat_ref, place_ref, hat_copy, lines_s, out_s, sem):
    save = pltpu.make_async_copy(hat_ref, hat_copy, sem)
    save.start()
    lane = lax.broadcasted_iota(jnp.int32, (384, QUERIES), 0)
    patch = lax.broadcasted_iota(jnp.int32, (384, QUERIES), 1)
    middle = (WINDOW - 1) * (SIDE + 1)
    picked = jnp.logical_and(lane == middle - patch - (SIDE - WINDOW) * (patch // WINDOW), patch < AREA)
    picked = picked.astype(f32).astype(bf16)
    tables = params_ref[8 : 8 + HEADS, 0:384]
    for place in range(AREA):
        offset = SIDE * (place // WINDOW) + place % WINDOW
        lines_s[HEADS * place : HEADS * (place + 1), :] = pltpu.roll(tables, (384 - offset) % 384, 1)
    for begin in range(0, HEADS * AREA, ROWS):
        here = slice(begin, begin + ROWS)
        rows = lines_s[here, :]
        high = rows.astype(bf16)
        rest = rows - high.astype(f32)
        middle_part = rest.astype(bf16)
        low = (rest - middle_part.astype(f32)).astype(bf16)
        out_s[here, :] = mm(high, picked) + mm(middle_part, picked) + mm(low, picked)
    for head in range(HEADS):
        lanes = slice(QUERIES * (head % 4), QUERIES * (head % 4 + 1))
        place_ref[head // 4, 0:AREA, lanes] = out_s[pl.ds(head, AREA, stride=HEADS), :]
        place_ref[head // 4, AREA:KEYS, lanes] = jnp.zeros((KEYS - AREA, QUERIES), f32)
    save.wait()


def expand(params, hat):
    return kernel_call(
        expand_body,
        (1,),
        [RESIDENT, RESIDENT],
        [RESIDENT, ANYWHERE],
        [shape_of((QUADS, KEYS, LANES), f32), pltpu.HBM(hat.shape, bf16)],
        [pltpu.VMEM((HEADS * AREA, 384), f32), pltpu.VMEM((HEADS * AREA, QUERIES), f32), pltpu.SemaphoreType.DMA],
        room=16,
    )(params, hat)


def fold_place(place_ref, stage_s):
    spread = spread_matrix().astype(bf16)
    lines = []
    for head in range(HEADS):
        stage = stage_s.at[head]
        rows = place_ref[head // 4, :, QUERIES * (head % 4) : QUERIES * (head % 4 + 1)]
        rows = jnp.concatenate([rows, jnp.zeros((QUERIES - KEYS, QUERIES), f32)], axis=0).T[:KEYS]
        high = rows.astype(bf16)
        rest = (rows - high.astype(f32)).astype(bf16)
        stage[...] = mm(high, spread) + mm(rest, spread)
        total = jnp.zeros((WINDOW, 384), f32)
        for y in range(WINDOW):
            part = jnp.concatenate(
                [stage[pl.ds(WINDOW * y, WINDOW), :], jnp.zeros((WINDOW, 128), f32)], axis=1
            )
            total += pltpu.roll(part, SIDE * (WINDOW - 1 - y), 1) if y < WINDOW - 1 else part
        line = total[WINDOW - 1 : WINDOW, :]
        for x in range(WINDOW - 1):
            line += pltpu.roll(total[x : x + 1, :], WINDOW - 1 - x, 1)
        lines.append(line)
    return jnp.concatenate(lines, axis=0)


class Ring:
    def __init__(self, place, rows_size):
        self.place = place
        self.rows_size = rows_size
        self.along = rows_size // 4

    def to(self, array, bits):
        return lax.ppermute(array, "rows", [(i, i ^ bits) for i in range(self.rows_size)])

    def core(self, array):
        return self.to(array, 1)

    def x(self, array):
        return self.to(array, 2)

    def z(self, array, step):
        return self.to(array, 4 * step)

    def y(self, array):
        return lax.ppermute(array, "tp", [(0, 1), (1, 0)])

    def xy(self, array):
        pairs = [(2 * i + t, 2 * (i ^ 2) + 1 - t) for i in range(self.rows_size) for t in range(2)]
        return lax.ppermute(array, ("rows", "tp"), pairs)


def rows_of(array, begin, rows):
    return lax.dynamic_slice_in_dim(array, begin, rows, 0).astype(f32)


def stage(body, place, after, rows, *operands, cost=COST, scratch=()):
    return plain_call_after(
        body, [pltpu.VMEM((count, D), bf16) for count in rows], place, after, operands, room=STAGE_ROOM, cost=cost,
        scratch=scratch,
    )


def added(refs, begin, rows):
    here = pl.ds(pl.multiple_of(begin, 16), rows)
    total = refs[0][here, :].astype(f32)
    for ref in refs[1:]:
        total = total + ref[here, :].astype(f32)
    return total


def part(ref, begin, rows):
    return ref.at[begin : begin + rows, :]


FEED_BLOCKS = ((0, 256), (256, 64), (320, 256))


def feed_first_body(
    place, own_keep, own_got, other_keep, other_got, proj_keep, proj_got, to_y, to_x, to_both, kept
):
    x = place[1]
    own, other = (own_keep, own_got), (other_keep, other_got)
    for target, blocks, shard, side in (
        (to_y, other, 1, x), (to_x, own, 0, 1 - x), (to_both, other, 1, 1 - x), (kept, own, 0, x)
    ):
        target[0:256, :] = added(blocks, 256 * side, 256).astype(bf16)
        target[256:320, :] = added((proj_keep, proj_got), PROJ_PACK * shard + 64 * side, 64).astype(bf16)
        target[320:576, :] = added(blocks, 512 + 256 * side, 256).astype(bf16)


def feed_second_body(place, *refs):
    blocks, outs = refs[:4], refs[4:]
    for step, out in enumerate(outs):
        offset = 0
        for begin, size in FEED_BLOCKS:
            span = size // len(outs)
            to = begin + (place[2] ^ step) * span
            out[offset : offset + span, :] = added(blocks, to, span).astype(bf16)
            offset += span


def total_body(place, *refs):
    refs[-1][...] = added(refs[:-1], 0, refs[-1].shape[0]).astype(bf16)


def beside_body(place, *refs):
    rows = refs[0].shape[0]
    for index, ref in enumerate(refs[:-1]):
        refs[-1][rows * index : rows * (index + 1), :] = ref[...]


def qkv_first_body(place, keep, got, to_y, to_x, to_both, kept):
    x = place[1]
    for target, other, side in ((to_y, 1, x), (to_x, 0, 1 - x), (to_both, 1, 1 - x), (kept, 0, x)):
        target[...] = added((keep, got), QKV_PACK * other + 192 * side, 192).astype(bf16)


def merge_first_body(place, keep, got, to_y, to_x, to_both, kept, sums_s):
    x = place[1]
    sums_s[...] = joined(keep[512:544, :]) + joined(got[512:544, :])
    for target, other, side in ((to_y, 1, x), (to_x, 0, 1 - x), (to_both, 1, 1 - x), (kept, 0, x)):
        target[0:128, :] = added((keep, got), MERGE_PACK * other + 128 * side, 128).astype(bf16)
        target[128:144, :] = split(sums_s[pl.ds(pl.multiple_of(8 * side, 8), 8), :])


def last_second_body(place, qkv_sum, *refs):
    blocks, outs = refs[:4], refs[4:]
    vectors = split(sum(joined(ref[128:144, :]) for ref in blocks))
    wide, narrow = 192 // len(outs), 128 // len(outs)
    for step, out in enumerate(outs):
        to = place[2] ^ step
        out[0:wide, :] = added((qkv_sum,), to * wide, wide).astype(bf16)
        out[wide : wide + narrow, :] = added(blocks, to * narrow, narrow).astype(bf16)
        out[wide + narrow :, :] = vectors


def merge_total_body(place, *refs):
    blocks, (out, vectors) = refs[:-2], refs[-2:]
    rows = out.shape[0]
    out[...] = added(blocks, 0, rows).astype(bf16)
    vectors[...] = split(sum(joined(ref[rows : rows + 16, :]) for ref in blocks))


def last_beside_body(place, vectors, *refs):
    rows = refs[0].shape[0]
    for index, ref in enumerate(refs[:-1]):
        refs[-1][rows * index : rows * (index + 1), :] = ref[...]
    refs[-1][rows * (len(refs) - 1) :, :] = vectors[...]


def in_order(place, near, far, stage, rows, along):
    piece = sum(rows) // 2 // along
    for side, ref in ((place[1], near), (1 - place[1], far)):
        for step in range(along):
            begin, offset = 0, piece * step
            for size in rows:
                span = size // 2 // along
                to = begin + side * (size // 2) + (place[2] ^ step) * span
                stage[pl.ds(pl.multiple_of(to, 16), span), :] = ref[offset : offset + span, :]
                begin += size
                offset += span


def feed_unpack_body(along, place, near, far, core_near, core_far, down_ref, up_ref, proj_ref, token_ref, stage):
    token_ref[...] = jnp.zeros_like(token_ref)
    for target, mine, beside in ((place[0], near, far), (1 - place[0], core_near, core_far)):
        in_order(place, mine, beside, stage, (512, PROJ_PACK, 512), along)
        wide = pl.ds(pl.multiple_of(512 * target, 512), 512)
        down_ref[wide, :] = stage[0:512, :].astype(f32)
        proj_ref[pl.ds(pl.multiple_of(128 * target, 128), 128), :] = stage[512:640, :].astype(f32)
        up_ref[:, wide] = stage[640:1152, :].astype(f32)


def feed_unpack(along, place, after, parts):
    return plain_call_after(
        partial(feed_unpack_body, along),
        [pltpu.HBM((FFN // 2, D), f32), pltpu.HBM((D, FFN // 2), f32), pltpu.HBM((D // 2, D), f32), shape_of((8, 128), f32)],
        place,
        after,
        parts,
        scratch=[pltpu.VMEM((FEED_PACK + PROJ_PACK, D), bf16)],
        room=14,
    )


def last_unpack_body(along, place, mine, beside, core_mine, core_beside, qkv_ref, merge_ref, *refs):
    vectors, stage, all_s = refs[:-2], refs[-2], refs[-1]
    rows = mine.shape[0] - 16
    for target, near, far in ((place[0], mine, beside), (1 - place[0], core_mine, core_beside)):
        in_order(place, near, far, stage, (QKV_PACK, MERGE_PACK), along)
        for side, ref in ((place[1], near), (1 - place[1], far)):
            all_s[pl.ds(pl.multiple_of(SUMS * target + 8 * side, 8), 8), :] = joined(ref[rows:, :])
        begin = pl.multiple_of(256 * target, 256)
        for part in range(2):
            qkv_ref[part, pl.ds(begin, 256), :] = stage[0:256, 256 * part : 256 * part + 256].astype(f32)
        qkv_ref[2, pl.ds(begin, 128), :] = stage[256:384, 0:256].astype(f32)
        qkv_ref[2, pl.ds(begin + 128, 128), :] = stage[256:384, 256:512].astype(f32)
        merge_ref[pl.ds(begin, 256), :] = stage[384:640, :].astype(f32)
    write_vectors(place[3], all_s, vectors)


VECTORS = [(1, D)] * 6 + [(2, D // 2), (1, FFN // 2), (1, MERGE_IN // 2), (1, MERGE_IN // 2), (HEADS // 2, SIDE * SIDE)]


def write_vectors(tp, sums, refs):
    for row in range(6):
        refs[row][...] = sums[row : row + 1, :]
    columns = pl.ds(pl.multiple_of(256 * tp, 256), 256)
    refs[6][...] = sums[6:8, columns]
    refs[7][:, 0:512] = sums[pl.ds(8 + 2 * tp, 1), :]
    refs[7][:, 512:1024] = sums[pl.ds(9 + 2 * tp, 1), :]
    refs[8][...] = sums[pl.ds(12 + tp, 1), :]
    refs[9][...] = sums[pl.ds(14 + tp, 1), :]
    refs[10][...] = sums[pl.ds(pl.multiple_of(16 + 8 * tp, 8), 8), 0 : SIDE * SIDE]


def last_unpack(along, place, *parts):
    outs = plain_call(
        partial(last_unpack_body, along),
        [pltpu.HBM(shape, f32) if shape[-2] >= 128 else shape_of(shape, f32) for shape in [(3, D, D // 2), (MERGE_IN // 2, D)] + VECTORS],
        (place, *parts),
        scratch=[pltpu.VMEM((QKV_PACK + MERGE_PACK, D), bf16), pltpu.VMEM((2 * SUMS, D), f32)],
    )
    return outs[0], outs[1], outs[2:]


def fetch_by_tp(ring, piece_of):
    near = ring.y(piece_of)
    return near, ring.core(near)


def plain_pieces(tp_size, weights, params):
    merge, qkv, proj, up, down = [
        lax.all_gather(array, "tp", axis=axis, tiled=True) for array, axis in zip(weights, (0, 2, 0, 1, 0))
    ]
    gain, bias, qv, up_bias, table = [
        lax.all_gather(array, "tp", axis=axis, tiled=True) for array, axis in zip(params, (0, 0, 1, 0, 1))
    ]

    def shard(array, axis, which):
        size = array.shape[axis] // 2
        return lax.slice_in_dim(array, which * size, (which + 1) * size, axis=axis)

    def rows_of(which):
        rows = jnp.zeros((PARAMS, D), f32)
        rows = rows.at[0].set(shard(gain.astype(f32), 0, which)).at[1].set(shard(bias.astype(f32), 0, which))
        rows = rows.at[2].set(shard(qv, 1, which).reshape(-1)).at[3:5].set(shard(up_bias, 0, which).reshape(2, D))
        return rows.at[8:16, : SIDE * SIDE].set(shard(table, 1, which).T)

    merge_other = shard(merge, 0, 1)
    qkv_other = shard(qkv, 2, 1).reshape(3 * D, 256)
    proj_other, up_other, down_other = shard(proj, 0, 1), shard(up, 1, 1), shard(down, 0, 1)

    def qkv_piece(half):
        rows = qkv_other[768 * half : 768 * half + 768]
        return jnp.concatenate(
            [jnp.concatenate([rows[:384], rows[384:]], axis=1), proj_other[128 * half : 128 * half + 128]], axis=0
        )

    def feed_piece(half):
        tile = slice(512 * half, 512 * half + 512)
        return jnp.concatenate([down_other[tile], up_other[:, tile]], axis=0)

    own = (
        shard(merge, 0, 0), shard(qkv, 2, 0).reshape(3 * D, 256), shard(proj, 0, 0), shard(up, 1, 0), shard(down, 0, 0)
    )
    return own, (rows_of(0), split(rows_of(1))), (merge_other[:256], merge_other[256:]), (qkv_piece(0), qkv_piece(1)), (feed_piece(0), feed_piece(1))


def sum_plainly(tp_size, feed_packs, proj_packs, qkv_packs, merge_packs):
    feed_packs, proj_packs, qkv_packs, merge_packs = lax.psum(
        (feed_packs, proj_packs, qkv_packs, merge_packs), ("rows", "tp")
    )
    own_send, own_keep, other_send, other_keep = feed_packs
    order = [own_keep, own_send, other_keep, other_send]
    down = jnp.concatenate([block[0:512] for block in order], axis=0)
    up = jnp.concatenate([block[512:1024] for block in order], axis=1)

    def blocks(packs, size):
        send, keep = packs
        return [keep[:size], send[:size], keep[size : 2 * size], send[size : 2 * size]]

    def qkv_rows(block):
        return jnp.stack(
            [block[0:256, 0:256], block[0:256, 256:512], jnp.concatenate([block[256:384, 0:256], block[256:384, 256:512]])]
        )

    order = blocks(qkv_packs, QKV_PACK)
    qkv = jnp.concatenate(
        [jnp.concatenate([qkv_rows(order[2 * shard + half]) for half in range(2)], axis=1) for shard in range(2)], axis=2
    )
    proj = jnp.concatenate(blocks(proj_packs, PROJ_PACK), axis=0)
    merge = jnp.concatenate(blocks(merge_packs, MERGE_PACK), axis=0)
    sums = jnp.concatenate([joined(merge_packs[1][2 * MERGE_PACK :]), joined(merge_packs[0][2 * MERGE_PACK :])], axis=0)
    index = lax.axis_index("tp")

    def own(array, axis):
        size = array.shape[axis] // tp_size
        return lax.dynamic_slice_in_dim(array, index * size, size, axis).astype(f32)

    vectors = [sums[row] for row in range(6)] + [
        own(sums[6:8], 1), own(sums[8:12].reshape(-1), 0), own(sums[12:14].reshape(-1), 0),
        own(sums[14:16].reshape(-1), 0), own(sums[16:32, : SIDE * SIDE], 0),
    ]
    return own(down, 0), own(up, 1), own(qkv, 2), own(proj, 0), own(merge, 0), vectors


def per_device(
    rows_size, tp_size,
    section_rows, window_mask, cotangent, merge_weight, merge_gain, merge_bias, norm1_gain, norm1_bias,
    qkv_weight, qv_bias, bias_table, proj_weight, proj_bias, norm2_gain, norm2_bias,
    up_weight, up_bias, down_weight, down_bias,
):
    fast = tp_size == 2 and rows_size in (8, 16)
    count = cotangent.shape[0]
    index, tp = lax.axis_index("rows"), lax.axis_index("tp")
    place = jnp.stack([index & 1, (index >> 1) & 1, index >> 2, tp]).astype(jnp.int32)
    ring = Ring(place, rows_size)
    if fast:
        flat_qkv = qkv_weight.reshape(3 * D, D // 2)
        merge_piece = pack_merge(place, merge_weight)
        merge_near = ring.y(merge_piece)
        params, piece = pack_params(
            place, merge_piece, merge_gain, merge_bias, qv_bias, up_bias[None], bias_table.T
        )
        others = ring.y(piece)
        mask, live = masks_of(place, params, window_mask, count)
        qkv_piece = gate(pack_qkv(place, (mask,), flat_qkv, proj_weight), others, merge_near)
        qkv_near = ring.y(qkv_piece)
        hat, inverse = section_norm(qkv_piece, section_rows)
        merge_far = ring.core(merge_near)
        kernel_place = place
    else:
        (merge_weight, flat_qkv, proj_weight, up_weight, down_weight), (params, others), merge_pair, qkv_pair, feed_pair = plain_pieces(
            tp_size,
            (merge_weight, qkv_weight, proj_weight, up_weight, down_weight),
            (merge_gain, merge_bias, qv_bias, up_bias, bias_table),
        )
        (merge_near, merge_far), (qkv_near, qkv_far), (feed_near_piece, feed_far_piece) = merge_pair, qkv_pair, feed_pair
        kernel_place = jnp.zeros_like(place)
        hat, inverse = section_norm(params, section_rows)
        own_mask = lax.dynamic_slice_in_dim(window_mask, tp * count, count, 0)
        mask, live = masks_of(kernel_place, params, own_mask, count)

    merged, first, first_copy, merge_full, params, column = merge_rows(
        kernel_place, hat, merge_weight, merge_near, merge_far, params, others, norm1_gain[None], norm1_bias[None]
    )
    position, hat = expand(params, hat)
    if fast:
        (feed_piece,) = plain_call_after(
            pack_feed_body, [shape_of((FEED_PACK, D), bf16)], place, (position, qkv_near), (up_weight, down_weight)
        )
        qkv_far = ring.core(qkv_near)
        feed_near_piece = ring.y(feed_piece)
        feed_far_piece = ring.core(feed_near_piece)
    qkv_rows, weights, attended, padded, inverse_sums, qkv_full = attend(
        kernel_place, first, flat_qkv, qkv_near, qkv_far, params, position, mask
    )
    rows = [row[None] for row in (proj_bias, norm2_gain, norm2_bias, down_bias)]
    second_hat, second_inverse, total, back, second, turned, branch, own_send, feed_sums, proj_full = feed_own(
        kernel_place, attended, merged, cotangent, live, *rows, params, proj_weight, qkv_near, qkv_far,
        up_weight, down_weight,
    )
    total, back, own_keep, feed_sums = feed_middle(
        True, kernel_place, second, turned, branch, total, back, params, feed_sums, (up_weight, down_weight), LONG
    )
    total, back, other_send, feed_sums = feed_middle(
        False, kernel_place, second, turned, branch, total, back, params, feed_sums, (feed_far_piece,)
    )
    block_out, grad_residual, attn, other_keep, proj_send, proj_keep, feed_sums = feed_near(
        kernel_place, second_hat, second_inverse, second, turned, branch, total, back, rows[1], params, feed_sums, feed_near_piece,
        attended,
    )
    after = feed_sums
    if fast:
        own_got, other_got, proj_got = ring.core(own_send), ring.core(other_send), ring.core(proj_send)
        feed_keeps = (own_keep, own_got, other_keep, other_got, proj_keep, proj_got)
        to_y, to_x, to_both, feed_kept = stage(feed_first_body, place, feed_sums, (576,) * 4, *feed_keeps)
        feed_from = (ring.y(to_y), ring.x(to_x), ring.xy(to_both))
        after = to_y
    stack, low, sums, vectors, position_grad, first_near = attend_back(
        after, attn, qkv_rows, weights, padded, inverse_sums, proj_full, merged, grad_residual, qkv_full,
        norm1_gain[None], first_copy,
    )
    qkv_send, qkv_keep, hat_near = qkv_back(kernel_place, sums, first_near, stack, hat)
    after = sums
    if fast:
        along = ring.along
        qkv_got = ring.core(qkv_send)
        span = 576 // along
        feed_parts = stage(
            feed_second_body, place, qkv_send, (span,) * along, feed_kept, *feed_from, cost=LONG
        )
        feed_got = [ring.z(feed_parts[step], step) for step in range(1, along)]
        to_y, to_x, to_both, qkv_kept = stage(
            qkv_first_body, place, feed_parts[0], (192,) * 4, qkv_keep, qkv_got
        )
        qkv_from = (ring.y(to_y), ring.x(to_x), ring.xy(to_both))
        after = to_y
    merge_send, merge_keep = merge_back(
        kernel_place, after, low, hat_near, merge_full, params, column, feed_sums, sums, vectors, position_grad
    )
    if fast:
        merge_got = ring.core(merge_send)
        (feed_total,) = stage(total_body, place, merge_send, (span,), feed_parts[0], *feed_got, cost=LONG)
        feed_all = [feed_total] + [ring.z(feed_total, step) for step in range(1, along)]
        (qkv_sum,) = stage(total_body, place, feed_total, (192,), qkv_kept, *qkv_from)
        to_y, to_x, to_both, merge_kept = stage(
            merge_first_body, place, qkv_sum, (144,) * 4, merge_keep, merge_got, scratch=[pltpu.VMEM((SUMS, D), f32)]
        )
        (feed_mine,) = stage(beside_body, place, to_y, (span * along,), *feed_all)
        feed_beside = ring.x(feed_mine)
        last_span = 320 // along
        last_parts = stage(
            last_second_body, place, feed_mine, (last_span + 16,) * along, qkv_sum,
            merge_kept, ring.y(to_y), ring.x(to_x), ring.xy(to_both),
        )
        last_got = [ring.z(last_parts[step], step) for step in range(1, along)]
        last_total, vectors = stage(
            merge_total_body, place, last_parts[0], (last_span, 16), *([last_parts[0]] + last_got), cost=LONG
        )
        last_all = [last_total] + [ring.z(last_total, step) for step in range(1, along)]
        section_grad, token = section_back(last_total, low, hat, inverse, merge_full, params)
        (last_near,) = stage(
            last_beside_body, place, (token, feed_beside), (336,), vectors, *last_all, cost=LONG
        )
        last_far = ring.x(last_near)
        feed_cores = ring.core(feed_mine), ring.core(feed_beside)
        down_grad, up_grad, proj_grad, token = feed_unpack(
            along, place, last_near, (feed_mine, feed_beside, *feed_cores)
        )
        (last_far,) = stage(beside_body, place, token, (336,), last_far)
        qkv_grad, merge_grad, vectors = last_unpack(
            along, place, last_near, last_far, ring.core(last_near), ring.core(last_far)
        )
    else:
        section_grad, _ = section_back(low, low, hat, inverse, merge_full, params)
        down_grad, up_grad, qkv_grad, proj_grad, merge_grad, vectors = sum_plainly(
            tp_size, (own_send, own_keep, other_send, other_keep), (proj_send, proj_keep), (qkv_send, qkv_keep),
            (merge_send, merge_keep),
        )
    norm1_gain_grad, norm1_bias_grad, proj_bias_grad, norm2_gain_grad, norm2_bias_grad, down_bias_grad = [
        row.reshape(D) for row in vectors[0:6]
    ]
    qv_grad, up_bias_grad, gain_grad, bias_grad, table_grad = vectors[6:]
    return (
        block_out, section_grad, merge_grad, gain_grad.reshape(-1), bias_grad.reshape(-1),
        norm1_gain_grad, norm1_bias_grad, qkv_grad, qv_grad, table_grad.T, proj_grad, proj_bias_grad,
        norm2_gain_grad, norm2_bias_grad, up_grad, up_bias_grad.reshape(-1), down_grad, down_bias_grad,
    )


def solution(mesh):
    rows_size, tp_size = mesh.shape["rows"], mesh.shape["tp"]
    both = ("rows", "tp")
    return jax.shard_map(
        partial(per_device, rows_size, tp_size),
        mesh=mesh,
        in_specs=(
            P(both, None), P("rows"), P(both, None), P("tp", None), P("tp"), P("tp"), P(), P(),
            P(None, None, "tp"), P(None, "tp"), P(None, "tp"), P("tp", None), P(), P(), P(),
            P(None, "tp"), P("tp"), P("tp", None), P(),
        ),
        out_specs=(
            P(both, None), P(both, None), P("tp", None), P("tp"), P("tp"), P(), P(),
            P(None, None, "tp"), P(None, "tp"), P(None, "tp"), P("tp", None), P(), P(), P(),
            P(None, "tp"), P("tp"), P("tp", None), P(),
        ),
        check_vma=False,
    )
```

```python
from functools import partial
import math

import jax
import jax.numpy as jnp
from jax import lax
from jax.experimental import pallas as pl
from jax.experimental.pallas import tpu as pltpu
from jax.sharding import PartitionSpec as P

MERGE_IN = 1024
D = 512
HEADS = 16
HEAD_DIM = 32
FFN = 2048
WINDOW = 10
AREA = WINDOW * WINDOW
SIDE = 2 * WINDOW - 1
EPSILON = 1e-05
MASKED_SCORE = -1e30
EXACT = lax.Precision.HIGHEST
SCALING = 1.0 / math.sqrt(HEAD_DIM)
GROUP = 4
ROWS = GROUP * AREA
KEYS = 112
QUERIES = 128
QUADS = 4
QUAD = 4 * HEAD_DIM
LANES = 4 * QUERIES

bf16 = jnp.bfloat16
f32 = jnp.float32


def mm(a, b):
    return jnp.dot(a, b, preferred_element_type=f32)


def mm_t(a, b):
    return lax.dot_general(a, b, (((1,), (1,)), ((), ())), preferred_element_type=f32)


def t_mm(a, b):
    return lax.dot_general(a, b, (((0,), (0,)), ((), ())), preferred_element_type=f32)


def normalize(values):
    center = jnp.mean(values, axis=-1, keepdims=True)
    spread = jnp.mean(values * values, axis=-1, keepdims=True) - center * center
    inverse = lax.rsqrt(spread + EPSILON)
    return (values - center) * inverse, inverse


def norm_back(grad_hat, normed, inverse):
    first_mean = jnp.mean(grad_hat, axis=-1, keepdims=True)
    second_mean = jnp.mean(grad_hat * normed, axis=-1, keepdims=True)
    return inverse * (grad_hat - first_mean - normed * second_mean)


def column_sum(values):
    return jnp.sum(values, axis=0, keepdims=True)


def head_masks():
    lane = lax.broadcasted_iota(jnp.int32, (1, QUAD), 1) // HEAD_DIM
    return [(lane == head).astype(f32).astype(bf16) for head in range(4)]


def spread_heads(rows, masks):
    return jnp.concatenate([rows * mask for mask in masks], axis=0)


def kernel_call(body, grid, in_specs, out_specs, out_shape, scratch=(), flops=0, moved=0, room=32, cost=None):
    return pl.pallas_call(
        body,
        grid=grid,
        in_specs=in_specs,
        out_specs=out_specs,
        out_shape=out_shape,
        scratch_shapes=list(scratch),
        compiler_params=pltpu.CompilerParams(
            dimension_semantics=("arbitrary",) * len(grid), vmem_limit_bytes=room * 1024 * 1024
        ),
        cost_estimate=cost or COST,
    )


def whole(shape):
    return pl.BlockSpec(shape, lambda *_: (0,) * len(shape), pipeline_mode=pl.Buffered(1))


def by_rows(rows, columns):
    return pl.BlockSpec((rows, columns), lambda i: (i, 0))


def by_windows(shape):
    return pl.BlockSpec((GROUP,) + shape, lambda i: (i,) + (0,) * len(shape))


SCALARS = pl.BlockSpec(memory_space=pltpu.SMEM)
RESIDENT = pl.BlockSpec(memory_space=pltpu.VMEM)
ANYWHERE = pl.BlockSpec(memory_space=pl.ANY)


def in_hbm(array):
    return pltpu.with_memory_space_constraint(array, pltpu.HBM)


FEED_PACK = 1024
QKV_PACK = 384
PROJ_PACK = 128
MERGE_PACK = 256
STAGE_ROOM = 9
COST = pl.CostEstimate(flops=1, bytes_accessed=1, transcendentals=0)
LONG = pl.CostEstimate(flops=10**12, bytes_accessed=1, transcendentals=0)
SUMS = 16
PARAMS = 16


def shape_of(shape, dtype):
    return jax.ShapeDtypeStruct(shape, dtype)


def split(rows):
    high = rows.astype(bf16).astype(f32)
    return jnp.concatenate([high, rows - high], axis=0).astype(bf16)


def joined(pair):
    half = pair.shape[0] // 2
    return pair[:half].astype(f32) + pair[half:].astype(f32)


def both_shards(tp, mine, other, axis):
    return jnp.where(
        tp == 0, jnp.concatenate([mine, other], axis=axis), jnp.concatenate([other, mine], axis=axis)
    )


def pack_merge_body(place, merge_ref, out_ref, sem):
    half = pl.ds(pl.multiple_of(256 * place[0], 256), 256)
    copy = pltpu.make_async_copy(merge_ref.at[half, :], out_ref, sem)
    copy.start()
    copy.wait()


def pack_merge(place, merge):
    return pl.pallas_call(
        pack_merge_body,
        in_specs=[SCALARS, ANYWHERE],
        out_specs=RESIDENT,
        out_shape=pltpu.VMEM((256, D), bf16),
        scratch_shapes=[pltpu.SemaphoreType.DMA],
        compiler_params=pltpu.CompilerParams(vmem_limit_bytes=4 * 1024 * 1024),
        cost_estimate=COST,
    )(place, in_hbm(merge))


def pack_params_body(
    place, after, gain_ref, bias_ref, qv_ref, up_bias_ref, table_ref,
    params_ref, out_ref, gain_s, bias_s, qv_s, up_bias_s, table_s, sems,
):
    pairs = (
        (gain_ref, gain_s), (bias_ref, bias_s), (qv_ref, qv_s), (up_bias_ref, up_bias_s), (table_ref, table_s)
    )
    copies = [pltpu.make_async_copy(source, target, sems.at[index]) for index, (source, target) in enumerate(pairs)]
    for copy in copies:
        copy.start()
    params_ref[...] = jnp.zeros_like(params_ref)
    for copy in copies:
        copy.wait()
    params_ref[0:1, :] = gain_s[...].astype(f32).reshape(1, D)
    params_ref[1:2, :] = bias_s[...].astype(f32).reshape(1, D)
    params_ref[2:3, 0:256] = qv_s[0:1, :]
    params_ref[2:3, 256:512] = qv_s[1:2, :]
    params_ref[3:4, :] = up_bias_s[:, 0:512]
    params_ref[4:5, :] = up_bias_s[:, 512:1024]
    params_ref[8:16, 0 : SIDE * SIDE] = table_s[...]
    out_ref[...] = split(params_ref[...])


def pack_params(place, after, *operands):
    operands = [in_hbm(array) for array in operands]
    return pl.pallas_call(
        pack_params_body,
        in_specs=[SCALARS] + [ANYWHERE] * 6,
        out_specs=[RESIDENT] * 2,
        out_shape=[pltpu.VMEM((PARAMS, D), f32), pltpu.VMEM((2 * PARAMS, D), bf16)],
        scratch_shapes=[pltpu.VMEM(array.shape, array.dtype) for array in operands] + [pltpu.SemaphoreType.DMA((5,))],
        compiler_params=pltpu.CompilerParams(vmem_limit_bytes=4 * 1024 * 1024),
        cost_estimate=COST,
    )(place, after, *operands)


def plain_call(body, outs, operands, room=16, scratch=(), flops=0):
    return pl.pallas_call(
        body,
        in_specs=[SCALARS] + [pl.BlockSpec(memory_space=pltpu.VMEM)] * (len(operands) - 1),
        out_specs=[pl.BlockSpec(memory_space=pltpu.VMEM)] * len(outs),
        out_shape=outs,
        scratch_shapes=list(scratch),
        compiler_params=pltpu.CompilerParams(vmem_limit_bytes=room * 1024 * 1024),
        cost_estimate=COST,
    )(*operands)


def pack_qkv_body(place, qkv_ref, proj_ref, *refs):
    out, qkv_s, proj_s, sems = refs[-4:]
    core = place[0]
    copies = [
        pltpu.make_async_copy(qkv_ref.at[pl.ds(pl.multiple_of(768 * core, 256), 768), :], qkv_s, sems.at[0]),
        pltpu.make_async_copy(proj_ref.at[pl.ds(pl.multiple_of(128 * core, 128), 128), :], proj_s, sems.at[1]),
    ]
    for copy in copies:
        copy.start()
    for copy in copies:
        copy.wait()
    for side in range(2):
        out[0:384, 256 * side : 256 * side + 256] = qkv_s[384 * side : 384 * side + 384, :]
    out[384:512, :] = proj_s[...]


def pack_qkv(place, after, qkv, proj):
    return pl.pallas_call(
        pack_qkv_body,
        in_specs=[SCALARS] + [ANYWHERE] * (2 + len(after)),
        out_specs=RESIDENT,
        out_shape=pltpu.VMEM((QKV_PACK + PROJ_PACK, D), bf16),
        scratch_shapes=[
            pltpu.VMEM((768, 256), bf16), pltpu.VMEM((128, D), bf16), pltpu.SemaphoreType.DMA((2,)),
        ],
        compiler_params=pltpu.CompilerParams(vmem_limit_bytes=4 * 1024 * 1024),
        cost_estimate=COST,
    )(place, in_hbm(qkv), in_hbm(proj), *after)


def pack_feed_body(place, up_ref, down_ref, out):
    half = pl.ds(pl.multiple_of(512 * place[0], 512), 512)
    out[0:512, :] = down_ref[half, :]
    out[512:1024, :] = up_ref[:, half]


def plain_call_after(body, outs, place, after, operands, room=16, scratch=(), flops=0, cost=COST):
    after = after if isinstance(after, tuple) else (after,)

    def without_after(place, *refs):
        return body(place, *refs[len(after) :])

    return pl.pallas_call(
        without_after,
        in_specs=[SCALARS] + [pl.BlockSpec(memory_space=pl.ANY)] * len(after) + [pl.BlockSpec(memory_space=pltpu.VMEM)] * len(operands),
        out_specs=[pl.BlockSpec(memory_space=pltpu.VMEM)] * len(outs),
        out_shape=outs,
        scratch_shapes=list(scratch),
        compiler_params=pltpu.CompilerParams(vmem_limit_bytes=room * 1024 * 1024),
        cost_estimate=cost,
    )(place, *after, *operands)


def nothing(array_ref, *refs):
    pass


def gate(array, *after):
    return pl.pallas_call(
        nothing,
        in_specs=[RESIDENT] + [ANYWHERE] * len(after),
        out_specs=RESIDENT,
        out_shape=pltpu.VMEM(array.shape, array.dtype),
        input_output_aliases={0: 0},
        compiler_params=pltpu.CompilerParams(vmem_limit_bytes=4 * 1024 * 1024),
        cost_estimate=COST,
    )(array, *after)


def masks_body(place, window_in, mask_ref, live_ref, stage, window_s, sem):
    copy = pltpu.make_async_copy(window_in, window_s, sem)
    copy.start()
    copy.wait()
    window_ref = window_s[...].reshape(1, window_s.shape[0])
    windows = mask_ref.shape[0]
    shards = window_ref.shape[1] // (windows * AREA)
    stage[...] = jnp.zeros_like(stage)
    for window in range(windows):
        patch = window_ref[:, AREA * window : AREA * (window + 1)]
        for shard in range(1, shards):
            begin = AREA * (windows * shard + window)
            patch = jnp.where(place[3] == shard, window_ref[:, begin : begin + AREA], patch)
        stage[window : window + 1, 0:AREA] = patch
    patches = jnp.minimum(stage[...], 1).astype(f32)
    live = jnp.max(patches, axis=1, keepdims=True)
    inside = lax.broadcasted_iota(jnp.int32, (windows, QUERIES), 1) < AREA
    keep = jnp.logical_and(jnp.maximum(patches, 1.0 - live) > 0.5, inside)
    added = jnp.where(keep, 0.0, MASKED_SCORE)
    for window in range(windows):
        mask_ref[window] = added[window : window + 1, :]
        live_ref[window] = jnp.broadcast_to(live[window : window + 1, :], (1, QUERIES))


def masks_of(place, after, window_mask, count):
    windows = count // AREA
    return pl.pallas_call(
        lambda place, after, *refs: masks_body(place, *refs),
        in_specs=[SCALARS, ANYWHERE, ANYWHERE],
        out_specs=[RESIDENT] * 2,
        out_shape=[pltpu.VMEM((windows, 1, QUERIES), f32)] * 2,
        scratch_shapes=[
            pltpu.VMEM((windows, QUERIES), jnp.int32), pltpu.VMEM(window_mask.shape, jnp.int32), pltpu.SemaphoreType.DMA,
        ],
        compiler_params=pltpu.CompilerParams(vmem_limit_bytes=4 * 1024 * 1024),
        cost_estimate=COST,
    )(place, after, in_hbm(window_mask))


def section_norm_body(after, rows_ref, hat_ref, inverse_ref, rows_s, sems):
    steps = rows_s.shape[0] // ROWS
    copies = []
    for step in range(steps):
        here = slice(ROWS * step, ROWS * (step + 1))
        copies.append(pltpu.make_async_copy(rows_ref.at[here, :], rows_s.at[here, :], sems.at[step]))
        copies[step].start()
    for step in range(steps):
        here = slice(ROWS * step, ROWS * (step + 1))
        copies[step].wait()
        hat, inverse = normalize(rows_s[here, :].astype(f32))
        hat_ref[here, :] = hat.astype(bf16)
        inverse_ref[here, :] = inverse


def section_norm(after, rows):
    count = rows.shape[0]
    return kernel_call(
        section_norm_body,
        (1,),
        [ANYWHERE, ANYWHERE],
        [RESIDENT, RESIDENT],
        [pltpu.VMEM((count, MERGE_IN), bf16), shape_of((count, 1), f32)],
        [pltpu.VMEM((count, MERGE_IN), bf16), pltpu.SemaphoreType.DMA((count // ROWS,))],
        room=16,
    )(after, in_hbm(rows))


def gain_rows(tp, params, others):
    return both_shards(tp, params[0:1], others[0:1], 1), both_shards(tp, params[1:2], others[1:2], 1)


def merge_body(
    place, hat_ref, own_ref, near_ref, far_ref, params_ref, others_ref, norm_gain, norm_bias,
    merged_ref, first_ref, first_copy, merge_ref, params_out_ref, column_ref,
    merge_s, shift_s, gain_s,
):

    @pl.when(pl.program_id(0) == 0)
    def _():
        core, tp = place[0], place[3]
        merge_s[pl.ds(pl.multiple_of(512 * tp, 512), 512), :] = own_ref[...]
        other = 512 * (1 - tp)
        merge_s[pl.ds(pl.multiple_of(other + 256 * core, 256), 256), :] = near_ref[...]
        merge_s[pl.ds(pl.multiple_of(other + 256 * (1 - core), 256), 256), :] = far_ref[...]
        merge_ref[...] = merge_s[...]
        params = params_ref[...]
        others = joined(others_ref[...])
        gain, bias = gain_rows(tp, params, others)
        gain_s[...] = gain.astype(bf16)
        shift_s[...] = mm(jnp.broadcast_to(bias, (16, MERGE_IN)).astype(bf16), merge_s[...])[0:1]
        params_out_ref[0:1, 0:1024] = gain
        params_out_ref[0:1, 1024:2048] = bias
        params_out_ref[1:2, 0:512] = both_shards(tp, params[2:3, 0:256], others[2:3, 0:256], 1)
        params_out_ref[1:2, 512:1024] = both_shards(tp, params[2:3, 256:512], others[2:3, 256:512], 1)
        params_out_ref[1:2, 1024:2048] = jnp.zeros((1, 1024), f32)
        params_out_ref[2:3, :] = both_shards(
            tp,
            jnp.concatenate([params[3:4], params[4:5]], axis=1),
            jnp.concatenate([others[3:4], others[4:5]], axis=1),
            1,
        )
        params_out_ref[3:8, :] = jnp.zeros((5, 2048), f32)
        params_out_ref[8:24, 0:512] = both_shards(tp, params[8:16], others[8:16], 0)
        params_out_ref[8:24, 512:2048] = jnp.zeros((16, 1536), f32)
        column_ref[...] = jnp.broadcast_to(gain, (128, MERGE_IN)).T

    here = pl.ds(pl.multiple_of(pl.program_id(0) * ROWS, 16), ROWS)
    merged = mm(hat_ref[here, :] * gain_s[...], merge_s[...]) + shift_s[...]
    merged_ref[...] = merged
    hat, _ = normalize(merged)
    first = (hat * norm_gain[...] + norm_bias[...]).astype(bf16)
    first_ref[here, :] = first
    first_copy[...] = first


def merge_rows(place, hat, own, near, far, params, others, gain, bias):
    count = hat.shape[0]
    return kernel_call(
        merge_body,
        (count // ROWS,),
        [
            SCALARS, RESIDENT, RESIDENT, RESIDENT, RESIDENT, RESIDENT, RESIDENT, RESIDENT, RESIDENT,
        ],
        [
            by_rows(ROWS, D), RESIDENT, by_rows(ROWS, D), whole((MERGE_IN, D)), RESIDENT,
            whole((MERGE_IN, 128)),
        ],
        [
            pltpu.HBM((count, D), f32), pltpu.VMEM((count, D), bf16), pltpu.HBM((count, D), bf16),
            pltpu.HBM((MERGE_IN, D), bf16),
            shape_of((24, 2048), f32), pltpu.HBM((MERGE_IN, 128), f32),
        ],
        [
            pltpu.VMEM((MERGE_IN, D), bf16), pltpu.VMEM((1, D), f32), pltpu.VMEM((1, MERGE_IN), bf16),
        ],
        flops=2 * count * D * MERGE_IN,
        moved=count * 10 * D + 4 * D * MERGE_IN,
        room=14,
    )(place, hat, own, near, far, params, others, gain, bias)


def value_blocks(values, masks):
    return [jnp.concatenate([values * mask, jnp.broadcast_to(mask, (QUERIES, QUAD))], axis=1) for mask in masks]


def turned_products(turned, scores):
    parts = []
    for pair in range(2):
        both = mm(turned[64 * pair : 64 * pair + 64], scores[:, 256 * pair : 256 * pair + 256])
        parts += [both[0:32, 0:128], both[32:64, 128:256]]
    return jnp.concatenate(parts, axis=0).T


def attend_body(
    place, first_ref, own_ref, near_ref, far_ref, params_ref, position_ref, mask_ref,
    qkv_out_ref, weights_ref, attended_ref, padded_ref, inverse_ref, qkv_ref,
    stage, mixed,
):
    @pl.when(pl.program_id(0) == 0)
    def _():
        core, tp = place[0], place[3]
        other = pl.ds(pl.multiple_of(256 * (1 - tp), 256), 256)
        qkv_ref[:, pl.ds(pl.multiple_of(256 * tp, 256), 256)] = own_ref[...]
        for ref, half in ((near_ref, core), (far_ref, 1 - core)):
            for side in range(2):
                rows = pl.ds(pl.multiple_of(768 * half + 384 * side, 128), 384)
                qkv_ref[rows, other] = ref[0:384, 256 * side : 256 * side + 256]

    here = pl.ds(pl.multiple_of(pl.program_id(0) * ROWS, 16), ROWS)
    stage[pl.ds(0, ROWS), :] = first_ref[here, :].astype(f32)
    stage[pl.ds(ROWS, 32), :] = jnp.zeros((32, D), f32)
    padded = jnp.concatenate(
        [stage[pl.ds(AREA * w, QUERIES), :].astype(bf16) for w in range(GROUP)], axis=0
    )
    queries = (SCALING * (mm(padded, qkv_ref[0:512, :]) + params_ref[1:2, 0:512])).astype(bf16)
    keys = mm(padded, qkv_ref[512:1024, :]).astype(bf16)
    values = (mm(padded, qkv_ref[1024:1536, :]) + params_ref[1:2, 512:1024]).astype(bf16)
    for w in range(GROUP):
        block = slice(QUERIES * w, QUERIES * (w + 1))
        qkv_out_ref[w, :, 0:D] = queries[block]
        qkv_out_ref[w, :, D : 2 * D] = keys[block]
        qkv_out_ref[w, :, 2 * D :] = values[block]
    masks = head_masks()
    for w in range(GROUP):
        mask = mask_ref[w]
        for quad in range(QUADS):
            columns = slice(QUAD * quad, QUAD * (quad + 1))
            rows = QUERIES * w
            spread = spread_heads(keys[rows : rows + QUERIES, columns], masks)
            scores = mm_t(queries[rows : rows + KEYS, columns], spread)
            raised = []
            for head in range(4):
                lanes = slice(QUERIES * head, QUERIES * (head + 1))
                part = scores[:, lanes] + position_ref[quad, :, lanes] + mask
                raised.append(jnp.exp(part - jnp.max(part, axis=1, keepdims=True)).astype(bf16))
            weights = jnp.concatenate(raised, axis=1)
            weights_ref[w, quad] = weights
            blocks = value_blocks(values[rows : rows + QUERIES, columns], masks)
            out = mm(weights, jnp.concatenate(blocks, axis=0))
            inverse = 1.0 / out[:, QUAD:]
            both = out[:, :QUAD] * inverse
            inverse_ref[w, :, columns] = inverse.astype(bf16)
            padded_ref[w, :, columns] = both.astype(bf16)
            mixed[pl.ds(AREA * w, AREA), columns] = both[0:AREA]
    attended_ref[...] = mixed[pl.ds(0, ROWS), :].astype(bf16)


def attend(place, first, own, near, far, params, position, mask):
    count = first.shape[0]
    windows = count // AREA
    return kernel_call(
        attend_body,
        (count // ROWS,),
        [
            SCALARS, RESIDENT, RESIDENT, RESIDENT, RESIDENT, RESIDENT, RESIDENT, by_windows((1, QUERIES)),
        ],
        [
            by_windows((QUERIES, 3 * D)), by_windows((QUADS, KEYS, LANES)), by_rows(ROWS, D),
            by_windows((KEYS, D)), by_windows((KEYS, D)), RESIDENT,
        ],
        [
            pltpu.HBM((windows, QUERIES, 3 * D), bf16), pltpu.HBM((windows, QUADS, KEYS, LANES), bf16),
            pltpu.HBM((count, D), bf16), pltpu.HBM((windows, KEYS, D), bf16), pltpu.HBM((windows, KEYS, D), bf16),
            shape_of((3 * D, D), bf16),
        ],
        [pltpu.VMEM((ROWS + 32, D), f32), pltpu.VMEM((ROWS + 8, D), f32)],
        flops=2 * count * D * (3 * D + 4 * AREA),
        moved=count * 10 * D + windows * QUADS * KEYS * LANES * 2,
        room=20,
    )(place, first, own, near, far, params, position, mask)


def gelu_parts(t):
    chance = 0.5 * lax.erf(t * math.sqrt(0.5)) + 0.5
    density = jnp.exp(t * t * -0.5) * (1.0 / math.sqrt(2.0 * math.pi))
    return t * chance, chance + t * density


TILE = 512
FEED_ROWS = 400
OWN_ROOM = 18
OTHER_ROOM = 12
AB_ROOM = 18
NEAR_ROOM = 20


def feed_tile(up, down, bias, second_ref, turned_ref, branch_ref, total_s, back_s, active_s, raise_s, target, first):
    sums = jnp.zeros((1, TILE), f32)

    def add_products(here, active, grad_raised):
        total_s[here, :] += mm(active, down)
        back = mm_t(grad_raised, up)
        if first:
            back_s[here, :] = back
        else:
            back_s[here, :] += back

    last = None
    for begin in range(0, second_ref.shape[0], FEED_ROWS):
        here = slice(begin, begin + FEED_ROWS)
        value, slope = gelu_parts(mm(second_ref[here, :], up) + bias)
        active = value.astype(bf16)
        grad_raised = (mm_t(branch_ref[here, :], down) * slope).astype(bf16)
        active_s[here, :] = active
        raise_s[here, :] = grad_raised
        sums += column_sum(grad_raised.astype(f32))
        if last is not None:
            add_products(*last)
        last = here, active, grad_raised
    add_products(*last)
    target[0:512, :] = t_mm(active_s[...], branch_ref[...]).astype(bf16)
    target[512:1024, :] = mm(turned_ref[...], raise_s[...]).astype(bf16)
    return sums


def feed_own_body(
    place, attended_ref, merged_ref, cotangent_ref, live_ref, proj_bias, norm_gain, norm_bias, down_bias, params_ref,
    proj_own, near_ref, far_ref, up_own, down_own,
    hat_ref, inverse_ref, total_ref, back_ref, second_ref, turned_ref, branch_ref, send_ref, sums_ref, proj_ref,
    active_s, raise_s,
):
    step = pl.program_id(0)
    blocks = pl.num_programs(0) - 1
    core, tp = place[0], place[3]

    @pl.when(step == 0)
    def _():
        proj_ref[pl.ds(pl.multiple_of(256 * tp, 256), 256), :] = proj_own[...]
        for ref, which in ((near_ref, core), (far_ref, 1 - core)):
            proj_ref[pl.ds(pl.multiple_of(256 * (1 - tp) + 128 * which, 128), 128), :] = ref[384:512, :]
        sums_ref[...] = jnp.zeros_like(sums_ref)

    @pl.when(step < blocks)
    def _():
        here = pl.ds(pl.multiple_of(step * ROWS, 16), ROWS)
        residual = merged_ref[...] + mm(attended_ref[...], proj_ref[...]) + proj_bias[...]
        total_ref[here, :] = residual + down_bias[...]
        hat, inverse = normalize(residual)
        hat_ref[here, :] = hat
        inverse_ref[here, :] = inverse
        second_ref[here, :] = (hat * norm_gain[...] + norm_bias[...]).astype(bf16)
        row = lax.broadcasted_iota(jnp.int32, (ROWS, 1), 0)
        live = live_ref[GROUP - 1, :, 0:1]
        for window in range(GROUP - 2, -1, -1):
            live = jnp.where(row < AREA * (window + 1), live_ref[window, :, 0:1], live)
        branch = cotangent_ref[...].astype(f32) * live
        branch_ref[here, :] = branch.astype(bf16)
        sums_ref[7:8, :] += column_sum(branch)

    @pl.when(step == blocks)
    def _():
        turned_ref[...] = second_ref[...].T
        shard = 2 * tp + 1 - core
        units = pl.ds(pl.multiple_of(TILE * (1 - core), TILE), TILE)
        bias = params_ref[2:3, pl.ds(pl.multiple_of(TILE * shard, TILE), TILE)]
        sums_ref[pl.ds(shard, 1), :] = feed_tile(
            up_own[:, units], down_own[units, :], bias, second_ref, turned_ref, branch_ref, total_ref, back_ref,
            active_s, raise_s, send_ref, True,
        )


def feed_own(
    place, attended, merged, cotangent, live, proj_bias, gain, bias, down_bias, params, proj, near, far, up, down
):
    count = attended.shape[0]
    blocks = count // ROWS

    def taken(columns):
        return pl.BlockSpec((ROWS, columns), lambda i: (jnp.minimum(i, blocks - 1), 0))

    return kernel_call(
        feed_own_body,
        (blocks + 1,),
        [
            SCALARS, taken(D), taken(D), taken(D),
            pl.BlockSpec((GROUP, 1, QUERIES), lambda i: (jnp.minimum(i, blocks - 1), 0, 0)), RESIDENT, RESIDENT, RESIDENT, RESIDENT, RESIDENT, RESIDENT, RESIDENT, RESIDENT,
            RESIDENT, RESIDENT,
        ],
        [RESIDENT] * 10,
        [pltpu.VMEM((count, D), f32), pltpu.VMEM((count, 1), f32)] + [pltpu.VMEM((count, D), f32)] * 2
        + [pltpu.VMEM((count, D), bf16), pltpu.VMEM((D, count), bf16), pltpu.VMEM((count, D), bf16)]
        + [pltpu.VMEM((FEED_PACK, D), bf16), shape_of((8, D), f32), shape_of((D, D), bf16)],
        [pltpu.VMEM((count, TILE), bf16)] * 2,
        room=OWN_ROOM,
    )(
        place, in_hbm(attended), in_hbm(merged), in_hbm(cotangent), live, proj_bias, gain, bias, down_bias, params, proj,
        near, far, up, down,
    )


def feed_middle_body(
    own, place, second_ref, turned_ref, branch_ref, total_in, back_in, params_ref, sums_in, *refs
):
    weights, (total_ref, back_ref, target_ref, sums_ref, active_s, raise_s) = refs[:-6], refs[-6:]
    core, tp = place[0], place[3]
    sums_ref[...] = sums_in[...]
    if own:
        shard = 2 * tp + core
        units = pl.ds(pl.multiple_of(TILE * core, TILE), TILE)
        up, down = weights[0][:, units], weights[1][units, :]
    else:
        shard = 2 * (1 - tp) + 1 - core
        up, down = weights[0][512:1024, :], weights[0][0:512, :]
    bias = params_ref[2:3, pl.ds(pl.multiple_of(TILE * shard, TILE), TILE)]
    sums_ref[pl.ds(shard, 1), :] = feed_tile(
        up, down, bias, second_ref, turned_ref, branch_ref, total_ref, back_ref, active_s, raise_s, target_ref, False
    )


def feed_middle(own, place, second, turned, branch, total, back, params, sums, weights, cost=COST):
    count = second.shape[0]
    return pl.pallas_call(
        partial(feed_middle_body, own),
        in_specs=[SCALARS] + [RESIDENT] * (7 + len(weights)),
        out_specs=[RESIDENT] * 4,
        out_shape=[pltpu.VMEM((count, D), f32)] * 2 + [pltpu.VMEM((FEED_PACK, D), bf16), shape_of((8, D), f32)],
        scratch_shapes=[pltpu.VMEM((count, TILE), bf16)] * 2,
        input_output_aliases={4: 0, 5: 1},
        compiler_params=pltpu.CompilerParams(vmem_limit_bytes=OTHER_ROOM * 1024 * 1024),
        cost_estimate=cost,
    )(place, second, turned, branch, total, back, params, sums, *weights)


def feed_near_body(
    place, hat_ref, inverse_ref, second_ref, turned_ref, branch_ref, total_in, back_in, norm_gain, params_ref,
    sums_in, near_ref, attended_ref,
    out_ref, grad_residual_ref, attn_ref, keep_ref, proj_send, proj_keep, sums_ref,
    total_s, back_s, active_s, raise_s, attended_s, proj_s, sem,
):
    step = pl.program_id(0)
    core, tp = place[0], place[3]
    fetch = pltpu.make_async_copy(attended_ref, attended_s, sem)

    @pl.when(step == 0)
    def _():
        fetch.start()
        sums_ref[...] = sums_in[...]
        total_s[...] = jnp.zeros_like(total_s)
        shard = 2 * (1 - tp) + core
        bias = params_ref[2:3, pl.ds(pl.multiple_of(TILE * shard, TILE), TILE)]
        sums_ref[pl.ds(shard, 1), :] = feed_tile(
            near_ref[512:1024, :], near_ref[0:512, :], bias, second_ref, turned_ref, branch_ref, total_s, back_s,
            active_s, raise_s, keep_ref, True,
        )

    @pl.when(step >= 1)
    def _():
        here = pl.ds(pl.multiple_of((step - 1) * ROWS, 16), ROWS)
        out_ref[...] = (total_in[here, :] + total_s[here, :]).astype(bf16)
        hat, inverse = hat_ref[here, :], inverse_ref[here, :]
        grad_second = back_in[here, :] + back_s[here, :]
        grad_residual = branch_ref[here, :].astype(f32) + norm_back(grad_second * norm_gain[...], hat, inverse)
        grad_residual_ref[here, :] = grad_residual
        attn_ref[here, :] = grad_residual.astype(bf16)
        sums_ref[4:5, :] += column_sum(grad_residual)
        sums_ref[5:6, :] += column_sum(grad_second * hat)
        sums_ref[6:7, :] += column_sum(grad_second)

    @pl.when(step == pl.num_programs(0) - 1)
    def _():
        fetch.wait()
        proj_s[...] = t_mm(attended_s[...], attn_ref[...]).astype(bf16)
        for target, half in ((proj_send, 1 - core), (proj_keep, core)):
            for other in range(2):
                shard = jnp.where(other == 0, tp, 1 - tp)
                rows = pl.ds(pl.multiple_of(256 * shard + 128 * half, 128), 128)
                target[PROJ_PACK * other : PROJ_PACK * (other + 1), :] = proj_s[rows, :]


def feed_near(place, hat, inverse, second, turned, branch, total, back, gain, params, sums, near, attended):
    count = hat.shape[0]
    blocks = count // ROWS

    def given(columns):
        return pl.BlockSpec((ROWS, columns), lambda i: (jnp.maximum(i - 1, 0), 0))

    return kernel_call(
        feed_near_body,
        (blocks + 1,),
        [SCALARS] + [RESIDENT] * 9 + [whole((8, D)), RESIDENT]
        + [pl.BlockSpec(memory_space=pl.ANY)],
        [given(D)] + [RESIDENT] * 5 + [whole((8, D))],
        [pltpu.HBM((count, D), bf16), pltpu.VMEM((count, D), f32), pltpu.VMEM((count, D), bf16)]
        + [pltpu.VMEM((FEED_PACK, D), bf16)] + [pltpu.VMEM((2 * PROJ_PACK, D), bf16)] * 2
        + [shape_of((8, D), f32)],
        [pltpu.VMEM((count, D), f32)] * 2 + [pltpu.VMEM((count, TILE), bf16)] * 2
        + [pltpu.VMEM((count, D), bf16), pltpu.VMEM((D, D), bf16), pltpu.SemaphoreType.DMA],
        room=NEAR_ROOM,
    )(
        place, hat, inverse, second, turned, branch, total, back, gain, params, sums, near, in_hbm(attended)
    )


def attend_back_body(
    after, attn_ref, qkv_in_ref, weights_ref, padded_ref, inverse_ref, proj_ref,
    merged_ref, grad_residual_ref, qkv_ref, rows_ref, first_in,
    stack_ref, low_ref, sums_ref, vectors_ref, position_ref, first_ref,
    stage, grads, sem,
):
    fetch = pltpu.make_async_copy(first_in, first_ref, sem)

    @pl.when(pl.program_id(0) == pl.num_programs(0) - 1)
    def _():
        fetch.wait()

    @pl.when(pl.program_id(0) == 0)
    def _():
        fetch.start()
        vectors_ref[...] = jnp.zeros_like(vectors_ref)
        sums_ref[...] = jnp.zeros_like(sums_ref)
        position_ref[...] = jnp.zeros_like(position_ref)

    here = pl.ds(pl.multiple_of(pl.program_id(0) * ROWS, 16), ROWS)
    stage[pl.ds(0, ROWS), :] = attn_ref[here, :].astype(f32)
    stage[pl.ds(ROWS, 32), :] = jnp.zeros((32, D), f32)
    real = lax.broadcasted_iota(jnp.int32, (KEYS, 1), 0) < AREA
    padded = jnp.concatenate(
        [jnp.where(real, stage[pl.ds(AREA * w, KEYS), :], 0.0).astype(bf16) for w in range(GROUP)], axis=0
    )
    grad_attended = mm_t(padded, proj_ref[...])
    masks = head_masks()
    empty = jnp.zeros((QUERIES - KEYS, QUAD), bf16)
    kept = {}
    for w in range(GROUP):
        for quad in range(QUADS):
            columns = slice(QUAD * quad, QUAD * (quad + 1))
            values = qkv_in_ref[w, :, 2 * D + QUAD * quad : 2 * D + QUAD * (quad + 1)]
            grad = grad_attended[KEYS * w : KEYS * (w + 1), columns] * inverse_ref[w, :, columns].astype(f32)
            low = grad.astype(bf16)
            taken = (grad * padded_ref[w, :, columns].astype(f32)).astype(bf16)
            both = jnp.concatenate([low, -taken], axis=1)
            change = jnp.concatenate([mm_t(both, block) for block in value_blocks(values, masks)], axis=1)
            grad_scores = (weights_ref[w, quad].astype(f32) * change).astype(bf16)
            position_ref[quad] += grad_scores.astype(f32)
            kept[w, quad] = (low, grad_scores)
    for w in range(GROUP):
        to = pl.ds(AREA * w, AREA)
        for quad in range(QUADS):
            low, grad_scores = kept[w, quad]
            queries = qkv_in_ref[w, :, QUAD * quad : QUAD * (quad + 1)]
            keys = qkv_in_ref[w, :, D + QUAD * quad : D + QUAD * (quad + 1)]
            grad_queries = mm(grad_scores, spread_heads(keys, masks)) * SCALING
            grad_keys = turned_products(queries.T[:, :KEYS], grad_scores)
            grad_values = turned_products(jnp.concatenate([low, empty], axis=0).T[:, :KEYS], weights_ref[w, quad])
            for part, grad in enumerate((grad_queries, grad_keys, grad_values)):
                grads[to, D * part + QUAD * quad : D * part + QUAD * (quad + 1)] = grad[0:AREA]
    stack = grads[pl.ds(0, ROWS), :].astype(bf16)
    stack_ref[here, :] = stack
    sums_ref[...] += column_sum(stack.astype(f32))
    grad_first = (
        mm_t(stack[:, 0:D], qkv_ref[0:D, :])
        + mm_t(stack[:, D : 2 * D], qkv_ref[D : 2 * D, :])
        + mm_t(stack[:, 2 * D :], qkv_ref[2 * D :, :])
    )
    normed, inverse = normalize(merged_ref[...])
    grad_merged = grad_residual_ref[here, :] + norm_back(grad_first * rows_ref[0:1, :], normed, inverse)
    low = grad_merged.astype(bf16)
    low_ref[here, :] = low
    vectors_ref[0:1, :] += column_sum(grad_first * normed)
    vectors_ref[1:2, :] += column_sum(grad_first)
    vectors_ref[2:3, :] += column_sum(low.astype(f32))


def attend_back(after, attn, qkv_in, weights, padded, inverse, proj, merged, grad_residual, qkv, rows, first):
    count = attn.shape[0]
    return kernel_call(
        attend_back_body,
        (count // ROWS,),
        [
            ANYWHERE, RESIDENT, by_windows((QUERIES, 3 * D)), by_windows((QUADS, KEYS, LANES)),
            by_windows((KEYS, D)), by_windows((KEYS, D)), RESIDENT, by_rows(ROWS, D), RESIDENT, RESIDENT, RESIDENT,
            ANYWHERE,
        ],
        [RESIDENT] * 6,
        [
            pltpu.VMEM((count, 3 * D), bf16), pltpu.VMEM((count, D), bf16), shape_of((1, 3 * D), f32),
            shape_of((8, D), f32), shape_of((QUADS, KEYS, LANES), f32), pltpu.VMEM((count, D), bf16),
        ],
        [pltpu.VMEM((ROWS + 32, D), f32), pltpu.VMEM((ROWS + 8, 3 * D), f32), pltpu.SemaphoreType.DMA],
        room=AB_ROOM,
    )(
        after, attn, *[in_hbm(array) for array in (qkv_in, weights, padded, inverse)], proj, in_hbm(merged),
        grad_residual, qkv, rows, in_hbm(first),
    )


def qkv_back_body(place, after, first_ref, stack_ref, hat_in, send_ref, keep_ref, hat_ref, qkv_s, turned_s, sem):
    part = pl.program_id(0)
    fetch = pltpu.make_async_copy(hat_in, hat_ref, sem)

    @pl.when(part == 0)
    def _():
        fetch.start()
        turned_s[...] = first_ref[...].T

    @pl.when(part == pl.num_programs(0) - 1)
    def _():
        fetch.wait()

    core, tp = place[0], place[3]
    qkv_s[...] = mm(turned_s[...], stack_ref[:, pl.ds(pl.multiple_of(D * part, D), D)]).astype(bf16)
    for target, half in ((send_ref, 1 - core), (keep_ref, core)):
        for other in range(2):
            shard = jnp.where(other == 0, tp, 1 - tp)
            base = QKV_PACK * other
            rows = pl.ds(pl.multiple_of(256 * half, 256), 256)
            columns = pl.ds(pl.multiple_of(256 * shard, 256), 256)

            @pl.when(part < 2)
            def _():
                target[base : base + 256, pl.ds(pl.multiple_of(256 * part, 256), 256)] = qkv_s[rows, columns]

            @pl.when(part == 2)
            def _():
                block = qkv_s[rows, columns]
                target[base + 256 : base + 384, 0:256] = block[0:128]
                target[base + 256 : base + 384, 256:512] = block[128:256]


def qkv_back(place, after, first, stack, hat):
    count = stack.shape[0]
    return kernel_call(
        qkv_back_body,
        (3,),
        [SCALARS, ANYWHERE, RESIDENT, RESIDENT, ANYWHERE],
        [RESIDENT] * 3,
        [pltpu.VMEM((2 * QKV_PACK, D), bf16)] * 2 + [pltpu.VMEM((count, MERGE_IN), bf16)],
        [pltpu.VMEM((D, D), bf16), pltpu.VMEM((D, count), bf16), pltpu.SemaphoreType.DMA],
        room=9,
    )(place, after, first, stack, in_hbm(hat))


def merge_back_body(
    place, after, low_ref, hat_ref, merge_ref, params_ref, column_ref, feed_sums_ref, qkv_sums_ref, vectors_ref,
    position_ref,
    send_ref, keep_ref,
    fold_s, all_s, raw_s,
):
    core, tp = place[0], place[3]
    total = vectors_ref[2:3, :]
    pair = jnp.concatenate([split(total), jnp.zeros((14, D), bf16)], axis=0)
    ones = jnp.ones((16, D), bf16)
    raw_s[...] = t_mm(hat_ref[...], low_ref[...])
    all_s[...] = jnp.zeros_like(all_s)
    all_s[0:2, :] = vectors_ref[0:2, :]
    all_s[2:6, :] = feed_sums_ref[4:8, :]
    all_s[6:7, :] = qkv_sums_ref[:, 0:D]
    all_s[7:8, :] = qkv_sums_ref[:, 2 * D :]
    all_s[8:12, :] = feed_sums_ref[0:4, :]
    all_s[16:32, 0:384] = fold_place(position_ref, fold_s)
    for tile in range(2):
        rows = slice(512 * tile, 512 * (tile + 1))
        merge = merge_ref[rows, :]
        scaled = raw_s[rows, :] * merge.astype(f32)
        scaled_high = scaled.astype(bf16)
        scaled_rest = (scaled - scaled_high.astype(f32)).astype(bf16)
        all_s[12 + tile : 13 + tile, :] = (mm_t(ones, scaled_high) + mm_t(ones, scaled_rest))[0:1]
        all_s[14 + tile : 15 + tile, :] = column_sum(mm_t(pair, merge))
    for target, half in ((send_ref, 1 - core), (keep_ref, core)):
        for other in range(2):
            begin = pl.multiple_of(512 * jnp.where(other == 0, tp, 1 - tp) + 256 * half, 256)
            bias = jnp.broadcast_to(params_ref[0:1, pl.ds(1024 + begin, 256)], (16, 256)).astype(bf16)
            gain = column_ref[pl.ds(begin, 256), 0:1]
            block = raw_s[pl.ds(begin, 256), :] * gain + t_mm(bias, pair)
            target[MERGE_PACK * other : MERGE_PACK * (other + 1), :] = block.astype(bf16)
        target[2 * MERGE_PACK :, :] = split(all_s[pl.ds(pl.multiple_of(SUMS * half, SUMS), SUMS), :])


def merge_back(place, after, low, hat, merge, params, column, feed_sums, sums, vectors, position):
    pack = 2 * MERGE_PACK + 2 * SUMS
    return pl.pallas_call(
        merge_back_body,
        in_specs=[SCALARS, ANYWHERE] + [RESIDENT] * 9,
        out_specs=[RESIDENT] * 2,
        out_shape=[pltpu.VMEM((pack, D), bf16), pltpu.VMEM((pack, D), bf16)],
        scratch_shapes=[
            pltpu.VMEM((HEADS, KEYS, 256), f32), pltpu.VMEM((32, D), f32), pltpu.VMEM((MERGE_IN, D), f32),
        ],
        compiler_params=pltpu.CompilerParams(vmem_limit_bytes=14 * 1024 * 1024),
        cost_estimate=COST,
    )(place, after, low, hat, merge, params, column, feed_sums, sums, vectors, position)


def section_back_body(after, low_ref, hat_ref, inverse_ref, merge_ref, params_ref, out_ref, token_ref):
    token_ref[...] = jnp.zeros_like(token_ref)
    scaled = mm_t(low_ref[...], merge_ref[...]) * params_ref[0:1, 0:MERGE_IN]
    out_ref[...] = norm_back(scaled, hat_ref[...].astype(f32), inverse_ref[...]).astype(bf16)


def section_back(after, low, hat, inverse, merge, params):
    count = low.shape[0]
    return kernel_call(
        section_back_body,
        (count // ROWS,),
        [
            pl.BlockSpec(memory_space=pl.ANY), by_rows(ROWS, D), by_rows(ROWS, MERGE_IN), by_rows(ROWS, 1),
            whole((MERGE_IN, D)), whole((24, 2048)),
        ],
        [by_rows(ROWS, MERGE_IN), whole((8, 128))],
        [pltpu.HBM((count, MERGE_IN), bf16), shape_of((8, 128), f32)],
        flops=2 * count * D * MERGE_IN,
        moved=count * 5 * MERGE_IN,
        room=16,
    )(after, in_hbm(low), in_hbm(hat), inverse, merge, params)


def spread_matrix():
    place = lax.broadcasted_iota(jnp.int32, (QUERIES, 256), 0)
    lane = lax.broadcasted_iota(jnp.int32, (QUERIES, 256), 1)
    target = place + (SIDE - WINDOW) * (place // WINDOW)
    return jnp.logical_and(lane == target, place < AREA).astype(f32)


def expand_body(params_ref, hat_ref, place_ref, hat_copy, lines_s, out_s, sem):
    save = pltpu.make_async_copy(hat_ref, hat_copy, sem)
    save.start()
    lane = lax.broadcasted_iota(jnp.int32, (384, QUERIES), 0)
    patch = lax.broadcasted_iota(jnp.int32, (384, QUERIES), 1)
    middle = (WINDOW - 1) * (SIDE + 1)
    picked = jnp.logical_and(lane == middle - patch - (SIDE - WINDOW) * (patch // WINDOW), patch < AREA)
    picked = picked.astype(f32).astype(bf16)
    tables = params_ref[8 : 8 + HEADS, 0:384]
    for place in range(AREA):
        offset = SIDE * (place // WINDOW) + place % WINDOW
        lines_s[HEADS * place : HEADS * (place + 1), :] = pltpu.roll(tables, (384 - offset) % 384, 1)
    for begin in range(0, HEADS * AREA, ROWS):
        here = slice(begin, begin + ROWS)
        rows = lines_s[here, :]
        high = rows.astype(bf16)
        rest = rows - high.astype(f32)
        middle_part = rest.astype(bf16)
        low = (rest - middle_part.astype(f32)).astype(bf16)
        out_s[here, :] = mm(high, picked) + mm(middle_part, picked) + mm(low, picked)
    out_s[HEADS * AREA :, :] = jnp.zeros((8 * HEADS, QUERIES), f32)
    for head in range(HEADS):
        lanes = slice(QUERIES * (head % 4), QUERIES * (head % 4 + 1))
        place_ref[head // 4, 0:AREA, lanes] = out_s[pl.ds(head, AREA, stride=HEADS), :]
        place_ref[head // 4, AREA:KEYS, lanes] = jnp.zeros((KEYS - AREA, QUERIES), f32)
    save.wait()


def expand(params, hat):
    return kernel_call(
        expand_body,
        (1,),
        [RESIDENT, RESIDENT],
        [RESIDENT, ANYWHERE],
        [shape_of((QUADS, KEYS, LANES), f32), pltpu.HBM(hat.shape, bf16)],
        [pltpu.VMEM((HEADS * AREA, 384), f32), pltpu.VMEM((HEADS * (AREA + 8), QUERIES), f32), pltpu.SemaphoreType.DMA],
        room=16,
    )(params, hat)


def fold_place(place_ref, stage_s):
    spread = spread_matrix().astype(bf16)
    lines = []
    for head in range(HEADS):
        stage = stage_s.at[head]
        rows = place_ref[head // 4, :, QUERIES * (head % 4) : QUERIES * (head % 4 + 1)]
        rows = jnp.concatenate([rows, jnp.zeros((QUERIES - KEYS, QUERIES), f32)], axis=0).T[:KEYS]
        high = rows.astype(bf16)
        rest = (rows - high.astype(f32)).astype(bf16)
        stage[...] = mm(high, spread) + mm(rest, spread)
        total = jnp.zeros((WINDOW, 384), f32)
        for y in range(WINDOW):
            part = jnp.concatenate(
                [stage[pl.ds(WINDOW * y, WINDOW), :], jnp.zeros((WINDOW, 128), f32)], axis=1
            )
            total += pltpu.roll(part, SIDE * (WINDOW - 1 - y), 1) if y < WINDOW - 1 else part
        line = total[WINDOW - 1 : WINDOW, :]
        for x in range(WINDOW - 1):
            line += pltpu.roll(total[x : x + 1, :], WINDOW - 1 - x, 1)
        lines.append(line)
    return jnp.concatenate(lines, axis=0)


class Ring:
    def __init__(self, place, rows_size):
        self.place = place
        self.rows_size = rows_size
        self.along = rows_size // 4

    def to(self, array, bits):
        return lax.ppermute(array, "rows", [(i, i ^ bits) for i in range(self.rows_size)])

    def core(self, array):
        return self.to(array, 1)

    def x(self, array):
        return self.to(array, 2)

    def z(self, array, step):
        return self.to(array, 4 * step)

    def y(self, array):
        return lax.ppermute(array, "tp", [(0, 1), (1, 0)])

    def xy(self, array):
        pairs = [(2 * i + t, 2 * (i ^ 2) + 1 - t) for i in range(self.rows_size) for t in range(2)]
        return lax.ppermute(array, ("rows", "tp"), pairs)


def rows_of(array, begin, rows):
    return lax.dynamic_slice_in_dim(array, begin, rows, 0).astype(f32)


def stage(body, place, after, rows, *operands, cost=COST, scratch=()):
    return plain_call_after(
        body, [pltpu.VMEM((count, D), bf16) for count in rows], place, after, operands, room=STAGE_ROOM, cost=cost,
        scratch=scratch,
    )


def added(refs, begin, rows):
    here = pl.ds(pl.multiple_of(begin, 16), rows)
    total = refs[0][here, :].astype(f32)
    for ref in refs[1:]:
        total = total + ref[here, :].astype(f32)
    return total


def part(ref, begin, rows):
    return ref.at[begin : begin + rows, :]


FEED_BLOCKS = ((0, 256), (256, 256), (512, 64))


def feed_first_body(place, own_keep, own_got, other_keep, other_got, to_y, to_x, to_both, kept):
    x = place[1]
    own, other = (own_keep, own_got), (other_keep, other_got)
    for target, blocks, side in ((to_y, other, x), (to_x, own, 1 - x), (to_both, other, 1 - x), (kept, own, x)):
        target[0:256, :] = added(blocks, 256 * side, 256).astype(bf16)
        target[256:512, :] = added(blocks, 512 + 256 * side, 256).astype(bf16)


def feed_proj_body(place, keep, got, *refs):
    x = place[1]
    for target, shard, side in zip(refs[-4:], (1, 0, 1, 0), (x, 1 - x, 1 - x, x)):
        target[512:576, :] = added((keep, got), PROJ_PACK * shard + 64 * side, 64).astype(bf16)


def feed_proj(place, keep, got, outs):
    return pl.pallas_call(
        feed_proj_body,
        in_specs=[SCALARS] + [RESIDENT] * 6,
        out_specs=[RESIDENT] * 4,
        out_shape=[pltpu.VMEM(out.shape, bf16) for out in outs],
        input_output_aliases={3: 0, 4: 1, 5: 2, 6: 3},
        compiler_params=pltpu.CompilerParams(vmem_limit_bytes=STAGE_ROOM * 1024 * 1024),
        cost_estimate=COST,
    )(place, keep, got, *outs)


def feed_second_body(place, *refs):
    blocks, outs = refs[:4], refs[4:]
    for step, out in enumerate(outs):
        offset = 0
        for begin, size in FEED_BLOCKS:
            span = size // len(outs)
            to = begin + (place[2] ^ step) * span
            out[offset : offset + span, :] = added(blocks, to, span).astype(bf16)
            offset += span


def total_body(place, *refs):
    refs[-1][...] = added(refs[:-1], 0, refs[-1].shape[0]).astype(bf16)


def beside_body(place, *refs):
    rows = refs[0].shape[0]
    for index, ref in enumerate(refs[:-1]):
        refs[-1][rows * index : rows * (index + 1), :] = ref[...]


def qkv_first_body(place, keep, got, to_y, to_x, to_both, kept):
    x = place[1]
    for target, other, side in ((to_y, 1, x), (to_x, 0, 1 - x), (to_both, 1, 1 - x), (kept, 0, x)):
        target[...] = added((keep, got), QKV_PACK * other + 192 * side, 192).astype(bf16)


def merge_first_body(place, keep, got, to_y, to_x, to_both, kept, sums_s):
    x = place[1]
    sums_s[...] = joined(keep[512:544, :]) + joined(got[512:544, :])
    for target, other, side in ((to_y, 1, x), (to_x, 0, 1 - x), (to_both, 1, 1 - x), (kept, 0, x)):
        target[0:128, :] = added((keep, got), MERGE_PACK * other + 128 * side, 128).astype(bf16)
        target[128:144, :] = split(sums_s[pl.ds(pl.multiple_of(8 * side, 8), 8), :])


def last_second_body(place, qkv_sum, *refs):
    blocks, outs = refs[:4], refs[4:]
    vectors = split(sum(joined(ref[128:144, :]) for ref in blocks))
    wide, narrow = 192 // len(outs), 128 // len(outs)
    for step, out in enumerate(outs):
        to = place[2] ^ step
        out[0:wide, :] = added((qkv_sum,), to * wide, wide).astype(bf16)
        out[wide : wide + narrow, :] = added(blocks, to * narrow, narrow).astype(bf16)
        out[wide + narrow :, :] = vectors


def merge_total_body(place, *refs):
    blocks, (out, vectors) = refs[:-2], refs[-2:]
    rows = out.shape[0]
    out[...] = added(blocks, 0, rows).astype(bf16)
    vectors[...] = split(sum(joined(ref[rows : rows + 16, :]) for ref in blocks))


def last_beside_body(place, vectors, *refs):
    rows = refs[0].shape[0]
    for index, ref in enumerate(refs[:-1]):
        refs[-1][rows * index : rows * (index + 1), :] = ref[...]
    refs[-1][rows * (len(refs) - 1) :, :] = vectors[...]


def in_order(place, near, far, stage, rows, along):
    piece = sum(rows) // 2 // along
    for side, ref in ((place[1], near), (1 - place[1], far)):
        for step in range(along):
            begin, offset = 0, piece * step
            for size in rows:
                span = size // 2 // along
                to = begin + side * (size // 2) + (place[2] ^ step) * span
                stage[pl.ds(pl.multiple_of(to, 16), span), :] = ref[offset : offset + span, :]
                begin += size
                offset += span


def feed_unpack_body(along, place, near, far, core_near, core_far, down_ref, up_ref, proj_ref, token_ref, stage):
    token_ref[...] = jnp.zeros_like(token_ref)
    for target, mine, beside in ((place[0], near, far), (1 - place[0], core_near, core_far)):
        in_order(place, mine, beside, stage, (512, 512, PROJ_PACK), along)
        wide = pl.ds(pl.multiple_of(512 * target, 512), 512)
        down_ref[wide, :] = stage[0:512, :].astype(f32)
        proj_ref[pl.ds(pl.multiple_of(128 * target, 128), 128), :] = stage[1024:1152, :].astype(f32)
        up_ref[:, wide] = stage[512:1024, :].astype(f32)


def feed_unpack(along, place, after, parts):
    return plain_call_after(
        partial(feed_unpack_body, along),
        [pltpu.HBM((FFN // 2, D), f32), pltpu.HBM((D, FFN // 2), f32), pltpu.HBM((D // 2, D), f32), shape_of((8, 128), f32)],
        place,
        after,
        parts,
        scratch=[pltpu.VMEM((FEED_PACK + PROJ_PACK, D), bf16)],
        room=14,
    )


def last_unpack_body(along, place, mine, beside, core_mine, core_beside, qkv_ref, merge_ref, *refs):
    vectors, stage, all_s = refs[:-2], refs[-2], refs[-1]
    rows = mine.shape[0] - 16
    for target, near, far in ((place[0], mine, beside), (1 - place[0], core_mine, core_beside)):
        in_order(place, near, far, stage, (QKV_PACK, MERGE_PACK), along)
        for side, ref in ((place[1], near), (1 - place[1], far)):
            all_s[pl.ds(pl.multiple_of(SUMS * target + 8 * side, 8), 8), :] = joined(ref[rows:, :])
        begin = pl.multiple_of(256 * target, 256)
        for part in range(2):
            qkv_ref[part, pl.ds(begin, 256), :] = stage[0:256, 256 * part : 256 * part + 256].astype(f32)
        qkv_ref[2, pl.ds(begin, 128), :] = stage[256:384, 0:256].astype(f32)
        qkv_ref[2, pl.ds(begin + 128, 128), :] = stage[256:384, 256:512].astype(f32)
        merge_ref[pl.ds(begin, 256), :] = stage[384:640, :].astype(f32)
    write_vectors(place[3], all_s, vectors)


VECTORS = [(1, D)] * 6 + [(2, D // 2), (1, FFN // 2), (1, MERGE_IN // 2), (1, MERGE_IN // 2), (HEADS // 2, SIDE * SIDE)]


def write_vectors(tp, sums, refs):
    for row in range(6):
        refs[row][...] = sums[row : row + 1, :]
    columns = pl.ds(pl.multiple_of(256 * tp, 256), 256)
    refs[6][...] = sums[6:8, columns]
    refs[7][:, 0:512] = sums[pl.ds(8 + 2 * tp, 1), :]
    refs[7][:, 512:1024] = sums[pl.ds(9 + 2 * tp, 1), :]
    refs[8][...] = sums[pl.ds(12 + tp, 1), :]
    refs[9][...] = sums[pl.ds(14 + tp, 1), :]
    refs[10][...] = sums[pl.ds(pl.multiple_of(16 + 8 * tp, 8), 8), 0 : SIDE * SIDE]


def last_unpack(along, place, *parts):
    outs = plain_call(
        partial(last_unpack_body, along),
        [pltpu.HBM(shape, f32) if shape[-2] >= 128 else shape_of(shape, f32) for shape in [(3, D, D // 2), (MERGE_IN // 2, D)] + VECTORS],
        (place, *parts),
        scratch=[pltpu.VMEM((QKV_PACK + MERGE_PACK, D), bf16), pltpu.VMEM((2 * SUMS, D), f32)],
    )
    return outs[0], outs[1], outs[2:]


def fetch_by_tp(ring, piece_of):
    near = ring.y(piece_of)
    return near, ring.core(near)


def plain_pieces(tp_size, weights, params):
    merge, qkv, proj, up, down = [
        lax.all_gather(array, "tp", axis=axis, tiled=True) for array, axis in zip(weights, (0, 2, 0, 1, 0))
    ]
    gain, bias, qv, up_bias, table = [
        lax.all_gather(array, "tp", axis=axis, tiled=True) for array, axis in zip(params, (0, 0, 1, 0, 1))
    ]

    def shard(array, axis, which):
        size = array.shape[axis] // 2
        return lax.slice_in_dim(array, which * size, (which + 1) * size, axis=axis)

    def rows_of(which):
        rows = jnp.zeros((PARAMS, D), f32)
        rows = rows.at[0].set(shard(gain.astype(f32), 0, which)).at[1].set(shard(bias.astype(f32), 0, which))
        rows = rows.at[2].set(shard(qv, 1, which).reshape(-1)).at[3:5].set(shard(up_bias, 0, which).reshape(2, D))
        return rows.at[8:16, : SIDE * SIDE].set(shard(table, 1, which).T)

    merge_other = shard(merge, 0, 1)
    qkv_other = shard(qkv, 2, 1).reshape(3 * D, 256)
    proj_other, up_other, down_other = shard(proj, 0, 1), shard(up, 1, 1), shard(down, 0, 1)

    def qkv_piece(half):
        rows = qkv_other[768 * half : 768 * half + 768]
        return jnp.concatenate(
            [jnp.concatenate([rows[:384], rows[384:]], axis=1), proj_other[128 * half : 128 * half + 128]], axis=0
        )

    def feed_piece(half):
        tile = slice(512 * half, 512 * half + 512)
        return jnp.concatenate([down_other[tile], up_other[:, tile]], axis=0)

    own = (
        shard(merge, 0, 0), shard(qkv, 2, 0).reshape(3 * D, 256), shard(proj, 0, 0), shard(up, 1, 0), shard(down, 0, 0)
    )
    return own, (rows_of(0), split(rows_of(1))), (merge_other[:256], merge_other[256:]), (qkv_piece(0), qkv_piece(1)), (feed_piece(0), feed_piece(1))


def sum_plainly(tp_size, feed_packs, proj_packs, qkv_packs, merge_packs):
    feed_packs, proj_packs, qkv_packs, merge_packs = lax.psum(
        (feed_packs, proj_packs, qkv_packs, merge_packs), ("rows", "tp")
    )
    own_send, own_keep, other_send, other_keep = feed_packs
    order = [own_keep, own_send, other_keep, other_send]
    down = jnp.concatenate([block[0:512] for block in order], axis=0)
    up = jnp.concatenate([block[512:1024] for block in order], axis=1)

    def blocks(packs, size):
        send, keep = packs
        return [keep[:size], send[:size], keep[size : 2 * size], send[size : 2 * size]]

    def qkv_rows(block):
        return jnp.stack(
            [block[0:256, 0:256], block[0:256, 256:512], jnp.concatenate([block[256:384, 0:256], block[256:384, 256:512]])]
        )

    order = blocks(qkv_packs, QKV_PACK)
    qkv = jnp.concatenate(
        [jnp.concatenate([qkv_rows(order[2 * shard + half]) for half in range(2)], axis=1) for shard in range(2)], axis=2
    )
    proj = jnp.concatenate(blocks(proj_packs, PROJ_PACK), axis=0)
    merge = jnp.concatenate(blocks(merge_packs, MERGE_PACK), axis=0)
    sums = jnp.concatenate([joined(merge_packs[1][2 * MERGE_PACK :]), joined(merge_packs[0][2 * MERGE_PACK :])], axis=0)
    index = lax.axis_index("tp")

    def own(array, axis):
        size = array.shape[axis] // tp_size
        return lax.dynamic_slice_in_dim(array, index * size, size, axis).astype(f32)

    vectors = [sums[row] for row in range(6)] + [
        own(sums[6:8], 1), own(sums[8:12].reshape(-1), 0), own(sums[12:14].reshape(-1), 0),
        own(sums[14:16].reshape(-1), 0), own(sums[16:32, : SIDE * SIDE], 0),
    ]
    return own(down, 0), own(up, 1), own(qkv, 2), own(proj, 0), own(merge, 0), vectors


def per_device(
    rows_size, tp_size,
    section_rows, window_mask, cotangent, merge_weight, merge_gain, merge_bias, norm1_gain, norm1_bias,
    qkv_weight, qv_bias, bias_table, proj_weight, proj_bias, norm2_gain, norm2_bias,
    up_weight, up_bias, down_weight, down_bias,
):
    fast = tp_size == 2 and rows_size in (8, 16)
    count = cotangent.shape[0]
    index, tp = lax.axis_index("rows"), lax.axis_index("tp")
    place = jnp.stack([index & 1, (index >> 1) & 1, index >> 2, tp]).astype(jnp.int32)
    ring = Ring(place, rows_size)
    if fast:
        flat_qkv = qkv_weight.reshape(3 * D, D // 2)
        merge_piece = pack_merge(place, merge_weight)
        merge_near = ring.y(merge_piece)
        params, piece = pack_params(
            place, merge_piece, merge_gain, merge_bias, qv_bias, up_bias[None], bias_table.T
        )
        others = ring.y(piece)
        mask, live = masks_of(place, params, window_mask, count)
        qkv_piece = gate(pack_qkv(place, (mask,), flat_qkv, proj_weight), others, merge_near)
        qkv_near = ring.y(qkv_piece)
        hat, inverse = section_norm(qkv_piece, section_rows)
        merge_far = ring.core(merge_near)
        kernel_place = place
    else:
        (merge_weight, flat_qkv, proj_weight, up_weight, down_weight), (params, others), merge_pair, qkv_pair, feed_pair = plain_pieces(
            tp_size,
            (merge_weight, qkv_weight, proj_weight, up_weight, down_weight),
            (merge_gain, merge_bias, qv_bias, up_bias, bias_table),
        )
        (merge_near, merge_far), (qkv_near, qkv_far), (feed_near_piece, feed_far_piece) = merge_pair, qkv_pair, feed_pair
        kernel_place = jnp.zeros_like(place)
        hat, inverse = section_norm(params, section_rows)
        own_mask = lax.dynamic_slice_in_dim(window_mask, tp * count, count, 0)
        mask, live = masks_of(kernel_place, params, own_mask, count)

    merged, first, first_copy, merge_full, params, column = merge_rows(
        kernel_place, hat, merge_weight, merge_near, merge_far, params, others, norm1_gain[None], norm1_bias[None]
    )
    position, hat = expand(params, hat)
    if fast:
        (feed_piece,) = plain_call_after(
            pack_feed_body, [shape_of((FEED_PACK, D), bf16)], place, (position, qkv_near), (up_weight, down_weight)
        )
        qkv_far = ring.core(qkv_near)
        feed_near_piece = ring.y(feed_piece)
        feed_far_piece = ring.core(feed_near_piece)
    qkv_rows, weights, attended, padded, inverse_sums, qkv_full = attend(
        kernel_place, first, flat_qkv, qkv_near, qkv_far, params, position, mask
    )
    rows = [row[None] for row in (proj_bias, norm2_gain, norm2_bias, down_bias)]
    second_hat, second_inverse, total, back, second, turned, branch, own_send, feed_sums, proj_full = feed_own(
        kernel_place, attended, merged, cotangent, live, *rows, params, proj_weight, qkv_near, qkv_far,
        up_weight, down_weight,
    )
    total, back, own_keep, feed_sums = feed_middle(
        True, kernel_place, second, turned, branch, total, back, params, feed_sums, (up_weight, down_weight), LONG
    )
    total, back, other_send, feed_sums = feed_middle(
        False, kernel_place, second, turned, branch, total, back, params, feed_sums, (feed_far_piece,)
    )
    block_out, grad_residual, attn, other_keep, proj_send, proj_keep, feed_sums = feed_near(
        kernel_place, second_hat, second_inverse, second, turned, branch, total, back, rows[1], params, feed_sums, feed_near_piece,
        attended,
    )
    after = feed_sums
    if fast:
        own_got, other_got, proj_got = ring.core(own_send), ring.core(other_send), ring.core(proj_send)
        outs = stage(feed_first_body, place, feed_sums, (576,) * 4, own_keep, own_got, other_keep, other_got)
        to_y, to_x, to_both, feed_kept = feed_proj(place, proj_keep, proj_got, outs)
        feed_from = (ring.y(to_y), ring.x(to_x), ring.xy(to_both))
        after = to_y
    stack, low, sums, vectors, position_grad, first_near = attend_back(
        after, attn, qkv_rows, weights, padded, inverse_sums, proj_full, merged, grad_residual, qkv_full,
        norm1_gain[None], first_copy,
    )
    qkv_send, qkv_keep, hat_near = qkv_back(kernel_place, sums, first_near, stack, hat)
    after = sums
    if fast:
        along = ring.along
        qkv_got = ring.core(qkv_send)
        span = 576 // along
        feed_parts = stage(
            feed_second_body, place, qkv_send, (span,) * along, feed_kept, *feed_from, cost=LONG
        )
        feed_got = [ring.z(feed_parts[step], step) for step in range(1, along)]
        to_y, to_x, to_both, qkv_kept = stage(
            qkv_first_body, place, feed_parts[0], (192,) * 4, qkv_keep, qkv_got
        )
        qkv_from = (ring.y(to_y), ring.x(to_x), ring.xy(to_both))
        after = to_y
    merge_send, merge_keep = merge_back(
        kernel_place, after, low, hat_near, merge_full, params, column, feed_sums, sums, vectors, position_grad
    )
    if fast:
        merge_got = ring.core(merge_send)
        (feed_total,) = stage(total_body, place, merge_send, (span,), feed_parts[0], *feed_got, cost=LONG)
        feed_all = [feed_total] + [ring.z(feed_total, step) for step in range(1, along)]
        (qkv_sum,) = stage(total_body, place, feed_total, (192,), qkv_kept, *qkv_from)
        to_y, to_x, to_both, merge_kept = stage(
            merge_first_body, place, qkv_sum, (144,) * 4, merge_keep, merge_got, scratch=[pltpu.VMEM((SUMS, D), f32)]
        )
        (feed_mine,) = stage(beside_body, place, to_y, (span * along,), *feed_all)
        feed_beside = ring.x(feed_mine)
        last_span = 320 // along
        last_parts = stage(
            last_second_body, place, feed_mine, (last_span + 16,) * along, qkv_sum,
            merge_kept, ring.y(to_y), ring.x(to_x), ring.xy(to_both),
        )
        last_got = [ring.z(last_parts[step], step) for step in range(1, along)]
        last_total, vectors = stage(
            merge_total_body, place, last_parts[0], (last_span, 16), *([last_parts[0]] + last_got), cost=LONG
        )
        last_all = [last_total] + [ring.z(last_total, step) for step in range(1, along)]
        section_grad, token = section_back(last_total, low, hat, inverse, merge_full, params)
        (last_near,) = stage(
            last_beside_body, place, (token, feed_beside), (336,), vectors, *last_all, cost=LONG
        )
        last_far = ring.x(last_near)
        feed_cores = ring.core(feed_mine), ring.core(feed_beside)
        down_grad, up_grad, proj_grad, token = feed_unpack(
            along, place, last_near, (feed_mine, feed_beside, *feed_cores)
        )
        (last_far,) = stage(beside_body, place, token, (336,), last_far)
        qkv_grad, merge_grad, vectors = last_unpack(
            along, place, last_near, last_far, ring.core(last_near), ring.core(last_far)
        )
    else:
        section_grad, _ = section_back(low, low, hat, inverse, merge_full, params)
        down_grad, up_grad, qkv_grad, proj_grad, merge_grad, vectors = sum_plainly(
            tp_size, (own_send, own_keep, other_send, other_keep), (proj_send, proj_keep), (qkv_send, qkv_keep),
            (merge_send, merge_keep),
        )
    norm1_gain_grad, norm1_bias_grad, proj_bias_grad, norm2_gain_grad, norm2_bias_grad, down_bias_grad = [
        row.reshape(D) for row in vectors[0:6]
    ]
    qv_grad, up_bias_grad, gain_grad, bias_grad, table_grad = vectors[6:]
    return (
        block_out, section_grad, merge_grad, gain_grad.reshape(-1), bias_grad.reshape(-1),
        norm1_gain_grad, norm1_bias_grad, qkv_grad, qv_grad, table_grad.T, proj_grad, proj_bias_grad,
        norm2_gain_grad, norm2_bias_grad, up_grad, up_bias_grad.reshape(-1), down_grad, down_bias_grad,
    )


def solution(mesh):
    rows_size, tp_size = mesh.shape["rows"], mesh.shape["tp"]
    both = ("rows", "tp")
    return jax.shard_map(
        partial(per_device, rows_size, tp_size),
        mesh=mesh,
        in_specs=(
            P(both, None), P("rows"), P(both, None), P("tp", None), P("tp"), P("tp"), P(), P(),
            P(None, None, "tp"), P(None, "tp"), P(None, "tp"), P("tp", None), P(), P(), P(),
            P(None, "tp"), P("tp"), P("tp", None), P(),
        ),
        out_specs=(
            P(both, None), P(both, None), P("tp", None), P("tp"), P("tp"), P(), P(),
            P(None, None, "tp"), P(None, "tp"), P(None, "tp"), P("tp", None), P(), P(), P(),
            P(None, "tp"), P("tp"), P("tp", None), P(),
        ),
        check_vma=False,
    )
```

```python
from functools import partial
import math

import jax
import jax.numpy as jnp
from jax import lax
from jax.experimental import pallas as pl
from jax.experimental.pallas import tpu as pltpu
from jax.sharding import PartitionSpec as P

MERGE_IN = 1024
D = 512
HEADS = 16
HEAD_DIM = 32
FFN = 2048
WINDOW = 10
AREA = WINDOW * WINDOW
SIDE = 2 * WINDOW - 1
EPSILON = 1e-05
MASKED_SCORE = -1e30
EXACT = lax.Precision.HIGHEST
SCALING = 1.0 / math.sqrt(HEAD_DIM)
GROUP = 4
ROWS = GROUP * AREA
KEYS = 112
QUERIES = 128
QUADS = 4
QUAD = 4 * HEAD_DIM
LANES = 4 * QUERIES

bf16 = jnp.bfloat16
f32 = jnp.float32


def mm(a, b):
    return jnp.dot(a, b, preferred_element_type=f32)


def mm_t(a, b):
    return lax.dot_general(a, b, (((1,), (1,)), ((), ())), preferred_element_type=f32)


def t_mm(a, b):
    return lax.dot_general(a, b, (((0,), (0,)), ((), ())), preferred_element_type=f32)


def normalize(values):
    center = jnp.mean(values, axis=-1, keepdims=True)
    spread = jnp.mean(values * values, axis=-1, keepdims=True) - center * center
    inverse = lax.rsqrt(spread + EPSILON)
    return (values - center) * inverse, inverse


def norm_back(grad_hat, normed, inverse):
    first_mean = jnp.mean(grad_hat, axis=-1, keepdims=True)
    second_mean = jnp.mean(grad_hat * normed, axis=-1, keepdims=True)
    return inverse * (grad_hat - first_mean - normed * second_mean)


def column_sum(values):
    return jnp.sum(values, axis=0, keepdims=True)


def head_masks():
    lane = lax.broadcasted_iota(jnp.int32, (1, QUAD), 1) // HEAD_DIM
    return [(lane == head).astype(f32).astype(bf16) for head in range(4)]


def spread_heads(rows, masks):
    return jnp.concatenate([rows * mask for mask in masks], axis=0)


def kernel_call(body, grid, in_specs, out_specs, out_shape, scratch=(), flops=0, moved=0, room=32, cost=None):
    return pl.pallas_call(
        body,
        grid=grid,
        in_specs=in_specs,
        out_specs=out_specs,
        out_shape=out_shape,
        scratch_shapes=list(scratch),
        compiler_params=pltpu.CompilerParams(
            dimension_semantics=("arbitrary",) * len(grid), vmem_limit_bytes=room * 1024 * 1024
        ),
        cost_estimate=cost or COST,
    )


def whole(shape):
    return pl.BlockSpec(shape, lambda *_: (0,) * len(shape), pipeline_mode=pl.Buffered(1))


def by_rows(rows, columns):
    return pl.BlockSpec((rows, columns), lambda i: (i, 0))


def by_windows(shape):
    return pl.BlockSpec((GROUP,) + shape, lambda i: (i,) + (0,) * len(shape))


SCALARS = pl.BlockSpec(memory_space=pltpu.SMEM)
RESIDENT = pl.BlockSpec(memory_space=pltpu.VMEM)
ANYWHERE = pl.BlockSpec(memory_space=pl.ANY)


def in_hbm(array):
    return pltpu.with_memory_space_constraint(array, pltpu.HBM)


FEED_PACK = 1024
QKV_PACK = 384
PROJ_PACK = 128
MERGE_PACK = 256
STAGE_ROOM = 9
COST = pl.CostEstimate(flops=1, bytes_accessed=1, transcendentals=0)
LONG = pl.CostEstimate(flops=10**12, bytes_accessed=1, transcendentals=0)
SUMS = 16
PARAMS = 16


def shape_of(shape, dtype):
    return jax.ShapeDtypeStruct(shape, dtype)


def split(rows):
    high = rows.astype(bf16).astype(f32)
    return jnp.concatenate([high, rows - high], axis=0).astype(bf16)


def joined(pair):
    half = pair.shape[0] // 2
    return pair[:half].astype(f32) + pair[half:].astype(f32)


def both_shards(tp, mine, other, axis):
    return jnp.where(
        tp == 0, jnp.concatenate([mine, other], axis=axis), jnp.concatenate([other, mine], axis=axis)
    )


def pack_merge_body(place, merge_ref, out_ref, sem):
    half = pl.ds(pl.multiple_of(256 * place[0], 256), 256)
    copy = pltpu.make_async_copy(merge_ref.at[half, :], out_ref, sem)
    copy.start()
    copy.wait()


def pack_merge(place, merge):
    return pl.pallas_call(
        pack_merge_body,
        in_specs=[SCALARS, ANYWHERE],
        out_specs=RESIDENT,
        out_shape=pltpu.VMEM((256, D), bf16),
        scratch_shapes=[pltpu.SemaphoreType.DMA],
        compiler_params=pltpu.CompilerParams(vmem_limit_bytes=4 * 1024 * 1024),
        cost_estimate=COST,
    )(place, in_hbm(merge))


def pack_params_body(
    place, after, gain_ref, bias_ref, qv_ref, up_bias_ref, table_ref,
    params_ref, out_ref, gain_s, bias_s, qv_s, up_bias_s, table_s, sems,
):
    pairs = (
        (gain_ref, gain_s), (bias_ref, bias_s), (qv_ref, qv_s), (up_bias_ref, up_bias_s), (table_ref, table_s)
    )
    copies = [pltpu.make_async_copy(source, target, sems.at[index]) for index, (source, target) in enumerate(pairs)]
    for copy in copies:
        copy.start()
    params_ref[...] = jnp.zeros_like(params_ref)
    for copy in copies:
        copy.wait()
    params_ref[0:1, :] = gain_s[...].astype(f32).reshape(1, D)
    params_ref[1:2, :] = bias_s[...].astype(f32).reshape(1, D)
    params_ref[2:3, 0:256] = qv_s[0:1, :]
    params_ref[2:3, 256:512] = qv_s[1:2, :]
    params_ref[3:4, :] = up_bias_s[:, 0:512]
    params_ref[4:5, :] = up_bias_s[:, 512:1024]
    params_ref[8:16, 0 : SIDE * SIDE] = table_s[...]
    out_ref[...] = split(params_ref[...])


def pack_params(place, after, *operands):
    operands = [in_hbm(array) for array in operands]
    return pl.pallas_call(
        pack_params_body,
        in_specs=[SCALARS] + [ANYWHERE] * 6,
        out_specs=[RESIDENT] * 2,
        out_shape=[pltpu.VMEM((PARAMS, D), f32), pltpu.VMEM((2 * PARAMS, D), bf16)],
        scratch_shapes=[pltpu.VMEM(array.shape, array.dtype) for array in operands] + [pltpu.SemaphoreType.DMA((5,))],
        compiler_params=pltpu.CompilerParams(vmem_limit_bytes=4 * 1024 * 1024),
        cost_estimate=COST,
    )(place, after, *operands)


def plain_call(body, outs, operands, room=16, scratch=(), flops=0):
    return pl.pallas_call(
        body,
        in_specs=[SCALARS] + [pl.BlockSpec(memory_space=pltpu.VMEM)] * (len(operands) - 1),
        out_specs=[pl.BlockSpec(memory_space=pltpu.VMEM)] * len(outs),
        out_shape=outs,
        scratch_shapes=list(scratch),
        compiler_params=pltpu.CompilerParams(vmem_limit_bytes=room * 1024 * 1024),
        cost_estimate=COST,
    )(*operands)


def pack_qkv_body(place, qkv_ref, proj_ref, *refs):
    out, qkv_s, proj_s, sems = refs[-4:]
    core = place[0]
    copies = [
        pltpu.make_async_copy(qkv_ref.at[pl.ds(pl.multiple_of(768 * core, 256), 768), :], qkv_s, sems.at[0]),
        pltpu.make_async_copy(proj_ref.at[pl.ds(pl.multiple_of(128 * core, 128), 128), :], proj_s, sems.at[1]),
    ]
    for copy in copies:
        copy.start()
    for copy in copies:
        copy.wait()
    for side in range(2):
        out[0:384, 256 * side : 256 * side + 256] = qkv_s[384 * side : 384 * side + 384, :]
    out[384:512, :] = proj_s[...]


def pack_qkv(place, after, qkv, proj):
    return pl.pallas_call(
        pack_qkv_body,
        in_specs=[SCALARS] + [ANYWHERE] * (2 + len(after)),
        out_specs=RESIDENT,
        out_shape=pltpu.VMEM((QKV_PACK + PROJ_PACK, D), bf16),
        scratch_shapes=[
            pltpu.VMEM((768, 256), bf16), pltpu.VMEM((128, D), bf16), pltpu.SemaphoreType.DMA((2,)),
        ],
        compiler_params=pltpu.CompilerParams(vmem_limit_bytes=4 * 1024 * 1024),
        cost_estimate=COST,
    )(place, in_hbm(qkv), in_hbm(proj), *after)


def pack_feed_body(place, up_ref, down_ref, out):
    half = pl.ds(pl.multiple_of(512 * place[0], 512), 512)
    out[0:512, :] = down_ref[half, :]
    out[512:1024, :] = up_ref[:, half]


def plain_call_after(body, outs, place, after, operands, room=16, scratch=(), flops=0, cost=COST):
    after = after if isinstance(after, tuple) else (after,)

    def without_after(place, *refs):
        return body(place, *refs[len(after) :])

    return pl.pallas_call(
        without_after,
        in_specs=[SCALARS] + [pl.BlockSpec(memory_space=pl.ANY)] * len(after) + [pl.BlockSpec(memory_space=pltpu.VMEM)] * len(operands),
        out_specs=[pl.BlockSpec(memory_space=pltpu.VMEM)] * len(outs),
        out_shape=outs,
        scratch_shapes=list(scratch),
        compiler_params=pltpu.CompilerParams(vmem_limit_bytes=room * 1024 * 1024),
        cost_estimate=cost,
    )(place, *after, *operands)


def nothing(array_ref, *refs):
    pass


def gate(array, *after):
    return pl.pallas_call(
        nothing,
        in_specs=[RESIDENT] + [ANYWHERE] * len(after),
        out_specs=RESIDENT,
        out_shape=pltpu.VMEM(array.shape, array.dtype),
        input_output_aliases={0: 0},
        compiler_params=pltpu.CompilerParams(vmem_limit_bytes=4 * 1024 * 1024),
        cost_estimate=COST,
    )(array, *after)


def masks_body(place, window_in, mask_ref, live_ref, stage, window_s, sem):
    copy = pltpu.make_async_copy(window_in, window_s, sem)
    copy.start()
    copy.wait()
    window_ref = window_s[...].reshape(1, window_s.shape[0])
    windows = mask_ref.shape[0]
    shards = window_ref.shape[1] // (windows * AREA)
    stage[...] = jnp.zeros_like(stage)
    for window in range(windows):
        patch = window_ref[:, AREA * window : AREA * (window + 1)]
        for shard in range(1, shards):
            begin = AREA * (windows * shard + window)
            patch = jnp.where(place[3] == shard, window_ref[:, begin : begin + AREA], patch)
        stage[window : window + 1, 0:AREA] = patch
    patches = jnp.minimum(stage[...], 1).astype(f32)
    live = jnp.max(patches, axis=1, keepdims=True)
    inside = lax.broadcasted_iota(jnp.int32, (windows, QUERIES), 1) < AREA
    keep = jnp.logical_and(jnp.maximum(patches, 1.0 - live) > 0.5, inside)
    added = jnp.where(keep, 0.0, MASKED_SCORE)
    for window in range(windows):
        mask_ref[window] = added[window : window + 1, :]
        live_ref[window] = jnp.broadcast_to(live[window : window + 1, :], (1, QUERIES))


def masks_of(place, after, window_mask, count):
    windows = count // AREA
    return pl.pallas_call(
        lambda place, after, *refs: masks_body(place, *refs),
        in_specs=[SCALARS, ANYWHERE, ANYWHERE],
        out_specs=[RESIDENT] * 2,
        out_shape=[pltpu.VMEM((windows, 1, QUERIES), f32)] * 2,
        scratch_shapes=[
            pltpu.VMEM((windows, QUERIES), jnp.int32), pltpu.VMEM(window_mask.shape, jnp.int32), pltpu.SemaphoreType.DMA,
        ],
        compiler_params=pltpu.CompilerParams(vmem_limit_bytes=4 * 1024 * 1024),
        cost_estimate=COST,
    )(place, after, in_hbm(window_mask))


def section_norm_body(after, rows_ref, hat_ref, inverse_ref, rows_s, sems):
    steps = rows_s.shape[0] // ROWS
    copies = []
    for step in range(steps):
        here = slice(ROWS * step, ROWS * (step + 1))
        copies.append(pltpu.make_async_copy(rows_ref.at[here, :], rows_s.at[here, :], sems.at[step]))
        copies[step].start()
    for step in range(steps):
        here = slice(ROWS * step, ROWS * (step + 1))
        copies[step].wait()
        hat, inverse = normalize(rows_s[here, :].astype(f32))
        hat_ref[here, :] = hat.astype(bf16)
        inverse_ref[here, :] = inverse


def section_norm(after, rows):
    count = rows.shape[0]
    return kernel_call(
        section_norm_body,
        (1,),
        [ANYWHERE, ANYWHERE],
        [RESIDENT, RESIDENT],
        [pltpu.VMEM((count, MERGE_IN), bf16), shape_of((count, 1), f32)],
        [pltpu.VMEM((count, MERGE_IN), bf16), pltpu.SemaphoreType.DMA((count // ROWS,))],
        room=16,
    )(after, in_hbm(rows))


def gain_rows(tp, params, others):
    return both_shards(tp, params[0:1], others[0:1], 1), both_shards(tp, params[1:2], others[1:2], 1)


def merge_body(
    place, hat_ref, own_ref, near_ref, far_ref, params_ref, others_ref, norm_gain, norm_bias,
    merged_ref, first_ref, first_copy, merge_ref, params_out_ref, column_ref,
    merge_s, shift_s, gain_s,
):

    @pl.when(pl.program_id(0) == 0)
    def _():
        core, tp = place[0], place[3]
        merge_s[pl.ds(pl.multiple_of(512 * tp, 512), 512), :] = own_ref[...]
        other = 512 * (1 - tp)
        merge_s[pl.ds(pl.multiple_of(other + 256 * core, 256), 256), :] = near_ref[...]
        merge_s[pl.ds(pl.multiple_of(other + 256 * (1 - core), 256), 256), :] = far_ref[...]
        merge_ref[...] = merge_s[...]
        params = params_ref[...]
        others = joined(others_ref[...])
        gain, bias = gain_rows(tp, params, others)
        gain_s[...] = gain.astype(bf16)
        shift_s[...] = mm(jnp.broadcast_to(bias, (16, MERGE_IN)).astype(bf16), merge_s[...])[0:1]
        params_out_ref[0:1, 0:1024] = gain
        params_out_ref[0:1, 1024:2048] = bias
        params_out_ref[1:2, 0:512] = both_shards(tp, params[2:3, 0:256], others[2:3, 0:256], 1)
        params_out_ref[1:2, 512:1024] = both_shards(tp, params[2:3, 256:512], others[2:3, 256:512], 1)
        params_out_ref[1:2, 1024:2048] = jnp.zeros((1, 1024), f32)
        params_out_ref[2:3, :] = both_shards(
            tp,
            jnp.concatenate([params[3:4], params[4:5]], axis=1),
            jnp.concatenate([others[3:4], others[4:5]], axis=1),
            1,
        )
        params_out_ref[3:8, :] = jnp.zeros((5, 2048), f32)
        params_out_ref[8:24, 0:512] = both_shards(tp, params[8:16], others[8:16], 0)
        params_out_ref[8:24, 512:2048] = jnp.zeros((16, 1536), f32)
        column_ref[...] = jnp.broadcast_to(gain, (128, MERGE_IN)).T

    here = pl.ds(pl.multiple_of(pl.program_id(0) * ROWS, 16), ROWS)
    merged = mm(hat_ref[here, :] * gain_s[...], merge_s[...]) + shift_s[...]
    merged_ref[...] = merged
    hat, _ = normalize(merged)
    first = (hat * norm_gain[...] + norm_bias[...]).astype(bf16)
    first_ref[here, :] = first
    first_copy[...] = first


def merge_rows(place, hat, own, near, far, params, others, gain, bias):
    count = hat.shape[0]
    return kernel_call(
        merge_body,
        (count // ROWS,),
        [
            SCALARS, RESIDENT, RESIDENT, RESIDENT, RESIDENT, RESIDENT, RESIDENT, RESIDENT, RESIDENT,
        ],
        [
            by_rows(ROWS, D), RESIDENT, by_rows(ROWS, D), whole((MERGE_IN, D)), RESIDENT,
            whole((MERGE_IN, 128)),
        ],
        [
            pltpu.HBM((count, D), f32), pltpu.VMEM((count, D), bf16), pltpu.HBM((count, D), bf16),
            pltpu.HBM((MERGE_IN, D), bf16),
            shape_of((24, 2048), f32), pltpu.HBM((MERGE_IN, 128), f32),
        ],
        [
            pltpu.VMEM((MERGE_IN, D), bf16), pltpu.VMEM((1, D), f32), pltpu.VMEM((1, MERGE_IN), bf16),
        ],
        flops=2 * count * D * MERGE_IN,
        moved=count * 10 * D + 4 * D * MERGE_IN,
        room=14,
    )(place, hat, own, near, far, params, others, gain, bias)


def value_blocks(values, masks):
    return [jnp.concatenate([values * mask, jnp.broadcast_to(mask, (QUERIES, QUAD))], axis=1) for mask in masks]


def turned_products(turned, scores):
    parts = []
    for pair in range(2):
        both = mm(turned[64 * pair : 64 * pair + 64], scores[:, 256 * pair : 256 * pair + 256])
        parts += [both[0:32, 0:128], both[32:64, 128:256]]
    return jnp.concatenate(parts, axis=0).T


def attend_body(
    place, first_ref, own_ref, near_ref, far_ref, params_ref, position_ref, mask_ref,
    qkv_out_ref, weights_ref, attended_ref, padded_ref, inverse_ref, qkv_ref,
    stage, mixed,
):
    @pl.when(pl.program_id(0) == 0)
    def _():
        core, tp = place[0], place[3]
        other = pl.ds(pl.multiple_of(256 * (1 - tp), 256), 256)
        qkv_ref[:, pl.ds(pl.multiple_of(256 * tp, 256), 256)] = own_ref[...]
        for ref, half in ((near_ref, core), (far_ref, 1 - core)):
            for side in range(2):
                rows = pl.ds(pl.multiple_of(768 * half + 384 * side, 128), 384)
                qkv_ref[rows, other] = ref[0:384, 256 * side : 256 * side + 256]

    here = pl.ds(pl.multiple_of(pl.program_id(0) * ROWS, 16), ROWS)
    stage[pl.ds(0, ROWS), :] = first_ref[here, :].astype(f32)
    stage[pl.ds(ROWS, 32), :] = jnp.zeros((32, D), f32)
    padded = jnp.concatenate(
        [stage[pl.ds(AREA * w, QUERIES), :].astype(bf16) for w in range(GROUP)], axis=0
    )
    queries = (SCALING * (mm(padded, qkv_ref[0:512, :]) + params_ref[1:2, 0:512])).astype(bf16)
    keys = mm(padded, qkv_ref[512:1024, :]).astype(bf16)
    values = (mm(padded, qkv_ref[1024:1536, :]) + params_ref[1:2, 512:1024]).astype(bf16)
    for w in range(GROUP):
        block = slice(QUERIES * w, QUERIES * (w + 1))
        qkv_out_ref[w, :, 0:D] = queries[block]
        qkv_out_ref[w, :, D : 2 * D] = keys[block]
        qkv_out_ref[w, :, 2 * D :] = values[block]
    masks = head_masks()
    for w in range(GROUP):
        mask = mask_ref[w]
        for quad in range(QUADS):
            columns = slice(QUAD * quad, QUAD * (quad + 1))
            rows = QUERIES * w
            spread = spread_heads(keys[rows : rows + QUERIES, columns], masks)
            scores = mm_t(queries[rows : rows + KEYS, columns], spread)
            raised = []
            for head in range(4):
                lanes = slice(QUERIES * head, QUERIES * (head + 1))
                part = scores[:, lanes] + position_ref[quad, :, lanes] + mask
                raised.append(jnp.exp(part - jnp.max(part, axis=1, keepdims=True)).astype(bf16))
            weights = jnp.concatenate(raised, axis=1)
            weights_ref[w, quad] = weights
            blocks = value_blocks(values[rows : rows + QUERIES, columns], masks)
            out = mm(weights, jnp.concatenate(blocks, axis=0))
            inverse = 1.0 / out[:, QUAD:]
            both = out[:, :QUAD] * inverse
            inverse_ref[w, :, columns] = inverse.astype(bf16)
            padded_ref[w, :, columns] = both.astype(bf16)
            mixed[pl.ds(AREA * w, AREA), columns] = both[0:AREA]
    attended_ref[...] = mixed[pl.ds(0, ROWS), :].astype(bf16)


def attend(place, first, own, near, far, params, position, mask):
    count = first.shape[0]
    windows = count // AREA
    return kernel_call(
        attend_body,
        (count // ROWS,),
        [
            SCALARS, RESIDENT, RESIDENT, RESIDENT, RESIDENT, RESIDENT, RESIDENT, by_windows((1, QUERIES)),
        ],
        [
            by_windows((QUERIES, 3 * D)), by_windows((QUADS, KEYS, LANES)), by_rows(ROWS, D),
            by_windows((KEYS, D)), by_windows((KEYS, D)), RESIDENT,
        ],
        [
            pltpu.HBM((windows, QUERIES, 3 * D), bf16), pltpu.HBM((windows, QUADS, KEYS, LANES), bf16),
            pltpu.HBM((count, D), bf16), pltpu.HBM((windows, KEYS, D), bf16), pltpu.HBM((windows, KEYS, D), bf16),
            shape_of((3 * D, D), bf16),
        ],
        [pltpu.VMEM((ROWS + 32, D), f32), pltpu.VMEM((ROWS + 8, D), f32)],
        flops=2 * count * D * (3 * D + 4 * AREA),
        moved=count * 10 * D + windows * QUADS * KEYS * LANES * 2,
        room=20,
    )(place, first, own, near, far, params, position, mask)


def gelu_parts(t):
    chance = 0.5 * lax.erf(t * math.sqrt(0.5)) + 0.5
    density = jnp.exp(t * t * -0.5) * (1.0 / math.sqrt(2.0 * math.pi))
    return t * chance, chance + t * density


TILE = 512
FEED_ROWS = 400
OWN_ROOM = 18
OTHER_ROOM = 12
AB_ROOM = 18
NEAR_ROOM = 20


def feed_tile(up, down, bias, second_ref, turned_ref, branch_ref, total_s, back_s, active_s, raise_s, target, first):
    sums = jnp.zeros((1, TILE), f32)

    def add_products(here, active, grad_raised):
        total_s[here, :] += mm(active, down)
        back = mm_t(grad_raised, up)
        if first:
            back_s[here, :] = back
        else:
            back_s[here, :] += back

    last = None
    for begin in range(0, second_ref.shape[0], FEED_ROWS):
        here = slice(begin, begin + FEED_ROWS)
        value, slope = gelu_parts(mm(second_ref[here, :], up) + bias)
        active = value.astype(bf16)
        grad_raised = (mm_t(branch_ref[here, :], down) * slope).astype(bf16)
        active_s[here, :] = active
        raise_s[here, :] = grad_raised
        sums += column_sum(grad_raised.astype(f32))
        if last is not None:
            add_products(*last)
        last = here, active, grad_raised
    add_products(*last)
    target[0:512, :] = t_mm(active_s[...], branch_ref[...]).astype(bf16)
    target[512:1024, :] = mm(turned_ref[...], raise_s[...]).astype(bf16)
    return sums


def feed_own_body(
    place, attended_ref, merged_ref, cotangent_ref, live_ref, proj_bias, norm_gain, norm_bias, down_bias, params_ref,
    proj_own, near_ref, far_ref, up_own, down_own,
    hat_ref, inverse_ref, total_ref, back_ref, second_ref, turned_ref, branch_ref, send_ref, sums_ref, proj_ref,
    active_s, raise_s,
):
    step = pl.program_id(0)
    blocks = pl.num_programs(0) - 1
    core, tp = place[0], place[3]

    @pl.when(step == 0)
    def _():
        proj_ref[pl.ds(pl.multiple_of(256 * tp, 256), 256), :] = proj_own[...]
        for ref, which in ((near_ref, core), (far_ref, 1 - core)):
            proj_ref[pl.ds(pl.multiple_of(256 * (1 - tp) + 128 * which, 128), 128), :] = ref[384:512, :]
        sums_ref[...] = jnp.zeros_like(sums_ref)

    @pl.when(step < blocks)
    def _():
        here = pl.ds(pl.multiple_of(step * ROWS, 16), ROWS)
        residual = merged_ref[...] + mm(attended_ref[...], proj_ref[...]) + proj_bias[...]
        total_ref[here, :] = residual + down_bias[...]
        hat, inverse = normalize(residual)
        hat_ref[here, :] = hat
        inverse_ref[here, :] = inverse
        second_ref[here, :] = (hat * norm_gain[...] + norm_bias[...]).astype(bf16)
        row = lax.broadcasted_iota(jnp.int32, (ROWS, 1), 0)
        live = live_ref[GROUP - 1, :, 0:1]
        for window in range(GROUP - 2, -1, -1):
            live = jnp.where(row < AREA * (window + 1), live_ref[window, :, 0:1], live)
        branch = cotangent_ref[...].astype(f32) * live
        branch_ref[here, :] = branch.astype(bf16)
        sums_ref[7:8, :] += column_sum(branch)

    @pl.when(step == blocks)
    def _():
        turned_ref[...] = second_ref[...].T
        shard = 2 * tp + 1 - core
        units = pl.ds(pl.multiple_of(TILE * (1 - core), TILE), TILE)
        bias = params_ref[2:3, pl.ds(pl.multiple_of(TILE * shard, TILE), TILE)]
        sums_ref[pl.ds(shard, 1), :] = feed_tile(
            up_own[:, units], down_own[units, :], bias, second_ref, turned_ref, branch_ref, total_ref, back_ref,
            active_s, raise_s, send_ref, True,
        )


def feed_own(
    place, attended, merged, cotangent, live, proj_bias, gain, bias, down_bias, params, proj, near, far, up, down
):
    count = attended.shape[0]
    blocks = count // ROWS

    def taken(columns):
        return pl.BlockSpec((ROWS, columns), lambda i: (jnp.minimum(i, blocks - 1), 0))

    return kernel_call(
        feed_own_body,
        (blocks + 1,),
        [
            SCALARS, taken(D), taken(D), taken(D),
            pl.BlockSpec((GROUP, 1, QUERIES), lambda i: (jnp.minimum(i, blocks - 1), 0, 0)), RESIDENT, RESIDENT, RESIDENT, RESIDENT, RESIDENT, RESIDENT, RESIDENT, RESIDENT,
            RESIDENT, RESIDENT,
        ],
        [RESIDENT] * 10,
        [pltpu.VMEM((count, D), f32), pltpu.VMEM((count, 1), f32)] + [pltpu.VMEM((count, D), f32)] * 2
        + [pltpu.VMEM((count, D), bf16), pltpu.VMEM((D, count), bf16), pltpu.VMEM((count, D), bf16)]
        + [pltpu.VMEM((FEED_PACK, D), bf16), shape_of((8, D), f32), shape_of((D, D), bf16)],
        [pltpu.VMEM((count, TILE), bf16)] * 2,
        room=OWN_ROOM,
    )(
        place, in_hbm(attended), in_hbm(merged), in_hbm(cotangent), live, proj_bias, gain, bias, down_bias, params, proj,
        near, far, up, down,
    )


def feed_middle_body(
    own, place, second_ref, turned_ref, branch_ref, total_in, back_in, params_ref, sums_in, *refs
):
    weights, (total_ref, back_ref, target_ref, sums_ref, active_s, raise_s) = refs[:-6], refs[-6:]
    core, tp = place[0], place[3]
    sums_ref[...] = sums_in[...]
    if own:
        shard = 2 * tp + core
        units = pl.ds(pl.multiple_of(TILE * core, TILE), TILE)
        up, down = weights[0][:, units], weights[1][units, :]
    else:
        shard = 2 * (1 - tp) + 1 - core
        up, down = weights[0][512:1024, :], weights[0][0:512, :]
    bias = params_ref[2:3, pl.ds(pl.multiple_of(TILE * shard, TILE), TILE)]
    sums_ref[pl.ds(shard, 1), :] = feed_tile(
        up, down, bias, second_ref, turned_ref, branch_ref, total_ref, back_ref, active_s, raise_s, target_ref, False
    )


def feed_middle(own, place, second, turned, branch, total, back, params, sums, weights, cost=COST):
    count = second.shape[0]
    return pl.pallas_call(
        partial(feed_middle_body, own),
        in_specs=[SCALARS] + [RESIDENT] * (7 + len(weights)),
        out_specs=[RESIDENT] * 4,
        out_shape=[pltpu.VMEM((count, D), f32)] * 2 + [pltpu.VMEM((FEED_PACK, D), bf16), shape_of((8, D), f32)],
        scratch_shapes=[pltpu.VMEM((count, TILE), bf16)] * 2,
        input_output_aliases={4: 0, 5: 1},
        compiler_params=pltpu.CompilerParams(vmem_limit_bytes=OTHER_ROOM * 1024 * 1024),
        cost_estimate=cost,
    )(place, second, turned, branch, total, back, params, sums, *weights)


def feed_near_body(
    place, hat_ref, inverse_ref, second_ref, turned_ref, branch_ref, total_in, back_in, norm_gain, params_ref,
    sums_in, near_ref, attended_ref,
    out_ref, grad_residual_ref, attn_ref, keep_ref, proj_send, proj_keep, sums_ref,
    total_s, back_s, active_s, raise_s, attended_s, proj_s, sem,
):
    step = pl.program_id(0)
    core, tp = place[0], place[3]
    fetch = pltpu.make_async_copy(attended_ref, attended_s, sem)

    @pl.when(step == 0)
    def _():
        fetch.start()
        sums_ref[...] = sums_in[...]
        total_s[...] = jnp.zeros_like(total_s)
        shard = 2 * (1 - tp) + core
        bias = params_ref[2:3, pl.ds(pl.multiple_of(TILE * shard, TILE), TILE)]
        sums_ref[pl.ds(shard, 1), :] = feed_tile(
            near_ref[512:1024, :], near_ref[0:512, :], bias, second_ref, turned_ref, branch_ref, total_s, back_s,
            active_s, raise_s, keep_ref, True,
        )

    @pl.when(step >= 1)
    def _():
        here = pl.ds(pl.multiple_of((step - 1) * ROWS, 16), ROWS)
        out_ref[...] = (total_in[here, :] + total_s[here, :]).astype(bf16)
        hat, inverse = hat_ref[here, :], inverse_ref[here, :]
        grad_second = back_in[here, :] + back_s[here, :]
        grad_residual = branch_ref[here, :].astype(f32) + norm_back(grad_second * norm_gain[...], hat, inverse)
        grad_residual_ref[here, :] = grad_residual
        attn_ref[here, :] = grad_residual.astype(bf16)
        sums_ref[4:5, :] += column_sum(grad_residual)
        sums_ref[5:6, :] += column_sum(grad_second * hat)
        sums_ref[6:7, :] += column_sum(grad_second)

    @pl.when(step == pl.num_programs(0) - 1)
    def _():
        fetch.wait()
        proj_s[...] = t_mm(attended_s[...], attn_ref[...]).astype(bf16)
        for target, half in ((proj_send, 1 - core), (proj_keep, core)):
            for other in range(2):
                shard = jnp.where(other == 0, tp, 1 - tp)
                rows = pl.ds(pl.multiple_of(256 * shard + 128 * half, 128), 128)
                target[PROJ_PACK * other : PROJ_PACK * (other + 1), :] = proj_s[rows, :]


def feed_near(place, hat, inverse, second, turned, branch, total, back, gain, params, sums, near, attended):
    count = hat.shape[0]
    blocks = count // ROWS

    def given(columns):
        return pl.BlockSpec((ROWS, columns), lambda i: (jnp.maximum(i - 1, 0), 0))

    return kernel_call(
        feed_near_body,
        (blocks + 1,),
        [SCALARS] + [RESIDENT] * 9 + [whole((8, D)), RESIDENT]
        + [pl.BlockSpec(memory_space=pl.ANY)],
        [given(D)] + [RESIDENT] * 5 + [whole((8, D))],
        [pltpu.HBM((count, D), bf16), pltpu.VMEM((count, D), f32), pltpu.VMEM((count, D), bf16)]
        + [pltpu.VMEM((FEED_PACK, D), bf16)] + [pltpu.VMEM((2 * PROJ_PACK, D), bf16)] * 2
        + [shape_of((8, D), f32)],
        [pltpu.VMEM((count, D), f32)] * 2 + [pltpu.VMEM((count, TILE), bf16)] * 2
        + [pltpu.VMEM((count, D), bf16), pltpu.VMEM((D, D), bf16), pltpu.SemaphoreType.DMA],
        room=NEAR_ROOM,
    )(
        place, hat, inverse, second, turned, branch, total, back, gain, params, sums, near, in_hbm(attended)
    )


def attend_back_body(
    after, attn_ref, qkv_in_ref, weights_ref, padded_ref, inverse_ref, proj_ref,
    merged_ref, grad_residual_ref, qkv_ref, rows_ref, first_in,
    stack_ref, low_ref, sums_ref, vectors_ref, position_ref, first_ref,
    stage, grads, sem,
):
    fetch = pltpu.make_async_copy(first_in, first_ref, sem)

    @pl.when(pl.program_id(0) == pl.num_programs(0) - 1)
    def _():
        fetch.wait()

    @pl.when(pl.program_id(0) == 0)
    def _():
        fetch.start()
        vectors_ref[...] = jnp.zeros_like(vectors_ref)
        sums_ref[...] = jnp.zeros_like(sums_ref)
        position_ref[...] = jnp.zeros_like(position_ref)

    here = pl.ds(pl.multiple_of(pl.program_id(0) * ROWS, 16), ROWS)
    stage[pl.ds(0, ROWS), :] = attn_ref[here, :].astype(f32)
    stage[pl.ds(ROWS, 32), :] = jnp.zeros((32, D), f32)
    real = lax.broadcasted_iota(jnp.int32, (KEYS, 1), 0) < AREA
    padded = jnp.concatenate(
        [jnp.where(real, stage[pl.ds(AREA * w, KEYS), :], 0.0).astype(bf16) for w in range(GROUP)], axis=0
    )
    grad_attended = mm_t(padded, proj_ref[...])
    masks = head_masks()
    empty = jnp.zeros((QUERIES - KEYS, QUAD), bf16)
    kept = {}
    for w in range(GROUP):
        for quad in range(QUADS):
            columns = slice(QUAD * quad, QUAD * (quad + 1))
            values = qkv_in_ref[w, :, 2 * D + QUAD * quad : 2 * D + QUAD * (quad + 1)]
            grad = grad_attended[KEYS * w : KEYS * (w + 1), columns] * inverse_ref[w, :, columns].astype(f32)
            low = grad.astype(bf16)
            taken = (grad * padded_ref[w, :, columns].astype(f32)).astype(bf16)
            both = jnp.concatenate([low, -taken], axis=1)
            change = jnp.concatenate([mm_t(both, block) for block in value_blocks(values, masks)], axis=1)
            grad_scores = (weights_ref[w, quad].astype(f32) * change).astype(bf16)
            position_ref[quad] += grad_scores.astype(f32)
            kept[w, quad] = (low, grad_scores)
    for w in range(GROUP):
        to = pl.ds(AREA * w, AREA)
        for quad in range(QUADS):
            low, grad_scores = kept[w, quad]
            queries = qkv_in_ref[w, :, QUAD * quad : QUAD * (quad + 1)]
            keys = qkv_in_ref[w, :, D + QUAD * quad : D + QUAD * (quad + 1)]
            grad_queries = mm(grad_scores, spread_heads(keys, masks)) * SCALING
            grad_keys = turned_products(queries.T[:, :KEYS], grad_scores)
            grad_values = turned_products(jnp.concatenate([low, empty], axis=0).T[:, :KEYS], weights_ref[w, quad])
            for part, grad in enumerate((grad_queries, grad_keys, grad_values)):
                grads[to, D * part + QUAD * quad : D * part + QUAD * (quad + 1)] = grad[0:AREA]
    stack = grads[pl.ds(0, ROWS), :].astype(bf16)
    stack_ref[here, :] = stack
    sums_ref[...] += column_sum(stack.astype(f32))
    grad_first = (
        mm_t(stack[:, 0:D], qkv_ref[0:D, :])
        + mm_t(stack[:, D : 2 * D], qkv_ref[D : 2 * D, :])
        + mm_t(stack[:, 2 * D :], qkv_ref[2 * D :, :])
    )
    normed, inverse = normalize(merged_ref[...])
    grad_merged = grad_residual_ref[here, :] + norm_back(grad_first * rows_ref[0:1, :], normed, inverse)
    low = grad_merged.astype(bf16)
    low_ref[here, :] = low
    vectors_ref[0:1, :] += column_sum(grad_first * normed)
    vectors_ref[1:2, :] += column_sum(grad_first)
    vectors_ref[2:3, :] += column_sum(low.astype(f32))


def attend_back(after, attn, qkv_in, weights, padded, inverse, proj, merged, grad_residual, qkv, rows, first):
    count = attn.shape[0]
    return kernel_call(
        attend_back_body,
        (count // ROWS,),
        [
            ANYWHERE, RESIDENT, by_windows((QUERIES, 3 * D)), by_windows((QUADS, KEYS, LANES)),
            by_windows((KEYS, D)), by_windows((KEYS, D)), RESIDENT, by_rows(ROWS, D), RESIDENT, RESIDENT, RESIDENT,
            ANYWHERE,
        ],
        [RESIDENT] * 6,
        [
            pltpu.VMEM((count, 3 * D), bf16), pltpu.VMEM((count, D), bf16), shape_of((1, 3 * D), f32),
            shape_of((8, D), f32), shape_of((QUADS, KEYS, LANES), f32), pltpu.VMEM((count, D), bf16),
        ],
        [pltpu.VMEM((ROWS + 32, D), f32), pltpu.VMEM((ROWS + 8, 3 * D), f32), pltpu.SemaphoreType.DMA],
        room=AB_ROOM,
    )(
        after, attn, *[in_hbm(array) for array in (qkv_in, weights, padded, inverse)], proj, in_hbm(merged),
        grad_residual, qkv, rows, in_hbm(first),
    )


def qkv_back_body(place, after, first_ref, stack_ref, hat_in, send_ref, keep_ref, hat_ref, qkv_s, turned_s, sem):
    part = pl.program_id(0)
    fetch = pltpu.make_async_copy(hat_in, hat_ref, sem)

    @pl.when(part == 0)
    def _():
        fetch.start()
        turned_s[...] = first_ref[...].T

    @pl.when(part == pl.num_programs(0) - 1)
    def _():
        fetch.wait()

    core, tp = place[0], place[3]
    qkv_s[...] = mm(turned_s[...], stack_ref[:, pl.ds(pl.multiple_of(D * part, D), D)]).astype(bf16)
    for target, half in ((send_ref, 1 - core), (keep_ref, core)):
        for other in range(2):
            shard = jnp.where(other == 0, tp, 1 - tp)
            base = QKV_PACK * other
            rows = pl.ds(pl.multiple_of(256 * half, 256), 256)
            columns = pl.ds(pl.multiple_of(256 * shard, 256), 256)

            @pl.when(part < 2)
            def _():
                target[base : base + 256, pl.ds(pl.multiple_of(256 * part, 256), 256)] = qkv_s[rows, columns]

            @pl.when(part == 2)
            def _():
                block = qkv_s[rows, columns]
                target[base + 256 : base + 384, 0:256] = block[0:128]
                target[base + 256 : base + 384, 256:512] = block[128:256]


def qkv_back(place, after, first, stack, hat):
    count = stack.shape[0]
    return kernel_call(
        qkv_back_body,
        (3,),
        [SCALARS, ANYWHERE, RESIDENT, RESIDENT, ANYWHERE],
        [RESIDENT] * 3,
        [pltpu.VMEM((2 * QKV_PACK, D), bf16)] * 2 + [pltpu.VMEM((count, MERGE_IN), bf16)],
        [pltpu.VMEM((D, D), bf16), pltpu.VMEM((D, count), bf16), pltpu.SemaphoreType.DMA],
        room=9,
    )(place, after, first, stack, in_hbm(hat))


def merge_back_body(
    place, after, low_ref, hat_ref, merge_ref, params_ref, column_ref, feed_sums_ref, qkv_sums_ref, vectors_ref,
    position_ref,
    send_ref, keep_ref,
    fold_s, all_s, raw_s,
):
    core, tp = place[0], place[3]
    total = vectors_ref[2:3, :]
    pair = jnp.concatenate([split(total), jnp.zeros((14, D), bf16)], axis=0)
    ones = jnp.ones((16, D), bf16)
    raw_s[...] = t_mm(hat_ref[...], low_ref[...])
    all_s[...] = jnp.zeros_like(all_s)
    all_s[0:2, :] = vectors_ref[0:2, :]
    all_s[2:6, :] = feed_sums_ref[4:8, :]
    all_s[6:7, :] = qkv_sums_ref[:, 0:D]
    all_s[7:8, :] = qkv_sums_ref[:, 2 * D :]
    all_s[8:12, :] = feed_sums_ref[0:4, :]
    all_s[16:32, 0:384] = fold_place(position_ref, fold_s)
    for tile in range(2):
        rows = slice(512 * tile, 512 * (tile + 1))
        merge = merge_ref[rows, :]
        scaled = raw_s[rows, :] * merge.astype(f32)
        scaled_high = scaled.astype(bf16)
        scaled_rest = (scaled - scaled_high.astype(f32)).astype(bf16)
        all_s[12 + tile : 13 + tile, :] = (mm_t(ones, scaled_high) + mm_t(ones, scaled_rest))[0:1]
        all_s[14 + tile : 15 + tile, :] = column_sum(mm_t(pair, merge))
    for target, half in ((send_ref, 1 - core), (keep_ref, core)):
        for other in range(2):
            begin = pl.multiple_of(512 * jnp.where(other == 0, tp, 1 - tp) + 256 * half, 256)
            bias = jnp.broadcast_to(params_ref[0:1, pl.ds(1024 + begin, 256)], (16, 256)).astype(bf16)
            gain = column_ref[pl.ds(begin, 256), 0:1]
            block = raw_s[pl.ds(begin, 256), :] * gain + t_mm(bias, pair)
            target[MERGE_PACK * other : MERGE_PACK * (other + 1), :] = block.astype(bf16)
        target[2 * MERGE_PACK :, :] = split(all_s[pl.ds(pl.multiple_of(SUMS * half, SUMS), SUMS), :])


def merge_back(place, after, low, hat, merge, params, column, feed_sums, sums, vectors, position):
    pack = 2 * MERGE_PACK + 2 * SUMS
    return pl.pallas_call(
        merge_back_body,
        in_specs=[SCALARS, ANYWHERE] + [RESIDENT] * 9,
        out_specs=[RESIDENT] * 2,
        out_shape=[pltpu.VMEM((pack, D), bf16), pltpu.VMEM((pack, D), bf16)],
        scratch_shapes=[
            pltpu.VMEM((HEADS, KEYS, 256), f32), pltpu.VMEM((32, D), f32), pltpu.VMEM((MERGE_IN, D), f32),
        ],
        compiler_params=pltpu.CompilerParams(vmem_limit_bytes=14 * 1024 * 1024),
        cost_estimate=COST,
    )(place, after, low, hat, merge, params, column, feed_sums, sums, vectors, position)


def section_back_body(after, low_ref, hat_ref, inverse_ref, merge_ref, params_ref, out_ref, token_ref):
    token_ref[...] = jnp.zeros_like(token_ref)
    scaled = mm_t(low_ref[...], merge_ref[...]) * params_ref[0:1, 0:MERGE_IN]
    out_ref[...] = norm_back(scaled, hat_ref[...].astype(f32), inverse_ref[...]).astype(bf16)


def section_back(after, out, low, hat, inverse, merge, params, begin, steps):
    count = low.shape[0]

    def rows_at(columns):
        return pl.BlockSpec((ROWS, columns), lambda i: (i + begin, 0))

    first = out is None

    def body(*refs):
        section_back_body(*(refs if first else refs[1:]))

    return pl.pallas_call(
        body,
        grid=(steps,),
        in_specs=([] if first else [ANYWHERE])
        + [ANYWHERE, rows_at(D), rows_at(MERGE_IN), rows_at(1), whole((MERGE_IN, D)), whole((24, 2048))],
        out_specs=[rows_at(MERGE_IN), whole((8, 128))],
        out_shape=[pltpu.HBM((count, MERGE_IN), bf16), shape_of((8, 128), f32)],
        input_output_aliases={} if first else {0: 0},
        compiler_params=pltpu.CompilerParams(
            dimension_semantics=("arbitrary",), vmem_limit_bytes=16 * 1024 * 1024
        ),
        cost_estimate=COST,
    )(*([] if first else [out]), after, in_hbm(low), in_hbm(hat), inverse, merge, params)


def spread_matrix():
    place = lax.broadcasted_iota(jnp.int32, (QUERIES, 256), 0)
    lane = lax.broadcasted_iota(jnp.int32, (QUERIES, 256), 1)
    target = place + (SIDE - WINDOW) * (place // WINDOW)
    return jnp.logical_and(lane == target, place < AREA).astype(f32)


def expand_body(params_ref, hat_ref, place_ref, hat_copy, lines_s, out_s, sem):
    save = pltpu.make_async_copy(hat_ref, hat_copy, sem)
    save.start()
    lane = lax.broadcasted_iota(jnp.int32, (384, QUERIES), 0)
    patch = lax.broadcasted_iota(jnp.int32, (384, QUERIES), 1)
    middle = (WINDOW - 1) * (SIDE + 1)
    picked = jnp.logical_and(lane == middle - patch - (SIDE - WINDOW) * (patch // WINDOW), patch < AREA)
    picked = picked.astype(f32).astype(bf16)
    tables = params_ref[8 : 8 + HEADS, 0:384]
    for place in range(AREA):
        offset = SIDE * (place // WINDOW) + place % WINDOW
        lines_s[HEADS * place : HEADS * (place + 1), :] = pltpu.roll(tables, (384 - offset) % 384, 1)
    for begin in range(0, HEADS * AREA, ROWS):
        here = slice(begin, begin + ROWS)
        rows = lines_s[here, :]
        high = rows.astype(bf16)
        rest = rows - high.astype(f32)
        middle_part = rest.astype(bf16)
        low = (rest - middle_part.astype(f32)).astype(bf16)
        out_s[here, :] = mm(high, picked) + mm(middle_part, picked) + mm(low, picked)
    out_s[HEADS * AREA :, :] = jnp.zeros((8 * HEADS, QUERIES), f32)
    for head in range(HEADS):
        lanes = slice(QUERIES * (head % 4), QUERIES * (head % 4 + 1))
        place_ref[head // 4, 0:AREA, lanes] = out_s[pl.ds(head, AREA, stride=HEADS), :]
        place_ref[head // 4, AREA:KEYS, lanes] = jnp.zeros((KEYS - AREA, QUERIES), f32)
    save.wait()


def expand(params, hat):
    return kernel_call(
        expand_body,
        (1,),
        [RESIDENT, RESIDENT],
        [RESIDENT, ANYWHERE],
        [shape_of((QUADS, KEYS, LANES), f32), pltpu.HBM(hat.shape, bf16)],
        [pltpu.VMEM((HEADS * AREA, 384), f32), pltpu.VMEM((HEADS * (AREA + 8), QUERIES), f32), pltpu.SemaphoreType.DMA],
        room=16,
    )(params, hat)


def fold_place(place_ref, stage_s):
    spread = spread_matrix().astype(bf16)
    lines = []
    for head in range(HEADS):
        stage = stage_s.at[head]
        rows = place_ref[head // 4, :, QUERIES * (head % 4) : QUERIES * (head % 4 + 1)]
        rows = jnp.concatenate([rows, jnp.zeros((QUERIES - KEYS, QUERIES), f32)], axis=0).T[:KEYS]
        high = rows.astype(bf16)
        rest = (rows - high.astype(f32)).astype(bf16)
        stage[...] = mm(high, spread) + mm(rest, spread)
        total = jnp.zeros((WINDOW, 384), f32)
        for y in range(WINDOW):
            part = jnp.concatenate(
                [stage[pl.ds(WINDOW * y, WINDOW), :], jnp.zeros((WINDOW, 128), f32)], axis=1
            )
            total += pltpu.roll(part, SIDE * (WINDOW - 1 - y), 1) if y < WINDOW - 1 else part
        line = total[WINDOW - 1 : WINDOW, :]
        for x in range(WINDOW - 1):
            line += pltpu.roll(total[x : x + 1, :], WINDOW - 1 - x, 1)
        lines.append(line)
    return jnp.concatenate(lines, axis=0)


class Ring:
    def __init__(self, place, rows_size):
        self.place = place
        self.rows_size = rows_size
        self.along = rows_size // 4

    def to(self, array, bits):
        return lax.ppermute(array, "rows", [(i, i ^ bits) for i in range(self.rows_size)])

    def core(self, array):
        return self.to(array, 1)

    def x(self, array):
        return self.to(array, 2)

    def z(self, array, step):
        return self.to(array, 4 * step)

    def y(self, array):
        return lax.ppermute(array, "tp", [(0, 1), (1, 0)])

    def xy(self, array):
        pairs = [(2 * i + t, 2 * (i ^ 2) + 1 - t) for i in range(self.rows_size) for t in range(2)]
        return lax.ppermute(array, ("rows", "tp"), pairs)


def rows_of(array, begin, rows):
    return lax.dynamic_slice_in_dim(array, begin, rows, 0).astype(f32)


def stage(body, place, after, rows, *operands, cost=COST, scratch=()):
    return plain_call_after(
        body, [pltpu.VMEM((count, D), bf16) for count in rows], place, after, operands, room=STAGE_ROOM, cost=cost,
        scratch=scratch,
    )


def added(refs, begin, rows):
    here = pl.ds(pl.multiple_of(begin, 16), rows)
    total = refs[0][here, :].astype(f32)
    for ref in refs[1:]:
        total = total + ref[here, :].astype(f32)
    return total


def part(ref, begin, rows):
    return ref.at[begin : begin + rows, :]


FEED_BLOCKS = ((0, 256), (256, 256), (512, 64))


def feed_first_body(place, own_keep, own_got, other_keep, other_got, to_y, to_x, to_both, kept):
    x = place[1]
    own, other = (own_keep, own_got), (other_keep, other_got)
    for target, blocks, side in ((to_y, other, x), (to_x, own, 1 - x), (to_both, other, 1 - x), (kept, own, x)):
        target[0:256, :] = added(blocks, 256 * side, 256).astype(bf16)
        target[256:512, :] = added(blocks, 512 + 256 * side, 256).astype(bf16)


def feed_proj_body(place, keep, got, *refs):
    x = place[1]
    for target, shard, side in zip(refs[-4:], (1, 0, 1, 0), (x, 1 - x, 1 - x, x)):
        target[512:576, :] = added((keep, got), PROJ_PACK * shard + 64 * side, 64).astype(bf16)


def feed_proj(place, keep, got, outs):
    return pl.pallas_call(
        feed_proj_body,
        in_specs=[SCALARS] + [RESIDENT] * 6,
        out_specs=[RESIDENT] * 4,
        out_shape=[pltpu.VMEM(out.shape, bf16) for out in outs],
        input_output_aliases={3: 0, 4: 1, 5: 2, 6: 3},
        compiler_params=pltpu.CompilerParams(vmem_limit_bytes=STAGE_ROOM * 1024 * 1024),
        cost_estimate=COST,
    )(place, keep, got, *outs)


def feed_second_body(place, *refs):
    blocks, outs = refs[:4], refs[4:]
    for step, out in enumerate(outs):
        offset = 0
        for begin, size in FEED_BLOCKS:
            span = size // len(outs)
            to = begin + (place[2] ^ step) * span
            out[offset : offset + span, :] = added(blocks, to, span).astype(bf16)
            offset += span


def total_body(place, *refs):
    refs[-1][...] = added(refs[:-1], 0, refs[-1].shape[0]).astype(bf16)


def beside_body(place, *refs):
    rows = refs[0].shape[0]
    for index, ref in enumerate(refs[:-1]):
        refs[-1][rows * index : rows * (index + 1), :] = ref[...]


def qkv_first_body(place, keep, got, to_y, to_x, to_both, kept):
    x = place[1]
    for target, other, side in ((to_y, 1, x), (to_x, 0, 1 - x), (to_both, 1, 1 - x), (kept, 0, x)):
        target[...] = added((keep, got), QKV_PACK * other + 192 * side, 192).astype(bf16)


def merge_first_body(place, keep, got, to_y, to_x, to_both, kept, sums_s):
    x = place[1]
    sums_s[...] = joined(keep[512:544, :]) + joined(got[512:544, :])
    for target, other, side in ((to_y, 1, x), (to_x, 0, 1 - x), (to_both, 1, 1 - x), (kept, 0, x)):
        target[0:128, :] = added((keep, got), MERGE_PACK * other + 128 * side, 128).astype(bf16)
        target[128:144, :] = split(sums_s[pl.ds(pl.multiple_of(8 * side, 8), 8), :])


def last_second_body(place, qkv_sum, *refs):
    blocks, outs = refs[:4], refs[4:]
    vectors = split(sum(joined(ref[128:144, :]) for ref in blocks))
    wide, narrow = 192 // len(outs), 128 // len(outs)
    for step, out in enumerate(outs):
        to = place[2] ^ step
        out[0:wide, :] = added((qkv_sum,), to * wide, wide).astype(bf16)
        out[wide : wide + narrow, :] = added(blocks, to * narrow, narrow).astype(bf16)
        out[wide + narrow :, :] = vectors


def merge_total_body(place, *refs):
    blocks, (out, vectors) = refs[:-2], refs[-2:]
    rows = out.shape[0]
    out[...] = added(blocks, 0, rows).astype(bf16)
    vectors[...] = split(sum(joined(ref[rows : rows + 16, :]) for ref in blocks))


def last_beside_body(place, vectors, *refs):
    rows = refs[0].shape[0]
    for index, ref in enumerate(refs[:-1]):
        refs[-1][rows * index : rows * (index + 1), :] = ref[...]
    refs[-1][rows * (len(refs) - 1) :, :] = vectors[...]


def in_order(place, near, far, stage, rows, along):
    piece = sum(rows) // 2 // along
    for side, ref in ((place[1], near), (1 - place[1], far)):
        for step in range(along):
            begin, offset = 0, piece * step
            for size in rows:
                span = size // 2 // along
                to = begin + side * (size // 2) + (place[2] ^ step) * span
                stage[pl.ds(pl.multiple_of(to, 16), span), :] = ref[offset : offset + span, :]
                begin += size
                offset += span


def feed_unpack_body(along, place, near, far, core_near, core_far, down_ref, up_ref, proj_ref, token_ref, stage):
    token_ref[...] = jnp.zeros_like(token_ref)
    for target, mine, beside in ((place[0], near, far), (1 - place[0], core_near, core_far)):
        in_order(place, mine, beside, stage, (512, 512, PROJ_PACK), along)
        wide = pl.ds(pl.multiple_of(512 * target, 512), 512)
        down_ref[wide, :] = stage[0:512, :].astype(f32)
        proj_ref[pl.ds(pl.multiple_of(128 * target, 128), 128), :] = stage[1024:1152, :].astype(f32)
        up_ref[:, wide] = stage[512:1024, :].astype(f32)


def feed_unpack(along, place, after, parts):
    return plain_call_after(
        partial(feed_unpack_body, along),
        [pltpu.HBM((FFN // 2, D), f32), pltpu.HBM((D, FFN // 2), f32), pltpu.HBM((D // 2, D), f32), shape_of((8, 128), f32)],
        place,
        after,
        parts,
        scratch=[pltpu.VMEM((FEED_PACK + PROJ_PACK, D), bf16)],
        room=14,
    )


def last_unpack_body(along, place, mine, beside, core_mine, core_beside, qkv_ref, merge_ref, *refs):
    vectors, stage, all_s = refs[:-2], refs[-2], refs[-1]
    rows = mine.shape[0] - 16
    for target, near, far in ((place[0], mine, beside), (1 - place[0], core_mine, core_beside)):
        in_order(place, near, far, stage, (QKV_PACK, MERGE_PACK), along)
        for side, ref in ((place[1], near), (1 - place[1], far)):
            all_s[pl.ds(pl.multiple_of(SUMS * target + 8 * side, 8), 8), :] = joined(ref[rows:, :])
        begin = pl.multiple_of(256 * target, 256)
        for part in range(2):
            qkv_ref[part, pl.ds(begin, 256), :] = stage[0:256, 256 * part : 256 * part + 256].astype(f32)
        qkv_ref[2, pl.ds(begin, 128), :] = stage[256:384, 0:256].astype(f32)
        qkv_ref[2, pl.ds(begin + 128, 128), :] = stage[256:384, 256:512].astype(f32)
        merge_ref[pl.ds(begin, 256), :] = stage[384:640, :].astype(f32)
    write_vectors(place[3], all_s, vectors)


VECTORS = [(1, D)] * 6 + [(2, D // 2), (1, FFN // 2), (1, MERGE_IN // 2), (1, MERGE_IN // 2), (HEADS // 2, SIDE * SIDE)]


def write_vectors(tp, sums, refs):
    for row in range(6):
        refs[row][...] = sums[row : row + 1, :]
    columns = pl.ds(pl.multiple_of(256 * tp, 256), 256)
    refs[6][...] = sums[6:8, columns]
    refs[7][:, 0:512] = sums[pl.ds(8 + 2 * tp, 1), :]
    refs[7][:, 512:1024] = sums[pl.ds(9 + 2 * tp, 1), :]
    refs[8][...] = sums[pl.ds(12 + tp, 1), :]
    refs[9][...] = sums[pl.ds(14 + tp, 1), :]
    refs[10][...] = sums[pl.ds(pl.multiple_of(16 + 8 * tp, 8), 8), 0 : SIDE * SIDE]


def last_unpack(along, place, *parts):
    outs = plain_call(
        partial(last_unpack_body, along),
        [pltpu.HBM(shape, f32) if shape[-2] >= 128 else shape_of(shape, f32) for shape in [(3, D, D // 2), (MERGE_IN // 2, D)] + VECTORS],
        (place, *parts),
        scratch=[pltpu.VMEM((QKV_PACK + MERGE_PACK, D), bf16), pltpu.VMEM((2 * SUMS, D), f32)],
    )
    return outs[0], outs[1], outs[2:]


def fetch_by_tp(ring, piece_of):
    near = ring.y(piece_of)
    return near, ring.core(near)


def plain_pieces(tp_size, weights, params):
    merge, qkv, proj, up, down = [
        lax.all_gather(array, "tp", axis=axis, tiled=True) for array, axis in zip(weights, (0, 2, 0, 1, 0))
    ]
    gain, bias, qv, up_bias, table = [
        lax.all_gather(array, "tp", axis=axis, tiled=True) for array, axis in zip(params, (0, 0, 1, 0, 1))
    ]

    def shard(array, axis, which):
        size = array.shape[axis] // 2
        return lax.slice_in_dim(array, which * size, (which + 1) * size, axis=axis)

    def rows_of(which):
        rows = jnp.zeros((PARAMS, D), f32)
        rows = rows.at[0].set(shard(gain.astype(f32), 0, which)).at[1].set(shard(bias.astype(f32), 0, which))
        rows = rows.at[2].set(shard(qv, 1, which).reshape(-1)).at[3:5].set(shard(up_bias, 0, which).reshape(2, D))
        return rows.at[8:16, : SIDE * SIDE].set(shard(table, 1, which).T)

    merge_other = shard(merge, 0, 1)
    qkv_other = shard(qkv, 2, 1).reshape(3 * D, 256)
    proj_other, up_other, down_other = shard(proj, 0, 1), shard(up, 1, 1), shard(down, 0, 1)

    def qkv_piece(half):
        rows = qkv_other[768 * half : 768 * half + 768]
        return jnp.concatenate(
            [jnp.concatenate([rows[:384], rows[384:]], axis=1), proj_other[128 * half : 128 * half + 128]], axis=0
        )

    def feed_piece(half):
        tile = slice(512 * half, 512 * half + 512)
        return jnp.concatenate([down_other[tile], up_other[:, tile]], axis=0)

    own = (
        shard(merge, 0, 0), shard(qkv, 2, 0).reshape(3 * D, 256), shard(proj, 0, 0), shard(up, 1, 0), shard(down, 0, 0)
    )
    return own, (rows_of(0), split(rows_of(1))), (merge_other[:256], merge_other[256:]), (qkv_piece(0), qkv_piece(1)), (feed_piece(0), feed_piece(1))


def sum_plainly(tp_size, feed_packs, proj_packs, qkv_packs, merge_packs):
    feed_packs, proj_packs, qkv_packs, merge_packs = lax.psum(
        (feed_packs, proj_packs, qkv_packs, merge_packs), ("rows", "tp")
    )
    own_send, own_keep, other_send, other_keep = feed_packs
    order = [own_keep, own_send, other_keep, other_send]
    down = jnp.concatenate([block[0:512] for block in order], axis=0)
    up = jnp.concatenate([block[512:1024] for block in order], axis=1)

    def blocks(packs, size):
        send, keep = packs
        return [keep[:size], send[:size], keep[size : 2 * size], send[size : 2 * size]]

    def qkv_rows(block):
        return jnp.stack(
            [block[0:256, 0:256], block[0:256, 256:512], jnp.concatenate([block[256:384, 0:256], block[256:384, 256:512]])]
        )

    order = blocks(qkv_packs, QKV_PACK)
    qkv = jnp.concatenate(
        [jnp.concatenate([qkv_rows(order[2 * shard + half]) for half in range(2)], axis=1) for shard in range(2)], axis=2
    )
    proj = jnp.concatenate(blocks(proj_packs, PROJ_PACK), axis=0)
    merge = jnp.concatenate(blocks(merge_packs, MERGE_PACK), axis=0)
    sums = jnp.concatenate([joined(merge_packs[1][2 * MERGE_PACK :]), joined(merge_packs[0][2 * MERGE_PACK :])], axis=0)
    index = lax.axis_index("tp")

    def own(array, axis):
        size = array.shape[axis] // tp_size
        return lax.dynamic_slice_in_dim(array, index * size, size, axis).astype(f32)

    vectors = [sums[row] for row in range(6)] + [
        own(sums[6:8], 1), own(sums[8:12].reshape(-1), 0), own(sums[12:14].reshape(-1), 0),
        own(sums[14:16].reshape(-1), 0), own(sums[16:32, : SIDE * SIDE], 0),
    ]
    return own(down, 0), own(up, 1), own(qkv, 2), own(proj, 0), own(merge, 0), vectors


def per_device(
    rows_size, tp_size,
    section_rows, window_mask, cotangent, merge_weight, merge_gain, merge_bias, norm1_gain, norm1_bias,
    qkv_weight, qv_bias, bias_table, proj_weight, proj_bias, norm2_gain, norm2_bias,
    up_weight, up_bias, down_weight, down_bias,
):
    fast = tp_size == 2 and rows_size in (8, 16)
    count = cotangent.shape[0]
    index, tp = lax.axis_index("rows"), lax.axis_index("tp")
    place = jnp.stack([index & 1, (index >> 1) & 1, index >> 2, tp]).astype(jnp.int32)
    ring = Ring(place, rows_size)
    if fast:
        flat_qkv = qkv_weight.reshape(3 * D, D // 2)
        merge_piece = pack_merge(place, merge_weight)
        merge_near = ring.y(merge_piece)
        params, piece = pack_params(
            place, merge_piece, merge_gain, merge_bias, qv_bias, up_bias[None], bias_table.T
        )
        others = ring.y(piece)
        mask, live = masks_of(place, params, window_mask, count)
        qkv_piece = gate(pack_qkv(place, (mask,), flat_qkv, proj_weight), others, merge_near)
        qkv_near = ring.y(qkv_piece)
        hat, inverse = section_norm(qkv_piece, section_rows)
        merge_far = ring.core(merge_near)
        kernel_place = place
    else:
        (merge_weight, flat_qkv, proj_weight, up_weight, down_weight), (params, others), merge_pair, qkv_pair, feed_pair = plain_pieces(
            tp_size,
            (merge_weight, qkv_weight, proj_weight, up_weight, down_weight),
            (merge_gain, merge_bias, qv_bias, up_bias, bias_table),
        )
        (merge_near, merge_far), (qkv_near, qkv_far), (feed_near_piece, feed_far_piece) = merge_pair, qkv_pair, feed_pair
        kernel_place = jnp.zeros_like(place)
        hat, inverse = section_norm(params, section_rows)
        own_mask = lax.dynamic_slice_in_dim(window_mask, tp * count, count, 0)
        mask, live = masks_of(kernel_place, params, own_mask, count)

    merged, first, first_copy, merge_full, params, column = merge_rows(
        kernel_place, hat, merge_weight, merge_near, merge_far, params, others, norm1_gain[None], norm1_bias[None]
    )
    position, hat = expand(params, hat)
    if fast:
        (feed_piece,) = plain_call_after(
            pack_feed_body, [shape_of((FEED_PACK, D), bf16)], place, (position, qkv_near), (up_weight, down_weight)
        )
        qkv_far = ring.core(qkv_near)
        feed_near_piece = ring.y(feed_piece)
        feed_far_piece = ring.core(feed_near_piece)
    qkv_rows, weights, attended, padded, inverse_sums, qkv_full = attend(
        kernel_place, first, flat_qkv, qkv_near, qkv_far, params, position, mask
    )
    rows = [row[None] for row in (proj_bias, norm2_gain, norm2_bias, down_bias)]
    second_hat, second_inverse, total, back, second, turned, branch, own_send, feed_sums, proj_full = feed_own(
        kernel_place, attended, merged, cotangent, live, *rows, params, proj_weight, qkv_near, qkv_far,
        up_weight, down_weight,
    )
    total, back, own_keep, feed_sums = feed_middle(
        True, kernel_place, second, turned, branch, total, back, params, feed_sums, (up_weight, down_weight), LONG
    )
    total, back, other_send, feed_sums = feed_middle(
        False, kernel_place, second, turned, branch, total, back, params, feed_sums, (feed_far_piece,)
    )
    block_out, grad_residual, attn, other_keep, proj_send, proj_keep, feed_sums = feed_near(
        kernel_place, second_hat, second_inverse, second, turned, branch, total, back, rows[1], params, feed_sums, feed_near_piece,
        attended,
    )
    after = feed_sums
    if fast:
        own_got, other_got, proj_got = ring.core(own_send), ring.core(other_send), ring.core(proj_send)
        outs = stage(feed_first_body, place, feed_sums, (576,) * 4, own_keep, own_got, other_keep, other_got)
        to_y, to_x, to_both, feed_kept = feed_proj(place, proj_keep, proj_got, outs)
        feed_from = (ring.y(to_y), ring.x(to_x), ring.xy(to_both))
        after = to_y
    stack, low, sums, vectors, position_grad, first_near = attend_back(
        after, attn, qkv_rows, weights, padded, inverse_sums, proj_full, merged, grad_residual, qkv_full,
        norm1_gain[None], first_copy,
    )
    qkv_send, qkv_keep, hat_near = qkv_back(kernel_place, sums, first_near, stack, hat)
    after = sums
    if fast:
        along = ring.along
        qkv_got = ring.core(qkv_send)
        span = 576 // along
        feed_parts = stage(
            feed_second_body, place, qkv_send, (span,) * along, feed_kept, *feed_from, cost=LONG
        )
        feed_got = [ring.z(feed_parts[step], step) for step in range(1, along)]
        to_y, to_x, to_both, qkv_kept = stage(
            qkv_first_body, place, feed_parts[0], (192,) * 4, qkv_keep, qkv_got
        )
        qkv_from = (ring.y(to_y), ring.x(to_x), ring.xy(to_both))
        after = to_y
    merge_send, merge_keep = merge_back(
        kernel_place, after, low, hat_near, merge_full, params, column, feed_sums, sums, vectors, position_grad
    )
    if fast:
        merge_got = ring.core(merge_send)
        (feed_total,) = stage(total_body, place, merge_send, (span,), feed_parts[0], *feed_got, cost=LONG)
        feed_all = [feed_total] + [ring.z(feed_total, step) for step in range(1, along)]
        (qkv_sum,) = stage(total_body, place, feed_total, (192,), qkv_kept, *qkv_from)
        to_y, to_x, to_both, merge_kept = stage(
            merge_first_body, place, qkv_sum, (144,) * 4, merge_keep, merge_got, scratch=[pltpu.VMEM((SUMS, D), f32)]
        )
        (feed_mine,) = stage(beside_body, place, to_y, (span * along,), *feed_all)
        feed_beside = ring.x(feed_mine)
        last_span = 320 // along
        last_parts = stage(
            last_second_body, place, feed_mine, (last_span + 16,) * along, qkv_sum,
            merge_kept, ring.y(to_y), ring.x(to_x), ring.xy(to_both),
        )
        last_got = [ring.z(last_parts[step], step) for step in range(1, along)]
        last_total, vectors = stage(
            merge_total_body, place, last_parts[0], (last_span, 16), *([last_parts[0]] + last_got), cost=LONG
        )
        last_all = [last_total] + [ring.z(last_total, step) for step in range(1, along)]
        steps = count // ROWS
        section_grad, token = section_back(last_total, None, low, hat, inverse, merge_full, params, 0, steps // 2)
        (last_near,) = stage(
            last_beside_body, place, (token, feed_beside), (336,), vectors, *last_all, cost=LONG
        )
        last_far = ring.x(last_near)
        feed_cores = ring.core(feed_mine), ring.core(feed_beside)
        section_grad, token = section_back(
            last_near, section_grad, low, hat, inverse, merge_full, params, steps // 2, steps - steps // 2
        )
        down_grad, up_grad, proj_grad, token = feed_unpack(
            along, place, token, (feed_mine, feed_beside, *feed_cores)
        )
        (last_far,) = stage(beside_body, place, token, (336,), last_far)
        qkv_grad, merge_grad, vectors = last_unpack(
            along, place, last_near, last_far, ring.core(last_near), ring.core(last_far)
        )
    else:
        section_grad, _ = section_back(low, None, low, hat, inverse, merge_full, params, 0, count // ROWS)
        down_grad, up_grad, qkv_grad, proj_grad, merge_grad, vectors = sum_plainly(
            tp_size, (own_send, own_keep, other_send, other_keep), (proj_send, proj_keep), (qkv_send, qkv_keep),
            (merge_send, merge_keep),
        )
    norm1_gain_grad, norm1_bias_grad, proj_bias_grad, norm2_gain_grad, norm2_bias_grad, down_bias_grad = [
        row.reshape(D) for row in vectors[0:6]
    ]
    qv_grad, up_bias_grad, gain_grad, bias_grad, table_grad = vectors[6:]
    return (
        block_out, section_grad, merge_grad, gain_grad.reshape(-1), bias_grad.reshape(-1),
        norm1_gain_grad, norm1_bias_grad, qkv_grad, qv_grad, table_grad.T, proj_grad, proj_bias_grad,
        norm2_gain_grad, norm2_bias_grad, up_grad, up_bias_grad.reshape(-1), down_grad, down_bias_grad,
    )


def solution(mesh):
    rows_size, tp_size = mesh.shape["rows"], mesh.shape["tp"]
    both = ("rows", "tp")
    return jax.shard_map(
        partial(per_device, rows_size, tp_size),
        mesh=mesh,
        in_specs=(
            P(both, None), P("rows"), P(both, None), P("tp", None), P("tp"), P("tp"), P(), P(),
            P(None, None, "tp"), P(None, "tp"), P(None, "tp"), P("tp", None), P(), P(), P(),
            P(None, "tp"), P("tp"), P("tp", None), P(),
        ),
        out_specs=(
            P(both, None), P(both, None), P("tp", None), P("tp"), P("tp"), P(), P(),
            P(None, None, "tp"), P(None, "tp"), P(None, "tp"), P("tp", None), P(), P(), P(),
            P(None, "tp"), P("tp"), P("tp", None), P(),
        ),
        check_vma=False,
    )
```

```python
from functools import partial
import math

import jax
import jax.numpy as jnp
from jax import lax
from jax.experimental import pallas as pl
from jax.experimental.pallas import tpu as pltpu
from jax.sharding import PartitionSpec as P

MERGE_IN = 1024
D = 512
HEADS = 16
HEAD_DIM = 32
FFN = 2048
WINDOW = 10
AREA = WINDOW * WINDOW
SIDE = 2 * WINDOW - 1
EPSILON = 1e-05
MASKED_SCORE = -1e30
EXACT = lax.Precision.HIGHEST
SCALING = 1.0 / math.sqrt(HEAD_DIM)
GROUP = 4
ROWS = GROUP * AREA
KEYS = 112
QUERIES = 128
QUADS = 4
QUAD = 4 * HEAD_DIM
LANES = 4 * QUERIES

bf16 = jnp.bfloat16
f32 = jnp.float32


def mm(a, b):
    return jnp.dot(a, b, preferred_element_type=f32)


def mm_t(a, b):
    return lax.dot_general(a, b, (((1,), (1,)), ((), ())), preferred_element_type=f32)


def t_mm(a, b):
    return lax.dot_general(a, b, (((0,), (0,)), ((), ())), preferred_element_type=f32)


def normalize(values):
    center = jnp.mean(values, axis=-1, keepdims=True)
    spread = jnp.mean(values * values, axis=-1, keepdims=True) - center * center
    inverse = lax.rsqrt(spread + EPSILON)
    return (values - center) * inverse, inverse


def norm_back(grad_hat, normed, inverse):
    first_mean = jnp.mean(grad_hat, axis=-1, keepdims=True)
    second_mean = jnp.mean(grad_hat * normed, axis=-1, keepdims=True)
    return inverse * (grad_hat - first_mean - normed * second_mean)


def column_sum(values):
    return jnp.sum(values, axis=0, keepdims=True)


def head_masks():
    lane = lax.broadcasted_iota(jnp.int32, (1, QUAD), 1) // HEAD_DIM
    return [(lane == head).astype(f32).astype(bf16) for head in range(4)]


def spread_heads(rows, masks):
    return jnp.concatenate([rows * mask for mask in masks], axis=0)


def kernel_call(body, grid, in_specs, out_specs, out_shape, scratch=(), flops=0, moved=0, room=32, cost=None):
    return pl.pallas_call(
        body,
        grid=grid,
        in_specs=in_specs,
        out_specs=out_specs,
        out_shape=out_shape,
        scratch_shapes=list(scratch),
        compiler_params=pltpu.CompilerParams(
            dimension_semantics=("arbitrary",) * len(grid), vmem_limit_bytes=room * 1024 * 1024
        ),
        cost_estimate=cost or COST,
    )


def whole(shape):
    return pl.BlockSpec(shape, lambda *_: (0,) * len(shape), pipeline_mode=pl.Buffered(1))


def by_rows(rows, columns):
    return pl.BlockSpec((rows, columns), lambda i: (i, 0))


def by_windows(shape):
    return pl.BlockSpec((GROUP,) + shape, lambda i: (i,) + (0,) * len(shape))


SCALARS = pl.BlockSpec(memory_space=pltpu.SMEM)
RESIDENT = pl.BlockSpec(memory_space=pltpu.VMEM)
ANYWHERE = pl.BlockSpec(memory_space=pl.ANY)


def in_hbm(array):
    return pltpu.with_memory_space_constraint(array, pltpu.HBM)


FEED_PACK = 1024
QKV_PACK = 384
PROJ_PACK = 128
MERGE_PACK = 256
STAGE_ROOM = 9
COST = pl.CostEstimate(flops=1, bytes_accessed=1, transcendentals=0)
LONG = pl.CostEstimate(flops=10**12, bytes_accessed=1, transcendentals=0)
SUMS = 16
PARAMS = 16


def shape_of(shape, dtype):
    return jax.ShapeDtypeStruct(shape, dtype)


def split(rows):
    high = rows.astype(bf16).astype(f32)
    return jnp.concatenate([high, rows - high], axis=0).astype(bf16)


def joined(pair):
    half = pair.shape[0] // 2
    return pair[:half].astype(f32) + pair[half:].astype(f32)


def both_shards(tp, mine, other, axis):
    return jnp.where(
        tp == 0, jnp.concatenate([mine, other], axis=axis), jnp.concatenate([other, mine], axis=axis)
    )


def pack_merge_body(place, merge_ref, out_ref, sem):
    half = pl.ds(pl.multiple_of(256 * place[0], 256), 256)
    copy = pltpu.make_async_copy(merge_ref.at[half, :], out_ref, sem)
    copy.start()
    copy.wait()


def pack_merge(place, merge):
    return pl.pallas_call(
        pack_merge_body,
        in_specs=[SCALARS, ANYWHERE],
        out_specs=RESIDENT,
        out_shape=pltpu.VMEM((256, D), bf16),
        scratch_shapes=[pltpu.SemaphoreType.DMA],
        compiler_params=pltpu.CompilerParams(vmem_limit_bytes=4 * 1024 * 1024),
        cost_estimate=COST,
    )(place, in_hbm(merge))


def pack_params_body(
    place, after, gain_ref, bias_ref, qv_ref, up_bias_ref, table_ref,
    params_ref, out_ref, gain_s, bias_s, qv_s, up_bias_s, table_s, sems,
):
    pairs = (
        (gain_ref, gain_s), (bias_ref, bias_s), (qv_ref, qv_s), (up_bias_ref, up_bias_s), (table_ref, table_s)
    )
    copies = [pltpu.make_async_copy(source, target, sems.at[index]) for index, (source, target) in enumerate(pairs)]
    for copy in copies:
        copy.start()
    params_ref[...] = jnp.zeros_like(params_ref)
    for copy in copies:
        copy.wait()
    params_ref[0:1, :] = gain_s[...].astype(f32).reshape(1, D)
    params_ref[1:2, :] = bias_s[...].astype(f32).reshape(1, D)
    params_ref[2:3, 0:256] = qv_s[0:1, :]
    params_ref[2:3, 256:512] = qv_s[1:2, :]
    params_ref[3:4, :] = up_bias_s[:, 0:512]
    params_ref[4:5, :] = up_bias_s[:, 512:1024]
    params_ref[8:16, 0 : SIDE * SIDE] = table_s[...]
    out_ref[...] = split(params_ref[...])


def pack_params(place, after, *operands):
    operands = [in_hbm(array) for array in operands]
    return pl.pallas_call(
        pack_params_body,
        in_specs=[SCALARS] + [ANYWHERE] * 6,
        out_specs=[RESIDENT] * 2,
        out_shape=[pltpu.VMEM((PARAMS, D), f32), pltpu.VMEM((2 * PARAMS, D), bf16)],
        scratch_shapes=[pltpu.VMEM(array.shape, array.dtype) for array in operands] + [pltpu.SemaphoreType.DMA((5,))],
        compiler_params=pltpu.CompilerParams(vmem_limit_bytes=4 * 1024 * 1024),
        cost_estimate=COST,
    )(place, after, *operands)


def plain_call(body, outs, operands, room=16, scratch=(), flops=0):
    return pl.pallas_call(
        body,
        in_specs=[SCALARS] + [pl.BlockSpec(memory_space=pltpu.VMEM)] * (len(operands) - 1),
        out_specs=[pl.BlockSpec(memory_space=pltpu.VMEM)] * len(outs),
        out_shape=outs,
        scratch_shapes=list(scratch),
        compiler_params=pltpu.CompilerParams(vmem_limit_bytes=room * 1024 * 1024),
        cost_estimate=COST,
    )(*operands)


def pack_qkv_body(place, qkv_ref, proj_ref, *refs):
    out, qkv_s, proj_s, sems = refs[-4:]
    core = place[0]
    copies = [
        pltpu.make_async_copy(qkv_ref.at[pl.ds(pl.multiple_of(768 * core, 256), 768), :], qkv_s, sems.at[0]),
        pltpu.make_async_copy(proj_ref.at[pl.ds(pl.multiple_of(128 * core, 128), 128), :], proj_s, sems.at[1]),
    ]
    for copy in copies:
        copy.start()
    for copy in copies:
        copy.wait()
    for side in range(2):
        out[0:384, 256 * side : 256 * side + 256] = qkv_s[384 * side : 384 * side + 384, :]
    out[384:512, :] = proj_s[...]


def pack_qkv(place, after, qkv, proj):
    return pl.pallas_call(
        pack_qkv_body,
        in_specs=[SCALARS] + [ANYWHERE] * (2 + len(after)),
        out_specs=RESIDENT,
        out_shape=pltpu.VMEM((QKV_PACK + PROJ_PACK, D), bf16),
        scratch_shapes=[
            pltpu.VMEM((768, 256), bf16), pltpu.VMEM((128, D), bf16), pltpu.SemaphoreType.DMA((2,)),
        ],
        compiler_params=pltpu.CompilerParams(vmem_limit_bytes=4 * 1024 * 1024),
        cost_estimate=COST,
    )(place, in_hbm(qkv), in_hbm(proj), *after)


def pack_feed_body(place, up_ref, down_ref, out):
    half = pl.ds(pl.multiple_of(512 * place[0], 512), 512)
    out[0:512, :] = down_ref[half, :]
    out[512:1024, :] = up_ref[:, half]


def plain_call_after(body, outs, place, after, operands, room=16, scratch=(), flops=0, cost=COST):
    after = after if isinstance(after, tuple) else (after,)

    def without_after(place, *refs):
        return body(place, *refs[len(after) :])

    return pl.pallas_call(
        without_after,
        in_specs=[SCALARS] + [pl.BlockSpec(memory_space=pl.ANY)] * len(after) + [pl.BlockSpec(memory_space=pltpu.VMEM)] * len(operands),
        out_specs=[pl.BlockSpec(memory_space=pltpu.VMEM)] * len(outs),
        out_shape=outs,
        scratch_shapes=list(scratch),
        compiler_params=pltpu.CompilerParams(vmem_limit_bytes=room * 1024 * 1024),
        cost_estimate=cost,
    )(place, *after, *operands)


def nothing(array_ref, *refs):
    pass


def gate(array, *after):
    return pl.pallas_call(
        nothing,
        in_specs=[RESIDENT] + [ANYWHERE] * len(after),
        out_specs=RESIDENT,
        out_shape=pltpu.VMEM(array.shape, array.dtype),
        input_output_aliases={0: 0},
        compiler_params=pltpu.CompilerParams(vmem_limit_bytes=4 * 1024 * 1024),
        cost_estimate=COST,
    )(array, *after)


def masks_body(place, window_in, mask_ref, live_ref, stage, window_s, sem):
    copy = pltpu.make_async_copy(window_in, window_s, sem)
    copy.start()
    copy.wait()
    window_ref = window_s[...].reshape(1, window_s.shape[0])
    windows = mask_ref.shape[0]
    shards = window_ref.shape[1] // (windows * AREA)
    stage[...] = jnp.zeros_like(stage)
    for window in range(windows):
        patch = window_ref[:, AREA * window : AREA * (window + 1)]
        for shard in range(1, shards):
            begin = AREA * (windows * shard + window)
            patch = jnp.where(place[3] == shard, window_ref[:, begin : begin + AREA], patch)
        stage[window : window + 1, 0:AREA] = patch
    patches = jnp.minimum(stage[...], 1).astype(f32)
    live = jnp.max(patches, axis=1, keepdims=True)
    inside = lax.broadcasted_iota(jnp.int32, (windows, QUERIES), 1) < AREA
    keep = jnp.logical_and(jnp.maximum(patches, 1.0 - live) > 0.5, inside)
    added = jnp.where(keep, 0.0, MASKED_SCORE)
    for window in range(windows):
        mask_ref[window] = added[window : window + 1, :]
        live_ref[window] = jnp.broadcast_to(live[window : window + 1, :], (1, QUERIES))


def masks_of(place, after, window_mask, count):
    windows = count // AREA
    return pl.pallas_call(
        lambda place, after, *refs: masks_body(place, *refs),
        in_specs=[SCALARS, ANYWHERE, ANYWHERE],
        out_specs=[RESIDENT] * 2,
        out_shape=[pltpu.VMEM((windows, 1, QUERIES), f32)] * 2,
        scratch_shapes=[
            pltpu.VMEM((windows, QUERIES), jnp.int32), pltpu.VMEM(window_mask.shape, jnp.int32), pltpu.SemaphoreType.DMA,
        ],
        compiler_params=pltpu.CompilerParams(vmem_limit_bytes=4 * 1024 * 1024),
        cost_estimate=COST,
    )(place, after, in_hbm(window_mask))


def section_norm_body(after, rows_ref, hat_ref, inverse_ref, rows_s, sems):
    steps = rows_s.shape[0] // ROWS
    copies = []
    for step in range(steps):
        here = slice(ROWS * step, ROWS * (step + 1))
        copies.append(pltpu.make_async_copy(rows_ref.at[here, :], rows_s.at[here, :], sems.at[step]))
        copies[step].start()
    for step in range(steps):
        here = slice(ROWS * step, ROWS * (step + 1))
        copies[step].wait()
        hat, inverse = normalize(rows_s[here, :].astype(f32))
        hat_ref[here, :] = hat.astype(bf16)
        inverse_ref[here, :] = inverse


def section_norm(after, rows):
    count = rows.shape[0]
    return kernel_call(
        section_norm_body,
        (1,),
        [ANYWHERE, ANYWHERE],
        [RESIDENT, RESIDENT],
        [pltpu.VMEM((count, MERGE_IN), bf16), shape_of((count, 1), f32)],
        [pltpu.VMEM((count, MERGE_IN), bf16), pltpu.SemaphoreType.DMA((count // ROWS,))],
        room=16,
    )(after, in_hbm(rows))


def gain_rows(tp, params, others):
    return both_shards(tp, params[0:1], others[0:1], 1), both_shards(tp, params[1:2], others[1:2], 1)


def merge_body(
    place, hat_ref, own_ref, near_ref, far_ref, params_ref, others_ref, norm_gain, norm_bias,
    merged_ref, first_ref, first_copy, merge_ref, params_out_ref, column_ref,
    merge_s, shift_s, gain_s,
):

    @pl.when(pl.program_id(0) == 0)
    def _():
        core, tp = place[0], place[3]
        merge_s[pl.ds(pl.multiple_of(512 * tp, 512), 512), :] = own_ref[...]
        other = 512 * (1 - tp)
        merge_s[pl.ds(pl.multiple_of(other + 256 * core, 256), 256), :] = near_ref[...]
        merge_s[pl.ds(pl.multiple_of(other + 256 * (1 - core), 256), 256), :] = far_ref[...]
        merge_ref[...] = merge_s[...]
        params = params_ref[...]
        others = joined(others_ref[...])
        gain, bias = gain_rows(tp, params, others)
        gain_s[...] = gain.astype(bf16)
        shift_s[...] = mm(jnp.broadcast_to(bias, (16, MERGE_IN)).astype(bf16), merge_s[...])[0:1]
        params_out_ref[0:1, 0:1024] = gain
        params_out_ref[0:1, 1024:2048] = bias
        params_out_ref[1:2, 0:512] = both_shards(tp, params[2:3, 0:256], others[2:3, 0:256], 1)
        params_out_ref[1:2, 512:1024] = both_shards(tp, params[2:3, 256:512], others[2:3, 256:512], 1)
        params_out_ref[1:2, 1024:2048] = jnp.zeros((1, 1024), f32)
        params_out_ref[2:3, :] = both_shards(
            tp,
            jnp.concatenate([params[3:4], params[4:5]], axis=1),
            jnp.concatenate([others[3:4], others[4:5]], axis=1),
            1,
        )
        params_out_ref[3:8, :] = jnp.zeros((5, 2048), f32)
        params_out_ref[8:24, 0:512] = both_shards(tp, params[8:16], others[8:16], 0)
        params_out_ref[8:24, 512:2048] = jnp.zeros((16, 1536), f32)
        column_ref[...] = jnp.broadcast_to(gain, (128, MERGE_IN)).T

    here = pl.ds(pl.multiple_of(pl.program_id(0) * ROWS, 16), ROWS)
    merged = mm(hat_ref[here, :] * gain_s[...], merge_s[...]) + shift_s[...]
    merged_ref[...] = merged
    hat, _ = normalize(merged)
    first = (hat * norm_gain[...] + norm_bias[...]).astype(bf16)
    first_ref[here, :] = first
    first_copy[...] = first


def merge_rows(place, hat, own, near, far, params, others, gain, bias):
    count = hat.shape[0]
    return kernel_call(
        merge_body,
        (count // ROWS,),
        [
            SCALARS, RESIDENT, RESIDENT, RESIDENT, RESIDENT, RESIDENT, RESIDENT, RESIDENT, RESIDENT,
        ],
        [
            by_rows(ROWS, D), RESIDENT, by_rows(ROWS, D), whole((MERGE_IN, D)), RESIDENT,
            whole((MERGE_IN, 128)),
        ],
        [
            pltpu.HBM((count, D), f32), pltpu.VMEM((count, D), bf16), pltpu.HBM((count, D), bf16),
            pltpu.HBM((MERGE_IN, D), bf16),
            shape_of((24, 2048), f32), pltpu.HBM((MERGE_IN, 128), f32),
        ],
        [
            pltpu.VMEM((MERGE_IN, D), bf16), pltpu.VMEM((1, D), f32), pltpu.VMEM((1, MERGE_IN), bf16),
        ],
        flops=2 * count * D * MERGE_IN,
        moved=count * 10 * D + 4 * D * MERGE_IN,
        room=14,
    )(place, hat, own, near, far, params, others, gain, bias)


def value_blocks(values, masks):
    return [jnp.concatenate([values * mask, jnp.broadcast_to(mask, (QUERIES, QUAD))], axis=1) for mask in masks]


def turned_products(turned, scores):
    parts = []
    for pair in range(2):
        both = mm(turned[64 * pair : 64 * pair + 64], scores[:, 256 * pair : 256 * pair + 256])
        parts += [both[0:32, 0:128], both[32:64, 128:256]]
    return jnp.concatenate(parts, axis=0).T


def attend_body(
    place, first_ref, own_ref, near_ref, far_ref, params_ref, position_ref, mask_ref,
    qkv_out_ref, weights_ref, attended_ref, padded_ref, inverse_ref, qkv_ref,
    stage, mixed,
):
    @pl.when(pl.program_id(0) == 0)
    def _():
        core, tp = place[0], place[3]
        other = pl.ds(pl.multiple_of(256 * (1 - tp), 256), 256)
        qkv_ref[:, pl.ds(pl.multiple_of(256 * tp, 256), 256)] = own_ref[...]
        for ref, half in ((near_ref, core), (far_ref, 1 - core)):
            for side in range(2):
                rows = pl.ds(pl.multiple_of(768 * half + 384 * side, 128), 384)
                qkv_ref[rows, other] = ref[0:384, 256 * side : 256 * side + 256]

    here = pl.ds(pl.multiple_of(pl.program_id(0) * ROWS, 16), ROWS)
    stage[pl.ds(0, ROWS), :] = first_ref[here, :].astype(f32)
    stage[pl.ds(ROWS, 32), :] = jnp.zeros((32, D), f32)
    padded = jnp.concatenate(
        [stage[pl.ds(AREA * w, QUERIES), :].astype(bf16) for w in range(GROUP)], axis=0
    )
    queries = (SCALING * (mm(padded, qkv_ref[0:512, :]) + params_ref[1:2, 0:512])).astype(bf16)
    keys = mm(padded, qkv_ref[512:1024, :]).astype(bf16)
    values = (mm(padded, qkv_ref[1024:1536, :]) + params_ref[1:2, 512:1024]).astype(bf16)
    for w in range(GROUP):
        block = slice(QUERIES * w, QUERIES * (w + 1))
        qkv_out_ref[w, :, 0:D] = queries[block]
        qkv_out_ref[w, :, D : 2 * D] = keys[block]
        qkv_out_ref[w, :, 2 * D :] = values[block]
    masks = head_masks()
    for w in range(GROUP):
        mask = mask_ref[w]
        for quad in range(QUADS):
            columns = slice(QUAD * quad, QUAD * (quad + 1))
            rows = QUERIES * w
            spread = spread_heads(keys[rows : rows + QUERIES, columns], masks)
            scores = mm_t(queries[rows : rows + KEYS, columns], spread)
            raised = []
            for head in range(4):
                lanes = slice(QUERIES * head, QUERIES * (head + 1))
                part = scores[:, lanes] + position_ref[quad, :, lanes] + mask
                raised.append(jnp.exp(part - jnp.max(part, axis=1, keepdims=True)).astype(bf16))
            weights = jnp.concatenate(raised, axis=1)
            weights_ref[w, quad] = weights
            blocks = value_blocks(values[rows : rows + QUERIES, columns], masks)
            out = mm(weights, jnp.concatenate(blocks, axis=0))
            inverse = 1.0 / out[:, QUAD:]
            both = out[:, :QUAD] * inverse
            inverse_ref[w, :, columns] = inverse.astype(bf16)
            padded_ref[w, :, columns] = both.astype(bf16)
            mixed[pl.ds(AREA * w, AREA), columns] = both[0:AREA]
    attended_ref[...] = mixed[pl.ds(0, ROWS), :].astype(bf16)


def attend(place, first, own, near, far, params, position, mask):
    count = first.shape[0]
    windows = count // AREA
    return kernel_call(
        attend_body,
        (count // ROWS,),
        [
            SCALARS, RESIDENT, RESIDENT, RESIDENT, RESIDENT, RESIDENT, RESIDENT, by_windows((1, QUERIES)),
        ],
        [
            by_windows((QUERIES, 3 * D)), by_windows((QUADS, KEYS, LANES)), by_rows(ROWS, D),
            by_windows((KEYS, D)), by_windows((KEYS, D)), RESIDENT,
        ],
        [
            pltpu.HBM((windows, QUERIES, 3 * D), bf16), pltpu.HBM((windows, QUADS, KEYS, LANES), bf16),
            pltpu.HBM((count, D), bf16), pltpu.HBM((windows, KEYS, D), bf16), pltpu.HBM((windows, KEYS, D), bf16),
            shape_of((3 * D, D), bf16),
        ],
        [pltpu.VMEM((ROWS + 32, D), f32), pltpu.VMEM((ROWS + 8, D), f32)],
        flops=2 * count * D * (3 * D + 4 * AREA),
        moved=count * 10 * D + windows * QUADS * KEYS * LANES * 2,
        room=20,
    )(place, first, own, near, far, params, position, mask)


def gelu_parts(t):
    chance = 0.5 * lax.erf(t * math.sqrt(0.5)) + 0.5
    density = jnp.exp(t * t * -0.5) * (1.0 / math.sqrt(2.0 * math.pi))
    return t * chance, chance + t * density


TILE = 512
FEED_ROWS = 400
OWN_ROOM = 18
OTHER_ROOM = 12
AB_ROOM = 18
NEAR_ROOM = 20


def feed_tile(up, down, bias, second_ref, turned_ref, branch_ref, total_s, back_s, active_s, raise_s, target, first):
    sums = jnp.zeros((1, TILE), f32)

    def add_products(here, active, grad_raised):
        total_s[here, :] += mm(active, down)
        back = mm_t(grad_raised, up)
        if first:
            back_s[here, :] = back
        else:
            back_s[here, :] += back

    last = None
    for begin in range(0, second_ref.shape[0], FEED_ROWS):
        here = slice(begin, begin + FEED_ROWS)
        value, slope = gelu_parts(mm(second_ref[here, :], up) + bias)
        active = value.astype(bf16)
        grad_raised = (mm_t(branch_ref[here, :], down) * slope).astype(bf16)
        active_s[here, :] = active
        raise_s[here, :] = grad_raised
        sums += column_sum(grad_raised.astype(f32))
        if last is not None:
            add_products(*last)
        last = here, active, grad_raised
    add_products(*last)
    target[0:512, :] = t_mm(active_s[...], branch_ref[...]).astype(bf16)
    target[512:1024, :] = mm(turned_ref[...], raise_s[...]).astype(bf16)
    return sums


def feed_own_body(
    place, attended_ref, merged_ref, cotangent_ref, live_ref, proj_bias, norm_gain, norm_bias, down_bias, params_ref,
    proj_own, near_ref, far_ref, up_own, down_own,
    hat_ref, inverse_ref, total_ref, back_ref, second_ref, turned_ref, branch_ref, send_ref, sums_ref, proj_ref,
    active_s, raise_s,
):
    step = pl.program_id(0)
    blocks = pl.num_programs(0) - 1
    core, tp = place[0], place[3]

    @pl.when(step == 0)
    def _():
        proj_ref[pl.ds(pl.multiple_of(256 * tp, 256), 256), :] = proj_own[...]
        for ref, which in ((near_ref, core), (far_ref, 1 - core)):
            proj_ref[pl.ds(pl.multiple_of(256 * (1 - tp) + 128 * which, 128), 128), :] = ref[384:512, :]
        sums_ref[...] = jnp.zeros_like(sums_ref)

    @pl.when(step < blocks)
    def _():
        here = pl.ds(pl.multiple_of(step * ROWS, 16), ROWS)
        residual = merged_ref[...] + mm(attended_ref[...], proj_ref[...]) + proj_bias[...]
        total_ref[here, :] = residual + down_bias[...]
        hat, inverse = normalize(residual)
        hat_ref[here, :] = hat
        inverse_ref[here, :] = inverse
        second_ref[here, :] = (hat * norm_gain[...] + norm_bias[...]).astype(bf16)
        row = lax.broadcasted_iota(jnp.int32, (ROWS, 1), 0)
        live = live_ref[GROUP - 1, :, 0:1]
        for window in range(GROUP - 2, -1, -1):
            live = jnp.where(row < AREA * (window + 1), live_ref[window, :, 0:1], live)
        branch = cotangent_ref[...].astype(f32) * live
        branch_ref[here, :] = branch.astype(bf16)
        sums_ref[7:8, :] += column_sum(branch)

    @pl.when(step == blocks)
    def _():
        turned_ref[...] = second_ref[...].T
        shard = 2 * tp + 1 - core
        units = pl.ds(pl.multiple_of(TILE * (1 - core), TILE), TILE)
        bias = params_ref[2:3, pl.ds(pl.multiple_of(TILE * shard, TILE), TILE)]
        sums_ref[pl.ds(shard, 1), :] = feed_tile(
            up_own[:, units], down_own[units, :], bias, second_ref, turned_ref, branch_ref, total_ref, back_ref,
            active_s, raise_s, send_ref, True,
        )


def feed_own(
    place, attended, merged, cotangent, live, proj_bias, gain, bias, down_bias, params, proj, near, far, up, down
):
    count = attended.shape[0]
    blocks = count // ROWS

    def taken(columns):
        return pl.BlockSpec((ROWS, columns), lambda i: (jnp.minimum(i, blocks - 1), 0))

    return kernel_call(
        feed_own_body,
        (blocks + 1,),
        [
            SCALARS, taken(D), taken(D), taken(D),
            pl.BlockSpec((GROUP, 1, QUERIES), lambda i: (jnp.minimum(i, blocks - 1), 0, 0)), RESIDENT, RESIDENT, RESIDENT, RESIDENT, RESIDENT, RESIDENT, RESIDENT, RESIDENT,
            RESIDENT, RESIDENT,
        ],
        [RESIDENT] * 10,
        [pltpu.VMEM((count, D), f32), pltpu.VMEM((count, 1), f32)] + [pltpu.VMEM((count, D), f32)] * 2
        + [pltpu.VMEM((count, D), bf16), pltpu.VMEM((D, count), bf16), pltpu.VMEM((count, D), bf16)]
        + [pltpu.VMEM((FEED_PACK, D), bf16), shape_of((8, D), f32), shape_of((D, D), bf16)],
        [pltpu.VMEM((count, TILE), bf16)] * 2,
        room=OWN_ROOM,
    )(
        place, in_hbm(attended), in_hbm(merged), in_hbm(cotangent), live, proj_bias, gain, bias, down_bias, params, proj,
        near, far, up, down,
    )


def feed_middle_body(
    own, place, second_ref, turned_ref, branch_ref, total_in, back_in, params_ref, sums_in, *refs
):
    weights, (total_ref, back_ref, target_ref, sums_ref, active_s, raise_s) = refs[:-6], refs[-6:]
    core, tp = place[0], place[3]
    sums_ref[...] = sums_in[...]
    if own:
        shard = 2 * tp + core
        units = pl.ds(pl.multiple_of(TILE * core, TILE), TILE)
        up, down = weights[0][:, units], weights[1][units, :]
    else:
        shard = 2 * (1 - tp) + 1 - core
        up, down = weights[0][512:1024, :], weights[0][0:512, :]
    bias = params_ref[2:3, pl.ds(pl.multiple_of(TILE * shard, TILE), TILE)]
    sums_ref[pl.ds(shard, 1), :] = feed_tile(
        up, down, bias, second_ref, turned_ref, branch_ref, total_ref, back_ref, active_s, raise_s, target_ref, False
    )


def feed_middle(own, place, second, turned, branch, total, back, params, sums, weights, cost=COST):
    count = second.shape[0]
    return pl.pallas_call(
        partial(feed_middle_body, own),
        in_specs=[SCALARS] + [RESIDENT] * (7 + len(weights)),
        out_specs=[RESIDENT] * 4,
        out_shape=[pltpu.VMEM((count, D), f32)] * 2 + [pltpu.VMEM((FEED_PACK, D), bf16), shape_of((8, D), f32)],
        scratch_shapes=[pltpu.VMEM((count, TILE), bf16)] * 2,
        input_output_aliases={4: 0, 5: 1},
        compiler_params=pltpu.CompilerParams(vmem_limit_bytes=OTHER_ROOM * 1024 * 1024),
        cost_estimate=cost,
    )(place, second, turned, branch, total, back, params, sums, *weights)


def feed_near_body(
    place, hat_ref, inverse_ref, second_ref, turned_ref, branch_ref, total_in, back_in, norm_gain, params_ref,
    sums_in, near_ref, attended_ref,
    out_ref, grad_residual_ref, attn_ref, keep_ref, proj_send, proj_keep, sums_ref,
    total_s, back_s, active_s, raise_s, attended_s, proj_s, sem,
):
    step = pl.program_id(0)
    core, tp = place[0], place[3]
    fetch = pltpu.make_async_copy(attended_ref, attended_s, sem)

    @pl.when(step == 0)
    def _():
        fetch.start()
        sums_ref[...] = sums_in[...]
        total_s[...] = jnp.zeros_like(total_s)
        shard = 2 * (1 - tp) + core
        bias = params_ref[2:3, pl.ds(pl.multiple_of(TILE * shard, TILE), TILE)]
        sums_ref[pl.ds(shard, 1), :] = feed_tile(
            near_ref[512:1024, :], near_ref[0:512, :], bias, second_ref, turned_ref, branch_ref, total_s, back_s,
            active_s, raise_s, keep_ref, True,
        )

    @pl.when(step >= 1)
    def _():
        here = pl.ds(pl.multiple_of((step - 1) * ROWS, 16), ROWS)
        out_ref[...] = (total_in[here, :] + total_s[here, :]).astype(bf16)
        hat, inverse = hat_ref[here, :], inverse_ref[here, :]
        grad_second = back_in[here, :] + back_s[here, :]
        grad_residual = branch_ref[here, :].astype(f32) + norm_back(grad_second * norm_gain[...], hat, inverse)
        grad_residual_ref[here, :] = grad_residual
        attn_ref[here, :] = grad_residual.astype(bf16)
        sums_ref[4:5, :] += column_sum(grad_residual)
        sums_ref[5:6, :] += column_sum(grad_second * hat)
        sums_ref[6:7, :] += column_sum(grad_second)

    @pl.when(step == pl.num_programs(0) - 1)
    def _():
        fetch.wait()
        proj_s[...] = t_mm(attended_s[...], attn_ref[...]).astype(bf16)
        for target, half in ((proj_send, 1 - core), (proj_keep, core)):
            for other in range(2):
                shard = jnp.where(other == 0, tp, 1 - tp)
                rows = pl.ds(pl.multiple_of(256 * shard + 128 * half, 128), 128)
                target[PROJ_PACK * other : PROJ_PACK * (other + 1), :] = proj_s[rows, :]


def feed_near(place, hat, inverse, second, turned, branch, total, back, gain, params, sums, near, attended):
    count = hat.shape[0]
    blocks = count // ROWS

    def given(columns):
        return pl.BlockSpec((ROWS, columns), lambda i: (jnp.maximum(i - 1, 0), 0))

    return kernel_call(
        feed_near_body,
        (blocks + 1,),
        [SCALARS] + [RESIDENT] * 9 + [whole((8, D)), RESIDENT]
        + [pl.BlockSpec(memory_space=pl.ANY)],
        [given(D)] + [RESIDENT] * 5 + [whole((8, D))],
        [pltpu.HBM((count, D), bf16), pltpu.VMEM((count, D), f32), pltpu.VMEM((count, D), bf16)]
        + [pltpu.VMEM((FEED_PACK, D), bf16)] + [pltpu.VMEM((2 * PROJ_PACK, D), bf16)] * 2
        + [shape_of((8, D), f32)],
        [pltpu.VMEM((count, D), f32)] * 2 + [pltpu.VMEM((count, TILE), bf16)] * 2
        + [pltpu.VMEM((count, D), bf16), pltpu.VMEM((D, D), bf16), pltpu.SemaphoreType.DMA],
        room=NEAR_ROOM,
    )(
        place, hat, inverse, second, turned, branch, total, back, gain, params, sums, near, in_hbm(attended)
    )


def attend_back_body(
    after, attn_ref, qkv_in_ref, weights_ref, padded_ref, inverse_ref, proj_ref,
    merged_ref, grad_residual_ref, qkv_ref, rows_ref, first_in,
    stack_ref, low_ref, sums_ref, vectors_ref, position_ref, first_ref,
    stage, grads, sem,
):
    fetch = pltpu.make_async_copy(first_in, first_ref, sem)

    @pl.when(pl.program_id(0) == pl.num_programs(0) - 1)
    def _():
        fetch.wait()

    @pl.when(pl.program_id(0) == 0)
    def _():
        fetch.start()
        vectors_ref[...] = jnp.zeros_like(vectors_ref)
        sums_ref[...] = jnp.zeros_like(sums_ref)
        position_ref[...] = jnp.zeros_like(position_ref)

    here = pl.ds(pl.multiple_of(pl.program_id(0) * ROWS, 16), ROWS)
    stage[pl.ds(0, ROWS), :] = attn_ref[here, :].astype(f32)
    stage[pl.ds(ROWS, 32), :] = jnp.zeros((32, D), f32)
    real = lax.broadcasted_iota(jnp.int32, (KEYS, 1), 0) < AREA
    padded = jnp.concatenate(
        [jnp.where(real, stage[pl.ds(AREA * w, KEYS), :], 0.0).astype(bf16) for w in range(GROUP)], axis=0
    )
    grad_attended = mm_t(padded, proj_ref[...])
    masks = head_masks()
    empty = jnp.zeros((QUERIES - KEYS, QUAD), bf16)
    kept = {}
    for w in range(GROUP):
        for quad in range(QUADS):
            columns = slice(QUAD * quad, QUAD * (quad + 1))
            values = qkv_in_ref[w, :, 2 * D + QUAD * quad : 2 * D + QUAD * (quad + 1)]
            grad = grad_attended[KEYS * w : KEYS * (w + 1), columns] * inverse_ref[w, :, columns].astype(f32)
            low = grad.astype(bf16)
            taken = (grad * padded_ref[w, :, columns].astype(f32)).astype(bf16)
            both = jnp.concatenate([low, -taken], axis=1)
            change = jnp.concatenate([mm_t(both, block) for block in value_blocks(values, masks)], axis=1)
            grad_scores = (weights_ref[w, quad].astype(f32) * change).astype(bf16)
            position_ref[quad] += grad_scores.astype(f32)
            kept[w, quad] = (low, grad_scores)
    for w in range(GROUP):
        to = pl.ds(AREA * w, AREA)
        for quad in range(QUADS):
            low, grad_scores = kept[w, quad]
            queries = qkv_in_ref[w, :, QUAD * quad : QUAD * (quad + 1)]
            keys = qkv_in_ref[w, :, D + QUAD * quad : D + QUAD * (quad + 1)]
            grad_queries = mm(grad_scores, spread_heads(keys, masks)) * SCALING
            grad_keys = turned_products(queries.T[:, :KEYS], grad_scores)
            grad_values = turned_products(jnp.concatenate([low, empty], axis=0).T[:, :KEYS], weights_ref[w, quad])
            for part, grad in enumerate((grad_queries, grad_keys, grad_values)):
                grads[to, D * part + QUAD * quad : D * part + QUAD * (quad + 1)] = grad[0:AREA]
    stack = grads[pl.ds(0, ROWS), :].astype(bf16)
    stack_ref[here, :] = stack
    sums_ref[...] += column_sum(stack.astype(f32))
    grad_first = (
        mm_t(stack[:, 0:D], qkv_ref[0:D, :])
        + mm_t(stack[:, D : 2 * D], qkv_ref[D : 2 * D, :])
        + mm_t(stack[:, 2 * D :], qkv_ref[2 * D :, :])
    )
    normed, inverse = normalize(merged_ref[...])
    grad_merged = grad_residual_ref[here, :] + norm_back(grad_first * rows_ref[0:1, :], normed, inverse)
    low = grad_merged.astype(bf16)
    low_ref[here, :] = low
    vectors_ref[0:1, :] += column_sum(grad_first * normed)
    vectors_ref[1:2, :] += column_sum(grad_first)
    vectors_ref[2:3, :] += column_sum(low.astype(f32))


def attend_back(after, attn, qkv_in, weights, padded, inverse, proj, merged, grad_residual, qkv, rows, first):
    count = attn.shape[0]
    return kernel_call(
        attend_back_body,
        (count // ROWS,),
        [
            ANYWHERE, RESIDENT, by_windows((QUERIES, 3 * D)), by_windows((QUADS, KEYS, LANES)),
            by_windows((KEYS, D)), by_windows((KEYS, D)), RESIDENT, by_rows(ROWS, D), RESIDENT, RESIDENT, RESIDENT,
            ANYWHERE,
        ],
        [RESIDENT] * 6,
        [
            pltpu.VMEM((count, 3 * D), bf16), pltpu.VMEM((count, D), bf16), shape_of((1, 3 * D), f32),
            shape_of((8, D), f32), shape_of((QUADS, KEYS, LANES), f32), pltpu.VMEM((count, D), bf16),
        ],
        [pltpu.VMEM((ROWS + 32, D), f32), pltpu.VMEM((ROWS + 8, 3 * D), f32), pltpu.SemaphoreType.DMA],
        room=AB_ROOM,
    )(
        after, attn, *[in_hbm(array) for array in (qkv_in, weights, padded, inverse)], proj, in_hbm(merged),
        grad_residual, qkv, rows, in_hbm(first),
    )


def qkv_back_body(place, after, first_ref, stack_ref, hat_in, send_ref, keep_ref, hat_ref, qkv_s, turned_s, sem):
    part = pl.program_id(0)
    fetch = pltpu.make_async_copy(hat_in, hat_ref, sem)

    @pl.when(part == 0)
    def _():
        fetch.start()
        turned_s[...] = first_ref[...].T

    @pl.when(part == pl.num_programs(0) - 1)
    def _():
        fetch.wait()

    core, tp = place[0], place[3]
    qkv_s[...] = mm(turned_s[...], stack_ref[:, pl.ds(pl.multiple_of(D * part, D), D)]).astype(bf16)
    for target, half in ((send_ref, 1 - core), (keep_ref, core)):
        for other in range(2):
            shard = jnp.where(other == 0, tp, 1 - tp)
            base = QKV_PACK * other
            rows = pl.ds(pl.multiple_of(256 * half, 256), 256)
            columns = pl.ds(pl.multiple_of(256 * shard, 256), 256)

            @pl.when(part < 2)
            def _():
                target[base : base + 256, pl.ds(pl.multiple_of(256 * part, 256), 256)] = qkv_s[rows, columns]

            @pl.when(part == 2)
            def _():
                block = qkv_s[rows, columns]
                target[base + 256 : base + 384, 0:256] = block[0:128]
                target[base + 256 : base + 384, 256:512] = block[128:256]


def qkv_back(place, after, first, stack, hat):
    count = stack.shape[0]
    return kernel_call(
        qkv_back_body,
        (3,),
        [SCALARS, ANYWHERE, RESIDENT, RESIDENT, ANYWHERE],
        [RESIDENT] * 3,
        [pltpu.VMEM((2 * QKV_PACK, D), bf16)] * 2 + [pltpu.VMEM((count, MERGE_IN), bf16)],
        [pltpu.VMEM((D, D), bf16), pltpu.VMEM((D, count), bf16), pltpu.SemaphoreType.DMA],
        room=9,
    )(place, after, first, stack, in_hbm(hat))


def merge_back_body(
    place, after, low_ref, hat_ref, merge_ref, params_ref, column_ref, feed_sums_ref, qkv_sums_ref, vectors_ref,
    position_ref,
    send_ref, keep_ref,
    fold_s, all_s, raw_s,
):
    core, tp = place[0], place[3]
    total = vectors_ref[2:3, :]
    pair = jnp.concatenate([split(total), jnp.zeros((14, D), bf16)], axis=0)
    ones = jnp.ones((16, D), bf16)
    raw_s[...] = t_mm(hat_ref[...], low_ref[...])
    all_s[...] = jnp.zeros_like(all_s)
    all_s[0:2, :] = vectors_ref[0:2, :]
    all_s[2:6, :] = feed_sums_ref[4:8, :]
    all_s[6:7, :] = qkv_sums_ref[:, 0:D]
    all_s[7:8, :] = qkv_sums_ref[:, 2 * D :]
    all_s[8:12, :] = feed_sums_ref[0:4, :]
    all_s[16:32, 0:384] = fold_place(position_ref, fold_s)
    for tile in range(2):
        rows = slice(512 * tile, 512 * (tile + 1))
        merge = merge_ref[rows, :]
        scaled = raw_s[rows, :] * merge.astype(f32)
        scaled_high = scaled.astype(bf16)
        scaled_rest = (scaled - scaled_high.astype(f32)).astype(bf16)
        all_s[12 + tile : 13 + tile, :] = (mm_t(ones, scaled_high) + mm_t(ones, scaled_rest))[0:1]
        all_s[14 + tile : 15 + tile, :] = column_sum(mm_t(pair, merge))
    for target, half in ((send_ref, 1 - core), (keep_ref, core)):
        for other in range(2):
            begin = pl.multiple_of(512 * jnp.where(other == 0, tp, 1 - tp) + 256 * half, 256)
            bias = jnp.broadcast_to(params_ref[0:1, pl.ds(1024 + begin, 256)], (16, 256)).astype(bf16)
            gain = column_ref[pl.ds(begin, 256), 0:1]
            block = raw_s[pl.ds(begin, 256), :] * gain + t_mm(bias, pair)
            target[MERGE_PACK * other : MERGE_PACK * (other + 1), :] = block.astype(bf16)
        target[2 * MERGE_PACK :, :] = split(all_s[pl.ds(pl.multiple_of(SUMS * half, SUMS), SUMS), :])


def merge_back(place, after, low, hat, merge, params, column, feed_sums, sums, vectors, position):
    pack = 2 * MERGE_PACK + 2 * SUMS
    return pl.pallas_call(
        merge_back_body,
        in_specs=[SCALARS, ANYWHERE] + [RESIDENT] * 9,
        out_specs=[RESIDENT] * 2,
        out_shape=[pltpu.VMEM((pack, D), bf16), pltpu.VMEM((pack, D), bf16)],
        scratch_shapes=[
            pltpu.VMEM((HEADS, KEYS, 256), f32), pltpu.VMEM((32, D), f32), pltpu.VMEM((MERGE_IN, D), f32),
        ],
        compiler_params=pltpu.CompilerParams(vmem_limit_bytes=14 * 1024 * 1024),
        cost_estimate=COST,
    )(place, after, low, hat, merge, params, column, feed_sums, sums, vectors, position)


def section_back_body(after, low_ref, hat_ref, inverse_ref, merge_ref, params_ref, out_ref, token_ref):
    token_ref[...] = jnp.zeros_like(token_ref)
    scaled = mm_t(low_ref[...], merge_ref[...]) * params_ref[0:1, 0:MERGE_IN]
    out_ref[...] = norm_back(scaled, hat_ref[...].astype(f32), inverse_ref[...]).astype(bf16)


def section_back(after, out, low, hat, inverse, merge, params, begin, steps):
    count = low.shape[0]

    def rows_at(columns):
        return pl.BlockSpec((ROWS, columns), lambda i: (i + begin, 0))

    first = out is None

    def body(*refs):
        section_back_body(*(refs if first else refs[1:]))

    return pl.pallas_call(
        body,
        grid=(steps,),
        in_specs=([] if first else [ANYWHERE])
        + [ANYWHERE, rows_at(D), rows_at(MERGE_IN), rows_at(1), whole((MERGE_IN, D)), whole((24, 2048))],
        out_specs=[rows_at(MERGE_IN), whole((8, 128))],
        out_shape=[pltpu.HBM((count, MERGE_IN), bf16), shape_of((8, 128), f32)],
        input_output_aliases={} if first else {0: 0},
        compiler_params=pltpu.CompilerParams(
            dimension_semantics=("arbitrary",), vmem_limit_bytes=16 * 1024 * 1024
        ),
        cost_estimate=COST,
    )(*([] if first else [out]), after, in_hbm(low), in_hbm(hat), inverse, merge, params)


def spread_matrix():
    place = lax.broadcasted_iota(jnp.int32, (QUERIES, 256), 0)
    lane = lax.broadcasted_iota(jnp.int32, (QUERIES, 256), 1)
    target = place + (SIDE - WINDOW) * (place // WINDOW)
    return jnp.logical_and(lane == target, place < AREA).astype(f32)


def expand_body(params_ref, hat_ref, place_ref, hat_copy, lines_s, out_s, sem):
    save = pltpu.make_async_copy(hat_ref, hat_copy, sem)
    save.start()
    lane = lax.broadcasted_iota(jnp.int32, (384, QUERIES), 0)
    patch = lax.broadcasted_iota(jnp.int32, (384, QUERIES), 1)
    middle = (WINDOW - 1) * (SIDE + 1)
    picked = jnp.logical_and(lane == middle - patch - (SIDE - WINDOW) * (patch // WINDOW), patch < AREA)
    picked = picked.astype(f32).astype(bf16)
    tables = params_ref[8 : 8 + HEADS, 0:384]
    for place in range(AREA):
        offset = SIDE * (place // WINDOW) + place % WINDOW
        lines_s[HEADS * place : HEADS * (place + 1), :] = pltpu.roll(tables, (384 - offset) % 384, 1)
    for begin in range(0, HEADS * AREA, ROWS):
        here = slice(begin, begin + ROWS)
        rows = lines_s[here, :]
        high = rows.astype(bf16)
        rest = rows - high.astype(f32)
        middle_part = rest.astype(bf16)
        low = (rest - middle_part.astype(f32)).astype(bf16)
        out_s[here, :] = mm(high, picked) + mm(middle_part, picked) + mm(low, picked)
    out_s[HEADS * AREA :, :] = jnp.zeros((8 * HEADS, QUERIES), f32)
    for head in range(HEADS):
        lanes = slice(QUERIES * (head % 4), QUERIES * (head % 4 + 1))
        place_ref[head // 4, 0:AREA, lanes] = out_s[pl.ds(head, AREA, stride=HEADS), :]
        place_ref[head // 4, AREA:KEYS, lanes] = jnp.zeros((KEYS - AREA, QUERIES), f32)
    save.wait()


def expand(params, hat):
    return kernel_call(
        expand_body,
        (1,),
        [RESIDENT, RESIDENT],
        [RESIDENT, ANYWHERE],
        [shape_of((QUADS, KEYS, LANES), f32), pltpu.HBM(hat.shape, bf16)],
        [pltpu.VMEM((HEADS * AREA, 384), f32), pltpu.VMEM((HEADS * (AREA + 8), QUERIES), f32), pltpu.SemaphoreType.DMA],
        room=16,
    )(params, hat)


def fold_place(place_ref, stage_s):
    spread = spread_matrix().astype(bf16)
    lines = []
    for head in range(HEADS):
        stage = stage_s.at[head]
        rows = place_ref[head // 4, :, QUERIES * (head % 4) : QUERIES * (head % 4 + 1)]
        rows = jnp.concatenate([rows, jnp.zeros((QUERIES - KEYS, QUERIES), f32)], axis=0).T[:KEYS]
        high = rows.astype(bf16)
        rest = (rows - high.astype(f32)).astype(bf16)
        stage[...] = mm(high, spread) + mm(rest, spread)
        total = jnp.zeros((WINDOW, 384), f32)
        for y in range(WINDOW):
            part = jnp.concatenate(
                [stage[pl.ds(WINDOW * y, WINDOW), :], jnp.zeros((WINDOW, 128), f32)], axis=1
            )
            total += pltpu.roll(part, SIDE * (WINDOW - 1 - y), 1) if y < WINDOW - 1 else part
        line = total[WINDOW - 1 : WINDOW, :]
        for x in range(WINDOW - 1):
            line += pltpu.roll(total[x : x + 1, :], WINDOW - 1 - x, 1)
        lines.append(line)
    return jnp.concatenate(lines, axis=0)


class Ring:
    def __init__(self, place, rows_size):
        self.place = place
        self.rows_size = rows_size
        self.along = rows_size // 4

    def to(self, array, bits):
        return lax.ppermute(array, "rows", [(i, i ^ bits) for i in range(self.rows_size)])

    def core(self, array):
        return self.to(array, 1)

    def x(self, array):
        return self.to(array, 2)

    def z(self, array, step):
        return self.to(array, 4 * step)

    def y(self, array):
        return lax.ppermute(array, "tp", [(0, 1), (1, 0)])

    def xy(self, array):
        pairs = [(2 * i + t, 2 * (i ^ 2) + 1 - t) for i in range(self.rows_size) for t in range(2)]
        return lax.ppermute(array, ("rows", "tp"), pairs)


def rows_of(array, begin, rows):
    return lax.dynamic_slice_in_dim(array, begin, rows, 0).astype(f32)


def stage(body, place, after, rows, *operands, cost=COST, scratch=()):
    return plain_call_after(
        body, [pltpu.VMEM((count, D), bf16) for count in rows], place, after, operands, room=STAGE_ROOM, cost=cost,
        scratch=scratch,
    )


def added(refs, begin, rows):
    here = pl.ds(pl.multiple_of(begin, 16), rows)
    total = refs[0][here, :].astype(f32)
    for ref in refs[1:]:
        total = total + ref[here, :].astype(f32)
    return total


def part(ref, begin, rows):
    return ref.at[begin : begin + rows, :]


FEED_BLOCKS = ((0, 256), (256, 256), (512, 64))


def feed_first_body(place, own_keep, own_got, other_keep, other_got, to_y, to_x, to_both, kept):
    x = place[1]
    own, other = (own_keep, own_got), (other_keep, other_got)
    for target, blocks, side in ((to_y, other, x), (to_x, own, 1 - x), (to_both, other, 1 - x), (kept, own, x)):
        target[0:256, :] = added(blocks, 256 * side, 256).astype(bf16)
        target[256:512, :] = added(blocks, 512 + 256 * side, 256).astype(bf16)


def feed_proj_body(place, keep, got, *refs):
    x = place[1]
    for target, shard, side in zip(refs[-4:], (1, 0, 1, 0), (x, 1 - x, 1 - x, x)):
        target[512:576, :] = added((keep, got), PROJ_PACK * shard + 64 * side, 64).astype(bf16)


def feed_proj(place, keep, got, outs):
    return pl.pallas_call(
        feed_proj_body,
        in_specs=[SCALARS] + [RESIDENT] * 6,
        out_specs=[RESIDENT] * 4,
        out_shape=[pltpu.VMEM(out.shape, bf16) for out in outs],
        input_output_aliases={3: 0, 4: 1, 5: 2, 6: 3},
        compiler_params=pltpu.CompilerParams(vmem_limit_bytes=STAGE_ROOM * 1024 * 1024),
        cost_estimate=COST,
    )(place, keep, got, *outs)


def feed_second_body(place, *refs):
    blocks, outs = refs[:4], refs[4:]
    for step, out in enumerate(outs):
        offset = 0
        for begin, size in FEED_BLOCKS:
            span = size // len(outs)
            to = begin + (place[2] ^ step) * span
            out[offset : offset + span, :] = added(blocks, to, span).astype(bf16)
            offset += span


def total_body(place, *refs):
    refs[-1][...] = added(refs[:-1], 0, refs[-1].shape[0]).astype(bf16)


def beside_body(place, *refs):
    rows = refs[0].shape[0]
    for index, ref in enumerate(refs[:-1]):
        refs[-1][rows * index : rows * (index + 1), :] = ref[...]


def qkv_first_body(place, keep, got, to_y, to_x, to_both, kept):
    x = place[1]
    for target, other, side in ((to_y, 1, x), (to_x, 0, 1 - x), (to_both, 1, 1 - x), (kept, 0, x)):
        target[...] = added((keep, got), QKV_PACK * other + 192 * side, 192).astype(bf16)


def merge_first_body(place, keep, got, to_y, to_x, to_both, kept, sums_s):
    x = place[1]
    sums_s[...] = joined(keep[512:544, :]) + joined(got[512:544, :])
    for target, other, side in ((to_y, 1, x), (to_x, 0, 1 - x), (to_both, 1, 1 - x), (kept, 0, x)):
        target[0:128, :] = added((keep, got), MERGE_PACK * other + 128 * side, 128).astype(bf16)
        target[128:144, :] = split(sums_s[pl.ds(pl.multiple_of(8 * side, 8), 8), :])


def last_second_body(place, qkv_sum, *refs):
    blocks, outs = refs[:4], refs[4:]
    vectors = split(sum(joined(ref[128:144, :]) for ref in blocks))
    wide, narrow = 192 // len(outs), 128 // len(outs)
    for step, out in enumerate(outs):
        to = place[2] ^ step
        out[0:wide, :] = added((qkv_sum,), to * wide, wide).astype(bf16)
        out[wide : wide + narrow, :] = added(blocks, to * narrow, narrow).astype(bf16)
        out[wide + narrow :, :] = vectors


def merge_total_body(place, *refs):
    blocks, (out, vectors) = refs[:-2], refs[-2:]
    rows = out.shape[0]
    out[...] = added(blocks, 0, rows).astype(bf16)
    vectors[...] = split(sum(joined(ref[rows : rows + 16, :]) for ref in blocks))


def last_beside_body(place, vectors, *refs):
    rows = refs[0].shape[0]
    for index, ref in enumerate(refs[:-1]):
        refs[-1][rows * index : rows * (index + 1), :] = ref[...]
    refs[-1][rows * (len(refs) - 1) :, :] = vectors[...]


def in_order(place, near, far, stage, rows, along):
    piece = sum(rows) // 2 // along
    for side, ref in ((place[1], near), (1 - place[1], far)):
        for step in range(along):
            begin, offset = 0, piece * step
            for size in rows:
                span = size // 2 // along
                to = begin + side * (size // 2) + (place[2] ^ step) * span
                stage[pl.ds(pl.multiple_of(to, 16), span), :] = ref[offset : offset + span, :]
                begin += size
                offset += span


def feed_unpack_body(along, place, near, far, core_near, core_far, down_ref, up_ref, proj_ref, token_ref, stage):
    token_ref[...] = jnp.zeros_like(token_ref)
    for target, mine, beside in ((place[0], near, far), (1 - place[0], core_near, core_far)):
        in_order(place, mine, beside, stage, (512, 512, PROJ_PACK), along)
        wide = pl.ds(pl.multiple_of(512 * target, 512), 512)
        down_ref[wide, :] = stage[0:512, :].astype(f32)
        proj_ref[pl.ds(pl.multiple_of(128 * target, 128), 128), :] = stage[1024:1152, :].astype(f32)
        up_ref[:, wide] = stage[512:1024, :].astype(f32)


def feed_unpack(along, place, after, parts):
    return plain_call_after(
        partial(feed_unpack_body, along),
        [pltpu.HBM((FFN // 2, D), f32), pltpu.HBM((D, FFN // 2), f32), pltpu.HBM((D // 2, D), f32), shape_of((8, 128), f32)],
        place,
        after,
        parts,
        scratch=[pltpu.VMEM((FEED_PACK + PROJ_PACK, D), bf16)],
        room=14,
    )


def last_unpack_body(along, place, mine, beside, core_mine, core_beside, qkv_ref, merge_ref, *refs):
    vectors, stage, all_s = refs[:-2], refs[-2], refs[-1]
    rows = mine.shape[0] - 16
    for target, near, far in ((place[0], mine, beside), (1 - place[0], core_mine, core_beside)):
        in_order(place, near, far, stage, (QKV_PACK, MERGE_PACK), along)
        for side, ref in ((place[1], near), (1 - place[1], far)):
            all_s[pl.ds(pl.multiple_of(SUMS * target + 8 * side, 8), 8), :] = joined(ref[rows:, :])
        begin = pl.multiple_of(256 * target, 256)
        for part in range(2):
            qkv_ref[part, pl.ds(begin, 256), :] = stage[0:256, 256 * part : 256 * part + 256].astype(f32)
        qkv_ref[2, pl.ds(begin, 128), :] = stage[256:384, 0:256].astype(f32)
        qkv_ref[2, pl.ds(begin + 128, 128), :] = stage[256:384, 256:512].astype(f32)
        merge_ref[pl.ds(begin, 256), :] = stage[384:640, :].astype(f32)
    write_vectors(place[3], all_s, vectors)


VECTORS = [(1, D)] * 6 + [(2, D // 2), (1, FFN // 2), (1, MERGE_IN // 2), (1, MERGE_IN // 2), (HEADS // 2, SIDE * SIDE)]


def write_vectors(tp, sums, refs):
    for row in range(6):
        refs[row][...] = sums[row : row + 1, :]
    columns = pl.ds(pl.multiple_of(256 * tp, 256), 256)
    refs[6][...] = sums[6:8, columns]
    refs[7][:, 0:512] = sums[pl.ds(8 + 2 * tp, 1), :]
    refs[7][:, 512:1024] = sums[pl.ds(9 + 2 * tp, 1), :]
    refs[8][...] = sums[pl.ds(12 + tp, 1), :]
    refs[9][...] = sums[pl.ds(14 + tp, 1), :]
    refs[10][...] = sums[pl.ds(pl.multiple_of(16 + 8 * tp, 8), 8), 0 : SIDE * SIDE]


def last_unpack(along, place, *parts):
    outs = plain_call(
        partial(last_unpack_body, along),
        [pltpu.HBM(shape, f32) if shape[-2] >= 128 else shape_of(shape, f32) for shape in [(3, D, D // 2), (MERGE_IN // 2, D)] + VECTORS],
        (place, *parts),
        scratch=[pltpu.VMEM((QKV_PACK + MERGE_PACK, D), bf16), pltpu.VMEM((2 * SUMS, D), f32)],
    )
    return outs[0], outs[1], outs[2:]


def fetch_by_tp(ring, piece_of):
    near = ring.y(piece_of)
    return near, ring.core(near)


def plain_pieces(tp_size, weights, params):
    merge, qkv, proj, up, down = [
        lax.all_gather(array, "tp", axis=axis, tiled=True) for array, axis in zip(weights, (0, 2, 0, 1, 0))
    ]
    gain, bias, qv, up_bias, table = [
        lax.all_gather(array, "tp", axis=axis, tiled=True) for array, axis in zip(params, (0, 0, 1, 0, 1))
    ]

    def shard(array, axis, which):
        size = array.shape[axis] // 2
        return lax.slice_in_dim(array, which * size, (which + 1) * size, axis=axis)

    def rows_of(which):
        rows = jnp.zeros((PARAMS, D), f32)
        rows = rows.at[0].set(shard(gain.astype(f32), 0, which)).at[1].set(shard(bias.astype(f32), 0, which))
        rows = rows.at[2].set(shard(qv, 1, which).reshape(-1)).at[3:5].set(shard(up_bias, 0, which).reshape(2, D))
        return rows.at[8:16, : SIDE * SIDE].set(shard(table, 1, which).T)

    merge_other = shard(merge, 0, 1)
    qkv_other = shard(qkv, 2, 1).reshape(3 * D, 256)
    proj_other, up_other, down_other = shard(proj, 0, 1), shard(up, 1, 1), shard(down, 0, 1)

    def qkv_piece(half):
        rows = qkv_other[768 * half : 768 * half + 768]
        return jnp.concatenate(
            [jnp.concatenate([rows[:384], rows[384:]], axis=1), proj_other[128 * half : 128 * half + 128]], axis=0
        )

    def feed_piece(half):
        tile = slice(512 * half, 512 * half + 512)
        return jnp.concatenate([down_other[tile], up_other[:, tile]], axis=0)

    own = (
        shard(merge, 0, 0), shard(qkv, 2, 0).reshape(3 * D, 256), shard(proj, 0, 0), shard(up, 1, 0), shard(down, 0, 0)
    )
    return own, (rows_of(0), split(rows_of(1))), (merge_other[:256], merge_other[256:]), (qkv_piece(0), qkv_piece(1)), (feed_piece(0), feed_piece(1))


def sum_plainly(tp_size, feed_packs, proj_packs, qkv_packs, merge_packs):
    feed_packs, proj_packs, qkv_packs, merge_packs = lax.psum(
        (feed_packs, proj_packs, qkv_packs, merge_packs), ("rows", "tp")
    )
    own_send, own_keep, other_send, other_keep = feed_packs
    order = [own_keep, own_send, other_keep, other_send]
    down = jnp.concatenate([block[0:512] for block in order], axis=0)
    up = jnp.concatenate([block[512:1024] for block in order], axis=1)

    def blocks(packs, size):
        send, keep = packs
        return [keep[:size], send[:size], keep[size : 2 * size], send[size : 2 * size]]

    def qkv_rows(block):
        return jnp.stack(
            [block[0:256, 0:256], block[0:256, 256:512], jnp.concatenate([block[256:384, 0:256], block[256:384, 256:512]])]
        )

    order = blocks(qkv_packs, QKV_PACK)
    qkv = jnp.concatenate(
        [jnp.concatenate([qkv_rows(order[2 * shard + half]) for half in range(2)], axis=1) for shard in range(2)], axis=2
    )
    proj = jnp.concatenate(blocks(proj_packs, PROJ_PACK), axis=0)
    merge = jnp.concatenate(blocks(merge_packs, MERGE_PACK), axis=0)
    sums = jnp.concatenate([joined(merge_packs[1][2 * MERGE_PACK :]), joined(merge_packs[0][2 * MERGE_PACK :])], axis=0)
    index = lax.axis_index("tp")

    def own(array, axis):
        size = array.shape[axis] // tp_size
        return lax.dynamic_slice_in_dim(array, index * size, size, axis).astype(f32)

    vectors = [sums[row] for row in range(6)] + [
        own(sums[6:8], 1), own(sums[8:12].reshape(-1), 0), own(sums[12:14].reshape(-1), 0),
        own(sums[14:16].reshape(-1), 0), own(sums[16:32, : SIDE * SIDE], 0),
    ]
    return own(down, 0), own(up, 1), own(qkv, 2), own(proj, 0), own(merge, 0), vectors


def per_device(
    rows_size, tp_size,
    section_rows, window_mask, cotangent, merge_weight, merge_gain, merge_bias, norm1_gain, norm1_bias,
    qkv_weight, qv_bias, bias_table, proj_weight, proj_bias, norm2_gain, norm2_bias,
    up_weight, up_bias, down_weight, down_bias,
):
    fast = tp_size == 2 and rows_size in (8, 16)
    count = cotangent.shape[0]
    index, tp = lax.axis_index("rows"), lax.axis_index("tp")
    place = jnp.stack([index & 1, (index >> 1) & 1, index >> 2, tp]).astype(jnp.int32)
    ring = Ring(place, rows_size)
    if fast:
        flat_qkv = qkv_weight.reshape(3 * D, D // 2)
        merge_piece = pack_merge(place, merge_weight)
        merge_near = ring.y(merge_piece)
        params, piece = pack_params(
            place, merge_piece, merge_gain, merge_bias, qv_bias, up_bias[None], bias_table.T
        )
        others = ring.y(piece)
        mask, live = masks_of(place, params, window_mask, count)
        qkv_piece = gate(pack_qkv(place, (mask,), flat_qkv, proj_weight), others, merge_near)
        qkv_near = ring.y(qkv_piece)
        hat, inverse = section_norm(qkv_piece, section_rows)
        merge_far = ring.core(merge_near)
        kernel_place = place
    else:
        (merge_weight, flat_qkv, proj_weight, up_weight, down_weight), (params, others), merge_pair, qkv_pair, feed_pair = plain_pieces(
            tp_size,
            (merge_weight, qkv_weight, proj_weight, up_weight, down_weight),
            (merge_gain, merge_bias, qv_bias, up_bias, bias_table),
        )
        (merge_near, merge_far), (qkv_near, qkv_far), (feed_near_piece, feed_far_piece) = merge_pair, qkv_pair, feed_pair
        kernel_place = jnp.zeros_like(place)
        hat, inverse = section_norm(params, section_rows)
        own_mask = lax.dynamic_slice_in_dim(window_mask, tp * count, count, 0)
        mask, live = masks_of(kernel_place, params, own_mask, count)

    merged, first, first_copy, merge_full, params, column = merge_rows(
        kernel_place, hat, merge_weight, merge_near, merge_far, params, others, norm1_gain[None], norm1_bias[None]
    )
    position, hat = expand(params, hat)
    if fast:
        (feed_piece,) = plain_call_after(
            pack_feed_body, [shape_of((FEED_PACK, D), bf16)], place, (position, qkv_near), (up_weight, down_weight)
        )
        qkv_far = ring.core(qkv_near)
        feed_near_piece = ring.y(feed_piece)
        feed_far_piece = ring.core(feed_near_piece)
    qkv_rows, weights, attended, padded, inverse_sums, qkv_full = attend(
        kernel_place, first, flat_qkv, qkv_near, qkv_far, params, position, mask
    )
    rows = [row[None] for row in (proj_bias, norm2_gain, norm2_bias, down_bias)]
    second_hat, second_inverse, total, back, second, turned, branch, own_send, feed_sums, proj_full = feed_own(
        kernel_place, attended, merged, cotangent, live, *rows, params, proj_weight, qkv_near, qkv_far,
        up_weight, down_weight,
    )
    total, back, own_keep, feed_sums = feed_middle(
        True, kernel_place, second, turned, branch, total, back, params, feed_sums, (up_weight, down_weight), LONG
    )
    total, back, other_send, feed_sums = feed_middle(
        False, kernel_place, second, turned, branch, total, back, params, feed_sums, (feed_far_piece,)
    )
    block_out, grad_residual, attn, other_keep, proj_send, proj_keep, feed_sums = feed_near(
        kernel_place, second_hat, second_inverse, second, turned, branch, total, back, rows[1], params, feed_sums, feed_near_piece,
        attended,
    )
    after = feed_sums
    if fast:
        own_got, other_got, proj_got = ring.core(own_send), ring.core(other_send), ring.core(proj_send)
        outs = stage(feed_first_body, place, feed_sums, (576,) * 4, own_keep, own_got, other_keep, other_got)
        to_y, to_x, to_both, feed_kept = feed_proj(place, proj_keep, proj_got, outs)
        feed_from = (ring.y(to_y), ring.x(to_x), ring.xy(to_both))
        after = to_y
    stack, low, sums, vectors, position_grad, first_near = attend_back(
        after, attn, qkv_rows, weights, padded, inverse_sums, proj_full, merged, grad_residual, qkv_full,
        norm1_gain[None], first_copy,
    )
    qkv_send, qkv_keep, hat_near = qkv_back(kernel_place, sums, first_near, stack, hat)
    after = sums
    if fast:
        along = ring.along
        qkv_got = ring.core(qkv_send)
        span = 576 // along
        feed_parts = stage(
            feed_second_body, place, qkv_send, (span,) * along, feed_kept, *feed_from, cost=LONG
        )
        feed_got = [ring.z(feed_parts[step], step) for step in range(1, along)]
        to_y, to_x, to_both, qkv_kept = stage(
            qkv_first_body, place, feed_parts[0], (192,) * 4, qkv_keep, qkv_got
        )
        qkv_from = (ring.y(to_y), ring.x(to_x), ring.xy(to_both))
        after = to_y
    merge_send, merge_keep = merge_back(
        kernel_place, after, low, hat_near, merge_full, params, column, feed_sums, sums, vectors, position_grad
    )
    if fast:
        merge_got = ring.core(merge_send)
        (feed_total,) = stage(total_body, place, merge_send, (span,), feed_parts[0], *feed_got, cost=LONG)
        feed_all = [feed_total] + [ring.z(feed_total, step) for step in range(1, along)]
        (qkv_sum,) = stage(total_body, place, feed_total, (192,), qkv_kept, *qkv_from)
        to_y, to_x, to_both, merge_kept = stage(
            merge_first_body, place, qkv_sum, (144,) * 4, merge_keep, merge_got, scratch=[pltpu.VMEM((SUMS, D), f32)]
        )
        (feed_mine,) = stage(beside_body, place, to_y, (span * along,), *feed_all)
        feed_beside = ring.x(feed_mine)
        last_span = 320 // along
        last_parts = stage(
            last_second_body, place, feed_mine, (last_span + 16,) * along, qkv_sum,
            merge_kept, ring.y(to_y), ring.x(to_x), ring.xy(to_both),
        )
        last_got = [ring.z(last_parts[step], step) for step in range(1, along)]
        steps = count // ROWS
        section_grad, token = section_back(last_parts[0], None, low, hat, inverse, merge_full, params, 0, steps // 2)
        last_total, vectors = stage(
            merge_total_body, place, token, (last_span, 16), *([last_parts[0]] + last_got), cost=LONG
        )
        last_all = [last_total] + [ring.z(last_total, step) for step in range(1, along)]
        (last_near,) = stage(
            last_beside_body, place, feed_beside, (336,), vectors, *last_all, cost=LONG
        )
        last_far = ring.x(last_near)
        feed_cores = ring.core(feed_mine), ring.core(feed_beside)
        section_grad, token = section_back(
            last_near, section_grad, low, hat, inverse, merge_full, params, steps // 2, steps - steps // 2
        )
        down_grad, up_grad, proj_grad, token = feed_unpack(
            along, place, token, (feed_mine, feed_beside, *feed_cores)
        )
        (last_far,) = stage(beside_body, place, token, (336,), last_far)
        qkv_grad, merge_grad, vectors = last_unpack(
            along, place, last_near, last_far, ring.core(last_near), ring.core(last_far)
        )
    else:
        section_grad, _ = section_back(low, None, low, hat, inverse, merge_full, params, 0, count // ROWS)
        down_grad, up_grad, qkv_grad, proj_grad, merge_grad, vectors = sum_plainly(
            tp_size, (own_send, own_keep, other_send, other_keep), (proj_send, proj_keep), (qkv_send, qkv_keep),
            (merge_send, merge_keep),
        )
    norm1_gain_grad, norm1_bias_grad, proj_bias_grad, norm2_gain_grad, norm2_bias_grad, down_bias_grad = [
        row.reshape(D) for row in vectors[0:6]
    ]
    qv_grad, up_bias_grad, gain_grad, bias_grad, table_grad = vectors[6:]
    return (
        block_out, section_grad, merge_grad, gain_grad.reshape(-1), bias_grad.reshape(-1),
        norm1_gain_grad, norm1_bias_grad, qkv_grad, qv_grad, table_grad.T, proj_grad, proj_bias_grad,
        norm2_gain_grad, norm2_bias_grad, up_grad, up_bias_grad.reshape(-1), down_grad, down_bias_grad,
    )


def solution(mesh):
    rows_size, tp_size = mesh.shape["rows"], mesh.shape["tp"]
    both = ("rows", "tp")
    return jax.shard_map(
        partial(per_device, rows_size, tp_size),
        mesh=mesh,
        in_specs=(
            P(both, None), P("rows"), P(both, None), P("tp", None), P("tp"), P("tp"), P(), P(),
            P(None, None, "tp"), P(None, "tp"), P(None, "tp"), P("tp", None), P(), P(), P(),
            P(None, "tp"), P("tp"), P("tp", None), P(),
        ),
        out_specs=(
            P(both, None), P(both, None), P("tp", None), P("tp"), P("tp"), P(), P(),
            P(None, None, "tp"), P(None, "tp"), P(None, "tp"), P("tp", None), P(), P(), P(),
            P(None, "tp"), P("tp"), P("tp", None), P(),
        ),
        check_vma=False,
    )
```
